256 devices in a mesh: grp: 4 (over z_lo), row: 8 (over z_hi, x), col: 8 (over y, core).
Axes of the slice: x: 4, y: 4, z: 8 (z_hi: 2, z_lo: 4; z = z_hi * 4 + z_lo), core: 2. Of those that a mesh axis runs over, the one named last changes fastest.
Arguments:
- dec_input: bfloat16 [3, 8, 64, 128, 128], P(None, None, 'row', 'col'), may hold values from -6 to 6
- target: bfloat16 [3, 3, 8, 64, 128], P(None, None, 'col', 'row'), may hold values from -5 to 5
- conv_first: bfloat16 [3456, 128], replicated, may hold values from -0.109375 to 0.109375
- conv_second: bfloat16 [3456, 128], replicated, may hold values from -0.109375 to 0.109375
- rgb_weight: bfloat16 [3, 128], replicated, may hold values from -0.5 to 0.5
- vgg_first: bfloat16 [27, 64], replicated, may hold values from -1.25 to 1.25
- vgg_second: bfloat16 [576, 64], replicated, may hold values from -0.25 to 0.25
- vgg_third: bfloat16 [576, 128], replicated, may hold values from -0.25 to 0.25
Outputs:
- grad_first: float32 [442368], P(('grp', 'row', 'col'))
- grad_second: float32 [442368], P(('grp', 'row', 'col'))
The draws below stay inside these ranges and needn't reach their ends.
All inputs are finite; a program needn't handle non-finite values.
Results may differ from the reference program's by a relative error of at most 0.015.
Values may be sent and summed in bfloat16 or wider, within the bound.
A program may use at most 128 MiB of HBM per device.

```python
import jax
import jax.numpy as jnp
from jax import lax

C = 128
V1 = 64
V2 = 128
FD = 8
H = 64
W = 128


def block_levels(rng, dims, shards, least, top_value):
    def one(axis_at, parts):
        heights = jax.random.uniform(jax.random.fold_in(jax.random.fold_in(rng, 6), axis_at), (parts,), jnp.float32, least / len(shards), top_value / len(shards))
        return jnp.repeat(jnp.exp(heights), dims[axis_at] // parts).reshape((-1,) + (1,) * (len(dims) - axis_at - 1))

    loudness = one(*shards[0])
    for cut in shards[1:]:
        loudness = loudness * one(*cut)
    return loudness


def normal_values(key, dims, width, limit, cuts=(), dtype=jnp.bfloat16):
    loudness = block_levels(key, dims, cuts, -0.22, 0.18) if cuts else 1.0
    entries = jax.random.normal(key, dims, jnp.float32) * width * loudness
    return jnp.minimum(jnp.maximum(entries, -limit), limit).astype(dtype)


def setup_inputs(seed: int = 0) -> dict:
    key_of = jax.random.split(jax.random.key(seed), 9)
    return {
        "dec_input": normal_values(key_of[0], (3, FD, H, W, C), 1.0, 6.0, ((2, 8), (3, 8))),
        "target": normal_values(key_of[1], (3, 3, FD, H, W), 1.0, 5.0, ((2, 8), (3, 8))),
        "conv_first": normal_values(key_of[2], (27 * C, C), (27 * C) ** -0.5, 0.109375),
        "conv_second": normal_values(key_of[3], (27 * C, C), (27 * C) ** -0.5, 0.109375),
        "rgb_weight": normal_values(key_of[4], (3, C), C ** -0.5, 0.5),
        "vgg_first": normal_values(key_of[5], (27, V1), 27 ** -0.5, 1.25),
        "vgg_second": normal_values(key_of[6], (9 * V1, V1), (9 * V1) ** -0.5, 0.25),
        "vgg_third": normal_values(key_of[7], (9 * V1, V2), (9 * V1) ** -0.5, 0.25),
    }


gelu_scale = 0.7978845608028654
gelu_cubic = 0.044715


def silu_slope(preact):
    sigmoid_value = jax.nn.sigmoid(preact)
    return sigmoid_value * (1.0 + preact * (1.0 - sigmoid_value))


def gelu_value(preact):
    return 0.5 * preact * (1.0 + jnp.tanh(gelu_scale * (preact + gelu_cubic * preact * preact * preact)))


def gelu_slope(preact):
    inner_tanh = jnp.tanh(gelu_scale * (preact + gelu_cubic * preact * preact * preact))
    return 0.5 * (1.0 + inner_tanh) + 0.5 * preact * (1.0 - inner_tanh * inner_tanh) * gelu_scale * (1.0 + 3.0 * gelu_cubic * preact * preact)


def conv_plane(images, weight):
    source_width = weight.shape[0] // 9
    kernel = weight.reshape(3, 3, source_width, weight.shape[1]).astype(jnp.float32)
    return lax.conv_general_dilated(images.astype(jnp.float32), kernel, (1, 1), "SAME", dimension_numbers=("NHWC", "HWIO", "NHWC"), precision=lax.Precision.HIGHEST, preferred_element_type=jnp.float32)


def flipped_plane(weight):
    source_width = weight.shape[0] // 9
    target_width = weight.shape[1]
    kernel = weight.reshape(3, 3, source_width, target_width)[::-1, ::-1]
    return jnp.transpose(kernel, (0, 1, 3, 2)).reshape(9 * target_width, source_width)


def conv_volume(volume, weight):
    source_width = weight.shape[0] // 27
    kernel = weight.reshape(3, 3, 3, source_width, weight.shape[1]).astype(jnp.float32)
    return lax.conv_general_dilated(volume[None].astype(jnp.float32), kernel, (1, 1, 1), "SAME", dimension_numbers=("NDHWC", "DHWIO", "NDHWC"), precision=lax.Precision.HIGHEST, preferred_element_type=jnp.float32)[0]


def flipped_volume(weight):
    source_width = weight.shape[0] // 27
    target_width = weight.shape[1]
    kernel = weight.reshape(3, 3, 3, source_width, target_width)[::-1, ::-1, ::-1]
    return jnp.transpose(kernel, (0, 1, 2, 4, 3)).reshape(27 * target_width, source_width)


def weight_gradient(source_cells, output_delta):
    frame_count, row_count, col_count, source_width = source_cells.shape
    padded = jnp.pad(source_cells, ((1, 1), (1, 1), (1, 1), (0, 0)))
    flat_delta = output_delta.reshape(-1, output_delta.shape[-1]).astype(jnp.float32)
    partial_terms = []
    for frame_step in range(3):
        for row_step in range(3):
            for col_step in range(3):
                shifted = padded[frame_step:frame_step + frame_count, row_step:row_step + row_count, col_step:col_step + col_count]
                shifted = shifted.reshape(-1, source_width).astype(jnp.float32)
                partial_terms.append(jnp.dot(shifted.T, flat_delta, precision=lax.Precision.HIGHEST, preferred_element_type=jnp.float32))
    return jnp.concatenate(partial_terms, axis=0).reshape(-1)


def pixel_gradient(images, guides, row_keep, vgg_first, vgg_second, vgg_third):
    cell_keep = row_keep[None, :, None, None]
    pool_keep = row_keep[::2][None, :, None, None]

    def features(source):
        first_plane = conv_plane(source, vgg_first)
        first_act = (gelu_value(first_plane) * cell_keep).astype(jnp.bfloat16)
        second_plane = conv_plane(first_act, vgg_second)
        second_feat = gelu_value(second_plane) * cell_keep
        image_count, row_count, col_count, channel_count = second_feat.shape
        pooled = second_feat.reshape(image_count, row_count // 2, 2, col_count // 2, 2, channel_count)
        pooled = (jnp.sum(pooled, axis=(2, 4)) * 0.25).astype(jnp.bfloat16)
        third_plane = conv_plane(pooled, vgg_third)
        third_feat = gelu_value(third_plane) * pool_keep
        return first_plane, second_plane, second_feat, third_plane, third_feat

    first_plane, second_plane, second_feat, third_plane, third_feat = features(images)
    guide_parts = features(guides)
    guide_second = guide_parts[2]
    guide_third = guide_parts[4]
    third_delta = ((64.0 / third_feat.shape[-1]) * (third_feat - guide_third) * gelu_slope(third_plane)).astype(jnp.bfloat16)
    pooled_grad = conv_plane(third_delta, flipped_plane(vgg_third))
    image_count, half_rows, half_cols, channel_count = pooled_grad.shape
    spread = jnp.broadcast_to(pooled_grad[:, :, None, :, None, :], (image_count, half_rows, 2, half_cols, 2, channel_count))
    spread = spread.reshape(image_count, 2 * half_rows, 2 * half_cols, channel_count)
    second_delta = ((0.25 * spread + (16.0 / channel_count) * (second_feat - guide_second)) * gelu_slope(second_plane) * cell_keep).astype(jnp.bfloat16)
    first_grad = conv_plane(second_delta, flipped_plane(vgg_second))
    first_delta = (first_grad * gelu_slope(first_plane) * cell_keep).astype(jnp.bfloat16)
    direct_term = (1.0 / 6.0) * (images.astype(jnp.float32) - guides.astype(jnp.float32))
    return conv_plane(first_delta, flipped_plane(vgg_first)) + direct_term


def reference(dec_input, target, conv_first, conv_second, rgb_weight, vgg_first, vgg_second, vgg_third):
    video_cells = dec_input.reshape(3 * FD, H, W, C)
    first_pre = conv_volume(video_cells, conv_first)
    first_out = jax.nn.silu(first_pre).astype(jnp.bfloat16)
    second_pre = conv_volume(first_out, conv_second)
    second_out = jax.nn.silu(second_pre).astype(jnp.bfloat16)
    colour = jnp.einsum("fhwc,kc->kfhw", second_out.astype(jnp.float32), rgb_weight.astype(jnp.float32), precision=lax.Precision.HIGHEST).astype(jnp.bfloat16)
    images = jnp.transpose(colour, (1, 2, 3, 0))
    guides = jnp.transpose(target.reshape(3, 3 * FD, H, W), (1, 2, 3, 0))
    row_keep = jnp.ones((H,), jnp.float32)
    pixel_grad = pixel_gradient(images, guides, row_keep, vgg_first, vgg_second, vgg_third)
    pixel_grad = jnp.transpose(pixel_grad, (3, 0, 1, 2))
    hidden_grad = jnp.einsum("kfhw,kc->fhwc", pixel_grad, rgb_weight.astype(jnp.float32), precision=lax.Precision.HIGHEST)
    decoder_second = (hidden_grad * silu_slope(second_pre)).astype(jnp.bfloat16)
    grad_second = weight_gradient(first_out, decoder_second)
    hidden_back = conv_volume(decoder_second, flipped_volume(conv_second))
    decoder_hidden = (hidden_back * silu_slope(first_pre)).astype(jnp.bfloat16)
    grad_first = weight_gradient(video_cells, decoder_hidden)
    return grad_first, grad_second
```

```python
import jax
import jax.numpy as jnp
from jax import lax
from jax.experimental import pallas as pl
from jax.experimental.pallas import tpu as pltpu
from jax.sharding import PartitionSpec as P

MESH = pl.DeviceIdType.MESH

gelu_scale = 0.7978845608028654
gelu_cubic = 0.044715


def padded_2(shard, sides, width):
    for axis, dim in sides:
        count, length = (lax.axis_size(axis), shard.shape[dim])
        up = [(i, (i + 1) % count) for i in range(count - 1)]
        down = [(j, i) for i, j in up]
        last = lax.slice_in_dim(shard, length - width, length, axis=dim)
        first = lax.slice_in_dim(shard, 0, width, axis=dim)
        before = lax.ppermute(last, axis, up)
        after = lax.ppermute(first, axis, down)
        shard = jnp.concatenate([before, shard, after], axis=dim)
    return shard


def shortened(shard):

    def short(part):
        return part.astype(jnp.bfloat16) if part.dtype == jnp.float32 else part

    return jax.tree.map(short, shard)


def silu_slope(preact):
    sigmoid_value = jax.nn.sigmoid(preact)
    return sigmoid_value * (1.0 + preact * (1.0 - sigmoid_value))


def gelu_value(preact):
    return (
        0.5
        * preact
        * (1.0 + jnp.tanh(gelu_scale * (preact + gelu_cubic * preact * preact * preact)))
    )


def gelu_slope(preact):
    inner_tanh = jnp.tanh(gelu_scale * (preact + gelu_cubic * preact * preact * preact))
    return 0.5 * (1.0 + inner_tanh) + 0.5 * preact * (
        1.0 - inner_tanh * inner_tanh
    ) * gelu_scale * (1.0 + 3.0 * gelu_cubic * preact * preact)


def conv_plane(images, weight):
    source_width = weight.shape[0] // 9
    kernel = weight.reshape(3, 3, source_width, weight.shape[1])
    return lax.conv_general_dilated(
        images,
        kernel,
        (1, 1),
        "SAME",
        dimension_numbers=("NHWC", "HWIO", "NHWC"),
        preferred_element_type=jnp.float32,
    )


def flipped_plane(weight):
    source_width = weight.shape[0] // 9
    target_width = weight.shape[1]
    kernel = weight.reshape(3, 3, source_width, target_width)[::-1, ::-1]
    return jnp.transpose(kernel, (0, 1, 3, 2)).reshape(9 * target_width, source_width)


def conv_volume(padded, weight):
    source_width = weight.shape[0] // 27
    kernel = weight.reshape(3, 3, 3, source_width, weight.shape[1])
    return lax.conv_general_dilated(
        padded[None],
        kernel,
        (1, 1, 1),
        "VALID",
        dimension_numbers=("NDHWC", "DHWIO", "NDHWC"),
        preferred_element_type=jnp.float32,
    )[0]


def flipped_volume(weight):
    source_width = weight.shape[0] // 27
    target_width = weight.shape[1]
    kernel = weight.reshape(3, 3, 3, source_width, target_width)[::-1, ::-1, ::-1]
    return jnp.transpose(kernel, (0, 1, 2, 4, 3)).reshape(27 * target_width, source_width)


def volume_patches(padded, frame_count, row_count, col_count):
    pieces = []
    for frame_step in range(3):
        for row_step in range(3):
            for col_step in range(3):
                pieces.append(
                    padded[
                        frame_step : frame_step + frame_count,
                        row_step : row_step + row_count,
                        col_step : col_step + col_count,
                    ]
                )
    stacked = jnp.concatenate(pieces, axis=-1)
    return stacked.reshape(frame_count * row_count * col_count, -1)


def widen(volume):
    return padded_2(volume, (("grp", 0), ("row", 1), ("col", 2)), 1)


def pixel_gradient(images, guides, row_keep, vgg_first, vgg_second, vgg_third):
    cell_keep = row_keep[None, :, None, None]
    pool_keep = row_keep[::2][None, :, None, None]

    def features(source):
        first_plane = conv_plane(source, vgg_first)
        first_act = (gelu_value(first_plane) * cell_keep).astype(jnp.bfloat16)
        second_plane = conv_plane(first_act, vgg_second)
        second_feat = gelu_value(second_plane) * cell_keep
        image_count, row_count, col_count, channel_count = second_feat.shape
        pooled = second_feat.reshape(
            image_count, row_count // 2, 2, col_count // 2, 2, channel_count
        )
        pooled = (jnp.sum(pooled, axis=(2, 4)) * 0.25).astype(jnp.bfloat16)
        third_plane = conv_plane(pooled, vgg_third)
        third_feat = gelu_value(third_plane) * pool_keep
        return (first_plane, second_plane, second_feat, third_plane, third_feat)

    first_plane, second_plane, second_feat, third_plane, third_feat = features(images)
    guide_parts = features(guides)
    guide_second = guide_parts[2]
    guide_third = guide_parts[4]
    third_delta = (
        64.0 / third_feat.shape[-1] * (third_feat - guide_third) * gelu_slope(third_plane)
    ).astype(jnp.bfloat16)
    pooled_grad = conv_plane(third_delta, flipped_plane(vgg_third))
    image_count, half_rows, half_cols, channel_count = pooled_grad.shape
    spread = jnp.broadcast_to(
        pooled_grad[:, :, None, :, None, :],
        (image_count, half_rows, 2, half_cols, 2, channel_count),
    )
    spread = spread.reshape(image_count, 2 * half_rows, 2 * half_cols, channel_count)
    second_delta = (
        (0.25 * spread + 16.0 / channel_count * (second_feat - guide_second))
        * gelu_slope(second_plane)
        * cell_keep
    ).astype(jnp.bfloat16)
    first_grad = conv_plane(second_delta, flipped_plane(vgg_second))
    first_delta = (first_grad * gelu_slope(first_plane) * cell_keep).astype(jnp.bfloat16)
    direct_term = 1.0 / 6.0 * (images.astype(jnp.float32) - guides.astype(jnp.float32))
    return conv_plane(first_delta, flipped_plane(vgg_first)) + direct_term


def reduce_kernel(
    a_ref, b_ref, out_ref, core_in, held, x_in, y_in, mid_a, mid_b, last, z_in, send_sem, recv_sem
):
    g, r, c = lax.axis_index("grp"), lax.axis_index("row"), lax.axis_index("col")
    zh, x, y, core = r // 4, lax.rem(r, 4), c // 2, lax.rem(c, 2)
    z = g * 2 + zh
    other = 1 - core

    def at_x(step):
        return (g, zh * 4 + lax.rem(x + step, 4), c)

    def at_y(step):
        return (g, r, lax.rem(y + step, 4) * 2 + core)

    def at_z(step):
        to = lax.rem(z + step, 8)
        return (to // 2, lax.rem(to, 2) * 4 + x, c)

    partner = (g, r, y * 2 + other)
    barrier = pltpu.get_barrier_semaphore()
    everyone = [partner] + [at_x(s) for s in (1, 2, 3)] + [at_y(s) for s in (1, 2, 3)]
    everyone += [at_z(s) for s in range(1, 8)]
    for peer in everyone:
        pl.semaphore_signal(barrier, inc=1, device_id=peer, device_id_type=MESH)
    pl.semaphore_wait(barrier, len(everyone))

    def send(src, dst, slot, peer):
        copy = pltpu.make_async_remote_copy(
            src_ref=src,
            dst_ref=dst,
            send_sem=send_sem.at[slot],
            recv_sem=recv_sem.at[slot],
            device_id=peer,
            device_id_type=MESH,
        )
        copy.start()
        return copy

    f32, b16 = jnp.float32, jnp.bfloat16
    first = [
        send(a_ref.at[other], core_in.at[0], 0, partner),
        send(b_ref.at[other], core_in.at[1], 1, partner),
    ]
    first[0].wait()
    held[0] = (a_ref[core].astype(f32) + core_in[0].astype(f32)).astype(b16)
    step_a = [
        send(held.at[0, :, lax.rem(x + s, 4)], x_in.at[s - 1], 1 + s, at_x(s)) for s in (1, 2, 3)
    ]
    first[1].wait()
    held[1] = (b_ref[core].astype(f32) + core_in[1].astype(f32)).astype(b16)
    step_b = [
        send(held.at[1, :, :, lax.rem(y + s, 4)], y_in.at[s - 1], 4 + s, at_y(s)) for s in (1, 2, 3)
    ]
    for copy in step_a:
        copy.wait()
    total = held[0, :, x].astype(f32)
    for s in range(3):
        total += x_in[s].astype(f32)
    mid_a[...] = total.astype(b16)
    next_a = [
        send(mid_a.at[:, lax.rem(y + s, 4)], last.at[0, s - 1], 7 + s, at_y(s)) for s in (1, 2, 3)
    ]
    for copy in step_b:
        copy.wait()
    total = held[1, :, :, y].astype(f32)
    for s in range(3):
        total += y_in[s].astype(f32)
    mid_b[...] = total.astype(b16)
    next_b = [
        send(mid_b.at[:, lax.rem(x + s, 4)], last.at[1, s - 1], 10 + s, at_x(s)) for s in (1, 2, 3)
    ]
    for copy in next_a:
        copy.wait()
    total = mid_a[:, y].astype(f32)
    for s in range(3):
        total += last[0, s].astype(f32)
    last[0, 3] = total.astype(b16)
    final_a = [
        send(last.at[0, 3, lax.rem(z + s, 8)], z_in.at[0, s - 1], 13 + s, at_z(s)) for s in range(1, 8)
    ]
    for copy in next_b:
        copy.wait()
    total = mid_b[:, x].astype(f32)
    for s in range(3):
        total += last[1, s].astype(f32)
    last[1, 3] = total.astype(b16)
    final_b = [
        send(last.at[1, 3, lax.rem(z + s, 8)], z_in.at[1, s - 1], 20 + s, at_z(s)) for s in range(1, 8)
    ]
    for which, copies in ((0, final_a), (1, final_b)):
        for copy in copies:
            copy.wait()
        total = last[which, 3, z].astype(f32)
        for s in range(7):
            total += z_in[which, s].astype(f32)
        out_ref[which] = total


def chip_layout(terms):
    rows = terms.astype(jnp.bfloat16).reshape(128, 27, 128)
    halves = jnp.stack([rows[:, :14], rows[:, 13:]])
    return jnp.pad(halves, ((0, 0), (0, 0), (0, 2), (0, 0))).reshape(2, 8, 4, 4, 16, 128)


def scattered_sums(first_terms, second_terms):
    b16 = jnp.bfloat16
    sums = pl.pallas_call(
        reduce_kernel,
        out_shape=jax.ShapeDtypeStruct((2, 16, 128), jnp.float32),
        in_specs=[pl.BlockSpec(memory_space=pltpu.VMEM)] * 2,
        out_specs=pl.BlockSpec(memory_space=pltpu.VMEM),
        scratch_shapes=[
            pltpu.VMEM((2, 8, 4, 4, 16, 128), b16),
            pltpu.VMEM((2, 8, 4, 4, 16, 128), b16),
            pltpu.VMEM((3, 8, 4, 16, 128), b16),
            pltpu.VMEM((3, 8, 4, 16, 128), b16),
            pltpu.VMEM((8, 4, 16, 128), b16),
            pltpu.VMEM((8, 4, 16, 128), b16),
            pltpu.VMEM((2, 4, 8, 16, 128), b16),
            pltpu.VMEM((2, 7, 16, 128), b16),
            pltpu.SemaphoreType.DMA((28,)),
            pltpu.SemaphoreType.DMA((28,)),
        ],
        compiler_params=pltpu.CompilerParams(
            collective_id=1, has_side_effects=True, vmem_limit_bytes=40 * 2**20
        ),
    )(chip_layout(first_terms), chip_layout(second_terms))
    flat = sums[:, :14].reshape(2, 14 * 128)
    start = lax.rem(lax.axis_index("col"), 2) * 64
    own = lax.dynamic_slice_in_dim(flat, start, 1728, axis=1)
    return own[0], own[1]


def local(dec_input, target, conv_first, conv_second, rgb_weight, vgg_first, vgg_second, vgg_third):
    group_index = lax.axis_index("grp")
    active = group_index < 3
    group_count = lax.axis_size("grp")
    column_count = lax.axis_size("col")
    row_devices = lax.axis_size("row")
    block_count, frames, tile_rows, tile_cols, channels = dec_input.shape
    per_column = frames // column_count
    own_frames = lax.dynamic_index_in_dim(dec_input, jnp.minimum(group_index, 2), 0, keepdims=False)
    own_frames = jnp.where(active, own_frames, jnp.zeros_like(own_frames))
    zero_field = jnp.zeros((frames, tile_rows, tile_cols, channels), jnp.float32)

    def no_layer(operand):
        return zero_field

    def first_layer(operand):
        return conv_volume(operand, conv_first)

    def second_layer(operand):
        return conv_volume(operand, conv_second)

    padded_input = widen(own_frames)
    first_pre = lax.cond(active, first_layer, no_layer, padded_input)
    first_out = jax.nn.silu(first_pre).astype(jnp.bfloat16)
    padded_first = widen(first_out)
    second_pre = lax.cond(active, second_layer, no_layer, padded_first)
    second_out = jax.nn.silu(second_pre).astype(jnp.bfloat16)
    colour = jnp.einsum(
        "fhwc,kc->kfhw", second_out, rgb_weight, preferred_element_type=jnp.float32
    ).astype(jnp.bfloat16)
    pieces = jnp.transpose(
        colour.reshape(3, column_count, per_column, tile_rows, tile_cols), (1, 0, 2, 3, 4)
    )
    outgoing = jnp.broadcast_to(pieces[None], (group_count,) + pieces.shape)
    arrived = lax.all_to_all(
        outgoing.reshape((group_count * column_count,) + pieces.shape[1:]),
        ("grp", "col"),
        split_axis=0,
        concat_axis=0,
        tiled=True,
    )
    arrived = arrived.reshape(outgoing.shape)
    strip_cells = jnp.transpose(arrived[:3], (2, 0, 3, 4, 1, 5)).reshape(
        3, 3, per_column, tile_rows, column_count * tile_cols
    )
    strip_wide, guide_wide = (
        padded_2(strip_cells, (("row", 3),), 8),
        padded_2(target, (("row", 3),), 8),
    )
    extended = tile_rows + 16
    positions = lax.axis_index("row") * tile_rows - 8 + jnp.arange(extended)
    row_keep = ((positions >= 0) & (positions < tile_rows * row_devices)).astype(jnp.float32)
    image_width = column_count * tile_cols

    def perceive(operands):
        colour_strip, target_strip = operands
        images = jnp.transpose(
            colour_strip.reshape(3, 3 * per_column, extended, image_width), (1, 2, 3, 0)
        )
        guides = jnp.transpose(
            target_strip.reshape(3, 3 * per_column, extended, image_width), (1, 2, 3, 0)
        )
        gradient = pixel_gradient(images, guides, row_keep, vgg_first, vgg_second, vgg_third)
        owned_rows = gradient[:, 8 : 8 + tile_rows]
        return jnp.transpose(owned_rows, (3, 0, 1, 2)).reshape(
            3, 3, per_column, tile_rows, image_width
        )

    def no_perceive(operands):
        return jnp.zeros((3, 3, per_column, tile_rows, image_width), jnp.float32)

    pixel_strip = lax.cond(active, no_perceive, perceive, (strip_wide, guide_wide))
    blocks_back = jnp.transpose(
        pixel_strip.reshape(3, 3, per_column, tile_rows, column_count, tile_cols),
        (1, 4, 0, 2, 3, 5),
    )
    empty_blocks = jnp.zeros((group_count - 3,) + blocks_back.shape[1:], jnp.float32)
    sending = jnp.concatenate([blocks_back, empty_blocks], axis=0)
    returned = lax.all_to_all(
        shortened(sending.reshape((group_count * column_count,) + sending.shape[2:])),
        ("grp", "col"),
        split_axis=0,
        concat_axis=0,
        tiled=True,
    )
    returned = returned.reshape(sending.shape)
    pixel_tile = jnp.transpose(returned[group_count - 1], (1, 0, 2, 3, 4)).reshape(
        3, frames, tile_rows, tile_cols
    )

    def second_back(operands):
        pixel_part, second_state, padded_state = operands
        hidden_grad = jnp.einsum(
            "kfhw,kc->fhwc",
            pixel_part,
            rgb_weight.astype(jnp.float32),
            precision=lax.Precision.HIGHEST,
        )
        decoder_second = (hidden_grad * silu_slope(second_state)).astype(jnp.bfloat16)
        patches = volume_patches(padded_state, frames, tile_rows, tile_cols)
        weight_part = jnp.dot(
            patches.T, decoder_second.reshape(-1, channels), preferred_element_type=jnp.float32
        )
        return (decoder_second, weight_part)

    def no_second(operands):
        return (
            jnp.zeros((frames, tile_rows, tile_cols, channels), jnp.bfloat16),
            jnp.zeros((27 * channels, channels), jnp.float32),
        )

    decoder_second, grad_second = lax.cond(
        active, second_back, no_second, (pixel_tile, second_pre, padded_first)
    )
    padded_delta = widen(decoder_second)

    def first_back(operands):
        delta_state, first_state, padded_state = operands
        hidden_back = conv_volume(delta_state, flipped_volume(conv_second))
        decoder_hidden = (hidden_back * silu_slope(first_state)).astype(jnp.bfloat16)
        patches = volume_patches(padded_state, frames, tile_rows, tile_cols)
        return jnp.dot(
            patches.T, decoder_hidden.reshape(-1, channels), preferred_element_type=jnp.float32
        )

    def no_first(operands):
        return jnp.zeros((27 * channels, channels), jnp.float32)

    grad_first = lax.cond(active, first_back, no_first, (padded_delta, first_pre, padded_input))
    return scattered_sums(grad_first, grad_second)


def solution(mesh):
    in_specs = (
        P(None, None, "row", "col", None),
        P(None, None, "col", "row", None),
        P(),
        P(),
        P(),
        P(),
        P(),
        P(),
    )
    out_specs = (P(("grp", "row", "col")), P(("grp", "row", "col")))
    return jax.shard_map(local, mesh=mesh, in_specs=in_specs, out_specs=out_specs, check_vma=False)
```

```python
import functools

import jax
import jax.numpy as jnp
from jax import lax
from jax.experimental import pallas as pl
from jax.experimental.pallas import tpu as pltpu
from jax.sharding import PartitionSpec as P

MESH = pl.DeviceIdType.MESH

gelu_scale = 0.7978845608028654
gelu_cubic = 0.044715


def silu_slope(preact):
    sigmoid_value = jax.nn.sigmoid(preact)
    return sigmoid_value * (1.0 + preact * (1.0 - sigmoid_value))


def gelu_value(preact):
    return (
        0.5
        * preact
        * (1.0 + jnp.tanh(gelu_scale * (preact + gelu_cubic * preact * preact * preact)))
    )


def gelu_slope(preact):
    inner_tanh = jnp.tanh(gelu_scale * (preact + gelu_cubic * preact * preact * preact))
    return 0.5 * (1.0 + inner_tanh) + 0.5 * preact * (
        1.0 - inner_tanh * inner_tanh
    ) * gelu_scale * (1.0 + 3.0 * gelu_cubic * preact * preact)


def conv_plane(images, weight):
    source_width = weight.shape[0] // 9
    kernel = weight.reshape(3, 3, source_width, weight.shape[1])
    return lax.conv_general_dilated(
        images,
        kernel,
        (1, 1),
        "SAME",
        dimension_numbers=("NHWC", "HWIO", "NHWC"),
        preferred_element_type=jnp.float32,
    )


def flipped_plane(weight):
    source_width = weight.shape[0] // 9
    target_width = weight.shape[1]
    kernel = weight.reshape(3, 3, source_width, target_width)[::-1, ::-1]
    return jnp.transpose(kernel, (0, 1, 3, 2)).reshape(9 * target_width, source_width)


def conv_volume(padded, weight):
    source_width = weight.shape[0] // 27
    kernel = weight.reshape(3, 3, 3, source_width, weight.shape[1])
    return lax.conv_general_dilated(
        padded[None],
        kernel,
        (1, 1, 1),
        "VALID",
        dimension_numbers=("NDHWC", "DHWIO", "NDHWC"),
        preferred_element_type=jnp.float32,
    )[0]


def flipped_volume(weight):
    source_width = weight.shape[0] // 27
    target_width = weight.shape[1]
    kernel = weight.reshape(3, 3, 3, source_width, target_width)[::-1, ::-1, ::-1]
    return jnp.transpose(kernel, (0, 1, 2, 4, 3)).reshape(27 * target_width, source_width)


def volume_patches(padded, frame_count, row_count, col_count):
    pieces = []
    for frame_step in range(3):
        for row_step in range(3):
            for col_step in range(3):
                pieces.append(
                    padded[
                        frame_step : frame_step + frame_count,
                        row_step : row_step + row_count,
                        col_step : col_step + col_count,
                    ]
                )
    stacked = jnp.concatenate(pieces, axis=-1)
    return stacked.reshape(frame_count * row_count * col_count, -1)


def pixel_gradient(images, guides, row_keep, vgg_first, vgg_second, vgg_third):
    cell_keep = row_keep[None, :, None, None]
    pool_keep = row_keep[::2][None, :, None, None]

    def features(source):
        first_plane = conv_plane(source, vgg_first)
        first_act = (gelu_value(first_plane) * cell_keep).astype(jnp.bfloat16)
        second_plane = conv_plane(first_act, vgg_second)
        second_feat = gelu_value(second_plane) * cell_keep
        image_count, row_count, col_count, channel_count = second_feat.shape
        pooled = second_feat.reshape(
            image_count, row_count // 2, 2, col_count // 2, 2, channel_count
        )
        pooled = (jnp.sum(pooled, axis=(2, 4)) * 0.25).astype(jnp.bfloat16)
        third_plane = conv_plane(pooled, vgg_third)
        third_feat = gelu_value(third_plane) * pool_keep
        return (first_plane, second_plane, second_feat, third_plane, third_feat)

    first_plane, second_plane, second_feat, third_plane, third_feat = features(images)
    guide_parts = features(guides)
    guide_second = guide_parts[2]
    guide_third = guide_parts[4]
    third_delta = (
        64.0 / third_feat.shape[-1] * (third_feat - guide_third) * gelu_slope(third_plane)
    ).astype(jnp.bfloat16)
    pooled_grad = conv_plane(third_delta, flipped_plane(vgg_third))
    image_count, half_rows, half_cols, channel_count = pooled_grad.shape
    spread = jnp.broadcast_to(
        pooled_grad[:, :, None, :, None, :],
        (image_count, half_rows, 2, half_cols, 2, channel_count),
    )
    spread = spread.reshape(image_count, 2 * half_rows, 2 * half_cols, channel_count)
    second_delta = (
        (0.25 * spread + 16.0 / channel_count * (second_feat - guide_second))
        * gelu_slope(second_plane)
        * cell_keep
    ).astype(jnp.bfloat16)
    first_grad = conv_plane(second_delta, flipped_plane(vgg_second))
    first_delta = (first_grad * gelu_slope(first_plane) * cell_keep).astype(jnp.bfloat16)
    direct_term = 1.0 / 6.0 * (images.astype(jnp.float32) - guides.astype(jnp.float32))
    return conv_plane(first_delta, flipped_plane(vgg_first)) + direct_term


def reduce_kernel(
    a_ref, b_ref, out_ref, core_in, held, x_in, y_in, mid_a, mid_b, last, z_in, send_sem, recv_sem
):
    g, r, c = lax.axis_index("grp"), lax.axis_index("row"), lax.axis_index("col")
    zh, x, y, core = r // 4, lax.rem(r, 4), c // 2, lax.rem(c, 2)
    z = g * 2 + zh
    other = 1 - core

    def at_x(step):
        return (g, zh * 4 + lax.rem(x + step, 4), c)

    def at_y(step):
        return (g, r, lax.rem(y + step, 4) * 2 + core)

    def at_z(step):
        to = lax.rem(z + step, 8)
        return (to // 2, lax.rem(to, 2) * 4 + x, c)

    partner = (g, r, y * 2 + other)
    barrier = pltpu.get_barrier_semaphore()
    everyone = [partner] + [at_x(s) for s in (1, 2, 3)] + [at_y(s) for s in (1, 2, 3)]
    everyone += [at_z(s) for s in range(1, 8)]
    for peer in everyone:
        pl.semaphore_signal(barrier, inc=1, device_id=peer, device_id_type=MESH)
    pl.semaphore_wait(barrier, len(everyone))

    def send(src, dst, slot, peer):
        copy = pltpu.make_async_remote_copy(
            src_ref=src,
            dst_ref=dst,
            send_sem=send_sem.at[slot],
            recv_sem=recv_sem.at[slot],
            device_id=peer,
            device_id_type=MESH,
        )
        copy.start()
        return copy

    f32, b16 = jnp.float32, jnp.bfloat16
    first = [
        send(a_ref.at[other], core_in.at[0], 0, partner),
        send(b_ref.at[other], core_in.at[1], 1, partner),
    ]
    first[0].wait()
    held[0] = (a_ref[core].astype(f32) + core_in[0].astype(f32)).astype(b16)
    step_a = [
        send(held.at[0, :, lax.rem(x + s, 4)], x_in.at[s - 1], 1 + s, at_x(s)) for s in (1, 2, 3)
    ]
    first[1].wait()
    held[1] = (b_ref[core].astype(f32) + core_in[1].astype(f32)).astype(b16)
    step_b = [
        send(held.at[1, :, :, lax.rem(y + s, 4)], y_in.at[s - 1], 4 + s, at_y(s)) for s in (1, 2, 3)
    ]
    for copy in step_a:
        copy.wait()
    total = held[0, :, x].astype(f32)
    for s in range(3):
        total += x_in[s].astype(f32)
    mid_a[...] = total.astype(b16)
    next_a = [
        send(mid_a.at[:, lax.rem(y + s, 4)], last.at[0, s - 1], 7 + s, at_y(s)) for s in (1, 2, 3)
    ]
    for copy in step_b:
        copy.wait()
    total = held[1, :, :, y].astype(f32)
    for s in range(3):
        total += y_in[s].astype(f32)
    mid_b[...] = total.astype(b16)
    next_b = [
        send(mid_b.at[:, lax.rem(x + s, 4)], last.at[1, s - 1], 10 + s, at_x(s)) for s in (1, 2, 3)
    ]
    for copy in next_a:
        copy.wait()
    total = mid_a[:, y].astype(f32)
    for s in range(3):
        total += last[0, s].astype(f32)
    last[0, 3] = total.astype(b16)
    final_a = [
        send(last.at[0, 3, lax.rem(z + s, 8)], z_in.at[0, s - 1], 13 + s, at_z(s)) for s in range(1, 8)
    ]
    for copy in next_b:
        copy.wait()
    total = mid_b[:, x].astype(f32)
    for s in range(3):
        total += last[1, s].astype(f32)
    last[1, 3] = total.astype(b16)
    final_b = [
        send(last.at[1, 3, lax.rem(z + s, 8)], z_in.at[1, s - 1], 20 + s, at_z(s)) for s in range(1, 8)
    ]
    for which, copies in ((0, final_a), (1, final_b)):
        for copy in copies:
            copy.wait()
        total = last[which, 3, z].astype(f32)
        for s in range(7):
            total += z_in[which, s].astype(f32)
        out_ref[which] = total


def chip_layout(terms):
    rows = terms.astype(jnp.bfloat16).reshape(128, 27, 128)
    halves = jnp.stack([rows[:, :14], rows[:, 13:]])
    return jnp.pad(halves, ((0, 0), (0, 0), (0, 2), (0, 0))).reshape(2, 8, 4, 4, 16, 128)


def scattered_sums(first_terms, second_terms):
    b16 = jnp.bfloat16
    sums = pl.pallas_call(
        reduce_kernel,
        out_shape=jax.ShapeDtypeStruct((2, 16, 128), jnp.float32),
        in_specs=[pl.BlockSpec(memory_space=pltpu.VMEM)] * 2,
        out_specs=pl.BlockSpec(memory_space=pltpu.VMEM),
        scratch_shapes=[
            pltpu.VMEM((2, 8, 4, 4, 16, 128), b16),
            pltpu.VMEM((2, 8, 4, 4, 16, 128), b16),
            pltpu.VMEM((3, 8, 4, 16, 128), b16),
            pltpu.VMEM((3, 8, 4, 16, 128), b16),
            pltpu.VMEM((8, 4, 16, 128), b16),
            pltpu.VMEM((8, 4, 16, 128), b16),
            pltpu.VMEM((2, 4, 8, 16, 128), b16),
            pltpu.VMEM((2, 7, 16, 128), b16),
            pltpu.SemaphoreType.DMA((28,)),
            pltpu.SemaphoreType.DMA((28,)),
        ],
        compiler_params=pltpu.CompilerParams(
            collective_id=1, has_side_effects=True, vmem_limit_bytes=40 * 2**20
        ),
    )(chip_layout(first_terms), chip_layout(second_terms))
    flat = sums[:, :14].reshape(2, 14 * 128)
    start = lax.rem(lax.axis_index("col"), 2) * 64
    own = lax.dynamic_slice_in_dim(flat, start, 1728, axis=1)
    return own[0], own[1]


def position():
    return lax.axis_index("grp"), lax.axis_index("row"), lax.axis_index("col")


def same_place(one, other):
    return (one[0] == other[0]) & (one[1] == other[1]) & (one[2] == other[2])


def row_count(r):
    return 1 + jnp.where(r > 0, 1, 0) + jnp.where(r < 7, 1, 0)


def remote(src, dst, sems, slot, peer):
    return pltpu.make_async_remote_copy(
        src_ref=src,
        dst_ref=dst,
        send_sem=sems[0].at[slot],
        recv_sem=sems[1].at[slot],
        device_id=peer,
        device_id_type=MESH,
    )


def halo_kernel(
    own_ref, left_ref, right_ref, guide_ref,
    top_out, bottom_out, left_out, right_out, corner_out, guide_out, send_sem, recv_sem,
):
    g, r, c = position()
    sems = (send_sem, recv_sem)
    west, east = (g, r, lax.rem(c + 7, 8)), (g, r, lax.rem(c + 1, 8))
    has_up, has_down = r > 0, r < 7
    barrier = pltpu.get_barrier_semaphore()

    def greet(row_index):
        for step in (7, 0, 1):
            peer = (g, row_index, lax.rem(c + step, 8))
            pl.semaphore_signal(barrier, inc=1, device_id=peer, device_id_type=MESH)

    for peer in (west, east):
        pl.semaphore_signal(barrier, inc=1, device_id=peer, device_id_type=MESH)
    pl.when(has_up)(lambda: greet(r - 1))
    pl.when(has_down)(lambda: greet(r + 1))
    pl.semaphore_wait(barrier, 3 * row_count(r) - 1)
    sideways = [
        remote(left_ref, right_out, sems, 0, west),
        remote(right_ref, left_out, sems, 1, east),
    ]

    def to_row(row_index, rows, strip_out, corners, guide_slot, first_slot):
        west_peer = (g, row_index, west[2])
        east_peer = (g, row_index, east[2])
        here = (g, row_index, c)
        return [
            remote(own_ref.at[:, rows], strip_out, sems, first_slot, here),
            remote(guide_ref, guide_out.at[guide_slot], sems, first_slot + 1, here),
            remote(left_ref.at[rows], corner_out.at[corners + 1], sems, first_slot + 2, west_peer),
            remote(right_ref.at[rows], corner_out.at[corners], sems, first_slot + 3, east_peer),
        ]

    upward = to_row(r - 1, pl.ds(0, 3), bottom_out, 2, 1, 2)
    downward = to_row(r + 1, pl.ds(5, 3), top_out, 0, 0, 6)

    def start(copies):
        for copy in copies:
            copy.start()

    def sent(copies):
        for copy in copies:
            copy.wait_send()

    def landed(copies):
        for copy in copies:
            copy.wait_recv()

    pl.when(has_up)(lambda: start(upward))
    pl.when(has_down)(lambda: start(downward))
    start(sideways)
    landed(sideways)
    pl.when(has_down)(lambda: landed(upward))
    pl.when(has_up)(lambda: landed(downward))
    sent(sideways)
    pl.when(has_up)(lambda: sent(upward))
    pl.when(has_down)(lambda: sent(downward))


def colour_kernel(colour_ref, out_ref, send_sem, recv_sem, own_sem):
    g, r, c = position()
    me = (g, r, c)
    barrier = pltpu.get_barrier_semaphore()
    perceives = g < 3
    source_group = (8 * g + c) // 6

    def signal(peer):
        @pl.when(jnp.logical_not(same_place(peer, me)))
        def _():
            pl.semaphore_signal(barrier, inc=1, device_id=peer, device_id_type=MESH)

    def on_rows(do):
        for step in (-1, 0, 1):
            pl.when((r + step >= 0) & (r + step < 8))(functools.partial(do, step))

    def greet(step):
        for column in range(8):
            signal((source_group, r + step, column))

    def targets(step):
        for slot in range(6):
            frame = 6 * g + slot
            yield slot, (frame // 8, r + step, lax.rem(frame, 8))

    pl.when(perceives)(lambda: on_rows(greet))
    to_itself = jnp.where(perceives & (2 * g + c < 6), 1, 0)
    pl.semaphore_wait(barrier, 6 * row_count(r) - to_itself)

    def outgoing(step, slot, peer):
        return pltpu.make_async_remote_copy(
            src_ref=colour_ref.at[slot],
            dst_ref=out_ref.at[1 - step, c],
            send_sem=send_sem.at[step + 1, slot],
            recv_sem=recv_sem.at[1 - step, c],
            device_id=peer,
            device_id_type=MESH,
        )

    def kept(slot):
        return pltpu.make_async_copy(colour_ref.at[slot], out_ref.at[1, c], own_sem)

    def start(step):
        for slot, peer in targets(step):
            away = jnp.logical_not(same_place(peer, me))
            pl.when(away)(lambda: outgoing(step, slot, peer).start())
            if step == 0:
                pl.when(jnp.logical_not(away))(lambda: kept(slot).start())

    def arrive(step):
        for column in range(8):
            source = (source_group, r + step, column)
            away = jnp.logical_not(same_place(source, me))

            @pl.when(away)
            def _():
                pltpu.make_async_remote_copy(
                    src_ref=colour_ref.at[0],
                    dst_ref=out_ref.at[step + 1, column],
                    send_sem=send_sem.at[0, 0],
                    recv_sem=recv_sem.at[step + 1, column],
                    device_id=source,
                    device_id_type=MESH,
                ).wait_recv()

    def finish(step):
        for slot, peer in targets(step):
            away = jnp.logical_not(same_place(peer, me))
            pl.when(away)(lambda: outgoing(step, slot, peer).wait_send())
            if step == 0:
                pl.when(jnp.logical_not(away))(lambda: kept(slot).wait())

    on_rows(start)
    pl.when(perceives)(lambda: on_rows(arrive))
    on_rows(finish)


def pixel_kernel(strip_ref, out_ref, send_sem, recv_sem, own_sem):
    g, r, c = position()
    me = (g, r, c)
    barrier = pltpu.get_barrier_semaphore()
    perceives = g < 3
    frame = 8 * g + c
    home = frame // 6
    place = lax.rem(frame, 6)
    before = perceives & (place == 0) & (home > 0)
    after = perceives & (place == 5) & (home < 3)

    def on_rows(do):
        for step in (-1, 0, 1):
            pl.when((r + step >= 0) & (r + step < 8))(functools.partial(do, step))

    def sources(do):
        for slot in range(8):
            source_frame = 6 * g - 1 + slot
            inside = (source_frame >= 0) & (source_frame < 24)

            def each(step, slot=slot, source_frame=source_frame):
                source = (source_frame // 8, r + step, lax.rem(source_frame, 8))
                pl.when(jnp.logical_not(same_place(source, me)))(
                    functools.partial(do, step, slot, source)
                )

            pl.when(inside)(functools.partial(on_rows, each))

    def greet(step, slot, source):
        pl.semaphore_signal(barrier, inc=1, device_id=source, device_id_type=MESH)

    def targets(do):
        for kind, (group, needed) in enumerate(
            ((home, perceives), (home - 1, before), (home + 1, after))
        ):

            def each(step, kind=kind, group=group):
                for column in range(8):
                    peer = (group, r + step, column)
                    do(kind, step, column, peer, jnp.logical_not(same_place(peer, me)))

            pl.when(needed)(functools.partial(on_rows, each))

    sources(greet)
    groups = jnp.where(perceives, 1, 0) + jnp.where(before, 1, 0) + jnp.where(after, 1, 0)
    to_itself = perceives & (home == g) | before & (home == g + 1) | after & (home == g - 1)
    awaited = 8 * row_count(r) * groups - jnp.where(to_itself, 1, 0)
    pl.when(perceives)(lambda: pl.semaphore_wait(barrier, awaited))

    def outgoing(kind, step, column, peer):
        return pltpu.make_async_remote_copy(
            src_ref=strip_ref,
            dst_ref=out_ref.at[frame - 6 * peer[0] + 1, 1 - step],
            send_sem=send_sem.at[kind, step + 1, column],
            recv_sem=recv_sem.at[frame - 6 * peer[0] + 1, 1 - step],
            device_id=peer,
            device_id_type=MESH,
        )

    def kept():
        return pltpu.make_async_copy(strip_ref, out_ref.at[frame - 6 * g + 1, 1], own_sem)

    def start(kind, step, column, peer, away):
        pl.when(away)(lambda: outgoing(kind, step, column, peer).start())
        if step == 0:
            pl.when(jnp.logical_not(away))(lambda: kept().start())

    def finish(kind, step, column, peer, away):
        pl.when(away)(lambda: outgoing(kind, step, column, peer).wait_send())
        if step == 0:
            pl.when(jnp.logical_not(away))(lambda: kept().wait())

    def arrive(step, slot, source):
        pltpu.make_async_remote_copy(
            src_ref=strip_ref,
            dst_ref=out_ref.at[slot, step + 1],
            send_sem=send_sem.at[0, 0, 0],
            recv_sem=recv_sem.at[slot, step + 1],
            device_id=source,
            device_id_type=MESH,
        ).wait_recv()

    targets(start)
    sources(arrive)
    targets(finish)


def in_vmem(count):
    return [pl.BlockSpec(memory_space=pltpu.VMEM)] * count


def b16(*shape):
    return jax.ShapeDtypeStruct(shape, jnp.bfloat16)


def exchange(kernel, ident, outs, sems, *operands):
    outs = tuple(outs)
    return pl.pallas_call(
        kernel,
        out_shape=outs,
        in_specs=in_vmem(len(operands)),
        out_specs=tuple(in_vmem(len(outs))),
        scratch_shapes=[pltpu.SemaphoreType.DMA(shape) for shape in sems],
        compiler_params=pltpu.CompilerParams(
            collective_id=ident, has_side_effects=True, vmem_limit_bytes=24 * 2**20
        ),
    )(*operands)


def inside(start, count, limit):
    positions = start + jnp.arange(count)
    return (positions >= 0) & (positions < limit)


def cell_mask(frame0, frames, row0, rows, col0, cols):
    keep_frames = inside(frame0, frames, 24)
    keep_rows = inside(row0, rows, 64)
    keep_cols = inside(col0, cols, 128)
    return (keep_frames[:, None, None] & keep_rows[None, :, None] & keep_cols[None, None, :])[
        ..., None
    ]


def local(dec_input, target, conv_first, conv_second, rgb_weight, vgg_first, vgg_second, vgg_third):
    g, r, c = position()
    channels = dec_input.shape[-1]
    frame0, row0, col0 = 6 * g, 8 * r, 16 * c
    video = jnp.pad(dec_input.reshape(24, 8, 16, channels), ((3, 3), (0, 0), (0, 0), (0, 0)))
    own = lax.dynamic_slice_in_dim(video, frame0, 12, axis=0)

    def columns(part):
        return jnp.transpose(part, (1, 0, 2, 3)).reshape(8, 48, channels)

    guide_own = lax.dynamic_index_in_dim(target, jnp.minimum(g, 2), 1, keepdims=False)
    guide_own = guide_own.reshape(24, 128)
    top, bottom, left, right, corners, guide_near = exchange(
        halo_kernel,
        2,
        (
            b16(12, 3, 16, channels), b16(12, 3, 16, channels), b16(8, 48, channels),
            b16(8, 48, channels), b16(4, 3, 48, channels), b16(2, 32, 128),
        ),
        ((10,), (10,)),
        own,
        columns(own[:, :, :4]),
        columns(own[:, :, 12:]),
        jnp.pad(guide_own, ((0, 8), (0, 0))),
    )

    def strip(part):
        return jnp.transpose(part.reshape(-1, 12, 4, channels), (1, 0, 2, 3))

    padded = jnp.concatenate(
        [
            jnp.concatenate([strip(corners[0]), top, strip(corners[1])], axis=2),
            jnp.concatenate([strip(left), own, strip(right)], axis=2),
            jnp.concatenate([strip(corners[2]), bottom, strip(corners[3])], axis=2),
        ],
        axis=1,
    )
    padded = jnp.where(
        inside(row0 - 3, 14, 64)[None, :, None, None] & inside(col0 - 4, 24, 128)[None, None, :, None],
        padded,
        jnp.zeros_like(padded),
    )
    first_pre = conv_volume(padded[:, :, 1:23], conv_first)
    first_keep = cell_mask(frame0 - 2, 10, row0 - 2, 12, col0 - 2, 20)
    first_out = jnp.where(first_keep, jax.nn.silu(first_pre), 0.0).astype(jnp.bfloat16)
    second_pre = conv_volume(first_out, conv_second)
    second_out = jax.nn.silu(second_pre[1:7, 1:9, 1:17]).astype(jnp.bfloat16)
    colour = jnp.einsum(
        "fnc,kc->fkn", second_out.reshape(6, 128, channels), rgb_weight, preferred_element_type=jnp.float32
    ).astype(jnp.bfloat16)
    colour_near = exchange(
        colour_kernel,
        3,
        (b16(3, 8, 16, 128),),
        ((3, 6), (3, 8), ()),
        jnp.pad(colour, ((0, 0), (0, 13), (0, 0))),
    )[0]
    images = jnp.transpose(colour_near[:, :, :3].reshape(3, 8, 3, 8, 16), (0, 3, 1, 4, 2))
    images = images.reshape(24, 128, 3)
    row_inside = inside(row0 - 8, 24, 64)
    guides = jnp.concatenate(
        [guide_near[0, :24].reshape(3, 8, 128), guide_own.reshape(3, 8, 128), guide_near[1, :24].reshape(3, 8, 128)],
        axis=1,
    )
    guides = jnp.transpose(guides, (1, 2, 0))
    shown = row_inside[:, None, None]
    images = jnp.where(shown, images, jnp.zeros_like(images))
    guides = jnp.where(shown, guides, jnp.zeros_like(guides))
    gradient = pixel_gradient(
        images[None], guides[None], row_inside.astype(jnp.float32), vgg_first, vgg_second, vgg_third
    )
    strip_out = jnp.transpose(gradient[0, 8:16], (2, 0, 1)).astype(jnp.bfloat16).reshape(24, 128)
    returned = exchange(
        pixel_kernel,
        4,
        (b16(8, 3, 32, 128),),
        ((3, 3, 8), (8, 3), ()),
        jnp.pad(strip_out, ((0, 8), (0, 0))),
    )[0]
    rows_near = jnp.transpose(returned[:, :, :24].reshape(8, 3, 3, 8, 128), (2, 0, 1, 3, 4))
    rows_near = rows_near.reshape(3, 8, 24, 128)[:, :, 7:17]
    rows_near = jnp.pad(rows_near, ((0, 0), (0, 0), (0, 0), (1, 1)))
    pixel_part = lax.dynamic_slice_in_dim(rows_near, col0, 18, axis=3).astype(jnp.float32)
    second_keep = cell_mask(frame0 - 1, 8, row0 - 1, 10, col0 - 1, 18)
    pixel_part = jnp.where(second_keep[None, ..., 0], pixel_part, 0.0)
    hidden_grad = jnp.einsum(
        "kfhw,kc->fhwc",
        pixel_part,
        rgb_weight.astype(jnp.float32),
        precision=lax.Precision.HIGHEST,
    )
    decoder_second = (hidden_grad * silu_slope(second_pre)).astype(jnp.bfloat16)
    second_patches = volume_patches(first_out[1:9, 1:11, 1:19], 6, 8, 16)
    grad_second = jnp.dot(
        second_patches.T,
        decoder_second[1:7, 1:9, 1:17].reshape(-1, channels),
        preferred_element_type=jnp.float32,
    )
    hidden_back = conv_volume(decoder_second, flipped_volume(conv_second))
    decoder_hidden = (hidden_back * silu_slope(first_pre[2:8, 2:10, 2:18])).astype(jnp.bfloat16)
    first_patches = volume_patches(padded[2:10, 2:12, 3:21], 6, 8, 16)
    grad_first = jnp.dot(
        first_patches.T, decoder_hidden.reshape(-1, channels), preferred_element_type=jnp.float32
    )
    return scattered_sums(grad_first, grad_second)


def solution(mesh):
    in_specs = (
        P(None, None, "row", "col", None),
        P(None, None, "col", "row", None),
        P(),
        P(),
        P(),
        P(),
        P(),
        P(),
    )
    out_specs = (P(("grp", "row", "col")), P(("grp", "row", "col")))
    return jax.shard_map(local, mesh=mesh, in_specs=in_specs, out_specs=out_specs, check_vma=False)
```

```python
import functools

import jax
import jax.numpy as jnp
from jax import lax
from jax.experimental import pallas as pl
from jax.experimental.pallas import tpu as pltpu
from jax.sharding import PartitionSpec as P

MESH = pl.DeviceIdType.MESH

gelu_scale = 0.7978845608028654
gelu_cubic = 0.044715


def silu_slope(preact):
    sigmoid_value = jax.nn.sigmoid(preact)
    return sigmoid_value * (1.0 + preact * (1.0 - sigmoid_value))


def conv_volume(padded, weight):
    source_width = weight.shape[0] // 27
    kernel = weight.reshape(3, 3, 3, source_width, weight.shape[1])
    return lax.conv_general_dilated(
        padded[None],
        kernel,
        (1, 1, 1),
        "VALID",
        dimension_numbers=("NDHWC", "DHWIO", "NDHWC"),
        preferred_element_type=jnp.float32,
    )[0]


def flipped_volume(weight):
    source_width = weight.shape[0] // 27
    target_width = weight.shape[1]
    kernel = weight.reshape(3, 3, 3, source_width, target_width)[::-1, ::-1, ::-1]
    return jnp.transpose(kernel, (0, 1, 2, 4, 3)).reshape(27 * target_width, source_width)


def volume_patches(padded, frame_count, row_count, col_count):
    pieces = []
    for frame_step in range(3):
        for row_step in range(3):
            for col_step in range(3):
                pieces.append(
                    padded[
                        frame_step : frame_step + frame_count,
                        row_step : row_step + row_count,
                        col_step : col_step + col_count,
                    ]
                )
    stacked = jnp.concatenate(pieces, axis=-1)
    return stacked.reshape(frame_count * row_count * col_count, -1)


def reduce_kernel(
    a_ref, b_ref, out_ref, core_in, held, x_in, y_in, mid_a, mid_b, last, z_in, send_sem, recv_sem
):
    g, r, c = lax.axis_index("grp"), lax.axis_index("row"), lax.axis_index("col")
    zh, x, y, core = r // 4, lax.rem(r, 4), c // 2, lax.rem(c, 2)
    z = g * 2 + zh
    other = 1 - core

    def at_x(step):
        return (g, zh * 4 + lax.rem(x + step, 4), c)

    def at_y(step):
        return (g, r, lax.rem(y + step, 4) * 2 + core)

    def at_z(step):
        to = lax.rem(z + step, 8)
        return (to // 2, lax.rem(to, 2) * 4 + x, c)

    partner = (g, r, y * 2 + other)
    barrier = pltpu.get_barrier_semaphore()
    everyone = [partner] + [at_x(s) for s in (1, 2, 3)] + [at_y(s) for s in (1, 2, 3)]
    everyone += [at_z(s) for s in range(1, 8)]
    for peer in everyone:
        pl.semaphore_signal(barrier, inc=1, device_id=peer, device_id_type=MESH)
    pl.semaphore_wait(barrier, len(everyone))

    def send(src, dst, slot, peer):
        copy = pltpu.make_async_remote_copy(
            src_ref=src,
            dst_ref=dst,
            send_sem=send_sem.at[slot],
            recv_sem=recv_sem.at[slot],
            device_id=peer,
            device_id_type=MESH,
        )
        copy.start()
        return copy

    f32, b16 = jnp.float32, jnp.bfloat16
    first = [
        send(a_ref.at[other], core_in.at[0], 0, partner),
        send(b_ref.at[other], core_in.at[1], 1, partner),
    ]
    first[0].wait()
    held[0] = (a_ref[core].astype(f32) + core_in[0].astype(f32)).astype(b16)
    step_a = [
        send(held.at[0, :, lax.rem(x + s, 4)], x_in.at[s - 1], 1 + s, at_x(s)) for s in (1, 2, 3)
    ]
    first[1].wait()
    held[1] = (b_ref[core].astype(f32) + core_in[1].astype(f32)).astype(b16)
    step_b = [
        send(held.at[1, :, :, lax.rem(y + s, 4)], y_in.at[s - 1], 4 + s, at_y(s)) for s in (1, 2, 3)
    ]
    for copy in step_a:
        copy.wait()
    total = held[0, :, x].astype(f32)
    for s in range(3):
        total += x_in[s].astype(f32)
    mid_a[...] = total.astype(b16)
    next_a = [
        send(mid_a.at[:, lax.rem(y + s, 4)], last.at[0, s - 1], 7 + s, at_y(s)) for s in (1, 2, 3)
    ]
    for copy in step_b:
        copy.wait()
    total = held[1, :, :, y].astype(f32)
    for s in range(3):
        total += y_in[s].astype(f32)
    mid_b[...] = total.astype(b16)
    next_b = [
        send(mid_b.at[:, lax.rem(x + s, 4)], last.at[1, s - 1], 10 + s, at_x(s)) for s in (1, 2, 3)
    ]
    for copy in next_a:
        copy.wait()
    total = mid_a[:, y].astype(f32)
    for s in range(3):
        total += last[0, s].astype(f32)
    last[0, 3] = total.astype(b16)
    final_a = [
        send(last.at[0, 3, lax.rem(z + s, 8)], z_in.at[0, s - 1], 13 + s, at_z(s)) for s in range(1, 8)
    ]
    for copy in next_b:
        copy.wait()
    total = mid_b[:, x].astype(f32)
    for s in range(3):
        total += last[1, s].astype(f32)
    last[1, 3] = total.astype(b16)
    final_b = [
        send(last.at[1, 3, lax.rem(z + s, 8)], z_in.at[1, s - 1], 20 + s, at_z(s)) for s in range(1, 8)
    ]
    for which, copies in ((0, final_a), (1, final_b)):
        for copy in copies:
            copy.wait()
        total = last[which, 3, z].astype(f32)
        for s in range(7):
            total += z_in[which, s].astype(f32)
        out_ref[which] = total


def chip_layout(terms):
    rows = terms.astype(jnp.bfloat16).reshape(128, 27, 128)
    halves = jnp.stack([rows[:, :14], rows[:, 13:]])
    return jnp.pad(halves, ((0, 0), (0, 0), (0, 2), (0, 0))).reshape(2, 8, 4, 4, 16, 128)


def scattered_sums(first_terms, second_terms):
    b16 = jnp.bfloat16
    sums = pl.pallas_call(
        reduce_kernel,
        out_shape=jax.ShapeDtypeStruct((2, 16, 128), jnp.float32),
        in_specs=[pl.BlockSpec(memory_space=pltpu.VMEM)] * 2,
        out_specs=pl.BlockSpec(memory_space=pltpu.VMEM),
        scratch_shapes=[
            pltpu.VMEM((2, 8, 4, 4, 16, 128), b16),
            pltpu.VMEM((2, 8, 4, 4, 16, 128), b16),
            pltpu.VMEM((3, 8, 4, 16, 128), b16),
            pltpu.VMEM((3, 8, 4, 16, 128), b16),
            pltpu.VMEM((8, 4, 16, 128), b16),
            pltpu.VMEM((8, 4, 16, 128), b16),
            pltpu.VMEM((2, 4, 8, 16, 128), b16),
            pltpu.VMEM((2, 7, 16, 128), b16),
            pltpu.SemaphoreType.DMA((28,)),
            pltpu.SemaphoreType.DMA((28,)),
        ],
        compiler_params=pltpu.CompilerParams(
            collective_id=1, has_side_effects=True, vmem_limit_bytes=40 * 2**20
        ),
    )(chip_layout(first_terms), chip_layout(second_terms))
    flat = sums[:, :14].reshape(2, 14 * 128)
    start = lax.rem(lax.axis_index("col"), 2) * 64
    own = lax.dynamic_slice_in_dim(flat, start, 1728, axis=1)
    return own[0], own[1]


def position():
    return lax.axis_index("grp"), lax.axis_index("row"), lax.axis_index("col")


def same_place(one, other):
    return (one[0] == other[0]) & (one[1] == other[1]) & (one[2] == other[2])


def row_count(r):
    return 1 + jnp.where(r > 0, 1, 0) + jnp.where(r < 7, 1, 0)


def remote(src, dst, sems, slot, peer):
    return pltpu.make_async_remote_copy(
        src_ref=src,
        dst_ref=dst,
        send_sem=sems[0].at[slot],
        recv_sem=sems[1].at[slot],
        device_id=peer,
        device_id_type=MESH,
    )


def halo_kernel(
    own_ref, left_ref, right_ref, guide_ref,
    top_out, bottom_out, left_out, right_out, corner_out, guide_out, send_sem, recv_sem,
):
    g, r, c = position()
    sems = (send_sem, recv_sem)
    west, east = (g, r, lax.rem(c + 7, 8)), (g, r, lax.rem(c + 1, 8))
    has_up, has_down = r > 0, r < 7
    barrier = pltpu.get_barrier_semaphore()

    def greet(row_index):
        for step in (7, 0, 1):
            peer = (g, row_index, lax.rem(c + step, 8))
            pl.semaphore_signal(barrier, inc=1, device_id=peer, device_id_type=MESH)

    for peer in (west, east):
        pl.semaphore_signal(barrier, inc=1, device_id=peer, device_id_type=MESH)
    pl.when(has_up)(lambda: greet(r - 1))
    pl.when(has_down)(lambda: greet(r + 1))
    pl.semaphore_wait(barrier, 3 * row_count(r) - 1)
    sideways = [
        remote(left_ref, right_out, sems, 0, west),
        remote(right_ref, left_out, sems, 1, east),
    ]

    def to_row(row_index, rows, strip_out, corners, guide_slot, first_slot):
        west_peer = (g, row_index, west[2])
        east_peer = (g, row_index, east[2])
        here = (g, row_index, c)
        return [
            remote(own_ref.at[:, rows], strip_out, sems, first_slot, here),
            remote(guide_ref, guide_out.at[guide_slot], sems, first_slot + 1, here),
            remote(left_ref.at[rows], corner_out.at[corners + 1], sems, first_slot + 2, west_peer),
            remote(right_ref.at[rows], corner_out.at[corners], sems, first_slot + 3, east_peer),
        ]

    upward = to_row(r - 1, pl.ds(0, 3), bottom_out, 2, 1, 2)
    downward = to_row(r + 1, pl.ds(5, 3), top_out, 0, 0, 6)

    def start(copies):
        for copy in copies:
            copy.start()

    def sent(copies):
        for copy in copies:
            copy.wait_send()

    def landed(copies):
        for copy in copies:
            copy.wait_recv()

    pl.when(has_up)(lambda: start(upward))
    pl.when(has_down)(lambda: start(downward))
    start(sideways)
    landed(sideways)
    pl.when(has_down)(lambda: landed(upward))
    pl.when(has_up)(lambda: landed(downward))
    sent(sideways)
    pl.when(has_up)(lambda: sent(upward))
    pl.when(has_down)(lambda: sent(downward))


def colour_kernel(colour_ref, out_ref, send_sem, recv_sem, own_sem):
    g, r, c = position()
    me = (g, r, c)
    barrier = pltpu.get_barrier_semaphore()
    perceives = g < 3
    source_group = (8 * g + c) // 6

    def signal(peer):
        @pl.when(jnp.logical_not(same_place(peer, me)))
        def _():
            pl.semaphore_signal(barrier, inc=1, device_id=peer, device_id_type=MESH)

    def on_rows(do):
        for step in (-1, 0, 1):
            pl.when((r + step >= 0) & (r + step < 8))(functools.partial(do, step))

    def greet(step):
        for column in range(8):
            signal((source_group, r + step, column))

    def targets(step):
        for slot in range(6):
            frame = 6 * g + slot
            yield slot, (frame // 8, r + step, lax.rem(frame, 8))

    pl.when(perceives)(lambda: on_rows(greet))
    to_itself = jnp.where(perceives & (2 * g + c < 6), 1, 0)
    pl.semaphore_wait(barrier, 6 * row_count(r) - to_itself)

    def outgoing(step, slot, peer):
        return pltpu.make_async_remote_copy(
            src_ref=colour_ref.at[slot],
            dst_ref=out_ref.at[1 - step, c],
            send_sem=send_sem.at[step + 1, slot],
            recv_sem=recv_sem.at[1 - step, c],
            device_id=peer,
            device_id_type=MESH,
        )

    def kept(slot):
        return pltpu.make_async_copy(colour_ref.at[slot], out_ref.at[1, c], own_sem)

    def start(step):
        for slot, peer in targets(step):
            away = jnp.logical_not(same_place(peer, me))
            pl.when(away)(lambda: outgoing(step, slot, peer).start())
            if step == 0:
                pl.when(jnp.logical_not(away))(lambda: kept(slot).start())

    def arrive(step):
        for column in range(8):
            source = (source_group, r + step, column)
            away = jnp.logical_not(same_place(source, me))

            @pl.when(away)
            def _():
                pltpu.make_async_remote_copy(
                    src_ref=colour_ref.at[0],
                    dst_ref=out_ref.at[step + 1, column],
                    send_sem=send_sem.at[0, 0],
                    recv_sem=recv_sem.at[step + 1, column],
                    device_id=source,
                    device_id_type=MESH,
                ).wait_recv()

    def finish(step):
        for slot, peer in targets(step):
            away = jnp.logical_not(same_place(peer, me))
            pl.when(away)(lambda: outgoing(step, slot, peer).wait_send())
            if step == 0:
                pl.when(jnp.logical_not(away))(lambda: kept(slot).wait())

    on_rows(start)
    pl.when(perceives)(lambda: on_rows(arrive))
    on_rows(finish)


def pixel_kernel(strip_ref, out_ref, send_sem, recv_sem, own_sem):
    g, r, c = position()
    me = (g, r, c)
    barrier = pltpu.get_barrier_semaphore()
    perceives = g < 3
    frame = 8 * g + c
    home = frame // 6
    place = lax.rem(frame, 6)
    before = perceives & (place == 0) & (home > 0)
    after = perceives & (place == 5) & (home < 3)

    def on_rows(do):
        for step in (-1, 0, 1):
            pl.when((r + step >= 0) & (r + step < 8))(functools.partial(do, step))

    def sources(do):
        for slot in range(8):
            source_frame = 6 * g - 1 + slot
            inside = (source_frame >= 0) & (source_frame < 24)

            def each(step, slot=slot, source_frame=source_frame):
                source = (source_frame // 8, r + step, lax.rem(source_frame, 8))
                pl.when(jnp.logical_not(same_place(source, me)))(
                    functools.partial(do, step, slot, source)
                )

            pl.when(inside)(functools.partial(on_rows, each))

    def greet(step, slot, source):
        pl.semaphore_signal(barrier, inc=1, device_id=source, device_id_type=MESH)

    def targets(do):
        for kind, (group, needed) in enumerate(
            ((home, perceives), (home - 1, before), (home + 1, after))
        ):

            def each(step, kind=kind, group=group):
                for column in range(8):
                    peer = (group, r + step, column)
                    do(kind, step, column, peer, jnp.logical_not(same_place(peer, me)))

            pl.when(needed)(functools.partial(on_rows, each))

    sources(greet)
    groups = jnp.where(perceives, 1, 0) + jnp.where(before, 1, 0) + jnp.where(after, 1, 0)
    to_itself = perceives & (home == g) | before & (home == g + 1) | after & (home == g - 1)
    awaited = 8 * row_count(r) * groups - jnp.where(to_itself, 1, 0)
    pl.when(perceives)(lambda: pl.semaphore_wait(barrier, awaited))

    def outgoing(kind, step, column, peer):
        return pltpu.make_async_remote_copy(
            src_ref=strip_ref,
            dst_ref=out_ref.at[frame - 6 * peer[0] + 1, 1 - step],
            send_sem=send_sem.at[kind, step + 1, column],
            recv_sem=recv_sem.at[frame - 6 * peer[0] + 1, 1 - step],
            device_id=peer,
            device_id_type=MESH,
        )

    def kept():
        return pltpu.make_async_copy(strip_ref, out_ref.at[frame - 6 * g + 1, 1], own_sem)

    def start(kind, step, column, peer, away):
        pl.when(away)(lambda: outgoing(kind, step, column, peer).start())
        if step == 0:
            pl.when(jnp.logical_not(away))(lambda: kept().start())

    def finish(kind, step, column, peer, away):
        pl.when(away)(lambda: outgoing(kind, step, column, peer).wait_send())
        if step == 0:
            pl.when(jnp.logical_not(away))(lambda: kept().wait())

    def arrive(step, slot, source):
        pltpu.make_async_remote_copy(
            src_ref=strip_ref,
            dst_ref=out_ref.at[slot, step + 1],
            send_sem=send_sem.at[0, 0, 0],
            recv_sem=recv_sem.at[slot, step + 1],
            device_id=source,
            device_id_type=MESH,
        ).wait_recv()

    targets(start)
    sources(arrive)
    targets(finish)


def in_vmem(count):
    return [pl.BlockSpec(memory_space=pltpu.VMEM)] * count


def b16(*shape):
    return jax.ShapeDtypeStruct(shape, jnp.bfloat16)


def exchange(kernel, ident, outs, sems, *operands):
    outs = tuple(outs)
    return pl.pallas_call(
        kernel,
        out_shape=outs,
        in_specs=in_vmem(len(operands)),
        out_specs=tuple(in_vmem(len(outs))),
        scratch_shapes=[pltpu.SemaphoreType.DMA(shape) for shape in sems],
        compiler_params=pltpu.CompilerParams(
            collective_id=ident, has_side_effects=True, vmem_limit_bytes=24 * 2**20
        ),
    )(*operands)


def transposed_dot(one, other):
    return lax.dot_general(one, other, (((0,), (0,)), ((), ())), preferred_element_type=jnp.float32)


def side_by_side(value):
    cols = value.shape[0]
    at = lax.broadcasted_iota(jnp.int32, value.shape, 0)
    before = jnp.where(at == 0, 0.0, pltpu.roll(value, 1, 0))
    after = jnp.where(at == cols - 1, 0.0, pltpu.roll(value, cols - 1, 0))
    return jnp.concatenate([before, value, after], axis=1).astype(jnp.bfloat16)


def three_rows(ref, row, count):
    parts = [ref[pl.ds(row + step, count)].reshape(-1, ref.shape[-1]) for step in range(3)]
    return jnp.concatenate(parts, axis=1)


def dot32(one, other):
    return jnp.dot(one, other, preferred_element_type=jnp.float32)


def gelu_both(preact, slope_too):
    square = preact * preact
    inner_tanh = jnp.tanh(gelu_scale * preact * (1.0 + gelu_cubic * square))
    half = 0.5 * (1.0 + inner_tanh)
    value = preact * half
    if not slope_too:
        return value, None
    bend = (0.5 * gelu_scale) * (1.0 + 3.0 * gelu_cubic * square)
    return value, half + preact * (1.0 - inner_tanh * inner_tanh) * bend


def perceptual_kernel(
    planes_ref, w1_ref, w2_ref, w3_ref, w3_back_ref, w2_back_ref, w1_back_ref, out_ref,
    taps, act1, slope1, pooled, delta3, diff2, slope2, delta2, delta1, tmp, pixels,
):
    row0 = lax.axis_index("row") * 8 - 8
    lane = lax.broadcasted_iota(jnp.int32, (192, 128), 1)
    planes = planes_ref[...].reshape(192, 128)
    before = jnp.where(lane == 0, 0.0, pltpu.roll(planes, 1, 1))
    after = jnp.where(lane == 127, 0.0, pltpu.roll(planes, 127, 1))
    taps[:, 0:8] = before.reshape(24, 8, 128)
    taps[:, 8:16] = planes.reshape(24, 8, 128)
    taps[:, 16:24] = after.reshape(24, 8, 128)

    def shown(row):
        return (row0 + row >= 0) & (row0 + row < 64)

    def kept(row, value):
        return jnp.where(shown(row), value, 0.0)

    def first_rows(low, high, slope_too):
        @pl.loop(low, high)
        def _(i):
            cells = taps[pl.ds(i, 3)].reshape(72, 128).astype(jnp.bfloat16)
            value, slope = gelu_both(transposed_dot(cells, w1_ref[...]), slope_too)
            act1[i] = side_by_side(kept(i + 1, value))
            if slope_too:
                slope1[i - 6] = slope

    first_rows(0, 6, False)
    first_rows(6, 16, True)
    first_rows(16, 22, False)

    def second_rows(low, high, slope_too):
        @pl.loop(low, high)
        def _(p):
            plane = dot32(three_rows(act1, 2 * p, 2), w2_ref[...])
            value, slope = gelu_both(plane, slope_too)
            value = kept(2 * p + 2, value)
            if slope_too:
                difference = 0.25 * (value - pltpu.roll(value, 64, 1))
                diff2[pl.ds(2 * p - 4, 2)] = difference.reshape(2, 128, 128)
                slope2[pl.ds(2 * p - 4, 2)] = slope.reshape(2, 128, 128)
            tmp[...] = value[:128] + value[128:]
            mean = 0.25 * (tmp[pl.ds(0, 64, 2)] + tmp[pl.ds(1, 64, 2)])
            pooled[p] = side_by_side(mean)

    second_rows(0, 2, False)
    second_rows(2, 8, True)
    second_rows(8, 10, False)

    @pl.loop(0, 4)
    def _(half):
        j = 2 * half
        plane = dot32(three_rows(pooled, j, 2), w3_ref[...])
        value, slope = gelu_both(plane[:, :128], True)
        guide, _ = gelu_both(plane[:, 128:], False)
        delta = 0.5 * (value - guide) * slope
        delta3[j] = side_by_side(kept(2 * j + 4, delta[:64]))
        delta3[j + 1] = side_by_side(kept(2 * j + 6, delta[64:]))

    @pl.loop(0, 6)
    def _(m):
        grad = 0.25 * dot32(three_rows(delta3, m, 1), w3_back_ref[...])
        tmp[pl.ds(0, 64, 2)] = grad
        tmp[pl.ds(1, 64, 2)] = grad
        spread = tmp[...]
        for k in range(2):
            delta = (spread + diff2[2 * m + k]) * slope2[2 * m + k]
            delta2[2 * m + k] = side_by_side(kept(2 * m + 6, delta))

    @pl.loop(0, 5)
    def _(half):
        n = 2 * half
        grad = dot32(three_rows(delta2, n, 2), w2_back_ref[...])
        for k in range(2):
            delta = grad[128 * k : 128 * (k + 1)] * slope1[n + k]
            delta1[n + k] = side_by_side(kept(n + k + 7, delta))

    @pl.loop(0, 8)
    def _(q):
        grad = lax.dot_general(
            w1_back_ref[...],
            three_rows(delta1, q, 1),
            (((1,), (1,)), ((), ())),
            preferred_element_type=jnp.float32,
        )
        own = planes_ref[q + 8]
        direct = (1.0 / 6.0) * (own - pltpu.roll(own, 5, 0))
        pixels[pl.ds(pl.multiple_of(q * 8, 8), 8)] = grad + direct

    rows = [pixels[pl.ds(k, 8, 8)] for k in range(3)] + [jnp.zeros((8, 128), jnp.float32)]
    out_ref[...] = jnp.concatenate(rows, axis=0).astype(jnp.bfloat16)


def two_blocks(weight):
    _, i, o = weight.shape
    return jnp.pad(weight, ((0, 0), (0, i), (0, o))) + jnp.pad(weight, ((0, 0), (i, 0), (o, 0)))


def perceptual_weights(vgg_first, vgg_second, vgg_third):
    first = vgg_first.reshape(9, 3, 64)
    w1 = jnp.pad(two_blocks(first), ((0, 0), (0, 2), (0, 0))).reshape(72, 128)
    second = vgg_second.reshape(9, 64, 64)
    third = vgg_third.reshape(9, 64, 128)
    w2 = two_blocks(second).reshape(1152, 128)
    w3 = two_blocks(third).reshape(1152, 256)
    w3_back = jnp.pad(jnp.transpose(third[::-1], (0, 2, 1)), ((0, 0), (0, 0), (0, 64))).reshape(1152, 128)
    w2_back = jnp.pad(jnp.transpose(second[::-1], (0, 2, 1)), ((0, 0), (0, 64), (0, 64))).reshape(1152, 128)
    w1_back = jnp.pad(jnp.transpose(first[::-1], (1, 0, 2)), ((0, 5), (0, 0), (0, 64))).reshape(8, 1152)
    return w1, w2, w3, w3_back, w2_back, w1_back


def perceptual_strip(planes, weights):
    f32, half = jnp.float32, jnp.bfloat16
    return pl.pallas_call(
        perceptual_kernel,
        out_shape=b16(32, 128),
        in_specs=in_vmem(7),
        out_specs=in_vmem(1)[0],
        scratch_shapes=[
            pltpu.VMEM((24, 24, 128), f32),
            pltpu.VMEM((22, 128, 384), half),
            pltpu.VMEM((10, 128, 128), f32),
            pltpu.VMEM((10, 64, 384), half),
            pltpu.VMEM((8, 64, 384), half),
            pltpu.VMEM((12, 128, 128), f32),
            pltpu.VMEM((12, 128, 128), f32),
            pltpu.VMEM((12, 128, 384), half),
            pltpu.VMEM((10, 128, 384), half),
            pltpu.VMEM((128, 128), f32),
            pltpu.VMEM((64, 128), f32),
        ],
        compiler_params=pltpu.CompilerParams(vmem_limit_bytes=40 * 2**20),
    )(planes, *weights)


def inside(start, count, limit):
    positions = start + jnp.arange(count)
    return (positions >= 0) & (positions < limit)


def cell_mask(frame0, frames, row0, rows, col0, cols):
    keep_frames = inside(frame0, frames, 24)
    keep_rows = inside(row0, rows, 64)
    keep_cols = inside(col0, cols, 128)
    return (keep_frames[:, None, None] & keep_rows[None, :, None] & keep_cols[None, None, :])[
        ..., None
    ]


def local(dec_input, target, conv_first, conv_second, rgb_weight, vgg_first, vgg_second, vgg_third):
    g, r, c = position()
    channels = dec_input.shape[-1]
    frame0, row0, col0 = 6 * g, 8 * r, 16 * c
    video = jnp.pad(dec_input.reshape(24, 8, 16, channels), ((3, 3), (0, 0), (0, 0), (0, 0)))
    own = lax.dynamic_slice_in_dim(video, frame0, 12, axis=0)

    def columns(part):
        return jnp.transpose(part, (1, 0, 2, 3)).reshape(8, 48, channels)

    guide_own = lax.dynamic_index_in_dim(target, jnp.minimum(g, 2), 1, keepdims=False)
    guide_own = guide_own.reshape(24, 128)
    top, bottom, left, right, corners, guide_near = exchange(
        halo_kernel,
        2,
        (
            b16(12, 3, 16, channels), b16(12, 3, 16, channels), b16(8, 48, channels),
            b16(8, 48, channels), b16(4, 3, 48, channels), b16(2, 32, 128),
        ),
        ((10,), (10,)),
        own,
        columns(own[:, :, :4]),
        columns(own[:, :, 12:]),
        jnp.pad(guide_own, ((0, 8), (0, 0))),
    )

    def strip(part):
        return jnp.transpose(part.reshape(-1, 12, 4, channels), (1, 0, 2, 3))

    padded = jnp.concatenate(
        [
            jnp.concatenate([strip(corners[0]), top, strip(corners[1])], axis=2),
            jnp.concatenate([strip(left), own, strip(right)], axis=2),
            jnp.concatenate([strip(corners[2]), bottom, strip(corners[3])], axis=2),
        ],
        axis=1,
    )
    padded = jnp.where(
        inside(row0 - 3, 14, 64)[None, :, None, None] & inside(col0 - 4, 24, 128)[None, None, :, None],
        padded,
        jnp.zeros_like(padded),
    )
    first_pre = conv_volume(padded[:, :, 1:23], conv_first)
    first_keep = cell_mask(frame0 - 2, 10, row0 - 2, 12, col0 - 2, 20)
    first_out = jnp.where(first_keep, jax.nn.silu(first_pre), 0.0).astype(jnp.bfloat16)
    second_pre = conv_volume(first_out, conv_second)
    second_out = jax.nn.silu(second_pre[1:7, 1:9, 1:17]).astype(jnp.bfloat16)
    colour = jnp.einsum(
        "fnc,kc->fkn", second_out.reshape(6, 128, channels), rgb_weight, preferred_element_type=jnp.float32
    ).astype(jnp.bfloat16)
    colour_near = exchange(
        colour_kernel,
        3,
        (b16(3, 8, 16, 128),),
        ((3, 6), (3, 8), ()),
        jnp.pad(colour, ((0, 0), (0, 13), (0, 0))),
    )[0]
    images = jnp.transpose(colour_near[:, :, :3].reshape(3, 8, 3, 8, 16), (0, 3, 2, 1, 4))
    guides = jnp.stack(
        [guide_near[0, :24].reshape(3, 8, 128), guide_own.reshape(3, 8, 128), guide_near[1, :24].reshape(3, 8, 128)]
    )
    guides = jnp.transpose(guides, (0, 2, 1, 3))
    planes = jnp.concatenate([images.reshape(24, 3, 128), guides.reshape(24, 3, 128)], axis=1)
    planes = jnp.where(inside(row0 - 8, 24, 64)[:, None, None], planes, jnp.zeros_like(planes))
    planes = jnp.pad(planes.astype(jnp.float32), ((0, 0), (0, 2), (0, 0)))
    strip_out = perceptual_strip(planes, perceptual_weights(vgg_first, vgg_second, vgg_third))
    returned = exchange(
        pixel_kernel,
        4,
        (b16(8, 3, 32, 128),),
        ((3, 3, 8), (8, 3), ()),
        strip_out,
    )[0]
    rows_near = jnp.transpose(returned[:, :, :24].reshape(8, 3, 3, 8, 128), (2, 0, 1, 3, 4))
    rows_near = rows_near.reshape(3, 8, 24, 128)[:, :, 7:17]
    rows_near = jnp.pad(rows_near, ((0, 0), (0, 0), (0, 0), (1, 1)))
    pixel_part = lax.dynamic_slice_in_dim(rows_near, col0, 18, axis=3).astype(jnp.float32)
    second_keep = cell_mask(frame0 - 1, 8, row0 - 1, 10, col0 - 1, 18)
    pixel_part = jnp.where(second_keep[None, ..., 0], pixel_part, 0.0)
    hidden_grad = jnp.einsum(
        "kfhw,kc->fhwc",
        pixel_part,
        rgb_weight.astype(jnp.float32),
        precision=lax.Precision.HIGHEST,
    )
    decoder_second = (hidden_grad * silu_slope(second_pre)).astype(jnp.bfloat16)
    second_patches = volume_patches(first_out[1:9, 1:11, 1:19], 6, 8, 16)
    grad_second = jnp.dot(
        second_patches.T,
        decoder_second[1:7, 1:9, 1:17].reshape(-1, channels),
        preferred_element_type=jnp.float32,
    )
    hidden_back = conv_volume(decoder_second, flipped_volume(conv_second))
    decoder_hidden = (hidden_back * silu_slope(first_pre[2:8, 2:10, 2:18])).astype(jnp.bfloat16)
    first_patches = volume_patches(padded[2:10, 2:12, 3:21], 6, 8, 16)
    grad_first = jnp.dot(
        first_patches.T, decoder_hidden.reshape(-1, channels), preferred_element_type=jnp.float32
    )
    return scattered_sums(grad_first, grad_second)


def solution(mesh):
    in_specs = (
        P(None, None, "row", "col", None),
        P(None, None, "col", "row", None),
        P(),
        P(),
        P(),
        P(),
        P(),
        P(),
    )
    out_specs = (P(("grp", "row", "col")), P(("grp", "row", "col")))
    return jax.shard_map(local, mesh=mesh, in_specs=in_specs, out_specs=out_specs, check_vma=False)
```

```python
import functools

import jax
import jax.numpy as jnp
from jax import lax
from jax.experimental import pallas as pl
from jax.experimental.pallas import tpu as pltpu
from jax.sharding import PartitionSpec as P

MESH = pl.DeviceIdType.MESH

gelu_scale = 0.7978845608028654
gelu_cubic = 0.044715


def reduce_kernel(
    a_ref, b_ref, out_ref, core_in, held, x_in, y_in, mid_a, mid_b, last, z_in, send_sem, recv_sem
):
    g, r, c = lax.axis_index("grp"), lax.axis_index("row"), lax.axis_index("col")
    zh, x, y, core = r // 4, lax.rem(r, 4), c // 2, lax.rem(c, 2)
    z = g * 2 + zh
    other = 1 - core

    def at_x(step):
        return (g, zh * 4 + lax.rem(x + step, 4), c)

    def at_y(step):
        return (g, r, lax.rem(y + step, 4) * 2 + core)

    def at_z(step):
        to = lax.rem(z + step, 8)
        return (to // 2, lax.rem(to, 2) * 4 + x, c)

    partner = (g, r, y * 2 + other)
    barrier = pltpu.get_barrier_semaphore()
    everyone = [partner] + [at_x(s) for s in (1, 2, 3)] + [at_y(s) for s in (1, 2, 3)]
    everyone += [at_z(s) for s in range(1, 8)]
    for peer in everyone:
        pl.semaphore_signal(barrier, inc=1, device_id=peer, device_id_type=MESH)
    pl.semaphore_wait(barrier, len(everyone))

    def send(src, dst, slot, peer):
        copy = pltpu.make_async_remote_copy(
            src_ref=src,
            dst_ref=dst,
            send_sem=send_sem.at[slot],
            recv_sem=recv_sem.at[slot],
            device_id=peer,
            device_id_type=MESH,
        )
        copy.start()
        return copy

    f32, b16 = jnp.float32, jnp.bfloat16
    first = [
        send(a_ref.at[other], core_in.at[0], 0, partner),
        send(b_ref.at[other], core_in.at[1], 1, partner),
    ]
    first[0].wait()
    held[0] = (a_ref[core].astype(f32) + core_in[0].astype(f32)).astype(b16)
    step_a = [
        send(held.at[0, :, lax.rem(x + s, 4)], x_in.at[s - 1], 1 + s, at_x(s)) for s in (1, 2, 3)
    ]
    first[1].wait()
    held[1] = (b_ref[core].astype(f32) + core_in[1].astype(f32)).astype(b16)
    step_b = [
        send(held.at[1, :, :, lax.rem(y + s, 4)], y_in.at[s - 1], 4 + s, at_y(s)) for s in (1, 2, 3)
    ]
    for copy in step_a:
        copy.wait()
    total = held[0, :, x].astype(f32)
    for s in range(3):
        total += x_in[s].astype(f32)
    mid_a[...] = total.astype(b16)
    next_a = [
        send(mid_a.at[:, lax.rem(y + s, 4)], last.at[0, s - 1], 7 + s, at_y(s)) for s in (1, 2, 3)
    ]
    for copy in step_b:
        copy.wait()
    total = held[1, :, :, y].astype(f32)
    for s in range(3):
        total += y_in[s].astype(f32)
    mid_b[...] = total.astype(b16)
    next_b = [
        send(mid_b.at[:, lax.rem(x + s, 4)], last.at[1, s - 1], 10 + s, at_x(s)) for s in (1, 2, 3)
    ]
    for copy in next_a:
        copy.wait()
    total = mid_a[:, y].astype(f32)
    for s in range(3):
        total += last[0, s].astype(f32)
    last[0, 3] = total.astype(b16)
    final_a = [
        send(last.at[0, 3, lax.rem(z + s, 8)], z_in.at[0, s - 1], 13 + s, at_z(s)) for s in range(1, 8)
    ]
    for copy in next_b:
        copy.wait()
    total = mid_b[:, x].astype(f32)
    for s in range(3):
        total += last[1, s].astype(f32)
    last[1, 3] = total.astype(b16)
    final_b = [
        send(last.at[1, 3, lax.rem(z + s, 8)], z_in.at[1, s - 1], 20 + s, at_z(s)) for s in range(1, 8)
    ]
    for which, copies in ((0, final_a), (1, final_b)):
        for copy in copies:
            copy.wait()
        total = last[which, 3, z].astype(f32)
        for s in range(7):
            total += z_in[which, s].astype(f32)
        out_ref[which] = total


def scattered_sums(first_terms, second_terms):
    b16 = jnp.bfloat16
    sums = pl.pallas_call(
        reduce_kernel,
        out_shape=jax.ShapeDtypeStruct((2, 16, 128), jnp.float32),
        in_specs=[pl.BlockSpec(memory_space=pltpu.VMEM)] * 2,
        out_specs=pl.BlockSpec(memory_space=pltpu.VMEM),
        scratch_shapes=[
            pltpu.VMEM((2, 8, 4, 4, 16, 128), b16),
            pltpu.VMEM((2, 8, 4, 4, 16, 128), b16),
            pltpu.VMEM((3, 8, 4, 16, 128), b16),
            pltpu.VMEM((3, 8, 4, 16, 128), b16),
            pltpu.VMEM((8, 4, 16, 128), b16),
            pltpu.VMEM((8, 4, 16, 128), b16),
            pltpu.VMEM((2, 4, 8, 16, 128), b16),
            pltpu.VMEM((2, 7, 16, 128), b16),
            pltpu.SemaphoreType.DMA((28,)),
            pltpu.SemaphoreType.DMA((28,)),
        ],
        compiler_params=pltpu.CompilerParams(
            collective_id=1, has_side_effects=True, vmem_limit_bytes=40 * 2**20
        ),
    )(first_terms.reshape(2, 8, 4, 4, 16, 128), second_terms.reshape(2, 8, 4, 4, 16, 128))
    flat = sums[:, :14].reshape(2, 14 * 128)
    start = lax.rem(lax.axis_index("col"), 2) * 64
    own = lax.dynamic_slice_in_dim(flat, start, 1728, axis=1)
    return own[0], own[1]


def position():
    return lax.axis_index("grp"), lax.axis_index("row"), lax.axis_index("col")


def same_place(one, other):
    return (one[0] == other[0]) & (one[1] == other[1]) & (one[2] == other[2])


def row_count(r):
    return 1 + jnp.where(r > 0, 1, 0) + jnp.where(r < 7, 1, 0)


def remote(src, dst, sems, slot, peer):
    return pltpu.make_async_remote_copy(
        src_ref=src,
        dst_ref=dst,
        send_sem=sems[0].at[slot],
        recv_sem=sems[1].at[slot],
        device_id=peer,
        device_id_type=MESH,
    )


def halo_kernel(
    own_ref, left_ref, right_ref, guide_ref,
    top_out, bottom_out, left_out, right_out, corner_out, guide_out, send_sem, recv_sem,
):
    g, r, c = position()
    sems = (send_sem, recv_sem)
    west, east = (g, r, lax.rem(c + 7, 8)), (g, r, lax.rem(c + 1, 8))
    has_up, has_down = r > 0, r < 7
    barrier = pltpu.get_barrier_semaphore()

    def greet(row_index):
        for step in (7, 0, 1):
            peer = (g, row_index, lax.rem(c + step, 8))
            pl.semaphore_signal(barrier, inc=1, device_id=peer, device_id_type=MESH)

    for peer in (west, east):
        pl.semaphore_signal(barrier, inc=1, device_id=peer, device_id_type=MESH)
    pl.when(has_up)(lambda: greet(r - 1))
    pl.when(has_down)(lambda: greet(r + 1))
    pl.semaphore_wait(barrier, 3 * row_count(r) - 1)
    sideways = [
        remote(left_ref, right_out, sems, 0, west),
        remote(right_ref, left_out, sems, 1, east),
    ]

    def to_row(row_index, rows, strip_out, corners, guide_slot, first_slot):
        west_peer = (g, row_index, west[2])
        east_peer = (g, row_index, east[2])
        here = (g, row_index, c)
        return [
            remote(own_ref.at[:, rows], strip_out, sems, first_slot, here),
            remote(guide_ref, guide_out.at[guide_slot], sems, first_slot + 1, here),
            remote(left_ref.at[rows], corner_out.at[corners + 1], sems, first_slot + 2, west_peer),
            remote(right_ref.at[rows], corner_out.at[corners], sems, first_slot + 3, east_peer),
        ]

    upward = to_row(r - 1, pl.ds(0, 3), bottom_out, 2, 1, 2)
    downward = to_row(r + 1, pl.ds(5, 3), top_out, 0, 0, 6)

    def start(copies):
        for copy in copies:
            copy.start()

    def sent(copies):
        for copy in copies:
            copy.wait_send()

    def landed(copies):
        for copy in copies:
            copy.wait_recv()

    pl.when(has_up)(lambda: start(upward))
    pl.when(has_down)(lambda: start(downward))
    start(sideways)
    landed(sideways)
    pl.when(has_down)(lambda: landed(upward))
    pl.when(has_up)(lambda: landed(downward))
    sent(sideways)
    pl.when(has_up)(lambda: sent(upward))
    pl.when(has_down)(lambda: sent(downward))


def colour_kernel(colour_ref, out_ref, send_sem, recv_sem, own_sem):
    g, r, c = position()
    me = (g, r, c)
    barrier = pltpu.get_barrier_semaphore()
    perceives = g < 3
    source_group = (8 * g + c) // 6

    def signal(peer):
        @pl.when(jnp.logical_not(same_place(peer, me)))
        def _():
            pl.semaphore_signal(barrier, inc=1, device_id=peer, device_id_type=MESH)

    def on_rows(do):
        for step in (-1, 0, 1):
            pl.when((r + step >= 0) & (r + step < 8))(functools.partial(do, step))

    def greet(step):
        for column in range(8):
            signal((source_group, r + step, column))

    def targets(step):
        for slot in range(6):
            frame = 6 * g + slot
            yield slot, (frame // 8, r + step, lax.rem(frame, 8))

    pl.when(perceives)(lambda: on_rows(greet))
    to_itself = jnp.where(perceives & (2 * g + c < 6), 1, 0)
    pl.semaphore_wait(barrier, 6 * row_count(r) - to_itself)

    def outgoing(step, slot, peer):
        return pltpu.make_async_remote_copy(
            src_ref=colour_ref.at[slot + 1],
            dst_ref=out_ref.at[1 - step, c],
            send_sem=send_sem.at[step + 1, slot],
            recv_sem=recv_sem.at[1 - step, c],
            device_id=peer,
            device_id_type=MESH,
        )

    def kept(slot):
        return pltpu.make_async_copy(colour_ref.at[slot + 1], out_ref.at[1, c], own_sem)

    def start(step):
        for slot, peer in targets(step):
            away = jnp.logical_not(same_place(peer, me))
            pl.when(away)(lambda: outgoing(step, slot, peer).start())
            if step == 0:
                pl.when(jnp.logical_not(away))(lambda: kept(slot).start())

    def arrive(step):
        for column in range(8):
            source = (source_group, r + step, column)
            away = jnp.logical_not(same_place(source, me))

            @pl.when(away)
            def _():
                pltpu.make_async_remote_copy(
                    src_ref=colour_ref.at[0],
                    dst_ref=out_ref.at[step + 1, column],
                    send_sem=send_sem.at[0, 0],
                    recv_sem=recv_sem.at[step + 1, column],
                    device_id=source,
                    device_id_type=MESH,
                ).wait_recv()

    def finish(step):
        for slot, peer in targets(step):
            away = jnp.logical_not(same_place(peer, me))
            pl.when(away)(lambda: outgoing(step, slot, peer).wait_send())
            if step == 0:
                pl.when(jnp.logical_not(away))(lambda: kept(slot).wait())

    on_rows(start)
    pl.when(perceives)(lambda: on_rows(arrive))
    on_rows(finish)


def pixel_kernel(strip_ref, out_ref, send_sem, recv_sem, own_sem):
    g, r, c = position()
    me = (g, r, c)
    barrier = pltpu.get_barrier_semaphore()
    perceives = g < 3
    frame = 8 * g + c
    home = frame // 6
    place = lax.rem(frame, 6)
    before = perceives & (place == 0) & (home > 0)
    after = perceives & (place == 5) & (home < 3)

    def on_rows(do):
        for step in (-1, 0, 1):
            pl.when((r + step >= 0) & (r + step < 8))(functools.partial(do, step))

    def sources(do):
        for slot in range(8):
            source_frame = 6 * g - 1 + slot
            inside = (source_frame >= 0) & (source_frame < 24)

            def each(step, slot=slot, source_frame=source_frame):
                source = (source_frame // 8, r + step, lax.rem(source_frame, 8))
                pl.when(jnp.logical_not(same_place(source, me)))(
                    functools.partial(do, step, slot, source)
                )

            pl.when(inside)(functools.partial(on_rows, each))

    def greet(step, slot, source):
        pl.semaphore_signal(barrier, inc=1, device_id=source, device_id_type=MESH)

    def targets(do):
        for kind, (group, needed) in enumerate(
            ((home, perceives), (home - 1, before), (home + 1, after))
        ):

            def each(step, kind=kind, group=group):
                for column in range(8):
                    peer = (group, r + step, column)
                    do(kind, step, column, peer, jnp.logical_not(same_place(peer, me)))

            pl.when(needed)(functools.partial(on_rows, each))

    sources(greet)
    groups = jnp.where(perceives, 1, 0) + jnp.where(before, 1, 0) + jnp.where(after, 1, 0)
    to_itself = perceives & (home == g) | before & (home == g + 1) | after & (home == g - 1)
    awaited = 8 * row_count(r) * groups - jnp.where(to_itself, 1, 0)
    pl.when(perceives)(lambda: pl.semaphore_wait(barrier, awaited))

    def outgoing(kind, step, column, peer):
        return pltpu.make_async_remote_copy(
            src_ref=strip_ref,
            dst_ref=out_ref.at[frame - 6 * peer[0] + 1, 1 - step],
            send_sem=send_sem.at[kind, step + 1, column],
            recv_sem=recv_sem.at[frame - 6 * peer[0] + 1, 1 - step],
            device_id=peer,
            device_id_type=MESH,
        )

    def kept():
        return pltpu.make_async_copy(strip_ref, out_ref.at[frame - 6 * g + 1, 1], own_sem)

    def start(kind, step, column, peer, away):
        pl.when(away)(lambda: outgoing(kind, step, column, peer).start())
        if step == 0:
            pl.when(jnp.logical_not(away))(lambda: kept().start())

    def finish(kind, step, column, peer, away):
        pl.when(away)(lambda: outgoing(kind, step, column, peer).wait_send())
        if step == 0:
            pl.when(jnp.logical_not(away))(lambda: kept().wait())

    def arrive(step, slot, source):
        pltpu.make_async_remote_copy(
            src_ref=strip_ref,
            dst_ref=out_ref.at[slot, step + 1],
            send_sem=send_sem.at[0, 0, 0],
            recv_sem=recv_sem.at[slot, step + 1],
            device_id=source,
            device_id_type=MESH,
        ).wait_recv()

    targets(start)
    sources(arrive)
    targets(finish)


def in_vmem(count):
    return [pl.BlockSpec(memory_space=pltpu.VMEM)] * count


def b16(*shape):
    return jax.ShapeDtypeStruct(shape, jnp.bfloat16)


def exchange(kernel, ident, outs, sems, *operands):
    outs = tuple(outs)
    return pl.pallas_call(
        kernel,
        out_shape=outs,
        in_specs=in_vmem(len(operands)),
        out_specs=tuple(in_vmem(len(outs))),
        scratch_shapes=[pltpu.SemaphoreType.DMA(shape) for shape in sems],
        compiler_params=pltpu.CompilerParams(
            collective_id=ident, has_side_effects=True, vmem_limit_bytes=24 * 2**20
        ),
    )(*operands)


def transposed_dot(one, other):
    return lax.dot_general(one, other, (((0,), (0,)), ((), ())), preferred_element_type=jnp.float32)


def side_by_side(value):
    cols = value.shape[0]
    at = lax.broadcasted_iota(jnp.int32, value.shape, 0)
    before = jnp.where(at == 0, 0.0, pltpu.roll(value, 1, 0))
    after = jnp.where(at == cols - 1, 0.0, pltpu.roll(value, cols - 1, 0))
    return jnp.concatenate([before, value, after], axis=1).astype(jnp.bfloat16)


def three_rows(ref, row, count):
    parts = [ref[pl.ds(row + step, count)].reshape(-1, ref.shape[-1]) for step in range(3)]
    return jnp.concatenate(parts, axis=1)


def dot32(one, other):
    return jnp.dot(one, other, preferred_element_type=jnp.float32)


def gelu_both(preact, slope_too):
    square = preact * preact
    inner_tanh = jnp.tanh(gelu_scale * preact * (1.0 + gelu_cubic * square))
    half = 0.5 * (1.0 + inner_tanh)
    value = preact * half
    if not slope_too:
        return value, None
    bend = (0.5 * gelu_scale) * (1.0 + 3.0 * gelu_cubic * square)
    return value, half + preact * (1.0 - inner_tanh * inner_tanh) * bend


def perceptual_kernel(
    planes_ref, w1_ref, w2_ref, w3_ref, w3_back_ref, w2_back_ref, w1_back_ref, out_ref,
    taps, act1, slope1, pooled, delta3, diff2, slope2, delta2, delta1, tmp, pixels,
):
    row0 = lax.axis_index("row") * 8 - 8
    lane = lax.broadcasted_iota(jnp.int32, (192, 128), 1)
    planes = planes_ref[...].reshape(192, 128)
    before = jnp.where(lane == 0, 0.0, pltpu.roll(planes, 1, 1))
    after = jnp.where(lane == 127, 0.0, pltpu.roll(planes, 127, 1))
    taps[:, 0:8] = before.reshape(24, 8, 128)
    taps[:, 8:16] = planes.reshape(24, 8, 128)
    taps[:, 16:24] = after.reshape(24, 8, 128)

    def shown(row):
        return (row0 + row >= 0) & (row0 + row < 64)

    def kept(row, value):
        return jnp.where(shown(row), value, 0.0)

    def first_rows(low, high, slope_too):
        @pl.loop(low, high)
        def _(i):
            cells = taps[pl.ds(i, 3)].reshape(72, 128).astype(jnp.bfloat16)
            value, slope = gelu_both(transposed_dot(cells, w1_ref[...]), slope_too)
            act1[i] = side_by_side(kept(i + 1, value))
            if slope_too:
                slope1[i - 6] = slope

    first_rows(0, 6, False)
    first_rows(6, 16, True)
    first_rows(16, 22, False)

    def second_rows(low, high, slope_too):
        @pl.loop(low, high)
        def _(p):
            plane = dot32(three_rows(act1, 2 * p, 2), w2_ref[...])
            value, slope = gelu_both(plane, slope_too)
            value = kept(2 * p + 2, value)
            if slope_too:
                difference = 0.25 * (value - pltpu.roll(value, 64, 1))
                diff2[pl.ds(2 * p - 4, 2)] = difference.reshape(2, 128, 128)
                slope2[pl.ds(2 * p - 4, 2)] = slope.reshape(2, 128, 128)
            tmp[...] = value[:128] + value[128:]
            mean = 0.25 * (tmp[pl.ds(0, 64, 2)] + tmp[pl.ds(1, 64, 2)])
            pooled[p] = side_by_side(mean)

    second_rows(0, 2, False)
    second_rows(2, 8, True)
    second_rows(8, 10, False)

    @pl.loop(0, 4)
    def _(half):
        j = 2 * half
        plane = dot32(three_rows(pooled, j, 2), w3_ref[...])
        value, slope = gelu_both(plane[:, :128], True)
        guide, _ = gelu_both(plane[:, 128:], False)
        delta = 0.5 * (value - guide) * slope
        delta3[j] = side_by_side(kept(2 * j + 4, delta[:64]))
        delta3[j + 1] = side_by_side(kept(2 * j + 6, delta[64:]))

    @pl.loop(0, 6)
    def _(m):
        grad = 0.25 * dot32(three_rows(delta3, m, 1), w3_back_ref[...])
        tmp[pl.ds(0, 64, 2)] = grad
        tmp[pl.ds(1, 64, 2)] = grad
        spread = tmp[...]
        for k in range(2):
            delta = (spread + diff2[2 * m + k]) * slope2[2 * m + k]
            delta2[2 * m + k] = side_by_side(kept(2 * m + 6, delta))

    @pl.loop(0, 5)
    def _(half):
        n = 2 * half
        grad = dot32(three_rows(delta2, n, 2), w2_back_ref[...])
        for k in range(2):
            delta = grad[128 * k : 128 * (k + 1)] * slope1[n + k]
            delta1[n + k] = side_by_side(kept(n + k + 7, delta))

    @pl.loop(0, 8)
    def _(q):
        grad = lax.dot_general(
            w1_back_ref[...],
            three_rows(delta1, q, 1),
            (((1,), (1,)), ((), ())),
            preferred_element_type=jnp.float32,
        )
        own = planes_ref[q + 8]
        direct = (1.0 / 6.0) * (own - pltpu.roll(own, 5, 0))
        pixels[pl.ds(pl.multiple_of(q * 8, 8), 8)] = grad + direct

    rows = [pixels[pl.ds(k, 8, 8)] for k in range(3)] + [jnp.zeros((8, 128), jnp.float32)]
    out_ref[...] = jnp.concatenate(rows, axis=0).astype(jnp.bfloat16)


def two_blocks(weight):
    _, i, o = weight.shape
    return jnp.pad(weight, ((0, 0), (0, i), (0, o))) + jnp.pad(weight, ((0, 0), (i, 0), (o, 0)))


def perceptual_weights(vgg_first, vgg_second, vgg_third):
    first = vgg_first.reshape(9, 3, 64)
    w1 = jnp.pad(two_blocks(first), ((0, 0), (0, 2), (0, 0))).reshape(72, 128)
    second = vgg_second.reshape(9, 64, 64)
    third = vgg_third.reshape(9, 64, 128)
    w2 = two_blocks(second).reshape(1152, 128)
    w3 = two_blocks(third).reshape(1152, 256)
    w3_back = jnp.pad(jnp.transpose(third[::-1], (0, 2, 1)), ((0, 0), (0, 0), (0, 64))).reshape(1152, 128)
    w2_back = jnp.pad(jnp.transpose(second[::-1], (0, 2, 1)), ((0, 0), (0, 64), (0, 64))).reshape(1152, 128)
    w1_back = jnp.pad(jnp.transpose(first[::-1], (1, 0, 2)), ((0, 5), (0, 0), (0, 64))).reshape(8, 1152)
    return w1, w2, w3, w3_back, w2_back, w1_back


def perceptual_strip(planes, weights):
    f32, half = jnp.float32, jnp.bfloat16
    return pl.pallas_call(
        perceptual_kernel,
        out_shape=b16(32, 128),
        in_specs=in_vmem(7),
        out_specs=in_vmem(1)[0],
        scratch_shapes=[
            pltpu.VMEM((24, 24, 128), f32),
            pltpu.VMEM((22, 128, 384), half),
            pltpu.VMEM((10, 128, 128), f32),
            pltpu.VMEM((10, 64, 384), half),
            pltpu.VMEM((8, 64, 384), half),
            pltpu.VMEM((12, 128, 128), f32),
            pltpu.VMEM((12, 128, 128), f32),
            pltpu.VMEM((12, 128, 384), half),
            pltpu.VMEM((10, 128, 384), half),
            pltpu.VMEM((128, 128), f32),
            pltpu.VMEM((64, 128), f32),
        ],
        compiler_params=pltpu.CompilerParams(vmem_limit_bytes=40 * 2**20),
    )(planes, *weights)


def taps_in_lanes(weight_ref, out_ref):
    for q in range(9):
        for k in range(3):
            tap = 3 * q + k
            out_ref[128 * q : 128 * (q + 1), 128 * k : 128 * (k + 1)] = weight_ref[
                128 * tap : 128 * (tap + 1), :
            ]


def turned_taps(weight_ref, out_ref):
    for q in range(9):
        for k in range(3):
            tap = 26 - 3 * q - k
            block = weight_ref[128 * tap : 128 * (tap + 1), :].astype(jnp.float32)
            out_ref[128 * q : 128 * (q + 1), 128 * k : 128 * (k + 1)] = block.T.astype(jnp.bfloat16)


def conv_frame(source, frame, rows, taps_ref):
    parts = [
        source[frame + dt, pl.ds(dr, rows)].reshape(rows * 32, 128) for dt in range(3) for dr in range(3)
    ]
    sums = dot32(jnp.concatenate(parts, axis=1), taps_ref[...])
    total = pltpu.roll(sums[:, :128], 1, 0) + sums[:, 128:256]
    total += pltpu.roll(sums[:, 256:], rows * 32 - 1, 0)
    return total.reshape(rows, 32, 128)


def silu_parts(preact):
    gate = 1.0 / (1.0 + jnp.exp(-preact))
    return preact * gate, gate * (1.0 + preact * (1.0 - gate))


def forward_kernel(
    cells_ref, first_ref, second_ref, rgb_ref, hidden_out, slope1_out, slope2_out, colour_out, taps1, taps2
):
    g, r, c = position()
    taps_in_lanes(first_ref, taps1)
    taps_in_lanes(second_ref, taps2)
    row = lax.broadcasted_iota(jnp.int32, (12, 32, 128), 0) + (8 * r - 2)
    col = lax.broadcasted_iota(jnp.int32, (12, 32, 128), 1) + (16 * c - 8)
    shown = (row >= 0) & (row < 64) & (col >= 0) & (col < 128)

    @pl.loop(0, 10)
    def _(f):
        value, slope = silu_parts(conv_frame(cells_ref, f, 12, taps1))
        frame = 6 * g - 2 + f
        value = jnp.where(shown, value, 0.0) * jnp.where((frame >= 0) & (frame < 24), 1.0, 0.0)
        hidden_out[f] = value.astype(jnp.bfloat16)
        slope1_out[f] = slope[2:10, 8:24].reshape(128, 128)

    @pl.loop(0, 8)
    def _(f):
        value, slope = silu_parts(conv_frame(hidden_out, f, 10, taps2))
        slope2_out[f] = slope
        own = value[1:9, 8:24].reshape(128, 128).astype(jnp.bfloat16)
        colour = lax.dot_general(
            rgb_ref[...], own, (((1,), (1,)), ((), ())), preferred_element_type=jnp.float32
        )
        colour_out[f] = colour.astype(jnp.bfloat16)


def columns_in_lanes(source, frame0, row0, out_ref):
    @pl.loop(0, 8)
    def _(f):
        value = source[f + frame0, pl.ds(row0, 10)].reshape(320, 128).astype(jnp.float32)
        parts = [pltpu.roll(value, 1, 0), value, pltpu.roll(value, 319, 0)]
        for k, part in enumerate(parts):
            own = part.reshape(10, 32, 128)[:, 8:24]
            out_ref[f, :, :, 128 * k : 128 * (k + 1)] = own.astype(jnp.bfloat16)


def weight_terms(columns, delta, terms, out_ref):
    @pl.loop(0, 9)
    def _(q):
        cells = columns[pl.ds(q // 3, 6), pl.ds(lax.rem(q, 3), 8)].reshape(768, 384)
        terms[pl.ds(pl.multiple_of(384 * q, 384), 384)] = transposed_dot(cells, delta[...])

    terms[pl.ds(3456, 8)] = jnp.zeros((8, 128), jnp.float32)

    @pl.loop(0, 128)
    def _(p):
        out_ref[0, p] = terms[pl.ds(27 * p, 16)].astype(jnp.bfloat16)
        out_ref[1, p] = terms[pl.ds(27 * p + 13, 16)].astype(jnp.bfloat16)


def backward_kernel(
    pixel_ref, cells_ref, hidden_ref, slope1_ref, slope2_ref, second_ref, rgb_ref, first_out, second_out,
    taps, columns, field, delta, terms,
):
    turned_taps(second_ref, taps)

    @pl.loop(0, 8)
    def _(f):
        hidden_grad = transposed_dot(pixel_ref[f], rgb_ref[...])
        value = hidden_grad.reshape(10, 32, 128) * slope2_ref[f]
        field[f] = value.astype(jnp.bfloat16)

        @pl.when((f >= 1) & (f < 7))
        def _():
            own = value[1:9, 8:24].reshape(128, 128).astype(jnp.bfloat16)
            delta[pl.ds(pl.multiple_of(128 * (f - 1), 128), 128)] = own

    columns_in_lanes(hidden_ref, 1, 1, columns)
    weight_terms(columns, delta, terms, second_out)

    @pl.loop(0, 6)
    def _(f):
        back = conv_frame(field, f, 8, taps)[:, 8:24].reshape(128, 128)
        value = (back * slope1_ref[f + 2]).astype(jnp.bfloat16)
        delta[pl.ds(pl.multiple_of(128 * f, 128), 128)] = value

    columns_in_lanes(cells_ref, 2, 2, columns)
    weight_terms(columns, delta, terms, first_out)


def f32_shape(*shape):
    return jax.ShapeDtypeStruct(shape, jnp.float32)


def plain_call(kernel, outs, scratch, *operands):
    return pl.pallas_call(
        kernel,
        out_shape=tuple(outs),
        in_specs=in_vmem(len(operands)),
        out_specs=tuple(in_vmem(len(outs))),
        scratch_shapes=scratch,
        compiler_params=pltpu.CompilerParams(vmem_limit_bytes=48 * 2**20),
    )(*operands)


def inside(start, count, limit):
    positions = start + jnp.arange(count)
    return (positions >= 0) & (positions < limit)


def cell_mask(frame0, frames, row0, rows, col0, cols):
    keep_frames = inside(frame0, frames, 24)
    keep_rows = inside(row0, rows, 64)
    keep_cols = inside(col0, cols, 128)
    return (keep_frames[:, None, None] & keep_rows[None, :, None] & keep_cols[None, None, :])[
        ..., None
    ]


def local(dec_input, target, conv_first, conv_second, rgb_weight, vgg_first, vgg_second, vgg_third):
    g, r, c = position()
    channels = dec_input.shape[-1]
    frame0, row0, col0 = 6 * g, 8 * r, 16 * c
    video = jnp.pad(dec_input.reshape(24, 8, 16, channels), ((3, 3), (0, 0), (0, 0), (0, 0)))
    own = lax.dynamic_slice_in_dim(video, frame0, 12, axis=0)

    def columns(part):
        return jnp.transpose(part, (1, 0, 2, 3)).reshape(8, 48, channels)

    guide_own = lax.dynamic_index_in_dim(target, jnp.minimum(g, 2), 1, keepdims=False)
    guide_own = guide_own.reshape(24, 128)
    top, bottom, left, right, corners, guide_near = exchange(
        halo_kernel,
        2,
        (
            b16(12, 3, 16, channels), b16(12, 3, 16, channels), b16(8, 48, channels),
            b16(8, 48, channels), b16(4, 3, 48, channels), b16(2, 32, 128),
        ),
        ((10,), (10,)),
        own,
        columns(own[:, :, :4]),
        columns(own[:, :, 12:]),
        jnp.pad(guide_own, ((0, 8), (0, 0))),
    )

    def strip(part):
        return jnp.transpose(part.reshape(-1, 12, 4, channels), (1, 0, 2, 3))

    gap = jnp.zeros((12, 14, 4, channels), jnp.bfloat16)
    cells = jnp.concatenate(
        [
            gap,
            jnp.concatenate([strip(corners[0]), strip(left), strip(corners[2])], axis=1),
            jnp.concatenate([top, own, bottom], axis=1),
            jnp.concatenate([strip(corners[1]), strip(right), strip(corners[3])], axis=1),
            gap,
        ],
        axis=2,
    )
    cells = jnp.where(
        inside(row0 - 3, 14, 64)[None, :, None, None] & inside(col0 - 8, 32, 128)[None, None, :, None],
        cells,
        jnp.zeros_like(cells),
    )
    half = jnp.bfloat16
    rgb = jnp.pad(rgb_weight, ((0, 13), (0, 0)))
    hidden, slope1, slope2, colour = plain_call(
        forward_kernel,
        (b16(10, 12, 32, 128), f32_shape(10, 128, 128), f32_shape(8, 10, 32, 128), b16(8, 16, 128)),
        [pltpu.VMEM((1152, 384), half), pltpu.VMEM((1152, 384), half)],
        cells, conv_first, conv_second, rgb,
    )
    colour_near = exchange(
        colour_kernel,
        3,
        (b16(3, 8, 16, 128),),
        ((3, 6), (3, 8), ()),
        colour,
    )[0]
    images = jnp.transpose(colour_near[:, :, :3].reshape(3, 8, 3, 8, 16), (0, 3, 2, 1, 4))
    guides = jnp.stack(
        [guide_near[0, :24].reshape(3, 8, 128), guide_own.reshape(3, 8, 128), guide_near[1, :24].reshape(3, 8, 128)]
    )
    guides = jnp.transpose(guides, (0, 2, 1, 3))
    planes = jnp.concatenate([images.reshape(24, 3, 128), guides.reshape(24, 3, 128)], axis=1)
    planes = jnp.where(inside(row0 - 8, 24, 64)[:, None, None], planes, jnp.zeros_like(planes))
    planes = jnp.pad(planes.astype(jnp.float32), ((0, 0), (0, 2), (0, 0)))
    strip_out = perceptual_strip(planes, perceptual_weights(vgg_first, vgg_second, vgg_third))
    returned = exchange(
        pixel_kernel,
        4,
        (b16(8, 3, 32, 128),),
        ((3, 3, 8), (8, 3), ()),
        strip_out,
    )[0]
    rows_near = jnp.transpose(returned[:, :, :24].reshape(8, 3, 3, 8, 128), (2, 0, 1, 3, 4))
    rows_near = rows_near.reshape(3, 8, 24, 128)[:, :, 7:17]
    rows_near = jnp.pad(rows_near, ((0, 0), (0, 0), (0, 0), (8, 8)))
    pixels = lax.dynamic_slice_in_dim(rows_near, col0, 32, axis=3)
    pixel_keep = cell_mask(frame0 - 1, 8, row0 - 1, 10, col0 - 8, 32)
    pixels = jnp.where(pixel_keep[None, ..., 0], pixels, jnp.zeros_like(pixels))
    pixels = jnp.pad(jnp.transpose(pixels, (1, 0, 2, 3)).reshape(8, 3, 320), ((0, 0), (0, 13), (0, 0)))
    first_terms, second_terms = plain_call(
        backward_kernel,
        (b16(2, 128, 16, 128), b16(2, 128, 16, 128)),
        [
            pltpu.VMEM((1152, 384), half),
            pltpu.VMEM((8, 10, 16, 384), half),
            pltpu.VMEM((8, 10, 32, 128), half),
            pltpu.VMEM((768, 128), half),
            pltpu.VMEM((3464, 128), jnp.float32),
        ],
        pixels, cells, hidden, slope1, slope2, conv_second, rgb,
    )
    return scattered_sums(first_terms, second_terms)


def solution(mesh):
    in_specs = (
        P(None, None, "row", "col", None),
        P(None, None, "col", "row", None),
        P(),
        P(),
        P(),
        P(),
        P(),
        P(),
    )
    out_specs = (P(("grp", "row", "col")), P(("grp", "row", "col")))
    return jax.shard_map(local, mesh=mesh, in_specs=in_specs, out_specs=out_specs, check_vma=False)
```

```python
import functools

import jax
import jax.numpy as jnp
from jax import lax
from jax.experimental import pallas as pl
from jax.experimental.pallas import tpu as pltpu
from jax.sharding import PartitionSpec as P

MESH = pl.DeviceIdType.MESH

gelu_scale = 0.7978845608028654
gelu_cubic = 0.044715


def position():
    return lax.axis_index("grp"), lax.axis_index("row"), lax.axis_index("col")


def same_place(one, other):
    return (one[0] == other[0]) & (one[1] == other[1]) & (one[2] == other[2])


def row_count(r):
    return 1 + jnp.where(r > 0, 1, 0) + jnp.where(r < 7, 1, 0)


def remote(src, dst, sems, slot, peer):
    return pltpu.make_async_remote_copy(
        src_ref=src,
        dst_ref=dst,
        send_sem=sems[0].at[slot],
        recv_sem=sems[1].at[slot],
        device_id=peer,
        device_id_type=MESH,
    )


def halo_kernel(
    own_ref, left_ref, right_ref, guide_ref,
    top_out, bottom_out, left_out, right_out, corner_out, guide_out, send_sem, recv_sem,
):
    g, r, c = position()
    sems = (send_sem, recv_sem)
    west, east = (g, r, lax.rem(c + 7, 8)), (g, r, lax.rem(c + 1, 8))
    has_up, has_down = r > 0, r < 7
    barrier = pltpu.get_barrier_semaphore()

    def greet(row_index):
        for step in (7, 0, 1):
            peer = (g, row_index, lax.rem(c + step, 8))
            pl.semaphore_signal(barrier, inc=1, device_id=peer, device_id_type=MESH)

    for peer in (west, east):
        pl.semaphore_signal(barrier, inc=1, device_id=peer, device_id_type=MESH)
    pl.when(has_up)(lambda: greet(r - 1))
    pl.when(has_down)(lambda: greet(r + 1))
    pl.semaphore_wait(barrier, 3 * row_count(r) - 1)
    sideways = [
        remote(left_ref, right_out, sems, 0, west),
        remote(right_ref, left_out, sems, 1, east),
    ]

    def to_row(row_index, rows, strip_out, corners, guide_slot, first_slot):
        west_peer = (g, row_index, west[2])
        east_peer = (g, row_index, east[2])
        here = (g, row_index, c)
        return [
            remote(own_ref.at[:, rows], strip_out, sems, first_slot, here),
            remote(guide_ref, guide_out.at[guide_slot], sems, first_slot + 1, here),
            remote(left_ref.at[rows], corner_out.at[corners + 1], sems, first_slot + 2, west_peer),
            remote(right_ref.at[rows], corner_out.at[corners], sems, first_slot + 3, east_peer),
        ]

    upward = to_row(r - 1, pl.ds(0, 3), bottom_out, 2, 1, 2)
    downward = to_row(r + 1, pl.ds(5, 3), top_out, 0, 0, 6)

    def start(copies):
        for copy in copies:
            copy.start()

    def sent(copies):
        for copy in copies:
            copy.wait_send()

    def landed(copies):
        for copy in copies:
            copy.wait_recv()

    pl.when(has_up)(lambda: start(upward))
    pl.when(has_down)(lambda: start(downward))
    start(sideways)
    landed(sideways)
    pl.when(has_down)(lambda: landed(upward))
    pl.when(has_up)(lambda: landed(downward))
    sent(sideways)
    pl.when(has_up)(lambda: sent(upward))
    pl.when(has_down)(lambda: sent(downward))


def in_vmem(count):
    return [pl.BlockSpec(memory_space=pltpu.VMEM)] * count


def b16(*shape):
    return jax.ShapeDtypeStruct(shape, jnp.bfloat16)


def exchange(kernel, ident, outs, sems, *operands):
    outs = tuple(outs)
    return pl.pallas_call(
        kernel,
        out_shape=outs,
        in_specs=in_vmem(len(operands)),
        out_specs=tuple(in_vmem(len(outs))),
        scratch_shapes=[pltpu.SemaphoreType.DMA(shape) for shape in sems],
        compiler_params=pltpu.CompilerParams(
            collective_id=ident, has_side_effects=True, vmem_limit_bytes=24 * 2**20
        ),
    )(*operands)


def transposed_dot(one, other):
    return lax.dot_general(one, other, (((0,), (0,)), ((), ())), preferred_element_type=jnp.float32)


def side_by_side(value):
    cols = value.shape[0]
    at = lax.broadcasted_iota(jnp.int32, value.shape, 0)
    before = jnp.where(at == 0, 0.0, pltpu.roll(value, 1, 0))
    after = jnp.where(at == cols - 1, 0.0, pltpu.roll(value, cols - 1, 0))
    return jnp.concatenate([before, value, after], axis=1).astype(jnp.bfloat16)


def three_rows(ref, row, count):
    parts = [ref[pl.ds(row + step, count)].reshape(-1, ref.shape[-1]) for step in range(3)]
    return jnp.concatenate(parts, axis=1)


def dot32(one, other):
    return jnp.dot(one, other, preferred_element_type=jnp.float32)


def gelu_both(preact, slope_too):
    square = preact * preact
    inner_tanh = jnp.tanh(gelu_scale * preact * (1.0 + gelu_cubic * square))
    half = 0.5 * (1.0 + inner_tanh)
    value = preact * half
    if not slope_too:
        return value, None
    bend = (0.5 * gelu_scale) * (1.0 + 3.0 * gelu_cubic * square)
    return value, half + preact * (1.0 - inner_tanh * inner_tanh) * bend


def perceptual_kernel(
    planes_ref, w1_ref, w2_ref, w3_ref, w3_back_ref, w2_back_ref, w1_back_ref, out_ref,
    taps, act1, slope1, pooled, delta3, diff2, slope2, delta2, delta1, tmp, pixels, strip, send_sem, recv_sem, own_sem,
):
    g, r, c = position()
    me = (g, r, c)
    barrier = pltpu.get_barrier_semaphore()
    perceives = g < 3
    own_frame = 8 * g + c
    home = own_frame // 6
    place = lax.rem(own_frame, 6)
    ahead = perceives & (place == 0) & (home > 0)
    behind = perceives & (place == 5) & (home < 3)

    def sources(do):
        for slot in range(8):
            source_frame = 6 * g - 1 + slot

            def each(step, slot=slot, source_frame=source_frame):
                source = (source_frame // 8, r + step, lax.rem(source_frame, 8))
                pl.when(jnp.logical_not(same_place(source, me)))(
                    functools.partial(do, step, slot, source)
                )

            pl.when((source_frame >= 0) & (source_frame < 24))(functools.partial(on_rows, r, each))

    def greet(step, slot, source):
        pl.semaphore_signal(barrier, inc=1, device_id=source, device_id_type=MESH)

    sources(greet)
    row0 = 8 * r - 8
    lane = lax.broadcasted_iota(jnp.int32, (192, 128), 1)
    planes = planes_ref[...].reshape(192, 128)
    before = jnp.where(lane == 0, 0.0, pltpu.roll(planes, 1, 1))
    after = jnp.where(lane == 127, 0.0, pltpu.roll(planes, 127, 1))
    taps[:, 0:8] = before.reshape(24, 8, 128)
    taps[:, 8:16] = planes.reshape(24, 8, 128)
    taps[:, 16:24] = after.reshape(24, 8, 128)

    def shown(row):
        return (row0 + row >= 0) & (row0 + row < 64)

    def kept(row, value):
        return jnp.where(shown(row), value, 0.0)

    def first_rows(low, high, slope_too):
        @pl.loop(low, high)
        def _(i):
            cells = taps[pl.ds(i, 3)].reshape(72, 128).astype(jnp.bfloat16)
            value, slope = gelu_both(transposed_dot(cells, w1_ref[...]), slope_too)
            act1[i] = side_by_side(kept(i + 1, value))
            if slope_too:
                slope1[i - 6] = slope

    first_rows(0, 6, False)
    first_rows(6, 16, True)
    first_rows(16, 22, False)

    def second_rows(low, high, slope_too):
        @pl.loop(low, high)
        def _(p):
            plane = dot32(three_rows(act1, 2 * p, 2), w2_ref[...])
            value, slope = gelu_both(plane, slope_too)
            value = kept(2 * p + 2, value)
            if slope_too:
                difference = 0.25 * (value - pltpu.roll(value, 64, 1))
                diff2[pl.ds(2 * p - 4, 2)] = difference.reshape(2, 128, 128)
                slope2[pl.ds(2 * p - 4, 2)] = slope.reshape(2, 128, 128)
            tmp[...] = value[:128] + value[128:]
            mean = 0.25 * (tmp[pl.ds(0, 64, 2)] + tmp[pl.ds(1, 64, 2)])
            pooled[p] = side_by_side(mean)

    second_rows(0, 2, False)
    second_rows(2, 8, True)
    second_rows(8, 10, False)

    @pl.loop(0, 4)
    def _(half):
        j = 2 * half
        plane = dot32(three_rows(pooled, j, 2), w3_ref[...])
        value, slope = gelu_both(plane[:, :128], True)
        guide, _ = gelu_both(plane[:, 128:], False)
        delta = 0.5 * (value - guide) * slope
        delta3[j] = side_by_side(kept(2 * j + 4, delta[:64]))
        delta3[j + 1] = side_by_side(kept(2 * j + 6, delta[64:]))

    @pl.loop(0, 6)
    def _(m):
        grad = 0.25 * dot32(three_rows(delta3, m, 1), w3_back_ref[...])
        tmp[pl.ds(0, 64, 2)] = grad
        tmp[pl.ds(1, 64, 2)] = grad
        spread = tmp[...]
        for k in range(2):
            delta = (spread + diff2[2 * m + k]) * slope2[2 * m + k]
            delta2[2 * m + k] = side_by_side(kept(2 * m + 6, delta))

    @pl.loop(0, 5)
    def _(half):
        n = 2 * half
        grad = dot32(three_rows(delta2, n, 2), w2_back_ref[...])
        for k in range(2):
            delta = grad[128 * k : 128 * (k + 1)] * slope1[n + k]
            delta1[n + k] = side_by_side(kept(n + k + 7, delta))

    @pl.loop(0, 8)
    def _(q):
        grad = lax.dot_general(
            w1_back_ref[...],
            three_rows(delta1, q, 1),
            (((1,), (1,)), ((), ())),
            preferred_element_type=jnp.float32,
        )
        own = planes_ref[q + 8]
        direct = (1.0 / 6.0) * (own - pltpu.roll(own, 5, 0))
        pixels[pl.ds(pl.multiple_of(q * 8, 8), 8)] = grad + direct

    rows = [pixels[pl.ds(k, 8, 8)] for k in range(3)] + [jnp.zeros((8, 128), jnp.float32)]
    strip[...] = jnp.concatenate(rows, axis=0).astype(jnp.bfloat16)

    groups = jnp.where(perceives, 1, 0) + jnp.where(ahead, 1, 0) + jnp.where(behind, 1, 0)
    to_itself = perceives & (home == g) | ahead & (home == g + 1) | behind & (home == g - 1)
    awaited = 8 * row_count(r) * groups - jnp.where(to_itself, 1, 0)
    pl.when(perceives)(lambda: pl.semaphore_wait(barrier, awaited))

    def targets(do):
        for kind, (group, needed) in enumerate(((home, perceives), (home - 1, ahead), (home + 1, behind))):

            def each(step, kind=kind, group=group):
                for column in range(8):
                    peer = (group, r + step, column)
                    do(kind, step, column, peer, jnp.logical_not(same_place(peer, me)))

            pl.when(needed)(functools.partial(on_rows, r, each))

    def outgoing(kind, step, column, peer):
        place_there = own_frame - 6 * peer[0] + 1
        return pltpu.make_async_remote_copy(
            src_ref=strip,
            dst_ref=out_ref.at[place_there, 1 - step],
            send_sem=send_sem.at[kind, step + 1, column],
            recv_sem=recv_sem.at[place_there, 1 - step],
            device_id=peer,
            device_id_type=MESH,
        )

    def kept():
        return pltpu.make_async_copy(strip, out_ref.at[own_frame - 6 * g + 1, 1], own_sem)

    def start(kind, step, column, peer, away):
        pl.when(away)(lambda: outgoing(kind, step, column, peer).start())
        if step == 0:
            pl.when(jnp.logical_not(away))(lambda: kept().start())

    def finish(kind, step, column, peer, away):
        pl.when(away)(lambda: outgoing(kind, step, column, peer).wait_send())
        if step == 0:
            pl.when(jnp.logical_not(away))(lambda: kept().wait())

    def arrive(step, slot, source):
        pltpu.make_async_remote_copy(
            src_ref=strip,
            dst_ref=out_ref.at[slot, step + 1],
            send_sem=send_sem.at[0, 0, 0],
            recv_sem=recv_sem.at[slot, step + 1],
            device_id=source,
            device_id_type=MESH,
        ).wait_recv()

    targets(start)
    sources(arrive)
    targets(finish)


def two_blocks(weight):
    _, i, o = weight.shape
    return jnp.pad(weight, ((0, 0), (0, i), (0, o))) + jnp.pad(weight, ((0, 0), (i, 0), (o, 0)))


def perceptual_weights(vgg_first, vgg_second, vgg_third):
    first = vgg_first.reshape(9, 3, 64)
    w1 = jnp.pad(two_blocks(first), ((0, 0), (0, 2), (0, 0))).reshape(72, 128)
    second = vgg_second.reshape(9, 64, 64)
    third = vgg_third.reshape(9, 64, 128)
    w2 = two_blocks(second).reshape(1152, 128)
    w3 = two_blocks(third).reshape(1152, 256)
    w3_back = jnp.pad(jnp.transpose(third[::-1], (0, 2, 1)), ((0, 0), (0, 0), (0, 64))).reshape(1152, 128)
    w2_back = jnp.pad(jnp.transpose(second[::-1], (0, 2, 1)), ((0, 0), (0, 64), (0, 64))).reshape(1152, 128)
    w1_back = jnp.pad(jnp.transpose(first[::-1], (1, 0, 2)), ((0, 5), (0, 0), (0, 64))).reshape(8, 1152)
    return w1, w2, w3, w3_back, w2_back, w1_back


def perceptual_strip(planes, weights):
    f32, half = jnp.float32, jnp.bfloat16
    return pl.pallas_call(
        perceptual_kernel,
        out_shape=b16(8, 3, 32, 128),
        in_specs=in_vmem(7),
        out_specs=in_vmem(1)[0],
        scratch_shapes=[
            pltpu.VMEM((24, 24, 128), f32),
            pltpu.VMEM((22, 128, 384), half),
            pltpu.VMEM((10, 128, 128), f32),
            pltpu.VMEM((10, 64, 384), half),
            pltpu.VMEM((8, 64, 384), half),
            pltpu.VMEM((12, 128, 128), f32),
            pltpu.VMEM((12, 128, 128), f32),
            pltpu.VMEM((12, 128, 384), half),
            pltpu.VMEM((10, 128, 384), half),
            pltpu.VMEM((128, 128), f32),
            pltpu.VMEM((64, 128), f32),
            pltpu.VMEM((32, 128), half),
            pltpu.SemaphoreType.DMA((3, 3, 8)),
            pltpu.SemaphoreType.DMA((8, 3)),
            pltpu.SemaphoreType.DMA(()),
        ],
        compiler_params=pltpu.CompilerParams(
            collective_id=4, has_side_effects=True, vmem_limit_bytes=40 * 2**20
        ),
    )(planes, *weights)


def taps_in_lanes(weight_ref, out_ref):
    for q in range(9):
        for k in range(3):
            tap = 3 * q + k
            out_ref[128 * q : 128 * (q + 1), 128 * k : 128 * (k + 1)] = weight_ref[
                128 * tap : 128 * (tap + 1), :
            ]


def turned_taps(weight_ref, out_ref):
    for q in range(9):
        for k in range(3):
            tap = 26 - 3 * q - k
            block = weight_ref[128 * tap : 128 * (tap + 1), :].astype(jnp.float32)
            out_ref[128 * q : 128 * (q + 1), 128 * k : 128 * (k + 1)] = block.T.astype(jnp.bfloat16)


def conv_frame(source, frame, rows, taps_ref):
    parts = [
        source[frame + dt, pl.ds(dr, rows)].reshape(rows * 32, 128) for dt in range(3) for dr in range(3)
    ]
    sums = dot32(jnp.concatenate(parts, axis=1), taps_ref[...])
    total = pltpu.roll(sums[:, :128], 1, 0) + sums[:, 128:256]
    total += pltpu.roll(sums[:, 256:], rows * 32 - 1, 0)
    return total.reshape(rows, 32, 128)


def silu_parts(preact):
    gate = 1.0 / (1.0 + jnp.exp(-preact))
    return preact * gate, gate * (1.0 + preact * (1.0 - gate))


def on_rows(r, do):
    for step in (-1, 0, 1):
        pl.when((r + step >= 0) & (r + step < 8))(functools.partial(do, step))


def forward_kernel(
    cells_ref, first_ref, second_ref, rgb_ref, hidden_out, slope1_out, slope2_out, near_out,
    taps1, taps2, colours, send_sem, recv_sem, own_sem,
):
    g, r, c = position()
    me = (g, r, c)
    barrier = pltpu.get_barrier_semaphore()
    perceives = g < 3
    source_group = (8 * g + c) // 6

    def sources(do):
        def each(step):
            for column in range(8):
                source = (source_group, r + step, column)
                pl.when(jnp.logical_not(same_place(source, me)))(
                    functools.partial(do, step, column, source)
                )

        pl.when(perceives)(lambda: on_rows(r, each))

    def greet(step, column, source):
        pl.semaphore_signal(barrier, inc=1, device_id=source, device_id_type=MESH)

    sources(greet)

    taps_in_lanes(first_ref, taps1)
    taps_in_lanes(second_ref, taps2)
    row = lax.broadcasted_iota(jnp.int32, (12, 32, 128), 0) + (8 * r - 2)
    col = lax.broadcasted_iota(jnp.int32, (12, 32, 128), 1) + (16 * c - 8)
    shown = (row >= 0) & (row < 64) & (col >= 0) & (col < 128)

    @pl.loop(0, 10)
    def _(f):
        value, slope = silu_parts(conv_frame(cells_ref, f, 12, taps1))
        frame = 6 * g - 2 + f
        value = jnp.where(shown, value, 0.0) * jnp.where((frame >= 0) & (frame < 24), 1.0, 0.0)
        hidden_out[f] = value.astype(jnp.bfloat16)
        slope1_out[f] = slope[2:10, 8:24].reshape(128, 128)

    to_itself = jnp.where(perceives & (2 * g + c < 6), 1, 0)
    pl.semaphore_wait(barrier, 6 * row_count(r) - to_itself)

    def target(step, slot):
        frame = 6 * g + slot
        return (frame // 8, r + step, lax.rem(frame, 8))

    def outgoing(step, slot):
        return pltpu.make_async_remote_copy(
            src_ref=colours.at[slot],
            dst_ref=near_out.at[1 - step, c],
            send_sem=send_sem.at[step + 1, slot],
            recv_sem=recv_sem.at[1 - step, c],
            device_id=target(step, slot),
            device_id_type=MESH,
        )

    def kept(slot):
        return pltpu.make_async_copy(colours.at[slot], near_out.at[1, c], own_sem)

    def start(slot, step):
        away = jnp.logical_not(same_place(target(step, slot), me))
        pl.when(away)(lambda: outgoing(step, slot).start())
        if step == 0:
            pl.when(jnp.logical_not(away))(lambda: kept(slot).start())

    def finish(slot, step):
        away = jnp.logical_not(same_place(target(step, slot), me))
        pl.when(away)(lambda: outgoing(step, slot).wait_send())
        if step == 0:
            pl.when(jnp.logical_not(away))(lambda: kept(slot).wait())

    def arrive(step, column, source):
        pltpu.make_async_remote_copy(
            src_ref=colours.at[0],
            dst_ref=near_out.at[step + 1, column],
            send_sem=send_sem.at[0, 0],
            recv_sem=recv_sem.at[step + 1, column],
            device_id=source,
            device_id_type=MESH,
        ).wait_recv()

    @pl.loop(0, 6)
    def _(slot):
        value, slope = silu_parts(conv_frame(hidden_out, slot + 1, 10, taps2))
        slope2_out[slot + 1] = slope
        own = value[1:9, 8:24].reshape(128, 128).astype(jnp.bfloat16)
        colour = lax.dot_general(
            rgb_ref[...], own, (((1,), (1,)), ((), ())), preferred_element_type=jnp.float32
        )
        colours[slot] = colour.astype(jnp.bfloat16)
        on_rows(r, functools.partial(start, slot))

    @pl.loop(0, 2)
    def _(end):
        slope2_out[7 * end] = silu_parts(conv_frame(hidden_out, 7 * end, 10, taps2))[1]

    sources(arrive)

    @pl.loop(0, 6)
    def _(slot):
        on_rows(r, functools.partial(finish, slot))


def columns_in_lanes(source, frame0, row0, out_ref):
    @pl.loop(0, 8)
    def _(f):
        value = source[f + frame0, pl.ds(row0, 10)].reshape(320, 128).astype(jnp.float32)
        parts = [pltpu.roll(value, 1, 0), value, pltpu.roll(value, 319, 0)]
        for k, part in enumerate(parts):
            own = part.reshape(10, 32, 128)[:, 8:24]
            out_ref[f, :, :, 128 * k : 128 * (k + 1)] = own.astype(jnp.bfloat16)


def weight_terms(columns, delta, terms):
    @pl.loop(0, 9)
    def _(q):
        cells = columns[pl.ds(q // 3, 6), pl.ds(lax.rem(q, 3), 8)].reshape(768, 384)
        terms[pl.ds(pl.multiple_of(384 * q, 384), 384)] = transposed_dot(cells, delta[...])


def by_chip(terms, out_ref, which):
    @pl.loop(0, 8)
    def _(z):
        for chip in range(16):
            start = 432 * z + 27 * chip
            out_ref[which, 0, z, chip // 4, chip % 4] = terms[pl.ds(start, 16)].astype(jnp.bfloat16)
            out_ref[which, 1, z, chip // 4, chip % 4] = terms[pl.ds(start + 13, 16)].astype(jnp.bfloat16)


def backward_kernel(
    pixel_ref, cells_ref, hidden_ref, slope1_ref, slope2_ref, second_ref, rgb_ref, out_ref,
    taps, columns, field, delta, terms,
    sending, core_in, held, x_in, y_in, mid_x, mid_y, yy_in, xx_in, last, z_in, send_sem, recv_sem,
):
    g, r, c = position()
    zh, x, y, core = r // 4, lax.rem(r, 4), c // 2, lax.rem(c, 2)
    z = g * 2 + zh
    other = 1 - core

    def at_x(step):
        return (g, zh * 4 + lax.rem(x + step, 4), c)

    def at_y(step):
        return (g, r, lax.rem(y + step, 4) * 2 + core)

    def at_z(step):
        to = lax.rem(z + step, 8)
        return (to // 2, lax.rem(to, 2) * 4 + x, c)

    partner = (g, r, y * 2 + other)
    barrier = pltpu.get_barrier_semaphore()
    everyone = [partner] + [at_x(s) for s in (1, 2, 3)] + [at_y(s) for s in (1, 2, 3)]
    everyone += [at_z(s) for s in range(1, 8)]
    for peer in everyone:
        pl.semaphore_signal(barrier, inc=1, device_id=peer, device_id_type=MESH)

    def send(src, dst, which, slot, peer):
        copy = pltpu.make_async_remote_copy(
            src_ref=src,
            dst_ref=dst,
            send_sem=send_sem.at[which, slot],
            recv_sem=recv_sem.at[which, slot],
            device_id=peer,
            device_id_type=MESH,
        )
        copy.start()
        return copy

    f32, half = jnp.float32, jnp.bfloat16

    def summed(own, received):
        total = own.astype(f32)
        for k in range(3):
            total += received[k].astype(f32)
        return total.astype(half)

    def to_partner(which):
        return send(sending.at[which, other], core_in.at[which], which, 0, partner)

    def first_step(which, copy):
        copy.wait()

        @pl.loop(0, 8)
        def _(k):
            pair = sending[which, core, k].astype(f32) + core_in[which, k].astype(f32)
            held[which, k] = pair.astype(half)

        low, high = held.at[which, pl.ds(0, 4)], held.at[which, pl.ds(4, 4)]
        copies = []
        for s in (1, 2, 3):
            copies.append(send(low.at[:, lax.rem(x + s, 4)], x_in.at[which, s - 1], which, s, at_x(s)))
            copies.append(send(high.at[:, :, lax.rem(y + s, 4)], y_in.at[which, s - 1], which, 3 + s, at_y(s)))
        return copies

    def second_step(which, copies):
        for copy in copies:
            copy.wait()
        mid_x[which] = summed(held[which, 0:4, x], [x_in[which, k] for k in range(3)])
        mid_y[which] = summed(held[which, 4:8, :, y], [y_in[which, k] for k in range(3)])
        after = []
        for s in (1, 2, 3):
            after.append(send(mid_x.at[which, :, lax.rem(y + s, 4)], yy_in.at[which, s - 1], which, 6 + s, at_y(s)))
            after.append(send(mid_y.at[which, :, lax.rem(x + s, 4)], xx_in.at[which, s - 1], which, 9 + s, at_x(s)))
        return after

    def third_step(which, copies):
        for copy in copies:
            copy.wait()
        last[which, 0:4] = summed(mid_x[which, :, y], [yy_in[which, k] for k in range(3)])
        last[which, 4:8] = summed(mid_y[which, :, x], [xx_in[which, k] for k in range(3)])
        return [
            send(last.at[which, lax.rem(z + s, 8)], z_in.at[which, s - 1], which, 12 + s, at_z(s))
            for s in range(1, 8)
        ]

    def result(which, copies):
        for copy in copies:
            copy.wait()
        total = last[which, z].astype(f32)
        for k in range(7):
            total += z_in[which, k].astype(f32)
        out_ref[which] = total

    turned_taps(second_ref, taps)

    @pl.loop(0, 8)
    def _(f):
        hidden_grad = transposed_dot(pixel_ref[f], rgb_ref[...])
        value = hidden_grad.reshape(10, 32, 128) * slope2_ref[f]
        field[f] = value.astype(half)

    @pl.loop(0, 6)
    def _(f):
        own = field[f + 1, 1:9].astype(f32)[:, 8:24].reshape(128, 128).astype(half)
        delta[pl.ds(pl.multiple_of(128 * f, 128), 128)] = own

    columns_in_lanes(hidden_ref, 1, 1, columns)
    terms[pl.ds(3456, 8)] = jnp.zeros((8, 128), f32)
    weight_terms(columns, delta, terms)
    by_chip(terms, sending, 1)
    pl.semaphore_wait(barrier, len(everyone))
    swap_second = to_partner(1)

    @pl.loop(0, 6)
    def _(f):
        back = conv_frame(field, f, 8, taps)[:, 8:24].reshape(128, 128)
        value = (back * slope1_ref[f + 2]).astype(half)
        delta[pl.ds(pl.multiple_of(128 * f, 128), 128)] = value

    moves_second = first_step(1, swap_second)
    columns_in_lanes(cells_ref, 2, 2, columns)
    weight_terms(columns, delta, terms)
    moves_second = second_step(1, moves_second)
    by_chip(terms, sending, 0)
    swap_first = to_partner(0)
    moves_second = third_step(1, moves_second)
    moves_first = first_step(0, swap_first)
    result(1, moves_second)
    moves_first = second_step(0, moves_first)
    moves_first = third_step(0, moves_first)
    result(0, moves_first)


def f32_shape(*shape):
    return jax.ShapeDtypeStruct(shape, jnp.float32)


def talking_call(kernel, ident, outs, scratch, *operands):
    return pl.pallas_call(
        kernel,
        out_shape=tuple(outs),
        in_specs=in_vmem(len(operands)),
        out_specs=tuple(in_vmem(len(outs))),
        scratch_shapes=scratch,
        compiler_params=pltpu.CompilerParams(
            collective_id=ident, has_side_effects=True, vmem_limit_bytes=48 * 2**20
        ),
    )(*operands)


def inside(start, count, limit):
    positions = start + jnp.arange(count)
    return (positions >= 0) & (positions < limit)


def cell_mask(frame0, frames, row0, rows, col0, cols):
    keep_frames = inside(frame0, frames, 24)
    keep_rows = inside(row0, rows, 64)
    keep_cols = inside(col0, cols, 128)
    return (keep_frames[:, None, None] & keep_rows[None, :, None] & keep_cols[None, None, :])[
        ..., None
    ]


def local(dec_input, target, conv_first, conv_second, rgb_weight, vgg_first, vgg_second, vgg_third):
    g, r, c = position()
    channels = dec_input.shape[-1]
    frame0, row0, col0 = 6 * g, 8 * r, 16 * c
    video = jnp.pad(dec_input.reshape(24, 8, 16, channels), ((3, 3), (0, 0), (0, 0), (0, 0)))
    own = lax.dynamic_slice_in_dim(video, frame0, 12, axis=0)

    def columns(part):
        return jnp.transpose(part, (1, 0, 2, 3)).reshape(8, 48, channels)

    guide_own = lax.dynamic_index_in_dim(target, jnp.minimum(g, 2), 1, keepdims=False)
    guide_own = guide_own.reshape(24, 128)
    top, bottom, left, right, corners, guide_near = exchange(
        halo_kernel,
        2,
        (
            b16(12, 3, 16, channels), b16(12, 3, 16, channels), b16(8, 48, channels),
            b16(8, 48, channels), b16(4, 3, 48, channels), b16(2, 32, 128),
        ),
        ((10,), (10,)),
        own,
        columns(own[:, :, :4]),
        columns(own[:, :, 12:]),
        jnp.pad(guide_own, ((0, 8), (0, 0))),
    )

    def strip(part):
        return jnp.transpose(part.reshape(-1, 12, 4, channels), (1, 0, 2, 3))

    gap = jnp.zeros((12, 14, 4, channels), jnp.bfloat16)
    cells = jnp.concatenate(
        [
            gap,
            jnp.concatenate([strip(corners[0]), strip(left), strip(corners[2])], axis=1),
            jnp.concatenate([top, own, bottom], axis=1),
            jnp.concatenate([strip(corners[1]), strip(right), strip(corners[3])], axis=1),
            gap,
        ],
        axis=2,
    )
    cells = jnp.where(
        inside(row0 - 3, 14, 64)[None, :, None, None] & inside(col0 - 8, 32, 128)[None, None, :, None],
        cells,
        jnp.zeros_like(cells),
    )
    half = jnp.bfloat16
    rgb = jnp.pad(rgb_weight, ((0, 13), (0, 0)))
    dma = pltpu.SemaphoreType.DMA
    hidden, slope1, slope2, colour_near = talking_call(
        forward_kernel,
        3,
        (b16(10, 12, 32, 128), f32_shape(10, 128, 128), f32_shape(8, 10, 32, 128), b16(3, 8, 16, 128)),
        [
            pltpu.VMEM((1152, 384), half), pltpu.VMEM((1152, 384), half), pltpu.VMEM((6, 16, 128), half),
            dma((3, 6)), dma((3, 8)), dma(()),
        ],
        cells, conv_first, conv_second, rgb,
    )
    images = jnp.transpose(colour_near[:, :, :3].reshape(3, 8, 3, 8, 16), (0, 3, 2, 1, 4))
    guides = jnp.stack(
        [guide_near[0, :24].reshape(3, 8, 128), guide_own.reshape(3, 8, 128), guide_near[1, :24].reshape(3, 8, 128)]
    )
    guides = jnp.transpose(guides, (0, 2, 1, 3))
    planes = jnp.concatenate([images.reshape(24, 3, 128), guides.reshape(24, 3, 128)], axis=1)
    planes = jnp.where(inside(row0 - 8, 24, 64)[:, None, None], planes, jnp.zeros_like(planes))
    planes = jnp.pad(planes.astype(jnp.float32), ((0, 0), (0, 2), (0, 0)))
    returned = perceptual_strip(planes, perceptual_weights(vgg_first, vgg_second, vgg_third))
    rows_near = jnp.transpose(returned[:, :, :24].reshape(8, 3, 3, 8, 128), (2, 0, 1, 3, 4))
    rows_near = rows_near.reshape(3, 8, 24, 128)[:, :, 7:17]
    rows_near = jnp.pad(rows_near, ((0, 0), (0, 0), (0, 0), (8, 8)))
    pixels = lax.dynamic_slice_in_dim(rows_near, col0, 32, axis=3)
    pixel_keep = cell_mask(frame0 - 1, 8, row0 - 1, 10, col0 - 8, 32)
    pixels = jnp.where(pixel_keep[None, ..., 0], pixels, jnp.zeros_like(pixels))
    pixels = jnp.pad(jnp.transpose(pixels, (1, 0, 2, 3)).reshape(8, 3, 320), ((0, 0), (0, 13), (0, 0)))
    sums = talking_call(
        backward_kernel,
        1,
        (f32_shape(2, 16, 128),),
        [
            pltpu.VMEM((1152, 384), half),
            pltpu.VMEM((8, 10, 16, 384), half),
            pltpu.VMEM((8, 10, 32, 128), half),
            pltpu.VMEM((768, 128), half),
            pltpu.VMEM((3464, 128), jnp.float32),
            pltpu.VMEM((2, 2, 8, 4, 4, 16, 128), half),
            pltpu.VMEM((2, 8, 4, 4, 16, 128), half),
            pltpu.VMEM((2, 8, 4, 4, 16, 128), half),
            pltpu.VMEM((2, 3, 4, 4, 16, 128), half),
            pltpu.VMEM((2, 3, 4, 4, 16, 128), half),
            pltpu.VMEM((2, 4, 4, 16, 128), half),
            pltpu.VMEM((2, 4, 4, 16, 128), half),
            pltpu.VMEM((2, 3, 4, 16, 128), half),
            pltpu.VMEM((2, 3, 4, 16, 128), half),
            pltpu.VMEM((2, 8, 16, 128), half),
            pltpu.VMEM((2, 7, 16, 128), half),
            dma((2, 20)),
            dma((2, 20)),
        ],
        pixels, cells, hidden, slope1, slope2, conv_second, rgb,
    )[0]
    flat = sums[:, :14].reshape(2, 14 * 128)
    own_sums = lax.dynamic_slice_in_dim(flat, lax.rem(c, 2) * 64, 1728, axis=1)
    return own_sums[0], own_sums[1]


def solution(mesh):
    in_specs = (
        P(None, None, "row", "col", None),
        P(None, None, "col", "row", None),
        P(),
        P(),
        P(),
        P(),
        P(),
        P(),
    )
    out_specs = (P(("grp", "row", "col")), P(("grp", "row", "col")))
    return jax.shard_map(local, mesh=mesh, in_specs=in_specs, out_specs=out_specs, check_vma=False)
```

```python
import functools

import jax
import jax.numpy as jnp
from jax import lax
from jax.experimental import pallas as pl
from jax.experimental.pallas import tpu as pltpu
from jax.sharding import PartitionSpec as P

MESH = pl.DeviceIdType.MESH

gelu_scale = 0.7978845608028654
gelu_cubic = 0.044715


def position():
    return lax.axis_index("grp"), lax.axis_index("row"), lax.axis_index("col")


def same_place(one, other):
    return (one[0] == other[0]) & (one[1] == other[1]) & (one[2] == other[2])


def row_count(r):
    return 1 + jnp.where(r > 0, 1, 0) + jnp.where(r < 7, 1, 0)


def in_vmem(count):
    return [pl.BlockSpec(memory_space=pltpu.VMEM)] * count


def b16(*shape):
    return jax.ShapeDtypeStruct(shape, jnp.bfloat16)


def transposed_dot(one, other):
    return lax.dot_general(one, other, (((0,), (0,)), ((), ())), preferred_element_type=jnp.float32)


def side_by_side(value):
    cols = value.shape[0]
    at = lax.broadcasted_iota(jnp.int32, value.shape, 0)
    before = jnp.where(at == 0, 0.0, pltpu.roll(value, 1, 0))
    after = jnp.where(at == cols - 1, 0.0, pltpu.roll(value, cols - 1, 0))
    return jnp.concatenate([before, value, after], axis=1).astype(jnp.bfloat16)


def three_rows(ref, row, count):
    parts = [ref[pl.ds(row + step, count)].reshape(-1, ref.shape[-1]) for step in range(3)]
    return jnp.concatenate(parts, axis=1)


def dot32(one, other):
    return jnp.dot(one, other, preferred_element_type=jnp.float32)


def gelu_both(preact, slope_too):
    square = preact * preact
    inner_tanh = jnp.tanh(gelu_scale * preact * (1.0 + gelu_cubic * square))
    half = 0.5 * (1.0 + inner_tanh)
    value = preact * half
    if not slope_too:
        return value, None
    bend = (0.5 * gelu_scale) * (1.0 + 3.0 * gelu_cubic * square)
    return value, half + preact * (1.0 - inner_tanh * inner_tanh) * bend


def perceptual_kernel(
    planes_ref, w1_ref, w2_ref, w3_ref, w3_back_ref, w2_back_ref, w1_back_ref, out_ref,
    taps, act1, slope1, pooled, delta3, diff2, slope2, delta2, delta1, tmp, pixels, strip, send_sem, recv_sem, own_sem,
):
    g, r, c = position()
    me = (g, r, c)
    barrier = pltpu.get_barrier_semaphore()
    perceives = g < 3
    own_frame = 8 * g + c
    home = own_frame // 6
    place = lax.rem(own_frame, 6)
    ahead = perceives & (place == 0) & (home > 0)
    behind = perceives & (place == 5) & (home < 3)

    def sources(do):
        for slot in range(8):
            source_frame = 6 * g - 1 + slot

            def each(step, slot=slot, source_frame=source_frame):
                source = (source_frame // 8, r + step, lax.rem(source_frame, 8))
                pl.when(jnp.logical_not(same_place(source, me)))(
                    functools.partial(do, step, slot, source)
                )

            pl.when((source_frame >= 0) & (source_frame < 24))(functools.partial(on_rows, r, each))

    def greet(step, slot, source):
        pl.semaphore_signal(barrier, inc=1, device_id=source, device_id_type=MESH)

    sources(greet)
    row0 = 8 * r - 8
    lane = lax.broadcasted_iota(jnp.int32, (192, 128), 1)
    planes = planes_ref[...].reshape(192, 128)
    before = jnp.where(lane == 0, 0.0, pltpu.roll(planes, 1, 1))
    after = jnp.where(lane == 127, 0.0, pltpu.roll(planes, 127, 1))
    taps[:, 0:8] = before.reshape(24, 8, 128)
    taps[:, 8:16] = planes.reshape(24, 8, 128)
    taps[:, 16:24] = after.reshape(24, 8, 128)

    def shown(row):
        return (row0 + row >= 0) & (row0 + row < 64)

    def kept(row, value):
        return jnp.where(shown(row), value, 0.0)

    def first_rows(low, high, slope_too):
        @pl.loop(low, high)
        def _(i):
            cells = taps[pl.ds(i, 3)].reshape(72, 128).astype(jnp.bfloat16)
            value, slope = gelu_both(transposed_dot(cells, w1_ref[...]), slope_too)
            act1[i] = side_by_side(kept(i + 1, value))
            if slope_too:
                slope1[i - 6] = slope

    first_rows(0, 6, False)
    first_rows(6, 16, True)
    first_rows(16, 22, False)

    def second_rows(low, high, slope_too):
        @pl.loop(low, high)
        def _(p):
            plane = dot32(three_rows(act1, 2 * p, 2), w2_ref[...])
            value, slope = gelu_both(plane, slope_too)
            value = kept(2 * p + 2, value)
            if slope_too:
                difference = 0.25 * (value - pltpu.roll(value, 64, 1))
                diff2[pl.ds(2 * p - 4, 2)] = difference.reshape(2, 128, 128)
                slope2[pl.ds(2 * p - 4, 2)] = slope.reshape(2, 128, 128)
            tmp[...] = value[:128] + value[128:]
            mean = 0.25 * (tmp[pl.ds(0, 64, 2)] + tmp[pl.ds(1, 64, 2)])
            pooled[p] = side_by_side(mean)

    second_rows(0, 2, False)
    second_rows(2, 8, True)
    second_rows(8, 10, False)

    @pl.loop(0, 4)
    def _(half):
        j = 2 * half
        plane = dot32(three_rows(pooled, j, 2), w3_ref[...])
        value, slope = gelu_both(plane[:, :128], True)
        guide, _ = gelu_both(plane[:, 128:], False)
        delta = 0.5 * (value - guide) * slope
        delta3[j] = side_by_side(kept(2 * j + 4, delta[:64]))
        delta3[j + 1] = side_by_side(kept(2 * j + 6, delta[64:]))

    @pl.loop(0, 6)
    def _(m):
        grad = 0.25 * dot32(three_rows(delta3, m, 1), w3_back_ref[...])
        tmp[pl.ds(0, 64, 2)] = grad
        tmp[pl.ds(1, 64, 2)] = grad
        spread = tmp[...]
        for k in range(2):
            delta = (spread + diff2[2 * m + k]) * slope2[2 * m + k]
            delta2[2 * m + k] = side_by_side(kept(2 * m + 6, delta))

    @pl.loop(0, 5)
    def _(half):
        n = 2 * half
        grad = dot32(three_rows(delta2, n, 2), w2_back_ref[...])
        for k in range(2):
            delta = grad[128 * k : 128 * (k + 1)] * slope1[n + k]
            delta1[n + k] = side_by_side(kept(n + k + 7, delta))

    @pl.loop(0, 8)
    def _(q):
        grad = lax.dot_general(
            w1_back_ref[...],
            three_rows(delta1, q, 1),
            (((1,), (1,)), ((), ())),
            preferred_element_type=jnp.float32,
        )
        own = planes_ref[q + 8]
        direct = (1.0 / 6.0) * (own - pltpu.roll(own, 5, 0))
        pixels[pl.ds(pl.multiple_of(q * 8, 8), 8)] = grad + direct

    rows = [pixels[pl.ds(k, 8, 8)] for k in range(3)] + [jnp.zeros((8, 128), jnp.float32)]
    strip[...] = jnp.concatenate(rows, axis=0).astype(jnp.bfloat16)

    groups = jnp.where(perceives, 1, 0) + jnp.where(ahead, 1, 0) + jnp.where(behind, 1, 0)
    to_itself = perceives & (home == g) | ahead & (home == g + 1) | behind & (home == g - 1)
    awaited = 8 * row_count(r) * groups - jnp.where(to_itself, 1, 0)
    pl.when(perceives)(lambda: pl.semaphore_wait(barrier, awaited))

    def targets(do):
        for kind, (group, needed) in enumerate(((home, perceives), (home - 1, ahead), (home + 1, behind))):

            def each(step, kind=kind, group=group):
                for column in range(8):
                    peer = (group, r + step, column)
                    do(kind, step, column, peer, jnp.logical_not(same_place(peer, me)))

            pl.when(needed)(functools.partial(on_rows, r, each))

    def outgoing(kind, step, column, peer):
        place_there = own_frame - 6 * peer[0] + 1
        return pltpu.make_async_remote_copy(
            src_ref=strip,
            dst_ref=out_ref.at[place_there, 1 - step],
            send_sem=send_sem.at[kind, step + 1, column],
            recv_sem=recv_sem.at[place_there, 1 - step],
            device_id=peer,
            device_id_type=MESH,
        )

    def kept():
        return pltpu.make_async_copy(strip, out_ref.at[own_frame - 6 * g + 1, 1], own_sem)

    def start(kind, step, column, peer, away):
        pl.when(away)(lambda: outgoing(kind, step, column, peer).start())
        if step == 0:
            pl.when(jnp.logical_not(away))(lambda: kept().start())

    def finish(kind, step, column, peer, away):
        pl.when(away)(lambda: outgoing(kind, step, column, peer).wait_send())
        if step == 0:
            pl.when(jnp.logical_not(away))(lambda: kept().wait())

    def arrive(step, slot, source):
        pltpu.make_async_remote_copy(
            src_ref=strip,
            dst_ref=out_ref.at[slot, step + 1],
            send_sem=send_sem.at[0, 0, 0],
            recv_sem=recv_sem.at[slot, step + 1],
            device_id=source,
            device_id_type=MESH,
        ).wait_recv()

    targets(start)
    sources(arrive)
    targets(finish)


def two_blocks(weight):
    _, i, o = weight.shape
    return jnp.pad(weight, ((0, 0), (0, i), (0, o))) + jnp.pad(weight, ((0, 0), (i, 0), (o, 0)))


def first_weights(vgg_first):
    first = vgg_first.reshape(9, 3, 64)
    w1 = jnp.pad(two_blocks(first), ((0, 0), (0, 2), (0, 0))).reshape(72, 128)
    w1_back = jnp.pad(jnp.transpose(first[::-1], (1, 0, 2)), ((0, 5), (0, 0), (0, 64))).reshape(8, 1152)
    return w1, w1_back


def perceptual_strip(planes, first, others):
    f32, half = jnp.float32, jnp.bfloat16
    return pl.pallas_call(
        perceptual_kernel,
        out_shape=b16(8, 3, 32, 128),
        in_specs=in_vmem(7),
        out_specs=in_vmem(1)[0],
        scratch_shapes=[
            pltpu.VMEM((24, 24, 128), f32),
            pltpu.VMEM((22, 128, 384), half),
            pltpu.VMEM((10, 128, 128), f32),
            pltpu.VMEM((10, 64, 384), half),
            pltpu.VMEM((8, 64, 384), half),
            pltpu.VMEM((12, 128, 128), f32),
            pltpu.VMEM((12, 128, 128), f32),
            pltpu.VMEM((12, 128, 384), half),
            pltpu.VMEM((10, 128, 384), half),
            pltpu.VMEM((128, 128), f32),
            pltpu.VMEM((64, 128), f32),
            pltpu.VMEM((32, 128), half),
            pltpu.SemaphoreType.DMA((3, 3, 8)),
            pltpu.SemaphoreType.DMA((8, 3)),
            pltpu.SemaphoreType.DMA(()),
        ],
        compiler_params=pltpu.CompilerParams(
            collective_id=4, has_side_effects=True, vmem_limit_bytes=24 * 2**20
        ),
    )(planes, first[0], *others, first[1])


def taps_in_lanes(weight_ref, out_ref):
    for q in range(9):
        for k in range(3):
            tap = 3 * q + k
            out_ref[128 * q : 128 * (q + 1), 128 * k : 128 * (k + 1)] = weight_ref[
                128 * tap : 128 * (tap + 1), :
            ]


def turned_taps(weight_ref, out_ref):
    for q in range(9):
        for k in range(3):
            tap = 26 - 3 * q - k
            block = weight_ref[128 * tap : 128 * (tap + 1), :].astype(jnp.float32)
            out_ref[128 * q : 128 * (q + 1), 128 * k : 128 * (k + 1)] = block.T.astype(jnp.bfloat16)


def conv_rows(source, frame, starts, count, taps_ref):
    size = len(starts) * count * 32

    def near(dt, dr):
        rows = [source[frame + dt, pl.ds(start + dr, count)].reshape(count * 32, 128) for start in starts]
        return rows[0] if len(rows) == 1 else jnp.concatenate(rows, axis=0)

    parts = [near(dt, dr) for dt in range(3) for dr in range(3)]
    sums = dot32(jnp.concatenate(parts, axis=1), taps_ref[...])
    total = pltpu.roll(sums[:, :128], 1, 0) + sums[:, 128:256]
    total += pltpu.roll(sums[:, 256:], size - 1, 0)
    return total.reshape(len(starts) * count, 32, 128)


def silu_parts(preact):
    gate = 1.0 / (1.0 + jnp.exp(-preact))
    return preact * gate, gate * (1.0 + preact * (1.0 - gate))


def on_rows(r, do):
    for step in (-1, 0, 1):
        pl.when((r + step >= 0) & (r + step < 8))(functools.partial(do, step))


def lay_out_perceptual(second_ref, third_ref, w2_out, w3_out, w3_back_out, w2_back_out):
    f32, half = jnp.float32, jnp.bfloat16
    for t in range(9):
        block = second_ref[64 * t : 64 * (t + 1), :].astype(f32)
        wide = third_ref[64 * t : 64 * (t + 1), :].astype(f32)
        none, low, high = jnp.zeros((64, 64), f32), 128 * t, 128 * (8 - t)
        w2_out[low : low + 64] = jnp.concatenate([block, none], axis=1).astype(half)
        w2_out[low + 64 : low + 128] = jnp.concatenate([none, block], axis=1).astype(half)
        w3_out[low : low + 64, :128] = wide.astype(half)
        w3_out[low : low + 64, 128:] = jnp.zeros((64, 128), half)
        w3_out[low + 64 : low + 128, :128] = jnp.zeros((64, 128), half)
        w3_out[low + 64 : low + 128, 128:] = wide.astype(half)
        w2_back_out[high : high + 64] = jnp.concatenate([block.T, none], axis=1).astype(half)
        w2_back_out[high + 64 : high + 128] = jnp.zeros((64, 128), half)
        turned = jnp.concatenate([wide.T, jnp.zeros((128, 64), f32)], axis=1)
        w3_back_out[high : high + 128] = turned.astype(half)


def forward_kernel(
    video_ref, target_ref, first_ref, second_ref, rgb_ref, vgg_second_ref, vgg_third_ref,
    cells, hidden_out, slope1_out, slope2_out, near_out, guide_out, w2_out, w3_out, w3_back_out, w2_back_out,
    tile, left_send, right_send, top_in, bottom_in, left_in, right_in, corner_in, halo_send, halo_recv,
    taps1, taps2, colours, send_sem, recv_sem, own_sem,
):
    g, r, c = position()
    me = (g, r, c)
    f32, half = jnp.float32, jnp.bfloat16
    barrier = pltpu.get_barrier_semaphore()
    perceives = g < 3
    source_group = (8 * g + c) // 6
    west, east = lax.rem(c + 7, 8), lax.rem(c + 1, 8)
    has_up, has_down = r > 0, r < 7

    def sources(do):
        def each(step):
            for column in range(8):
                source = (source_group, r + step, column)
                pl.when(jnp.logical_not(same_place(source, me)))(
                    functools.partial(do, step, column, source)
                )

        pl.when(perceives)(lambda: on_rows(r, each))

    def signal(peer):
        pl.semaphore_signal(barrier, inc=1, device_id=peer, device_id_type=MESH)

    signal((g, r, west))
    signal((g, r, east))

    @pl.when(has_up)
    def _():
        for column in (west, c, east):
            signal((g, r - 1, column))

    @pl.when(has_down)
    def _():
        for column in (west, c, east):
            signal((g, r + 1, column))

    sources(lambda step, column, source: signal(source))

    for f in range(12):
        frame = 6 * g - 3 + f
        real = (frame >= 0) & (frame < 24)
        value = video_ref[jnp.minimum(jnp.maximum(frame, 0), 23)]
        tile[f] = jnp.where(real, value, jnp.zeros_like(value))
    for row in range(8):
        near = [tile[f, row].astype(f32) for f in range(12)]
        left_send[row] = jnp.concatenate([v[0:4] for v in near], axis=0).astype(half)
        right_send[row] = jnp.concatenate([v[12:16] for v in near], axis=0).astype(half)
    block = jnp.minimum(g, 2)
    planes = [target_ref[k, block, 0].astype(f32) for k in range(3)] + [jnp.zeros((8, 128), f32)]
    guide_out[1] = jnp.concatenate(planes, axis=0).astype(half)

    to_itself = jnp.where(perceives & (2 * g + c < 6), 1, 0)
    pl.semaphore_wait(barrier, 9 * row_count(r) - 1 - to_itself)

    def remote(src, dst, slot, peer):
        return pltpu.make_async_remote_copy(
            src_ref=src,
            dst_ref=dst,
            send_sem=halo_send.at[slot],
            recv_sem=halo_recv.at[slot],
            device_id=peer,
            device_id_type=MESH,
        )

    sideways = [remote(left_send, right_in, 0, (g, r, west)), remote(right_send, left_in, 1, (g, r, east))]

    def to_row(row_index, rows, strip_in, corners, guide_slot, first_slot):
        rows = pl.ds(rows, 3)
        return [
            remote(tile.at[:, rows], strip_in, first_slot, (g, row_index, c)),
            remote(left_send.at[rows], corner_in.at[corners + 1], first_slot + 1, (g, row_index, west)),
            remote(right_send.at[rows], corner_in.at[corners], first_slot + 2, (g, row_index, east)),
            remote(guide_out.at[1], guide_out.at[guide_slot], first_slot + 3, (g, row_index, c)),
        ]

    upward = to_row(r - 1, 0, bottom_in, 2, 2, 2)
    downward = to_row(r + 1, 5, top_in, 0, 0, 6)

    def start(copies):
        for copy in copies:
            copy.start()

    def sent(copies):
        for copy in copies:
            copy.wait_send()

    def landed(copies):
        for copy in copies:
            copy.wait_recv()

    pl.when(has_up)(lambda: start(upward))
    pl.when(has_down)(lambda: start(downward))
    start(sideways)

    taps_in_lanes(first_ref, taps1)
    taps_in_lanes(second_ref, taps2)

    def assemble(first_row, count, real, own, left, right):
        col = lax.broadcasted_iota(jnp.int32, (count, 32, 128), 1) + (16 * c - 8)
        shown = (col >= 0) & (col < 128) & real
        for quad in range(3):
            before = left[:, 16 * quad : 16 * (quad + 1)].astype(f32)
            after = right[:, 16 * quad : 16 * (quad + 1)].astype(f32)
            for k in range(4):
                f, eight = 4 * quad + k, slice(8 * (k // 2), 8 * (k // 2) + 8)
                one = before[:, eight].reshape(8 * count, 128)
                two = after[:, eight].reshape(8 * count, 128)
                if k % 2 == 0:
                    one = pltpu.roll(one, 4, 0)
                else:
                    two = pltpu.roll(two, 8 * count - 4, 0)
                sides = [one.reshape(count, 8, 128), own(f).astype(f32), two.reshape(count, 8, 128)]
                value = jnp.where(shown, jnp.concatenate(sides, axis=1), 0.0)
                cells[f, first_row : first_row + count] = value.astype(half)

    row = lax.broadcasted_iota(jnp.int32, (6, 32, 128), 0)
    col = lax.broadcasted_iota(jnp.int32, (6, 32, 128), 1) + (16 * c - 8)
    in_cols = (col >= 0) & (col < 128)

    def in_frames(f):
        frame = 6 * g - 2 + f
        return jnp.where((frame >= 0) & (frame < 24), 1.0, 0.0)

    landed(sideways)
    assemble(3, 8, True, lambda f: tile[f], left_in[...], right_in[...])

    @pl.loop(0, 10)
    def _(f):
        value, slope = silu_parts(conv_rows(cells, f, (3,), 6, taps1))
        value = jnp.where(in_cols, value, 0.0) * in_frames(f)
        hidden_out[f, 3:9] = value.astype(half)
        slope1_out[f, 16:112] = slope[:, 8:24].reshape(96, 128)

    lay_out_perceptual(vgg_second_ref, vgg_third_ref, w2_out, w3_out, w3_back_out, w2_back_out)
    pl.when(has_up)(lambda: landed(downward))
    pl.when(has_down)(lambda: landed(upward))
    assemble(0, 3, has_up, lambda f: top_in[f], corner_in[0], corner_in[1])
    assemble(11, 3, has_down, lambda f: bottom_in[f], corner_in[2], corner_in[3])
    image_row = jnp.where(row < 3, row, row + 6) + (8 * r - 2)
    in_image = in_cols & (image_row >= 0) & (image_row < 64)

    @pl.loop(0, 10)
    def _(f):
        value, slope = silu_parts(conv_rows(cells, f, (0, 9), 3, taps1))
        value = (jnp.where(in_image, value, 0.0) * in_frames(f)).astype(half)
        hidden_out[f, 0:3] = value[0:3]
        hidden_out[f, 9:12] = value[3:6]
        slope1_out[f, 0:16] = slope[2, 8:24]
        slope1_out[f, 112:128] = slope[3, 8:24]

    def target(step, slot):
        frame = 6 * g + slot
        return (frame // 8, r + step, lax.rem(frame, 8))

    def outgoing(step, slot):
        return pltpu.make_async_remote_copy(
            src_ref=colours.at[slot],
            dst_ref=near_out.at[1 - step, c],
            send_sem=send_sem.at[step + 1, slot],
            recv_sem=recv_sem.at[1 - step, c],
            device_id=target(step, slot),
            device_id_type=MESH,
        )

    def kept(slot):
        return pltpu.make_async_copy(colours.at[slot], near_out.at[1, c], own_sem)

    def start_colour(slot, step):
        away = jnp.logical_not(same_place(target(step, slot), me))
        pl.when(away)(lambda: outgoing(step, slot).start())
        if step == 0:
            pl.when(jnp.logical_not(away))(lambda: kept(slot).start())

    def finish(slot, step):
        away = jnp.logical_not(same_place(target(step, slot), me))
        pl.when(away)(lambda: outgoing(step, slot).wait_send())
        if step == 0:
            pl.when(jnp.logical_not(away))(lambda: kept(slot).wait())

    def arrive(step, column, source):
        pltpu.make_async_remote_copy(
            src_ref=colours.at[0],
            dst_ref=near_out.at[step + 1, column],
            send_sem=send_sem.at[0, 0],
            recv_sem=recv_sem.at[step + 1, column],
            device_id=source,
            device_id_type=MESH,
        ).wait_recv()

    @pl.loop(0, 6)
    def _(slot):
        value, slope = silu_parts(conv_rows(hidden_out, slot + 1, (0,), 10, taps2))
        slope2_out[slot + 1] = slope
        own = value[1:9, 8:24].reshape(128, 128).astype(jnp.bfloat16)
        colour = lax.dot_general(
            rgb_ref[...], own, (((1,), (1,)), ((), ())), preferred_element_type=jnp.float32
        )
        colours[slot] = colour.astype(jnp.bfloat16)
        on_rows(r, functools.partial(start_colour, slot))

    @pl.loop(0, 2)
    def _(end):
        slope2_out[7 * end] = silu_parts(conv_rows(hidden_out, 7 * end, (0,), 10, taps2))[1]

    sources(arrive)

    @pl.loop(0, 6)
    def _(slot):
        on_rows(r, functools.partial(finish, slot))

    sent(sideways)
    pl.when(has_up)(lambda: sent(upward))
    pl.when(has_down)(lambda: sent(downward))


def columns_in_lanes(source, frame0, row0, out_ref):
    @pl.loop(0, 8)
    def _(f):
        value = source[f + frame0, pl.ds(row0, 10)].reshape(320, 128).astype(jnp.float32)
        parts = [pltpu.roll(value, 1, 0), value, pltpu.roll(value, 319, 0)]
        for k, part in enumerate(parts):
            own = part.reshape(10, 32, 128)[:, 8:24]
            out_ref[f, :, :, 128 * k : 128 * (k + 1)] = own.astype(jnp.bfloat16)


def weight_terms(columns, delta, terms):
    @pl.loop(0, 9)
    def _(q):
        cells = columns[pl.ds(q // 3, 6), pl.ds(lax.rem(q, 3), 8)].reshape(768, 384)
        terms[pl.ds(pl.multiple_of(384 * q, 384), 384)] = transposed_dot(cells, delta[...])


def by_chip(terms, out_ref, which):
    @pl.loop(0, 8)
    def _(z):
        for chip in range(16):
            start = 432 * z + 27 * chip
            out_ref[which, 0, z, chip // 4, chip % 4] = terms[pl.ds(start, 16)].astype(jnp.bfloat16)
            out_ref[which, 1, z, chip // 4, chip % 4] = terms[pl.ds(start + 13, 16)].astype(jnp.bfloat16)


def backward_kernel(
    pixel_ref, cells_ref, hidden_ref, slope1_ref, slope2_ref, second_ref, rgb_ref, out_ref,
    taps, columns, field, delta, terms,
    sending, core_in, held, x_in, y_in, mid_x, mid_y, yy_in, xx_in, last, z_in, send_sem, recv_sem,
):
    g, r, c = position()
    zh, x, y, core = r // 4, lax.rem(r, 4), c // 2, lax.rem(c, 2)
    z = g * 2 + zh
    other = 1 - core

    def at_x(step):
        return (g, zh * 4 + lax.rem(x + step, 4), c)

    def at_y(step):
        return (g, r, lax.rem(y + step, 4) * 2 + core)

    def at_z(step):
        to = lax.rem(z + step, 8)
        return (to // 2, lax.rem(to, 2) * 4 + x, c)

    partner = (g, r, y * 2 + other)
    barrier = pltpu.get_barrier_semaphore()
    everyone = [partner] + [at_x(s) for s in (1, 2, 3)] + [at_y(s) for s in (1, 2, 3)]
    everyone += [at_z(s) for s in range(1, 8)]
    for peer in everyone:
        pl.semaphore_signal(barrier, inc=1, device_id=peer, device_id_type=MESH)

    def send(src, dst, which, slot, peer):
        copy = pltpu.make_async_remote_copy(
            src_ref=src,
            dst_ref=dst,
            send_sem=send_sem.at[which, slot],
            recv_sem=recv_sem.at[which, slot],
            device_id=peer,
            device_id_type=MESH,
        )
        copy.start()
        return copy

    f32, half = jnp.float32, jnp.bfloat16

    def summed(own, received):
        total = own.astype(f32)
        for k in range(3):
            total += received[k].astype(f32)
        return total.astype(half)

    def to_partner(which):
        return send(sending.at[which, other], core_in.at[which], which, 0, partner)

    def first_step(which, copy):
        copy.wait()

        @pl.loop(0, 8)
        def _(k):
            pair = sending[which, core, k].astype(f32) + core_in[which, k].astype(f32)
            held[which, k] = pair.astype(half)

        low, high = held.at[which, pl.ds(0, 4)], held.at[which, pl.ds(4, 4)]
        copies = []
        for s in (1, 2, 3):
            copies.append(send(low.at[:, lax.rem(x + s, 4)], x_in.at[which, s - 1], which, s, at_x(s)))
            copies.append(send(high.at[:, :, lax.rem(y + s, 4)], y_in.at[which, s - 1], which, 3 + s, at_y(s)))
        return copies

    def second_step(which, copies):
        for copy in copies:
            copy.wait()
        mid_x[which] = summed(held[which, 0:4, x], [x_in[which, k] for k in range(3)])
        mid_y[which] = summed(held[which, 4:8, :, y], [y_in[which, k] for k in range(3)])
        after = []
        for s in (1, 2, 3):
            after.append(send(mid_x.at[which, :, lax.rem(y + s, 4)], yy_in.at[which, s - 1], which, 6 + s, at_y(s)))
            after.append(send(mid_y.at[which, :, lax.rem(x + s, 4)], xx_in.at[which, s - 1], which, 9 + s, at_x(s)))
        return after

    def third_step(which, copies):
        for copy in copies:
            copy.wait()
        last[which, 0:4] = summed(mid_x[which, :, y], [yy_in[which, k] for k in range(3)])
        last[which, 4:8] = summed(mid_y[which, :, x], [xx_in[which, k] for k in range(3)])
        return [
            send(last.at[which, lax.rem(z + s, 8)], z_in.at[which, s - 1], which, 12 + s, at_z(s))
            for s in range(1, 8)
        ]

    def result(which, copies):
        for copy in copies:
            copy.wait()
        total = last[which, z].astype(f32)
        for k in range(7):
            total += z_in[which, k].astype(f32)
        out_ref[which] = total

    turned_taps(second_ref, taps)

    @pl.loop(0, 8)
    def _(f):
        hidden_grad = transposed_dot(pixel_ref[f], rgb_ref[...])
        value = hidden_grad.reshape(10, 32, 128) * slope2_ref[f]
        field[f] = value.astype(half)

    @pl.loop(0, 6)
    def _(f):
        own = field[f + 1, 1:9].astype(f32)[:, 8:24].reshape(128, 128).astype(half)
        delta[pl.ds(pl.multiple_of(128 * f, 128), 128)] = own

    columns_in_lanes(hidden_ref, 1, 1, columns)
    terms[pl.ds(3456, 8)] = jnp.zeros((8, 128), f32)
    weight_terms(columns, delta, terms)
    by_chip(terms, sending, 1)
    pl.semaphore_wait(barrier, len(everyone))
    swap_second = to_partner(1)

    @pl.loop(0, 6)
    def _(f):
        back = conv_rows(field, f, (0,), 8, taps)[:, 8:24].reshape(128, 128)
        value = (back * slope1_ref[f + 2]).astype(half)
        delta[pl.ds(pl.multiple_of(128 * f, 128), 128)] = value

    moves_second = first_step(1, swap_second)
    columns_in_lanes(cells_ref, 2, 2, columns)
    weight_terms(columns, delta, terms)
    moves_second = second_step(1, moves_second)
    by_chip(terms, sending, 0)
    swap_first = to_partner(0)
    moves_second = third_step(1, moves_second)
    moves_first = first_step(0, swap_first)
    result(1, moves_second)
    moves_first = second_step(0, moves_first)
    moves_first = third_step(0, moves_first)
    result(0, moves_first)


def f32_shape(*shape):
    return jax.ShapeDtypeStruct(shape, jnp.float32)


def talking_call(kernel, ident, mebibytes, outs, scratch, *operands):
    return pl.pallas_call(
        kernel,
        out_shape=tuple(outs),
        in_specs=in_vmem(len(operands)),
        out_specs=tuple(in_vmem(len(outs))),
        scratch_shapes=scratch,
        compiler_params=pltpu.CompilerParams(
            collective_id=ident, has_side_effects=True, vmem_limit_bytes=mebibytes * 2**20
        ),
    )(*operands)


def inside(start, count, limit):
    positions = start + jnp.arange(count)
    return (positions >= 0) & (positions < limit)


def local(dec_input, target, conv_first, conv_second, rgb_weight, vgg_first, vgg_second, vgg_third):
    g, r, c = position()
    channels = dec_input.shape[-1]
    frame0, row0, col0 = 6 * g, 8 * r, 16 * c
    half, f32, dma, vmem = jnp.bfloat16, jnp.float32, pltpu.SemaphoreType.DMA, pltpu.VMEM
    rgb = jnp.pad(rgb_weight, ((0, 13), (0, 0)))
    cells, hidden, slope1, slope2, colour_near, guide_near, w2, w3, w3_back, w2_back = talking_call(
        forward_kernel,
        3,
        24,
        (
            b16(12, 14, 32, 128), b16(10, 12, 32, 128), f32_shape(10, 128, 128), f32_shape(8, 10, 32, 128),
            b16(3, 8, 16, 128), b16(3, 32, 128),
            b16(1152, 128), b16(1152, 256), b16(1152, 128), b16(1152, 128),
        ),
        [
            vmem((12, 8, 16, 128), half), vmem((8, 48, 128), half), vmem((8, 48, 128), half),
            vmem((12, 3, 16, 128), half), vmem((12, 3, 16, 128), half),
            vmem((8, 48, 128), half), vmem((8, 48, 128), half), vmem((4, 3, 48, 128), half),
            dma((10,)), dma((10,)),
            vmem((1152, 384), half), vmem((1152, 384), half), vmem((6, 16, 128), half),
            dma((3, 6)), dma((3, 8)), dma(()),
        ],
        dec_input.reshape(24, 8, 16, channels), target, conv_first, conv_second, rgb, vgg_second, vgg_third,
    )
    images = jnp.transpose(colour_near[:, :, :3].reshape(3, 8, 3, 8, 16), (0, 3, 2, 1, 4))
    guides = jnp.transpose(guide_near[:, :24].reshape(3, 3, 8, 128), (0, 2, 1, 3))
    planes = jnp.concatenate([images.reshape(24, 3, 128), guides.reshape(24, 3, 128)], axis=1)
    planes = jnp.where(inside(row0 - 8, 24, 64)[:, None, None], planes, jnp.zeros_like(planes))
    planes = jnp.pad(planes.astype(jnp.float32), ((0, 0), (0, 2), (0, 0)))
    returned = perceptual_strip(planes, first_weights(vgg_first), (w2, w3, w3_back, w2_back))
    rows_near = jnp.transpose(returned[:, :, :24].reshape(8, 3, 3, 8, 128), (2, 0, 1, 3, 4))
    rows_near = rows_near.reshape(3, 8, 24, 128)[:, :, 7:17]
    rows_near = jnp.pad(rows_near, ((0, 0), (0, 0), (0, 0), (8, 8)))
    pixels = lax.dynamic_slice_in_dim(rows_near, col0, 32, axis=3)
    keep_frames = inside(frame0 - 1, 8, 24)[None, :, None, None]
    keep_rows = inside(row0 - 1, 10, 64)[None, None, :, None]
    keep_cols = inside(col0 - 8, 32, 128)[None, None, None, :]
    pixels = jnp.where(keep_frames & keep_rows & keep_cols, pixels, jnp.zeros_like(pixels))
    pixels = jnp.pad(jnp.transpose(pixels, (1, 0, 2, 3)).reshape(8, 3, 320), ((0, 0), (0, 13), (0, 0)))
    sums = talking_call(
        backward_kernel,
        1,
        30,
        (f32_shape(2, 16, 128),),
        [
            pltpu.VMEM((1152, 384), half),
            pltpu.VMEM((8, 10, 16, 384), half),
            pltpu.VMEM((8, 10, 32, 128), half),
            pltpu.VMEM((768, 128), half),
            pltpu.VMEM((3464, 128), jnp.float32),
            pltpu.VMEM((2, 2, 8, 4, 4, 16, 128), half),
            pltpu.VMEM((2, 8, 4, 4, 16, 128), half),
            pltpu.VMEM((2, 8, 4, 4, 16, 128), half),
            pltpu.VMEM((2, 3, 4, 4, 16, 128), half),
            pltpu.VMEM((2, 3, 4, 4, 16, 128), half),
            pltpu.VMEM((2, 4, 4, 16, 128), half),
            pltpu.VMEM((2, 4, 4, 16, 128), half),
            pltpu.VMEM((2, 3, 4, 16, 128), half),
            pltpu.VMEM((2, 3, 4, 16, 128), half),
            pltpu.VMEM((2, 8, 16, 128), half),
            pltpu.VMEM((2, 7, 16, 128), half),
            dma((2, 20)),
            dma((2, 20)),
        ],
        pixels, cells, hidden, slope1, slope2, conv_second, rgb,
    )[0]
    flat = sums[:, :14].reshape(2, 14 * 128)
    own_sums = lax.dynamic_slice_in_dim(flat, lax.rem(c, 2) * 64, 1728, axis=1)
    return own_sums[0], own_sums[1]


def solution(mesh):
    in_specs = (
        P(None, None, "row", "col", None),
        P(None, None, "col", "row", None),
        P(),
        P(),
        P(),
        P(),
        P(),
        P(),
    )
    out_specs = (P(("grp", "row", "col")), P(("grp", "row", "col")))
    return jax.shard_map(local, mesh=mesh, in_specs=in_specs, out_specs=out_specs, check_vma=False)
```

```python
import functools

import jax
import jax.numpy as jnp
from jax import lax
from jax.experimental import pallas as pl
from jax.experimental.pallas import tpu as pltpu
from jax.sharding import PartitionSpec as P

MESH = pl.DeviceIdType.MESH

gelu_scale = 0.7978845608028654
gelu_cubic = 0.044715


def position():
    return lax.axis_index("grp"), lax.axis_index("row"), lax.axis_index("col")


def same_place(one, other):
    return (one[0] == other[0]) & (one[1] == other[1]) & (one[2] == other[2])


def row_count(r):
    return 1 + jnp.where(r > 0, 1, 0) + jnp.where(r < 7, 1, 0)


def in_vmem(count):
    return [pl.BlockSpec(memory_space=pltpu.VMEM)] * count


def b16(*shape):
    return jax.ShapeDtypeStruct(shape, jnp.bfloat16)


def transposed_dot(one, other):
    return lax.dot_general(one, other, (((0,), (0,)), ((), ())), preferred_element_type=jnp.float32)


def side_by_side(value):
    cols = value.shape[0]
    at = lax.broadcasted_iota(jnp.int32, value.shape, 0)
    before = jnp.where(at == 0, 0.0, pltpu.roll(value, 1, 0))
    after = jnp.where(at == cols - 1, 0.0, pltpu.roll(value, cols - 1, 0))
    return jnp.concatenate([before, value, after], axis=1).astype(jnp.bfloat16)


def three_rows(ref, row, count):
    parts = [ref[pl.ds(row + step, count)].reshape(-1, ref.shape[-1]) for step in range(3)]
    return jnp.concatenate(parts, axis=1)


def dot32(one, other):
    return jnp.dot(one, other, preferred_element_type=jnp.float32)


def gelu_both(preact, slope_too):
    square = preact * preact
    inner_tanh = jnp.tanh(gelu_scale * preact * (1.0 + gelu_cubic * square))
    half = 0.5 * (1.0 + inner_tanh)
    value = preact * half
    if not slope_too:
        return value, None
    bend = (0.5 * gelu_scale) * (1.0 + 3.0 * gelu_cubic * square)
    return value, half + preact * (1.0 - inner_tanh * inner_tanh) * bend


def perceptual_kernel(
    planes_ref, w1_ref, vgg_second_ref, vgg_third_ref, w1_back_ref, out_ref,
    taps, act1, slope1, pooled, delta3, diff2, slope2, delta2, delta1, tmp, pixels, strip,
    w2_ref, w3_ref, w3_back_ref, w2_back_ref, send_sem, recv_sem, own_sem,
):
    g, r, c = position()
    me = (g, r, c)
    barrier = pltpu.get_barrier_semaphore()
    perceives = g < 3
    own_frame = 8 * g + c
    home = own_frame // 6
    place = lax.rem(own_frame, 6)
    ahead = perceives & (place == 0) & (home > 0)
    behind = perceives & (place == 5) & (home < 3)

    def sources(do):
        for slot in range(8):
            source_frame = 6 * g - 1 + slot

            def each(step, slot=slot, source_frame=source_frame):
                source = (source_frame // 8, r + step, lax.rem(source_frame, 8))
                pl.when(jnp.logical_not(same_place(source, me)))(
                    functools.partial(do, step, slot, source)
                )

            pl.when((source_frame >= 0) & (source_frame < 24))(functools.partial(on_rows, r, each))

    def greet(step, slot, source):
        pl.semaphore_signal(barrier, inc=1, device_id=source, device_id_type=MESH)

    sources(greet)
    lay_out_perceptual(vgg_second_ref, vgg_third_ref, w2_ref, w3_ref, w3_back_ref, w2_back_ref)
    row0 = 8 * r - 8
    lane = lax.broadcasted_iota(jnp.int32, (192, 128), 1)
    planes = planes_ref[...].reshape(192, 128)
    before = jnp.where(lane == 0, 0.0, pltpu.roll(planes, 1, 1))
    after = jnp.where(lane == 127, 0.0, pltpu.roll(planes, 127, 1))
    taps[:, 0:8] = before.reshape(24, 8, 128)
    taps[:, 8:16] = planes.reshape(24, 8, 128)
    taps[:, 16:24] = after.reshape(24, 8, 128)

    def shown(row):
        return (row0 + row >= 0) & (row0 + row < 64)

    def kept(row, value):
        return jnp.where(shown(row), value, 0.0)

    def first_rows(low, high, slope_too):
        @pl.loop(low, high)
        def _(i):
            cells = taps[pl.ds(i, 3)].reshape(72, 128).astype(jnp.bfloat16)
            value, slope = gelu_both(transposed_dot(cells, w1_ref[...]), slope_too)
            act1[i] = side_by_side(kept(i + 1, value))
            if slope_too:
                slope1[i - 6] = slope

    first_rows(0, 6, False)
    first_rows(6, 16, True)
    first_rows(16, 22, False)

    def second_rows(low, high, slope_too):
        @pl.loop(low, high)
        def _(p):
            plane = dot32(three_rows(act1, 2 * p, 2), w2_ref[...])
            value, slope = gelu_both(plane, slope_too)
            value = kept(2 * p + 2, value)
            if slope_too:
                difference = 0.25 * (value - pltpu.roll(value, 64, 1))
                diff2[pl.ds(2 * p - 4, 2)] = difference.reshape(2, 128, 128)
                slope2[pl.ds(2 * p - 4, 2)] = slope.reshape(2, 128, 128)
            tmp[...] = value[:128] + value[128:]
            mean = 0.25 * (tmp[pl.ds(0, 64, 2)] + tmp[pl.ds(1, 64, 2)])
            pooled[p] = side_by_side(mean)

    second_rows(0, 2, False)
    second_rows(2, 8, True)
    second_rows(8, 10, False)

    @pl.loop(0, 4)
    def _(half):
        j = 2 * half
        plane = dot32(three_rows(pooled, j, 2), w3_ref[...])
        value, slope = gelu_both(plane[:, :128], True)
        guide, _ = gelu_both(plane[:, 128:], False)
        delta = 0.5 * (value - guide) * slope
        delta3[j] = side_by_side(kept(2 * j + 4, delta[:64]))
        delta3[j + 1] = side_by_side(kept(2 * j + 6, delta[64:]))

    @pl.loop(0, 6)
    def _(m):
        grad = 0.25 * dot32(three_rows(delta3, m, 1), w3_back_ref[...])
        tmp[pl.ds(0, 64, 2)] = grad
        tmp[pl.ds(1, 64, 2)] = grad
        spread = tmp[...]
        for k in range(2):
            delta = (spread + diff2[2 * m + k]) * slope2[2 * m + k]
            delta2[2 * m + k] = side_by_side(kept(2 * m + 6, delta))

    @pl.loop(0, 5)
    def _(half):
        n = 2 * half
        grad = dot32(three_rows(delta2, n, 2), w2_back_ref[...])
        for k in range(2):
            delta = grad[128 * k : 128 * (k + 1)] * slope1[n + k]
            delta1[n + k] = side_by_side(kept(n + k + 7, delta))

    @pl.loop(0, 8)
    def _(q):
        grad = lax.dot_general(
            w1_back_ref[...],
            three_rows(delta1, q, 1),
            (((1,), (1,)), ((), ())),
            preferred_element_type=jnp.float32,
        )
        own = planes_ref[q + 8]
        direct = (1.0 / 6.0) * (own - pltpu.roll(own, 5, 0))
        pixels[pl.ds(pl.multiple_of(q * 8, 8), 8)] = grad + direct

    colour_rows = [pixels[pl.ds(k, 8, 8)] for k in range(3)]
    third = lax.broadcasted_iota(jnp.int32, (8, 128), 1) // 32
    for column in range(8):
        turned = [pltpu.roll(v, (32 * k + 8 - 16 * column) % 128, 1) for k, v in enumerate(colour_rows)]
        part = jnp.where(third == 0, turned[0], jnp.where(third == 1, turned[1], turned[2]))
        strip[column] = jnp.concatenate([part, jnp.zeros((8, 128), jnp.float32)], axis=0).astype(jnp.bfloat16)

    groups = jnp.where(perceives, 1, 0) + jnp.where(ahead, 1, 0) + jnp.where(behind, 1, 0)
    to_itself = perceives & (home == g) | ahead & (home == g + 1) | behind & (home == g - 1)
    awaited = 8 * row_count(r) * groups - jnp.where(to_itself, 1, 0)
    pl.when(perceives)(lambda: pl.semaphore_wait(barrier, awaited))

    def targets(do):
        for kind, (group, needed) in enumerate(((home, perceives), (home - 1, ahead), (home + 1, behind))):

            def each(step, kind=kind, group=group):
                for column in range(8):
                    peer = (group, r + step, column)
                    do(kind, step, column, peer, jnp.logical_not(same_place(peer, me)))

            pl.when(needed)(functools.partial(on_rows, r, each))

    def outgoing(kind, step, column, peer):
        place_there = own_frame - 6 * peer[0] + 1
        return pltpu.make_async_remote_copy(
            src_ref=strip.at[column],
            dst_ref=out_ref.at[place_there, 1 - step],
            send_sem=send_sem.at[kind, step + 1, column],
            recv_sem=recv_sem.at[place_there, 1 - step],
            device_id=peer,
            device_id_type=MESH,
        )

    def kept():
        return pltpu.make_async_copy(strip.at[c], out_ref.at[own_frame - 6 * g + 1, 1], own_sem)

    def start(kind, step, column, peer, away):
        pl.when(away)(lambda: outgoing(kind, step, column, peer).start())
        if step == 0:
            pl.when(jnp.logical_not(away))(lambda: kept().start())

    def finish(kind, step, column, peer, away):
        pl.when(away)(lambda: outgoing(kind, step, column, peer).wait_send())
        if step == 0:
            pl.when(jnp.logical_not(away))(lambda: kept().wait())

    def arrive(step, slot, source):
        pltpu.make_async_remote_copy(
            src_ref=strip.at[0],
            dst_ref=out_ref.at[slot, step + 1],
            send_sem=send_sem.at[0, 0, 0],
            recv_sem=recv_sem.at[slot, step + 1],
            device_id=source,
            device_id_type=MESH,
        ).wait_recv()

    targets(start)
    sources(arrive)
    targets(finish)


def two_blocks(weight):
    _, i, o = weight.shape
    return jnp.pad(weight, ((0, 0), (0, i), (0, o))) + jnp.pad(weight, ((0, 0), (i, 0), (o, 0)))


def first_weights(vgg_first):
    first = vgg_first.reshape(9, 3, 64)
    w1 = jnp.pad(two_blocks(first), ((0, 0), (0, 2), (0, 0))).reshape(72, 128)
    w1_back = jnp.pad(jnp.transpose(first[::-1], (1, 0, 2)), ((0, 5), (0, 0), (0, 64))).reshape(8, 1152)
    return w1, w1_back


def perceptual_strip(planes, first, others):
    f32, half = jnp.float32, jnp.bfloat16
    return pl.pallas_call(
        perceptual_kernel,
        out_shape=b16(8, 3, 16, 128),
        in_specs=in_vmem(5),
        out_specs=in_vmem(1)[0],
        scratch_shapes=[
            pltpu.VMEM((24, 24, 128), f32),
            pltpu.VMEM((22, 128, 384), half),
            pltpu.VMEM((10, 128, 128), f32),
            pltpu.VMEM((10, 64, 384), half),
            pltpu.VMEM((8, 64, 384), half),
            pltpu.VMEM((12, 128, 128), f32),
            pltpu.VMEM((12, 128, 128), f32),
            pltpu.VMEM((12, 128, 384), half),
            pltpu.VMEM((10, 128, 384), half),
            pltpu.VMEM((128, 128), f32),
            pltpu.VMEM((64, 128), f32),
            pltpu.VMEM((8, 16, 128), half),
            pltpu.VMEM((1152, 128), half),
            pltpu.VMEM((1152, 256), half),
            pltpu.VMEM((1152, 128), half),
            pltpu.VMEM((1152, 128), half),
            pltpu.SemaphoreType.DMA((3, 3, 8)),
            pltpu.SemaphoreType.DMA((8, 3)),
            pltpu.SemaphoreType.DMA(()),
        ],
        compiler_params=pltpu.CompilerParams(
            collective_id=4, has_side_effects=True, vmem_limit_bytes=24 * 2**20
        ),
    )(planes, first[0], *others, first[1])


def taps_in_lanes(weight_ref, out_ref):
    for q in range(9):
        for k in range(3):
            tap = 3 * q + k
            out_ref[128 * q : 128 * (q + 1), 128 * k : 128 * (k + 1)] = weight_ref[
                128 * tap : 128 * (tap + 1), :
            ]


def turned_taps(weight_ref, out_ref):
    for q in range(9):
        for k in range(3):
            tap = 26 - 3 * q - k
            block = weight_ref[128 * tap : 128 * (tap + 1), :].astype(jnp.float32)
            out_ref[128 * q : 128 * (q + 1), 128 * k : 128 * (k + 1)] = block.T.astype(jnp.bfloat16)


def conv_rows(source, frame, starts, count, taps_ref):
    size = len(starts) * count * 32

    def near(dt, dr):
        rows = [source[frame + dt, pl.ds(start + dr, count)].reshape(count * 32, 128) for start in starts]
        return rows[0] if len(rows) == 1 else jnp.concatenate(rows, axis=0)

    parts = [near(dt, dr) for dt in range(3) for dr in range(3)]
    sums = dot32(jnp.concatenate(parts, axis=1), taps_ref[...])
    total = pltpu.roll(sums[:, :128], 1, 0) + sums[:, 128:256]
    total += pltpu.roll(sums[:, 256:], size - 1, 0)
    return total.reshape(len(starts) * count, 32, 128)


def silu_parts(preact):
    gate = 1.0 / (1.0 + jnp.exp(-preact))
    return preact * gate, gate * (1.0 + preact * (1.0 - gate))


def on_rows(r, do):
    for step in (-1, 0, 1):
        pl.when((r + step >= 0) & (r + step < 8))(functools.partial(do, step))


def lay_out_perceptual(second_ref, third_ref, w2_out, w3_out, w3_back_out, w2_back_out):
    f32, half = jnp.float32, jnp.bfloat16
    for t in range(9):
        block = second_ref[64 * t : 64 * (t + 1), :].astype(f32)
        wide = third_ref[64 * t : 64 * (t + 1), :].astype(f32)
        none, low, high = jnp.zeros((64, 64), f32), 128 * t, 128 * (8 - t)
        w2_out[low : low + 64] = jnp.concatenate([block, none], axis=1).astype(half)
        w2_out[low + 64 : low + 128] = jnp.concatenate([none, block], axis=1).astype(half)
        w3_out[low : low + 64, :128] = wide.astype(half)
        w3_out[low : low + 64, 128:] = jnp.zeros((64, 128), half)
        w3_out[low + 64 : low + 128, :128] = jnp.zeros((64, 128), half)
        w3_out[low + 64 : low + 128, 128:] = wide.astype(half)
        w2_back_out[high : high + 64] = jnp.concatenate([block.T, none], axis=1).astype(half)
        w2_back_out[high + 64 : high + 128] = jnp.zeros((64, 128), half)
        turned = jnp.concatenate([wide.T, jnp.zeros((128, 64), f32)], axis=1)
        w3_back_out[high : high + 128] = turned.astype(half)


def forward_kernel(
    video_hbm, target_ref, first_hbm, second_hbm, rgb_ref,
    cells_hbm, hidden_hbm, slope1_hbm, slope2_hbm, near_out, guide_out,
    video, first_ref, second_ref, rgb16, cells, hidden_out, slope1_out, slope2_out, load_sem, store_sem,
    tile, left_send, right_send, edge_tile, edge_left, edge_right, guide_send,
    top_in, bottom_in, left_in, right_in, corner_in, halo_send, halo_recv,
    taps1, taps2, colours, send_sem, recv_sem, own_sem,
):
    loads = [
        pltpu.make_async_copy(video_hbm, video, load_sem.at[0]),
        pltpu.make_async_copy(first_hbm, first_ref, load_sem.at[1]),
        pltpu.make_async_copy(second_hbm, second_ref, load_sem.at[2]),
    ]
    for load in loads:
        load.start()
    g, r, c = position()
    me = (g, r, c)
    f32, half = jnp.float32, jnp.bfloat16
    barrier = pltpu.get_barrier_semaphore()
    perceives = g < 3
    source_group = (8 * g + c) // 6
    west, east = lax.rem(c + 7, 8), lax.rem(c + 1, 8)
    has_up, has_down = r > 0, r < 7
    group_up, group_down = jnp.where(r == 4, 3 - g, g), jnp.where(r == 3, 3 - g, g)

    def sources(do):
        def each(step):
            for column in range(8):
                source = (source_group, r + step, column)
                pl.when(jnp.logical_not(same_place(source, me)))(
                    functools.partial(do, step, column, source)
                )

        pl.when(perceives)(lambda: on_rows(r, each))

    def signal(peer):
        pl.semaphore_signal(barrier, inc=1, device_id=peer, device_id_type=MESH)

    signal((g, r, west))
    signal((g, r, east))

    @pl.when(has_up)
    def _():
        for column in (west, c, east):
            signal((group_up, r - 1, column))

    @pl.when(has_down)
    def _():
        for column in (west, c, east):
            signal((group_down, r + 1, column))

    sources(lambda step, column, source: signal(source))

    def guide_of(group):
        block = jnp.minimum(group, 2)
        rows = [target_ref[k, block, 0].astype(f32) for k in range(3)] + [jnp.zeros((8, 128), f32)]
        return jnp.concatenate(rows, axis=0).astype(half)

    guide_out[1] = guide_of(g)
    guide_send[0] = guide_of(group_up)
    guide_send[1] = guide_of(group_down)
    rgb16[...] = jnp.zeros((16, 128), f32)
    rgb16[0:3] = rgb_ref[...].astype(f32)
    loads[0].wait()

    def frames_of(group, rows):
        values = []
        for f in range(12):
            frame = 6 * group - 3 + f
            value = video[jnp.minimum(jnp.maximum(frame, 0), 23), rows]
            values.append(jnp.where((frame >= 0) & (frame < 24), value, jnp.zeros_like(value)))
        return values

    def sides(values, row):
        near = [value[row].astype(f32) for value in values]
        west_side = jnp.concatenate([v[0:4] for v in near], axis=0).astype(half)
        return west_side, jnp.concatenate([v[12:16] for v in near], axis=0).astype(half)

    for edge, (group, rows) in enumerate(((group_up, slice(0, 3)), (group_down, slice(5, 8)))):
        values = frames_of(group, rows)
        for f in range(12):
            edge_tile[edge, f] = values[f]
        for row in range(3):
            edge_left[edge, row], edge_right[edge, row] = sides(values, row)
    values = frames_of(g, slice(0, 8))
    for f in range(12):
        tile[f] = values[f]
    for row in range(8):
        left_send[row], right_send[row] = sides(values, row)

    to_itself = jnp.where(perceives & (2 * g + c < 6), 1, 0)
    pl.semaphore_wait(barrier, 9 * row_count(r) - 1 - to_itself)

    def remote(src, dst, slot, peer):
        return pltpu.make_async_remote_copy(
            src_ref=src,
            dst_ref=dst,
            send_sem=halo_send.at[slot],
            recv_sem=halo_recv.at[slot],
            device_id=peer,
            device_id_type=MESH,
        )

    sideways = [remote(left_send, right_in, 0, (g, r, west)), remote(right_send, left_in, 1, (g, r, east))]

    def to_row(edge, group, row_index, strip_in, corners, guide_slot, first_slot):
        return [
            remote(edge_tile.at[edge], strip_in, first_slot, (group, row_index, c)),
            remote(edge_left.at[edge], corner_in.at[corners + 1], first_slot + 1, (group, row_index, west)),
            remote(edge_right.at[edge], corner_in.at[corners], first_slot + 2, (group, row_index, east)),
            remote(guide_send.at[edge], guide_out.at[guide_slot], first_slot + 3, (group, row_index, c)),
        ]

    upward = to_row(0, group_up, r - 1, bottom_in, 2, 2, 2)
    downward = to_row(1, group_down, r + 1, top_in, 0, 0, 6)

    def start(copies):
        for copy in copies:
            copy.start()

    def sent(copies):
        for copy in copies:
            copy.wait_send()

    def landed(copies):
        for copy in copies:
            copy.wait_recv()

    pl.when(has_up)(lambda: start(upward))
    pl.when(has_down)(lambda: start(downward))
    start(sideways)

    loads[1].wait()
    taps_in_lanes(first_ref, taps1)
    loads[2].wait()
    taps_in_lanes(second_ref, taps2)

    def assemble(first_row, count, real, own, left, right):
        col = lax.broadcasted_iota(jnp.int32, (count, 32, 128), 1) + (16 * c - 8)
        shown = (col >= 0) & (col < 128) & real
        for quad in range(3):
            before = left[:, 16 * quad : 16 * (quad + 1)].astype(f32)
            after = right[:, 16 * quad : 16 * (quad + 1)].astype(f32)
            for k in range(4):
                f, eight = 4 * quad + k, slice(8 * (k // 2), 8 * (k // 2) + 8)
                one = before[:, eight].reshape(8 * count, 128)
                two = after[:, eight].reshape(8 * count, 128)
                if k % 2 == 0:
                    one = pltpu.roll(one, 4, 0)
                else:
                    two = pltpu.roll(two, 8 * count - 4, 0)
                sides = [one.reshape(count, 8, 128), own(f).astype(f32), two.reshape(count, 8, 128)]
                value = jnp.where(shown, jnp.concatenate(sides, axis=1), 0.0)
                cells[f, first_row : first_row + count] = value.astype(half)

    row = lax.broadcasted_iota(jnp.int32, (6, 32, 128), 0)
    col = lax.broadcasted_iota(jnp.int32, (6, 32, 128), 1) + (16 * c - 8)
    in_cols = (col >= 0) & (col < 128)

    def in_frames(f):
        frame = 6 * g - 2 + f
        return jnp.where((frame >= 0) & (frame < 24), 1.0, 0.0)

    landed(sideways)
    assemble(3, 8, True, lambda f: tile[f], left_in[...], right_in[...])

    @pl.loop(0, 10)
    def _(f):
        value, slope = silu_parts(conv_rows(cells, f, (3,), 6, taps1))
        value = jnp.where(in_cols, value, 0.0) * in_frames(f)
        hidden_out[f, 3:9] = value.astype(half)
        slope1_out[f, 16:112] = slope[:, 8:24].reshape(96, 128)

    pl.when(has_up)(lambda: landed(downward))
    pl.when(has_down)(lambda: landed(upward))
    assemble(0, 3, has_up, lambda f: top_in[f], corner_in[0], corner_in[1])
    assemble(11, 3, has_down, lambda f: bottom_in[f], corner_in[2], corner_in[3])
    image_row = jnp.where(row < 3, row, row + 6) + (8 * r - 2)
    in_image = in_cols & (image_row >= 0) & (image_row < 64)

    @pl.loop(0, 10)
    def _(f):
        value, slope = silu_parts(conv_rows(cells, f, (0, 9), 3, taps1))
        value = (jnp.where(in_image, value, 0.0) * in_frames(f)).astype(half)
        hidden_out[f, 0:3] = value[0:3]
        hidden_out[f, 9:12] = value[3:6]
        slope1_out[f, 0:16] = slope[2, 8:24]
        slope1_out[f, 112:128] = slope[3, 8:24]

    stores = [
        pltpu.make_async_copy(cells.at[pl.ds(2, 8), pl.ds(2, 10)], cells_hbm, store_sem.at[0]),
        pltpu.make_async_copy(hidden_out.at[pl.ds(1, 8), pl.ds(1, 10)], hidden_hbm, store_sem.at[1]),
        pltpu.make_async_copy(slope1_out.at[pl.ds(2, 6)], slope1_hbm, store_sem.at[2]),
        pltpu.make_async_copy(slope2_out, slope2_hbm, store_sem.at[3]),
    ]
    start(stores[:3])

    def target(step, slot):
        frame = 6 * g + slot
        return (frame // 8, r + step, lax.rem(frame, 8))

    def outgoing(step, slot):
        return pltpu.make_async_remote_copy(
            src_ref=colours.at[slot],
            dst_ref=near_out.at[1 - step, c],
            send_sem=send_sem.at[step + 1, slot],
            recv_sem=recv_sem.at[1 - step, c],
            device_id=target(step, slot),
            device_id_type=MESH,
        )

    def kept(slot):
        return pltpu.make_async_copy(colours.at[slot], near_out.at[1, c], own_sem)

    def start_colour(slot, step):
        away = jnp.logical_not(same_place(target(step, slot), me))
        pl.when(away)(lambda: outgoing(step, slot).start())
        if step == 0:
            pl.when(jnp.logical_not(away))(lambda: kept(slot).start())

    def finish(slot, step):
        away = jnp.logical_not(same_place(target(step, slot), me))
        pl.when(away)(lambda: outgoing(step, slot).wait_send())
        if step == 0:
            pl.when(jnp.logical_not(away))(lambda: kept(slot).wait())

    def arrive(step, column, source):
        pltpu.make_async_remote_copy(
            src_ref=colours.at[0],
            dst_ref=near_out.at[step + 1, column],
            send_sem=send_sem.at[0, 0],
            recv_sem=recv_sem.at[step + 1, column],
            device_id=source,
            device_id_type=MESH,
        ).wait_recv()

    @pl.loop(0, 6)
    def _(slot):
        value, slope = silu_parts(conv_rows(hidden_out, slot + 1, (0,), 10, taps2))
        slope2_out[slot + 1] = slope
        own = value[1:9, 8:24].reshape(128, 128).astype(jnp.bfloat16)
        colour = lax.dot_general(
            rgb16[...].astype(half), own, (((1,), (1,)), ((), ())), preferred_element_type=jnp.float32
        )
        colours[slot] = colour.astype(jnp.bfloat16)
        on_rows(r, functools.partial(start_colour, slot))

    @pl.loop(0, 2)
    def _(end):
        slope2_out[7 * end] = silu_parts(conv_rows(hidden_out, 7 * end, (0,), 10, taps2))[1]

    stores[3].start()
    sources(arrive)

    @pl.loop(0, 6)
    def _(slot):
        on_rows(r, functools.partial(finish, slot))

    for store in stores:
        store.wait()

    sent(sideways)
    pl.when(has_up)(lambda: sent(upward))
    pl.when(has_down)(lambda: sent(downward))


def columns_in_lanes(source, frame0, row0, out_ref):
    @pl.loop(0, 8)
    def _(f):
        value = source[f + frame0, pl.ds(row0, 10)].reshape(320, 128).astype(jnp.float32)
        parts = [pltpu.roll(value, 1, 0), value, pltpu.roll(value, 319, 0)]
        for k, part in enumerate(parts):
            own = part.reshape(10, 32, 128)[:, 8:24]
            out_ref[f, :, :, 128 * k : 128 * (k + 1)] = own.astype(jnp.bfloat16)


def weight_terms(columns, delta, terms):
    @pl.loop(0, 9)
    def _(q):
        cells = columns[pl.ds(q // 3, 6), pl.ds(lax.rem(q, 3), 8)].reshape(768, 384)
        terms[pl.ds(pl.multiple_of(384 * q, 384), 384)] = transposed_dot(cells, delta[...])


def by_chip(terms, out_ref, which):
    @pl.loop(0, 8)
    def _(z):
        for chip in range(16):
            start = 432 * z + 27 * chip
            out_ref[which, 0, z, chip // 4, chip % 4] = terms[pl.ds(start, 16)].astype(jnp.bfloat16)
            out_ref[which, 1, z, chip // 4, chip % 4] = terms[pl.ds(start + 13, 16)].astype(jnp.bfloat16)


def backward_kernel(
    pixel_ref, cells_hbm, hidden_hbm, slope1_hbm, slope2_hbm, second_hbm, rgb_ref, out_ref,
    cells_ref, hidden_ref, slope1_ref, slope2_ref, second_ref, rgb16, load_sem,
    taps, columns, field, delta, terms,
    sending, core_in, held, x_in, y_in, mid_x, mid_y, yy_in, xx_in, last, z_in, send_sem, recv_sem,
):
    g, r, c = position()
    loads = [
        pltpu.make_async_copy(src, dst, load_sem.at[k])
        for k, (src, dst) in enumerate(
            (
                (second_hbm, second_ref), (slope2_hbm, slope2_ref), (hidden_hbm, hidden_ref),
                (slope1_hbm, slope1_ref), (cells_hbm, cells_ref),
            )
        )
    ]
    for load in loads:
        load.start()
    zh, x, y, core = r // 4, lax.rem(r, 4), c // 2, lax.rem(c, 2)
    z = g * 2 + zh
    other = 1 - core

    def at_x(step):
        return (g, zh * 4 + lax.rem(x + step, 4), c)

    def at_y(step):
        return (g, r, lax.rem(y + step, 4) * 2 + core)

    def at_z(step):
        to = lax.rem(z + step, 8)
        return (to // 2, lax.rem(to, 2) * 4 + x, c)

    partner = (g, r, y * 2 + other)
    barrier = pltpu.get_barrier_semaphore()
    everyone = [partner] + [at_x(s) for s in (1, 2, 3)] + [at_y(s) for s in (1, 2, 3)]
    everyone += [at_z(s) for s in range(1, 8)]
    for peer in everyone:
        pl.semaphore_signal(barrier, inc=1, device_id=peer, device_id_type=MESH)

    def send(src, dst, which, slot, peer):
        copy = pltpu.make_async_remote_copy(
            src_ref=src,
            dst_ref=dst,
            send_sem=send_sem.at[which, slot],
            recv_sem=recv_sem.at[which, slot],
            device_id=peer,
            device_id_type=MESH,
        )
        copy.start()
        return copy

    f32, half = jnp.float32, jnp.bfloat16

    def summed(own, received):
        total = own.astype(f32)
        for k in range(3):
            total += received[k].astype(f32)
        return total.astype(half)

    def to_partner(which):
        return send(sending.at[which, other], core_in.at[which], which, 0, partner)

    def first_step(which, copy):
        copy.wait()

        @pl.loop(0, 8)
        def _(k):
            pair = sending[which, core, k].astype(f32) + core_in[which, k].astype(f32)
            held[which, k] = pair.astype(half)

        low, high = held.at[which, pl.ds(0, 4)], held.at[which, pl.ds(4, 4)]
        copies = []
        for s in (1, 2, 3):
            copies.append(send(low.at[:, lax.rem(x + s, 4)], x_in.at[which, s - 1], which, s, at_x(s)))
            copies.append(send(high.at[:, :, lax.rem(y + s, 4)], y_in.at[which, s - 1], which, 3 + s, at_y(s)))
        return copies

    def second_step(which, copies):
        for copy in copies:
            copy.wait()
        mid_x[which] = summed(held[which, 0:4, x], [x_in[which, k] for k in range(3)])
        mid_y[which] = summed(held[which, 4:8, :, y], [y_in[which, k] for k in range(3)])
        after = []
        for s in (1, 2, 3):
            after.append(send(mid_x.at[which, :, lax.rem(y + s, 4)], yy_in.at[which, s - 1], which, 6 + s, at_y(s)))
            after.append(send(mid_y.at[which, :, lax.rem(x + s, 4)], xx_in.at[which, s - 1], which, 9 + s, at_x(s)))
        return after

    def third_step(which, copies):
        for copy in copies:
            copy.wait()
        last[which, 0:4] = summed(mid_x[which, :, y], [yy_in[which, k] for k in range(3)])
        last[which, 4:8] = summed(mid_y[which, :, x], [xx_in[which, k] for k in range(3)])
        return [
            send(last.at[which, lax.rem(z + s, 8)], z_in.at[which, s - 1], which, 12 + s, at_z(s))
            for s in range(1, 8)
        ]

    def result(which, copies):
        for copy in copies:
            copy.wait()
        total = last[which, z].astype(f32)
        for k in range(7):
            total += z_in[which, k].astype(f32)
        out_ref[which] = total

    rgb16[...] = jnp.zeros((16, 128), f32)
    rgb16[0:3] = rgb_ref[...].astype(f32)
    loads[0].wait()
    turned_taps(second_ref, taps)
    loads[1].wait()

    @pl.loop(0, 8)
    def _(f):
        hidden_grad = transposed_dot(pixel_ref[f], rgb16[...].astype(half))
        value = hidden_grad.reshape(10, 32, 128) * slope2_ref[f]
        field[f] = value.astype(half)

    @pl.loop(0, 6)
    def _(f):
        own = field[f + 1, 1:9].astype(f32)[:, 8:24].reshape(128, 128).astype(half)
        delta[pl.ds(pl.multiple_of(128 * f, 128), 128)] = own

    loads[2].wait()
    columns_in_lanes(hidden_ref, 0, 0, columns)
    terms[pl.ds(3456, 8)] = jnp.zeros((8, 128), f32)
    weight_terms(columns, delta, terms)
    by_chip(terms, sending, 1)
    pl.semaphore_wait(barrier, len(everyone))
    swap_second = to_partner(1)
    loads[3].wait()

    @pl.loop(0, 6)
    def _(f):
        back = conv_rows(field, f, (0,), 8, taps)[:, 8:24].reshape(128, 128)
        value = (back * slope1_ref[f]).astype(half)
        delta[pl.ds(pl.multiple_of(128 * f, 128), 128)] = value

    moves_second = first_step(1, swap_second)
    loads[4].wait()
    columns_in_lanes(cells_ref, 0, 0, columns)
    weight_terms(columns, delta, terms)
    moves_second = second_step(1, moves_second)
    by_chip(terms, sending, 0)
    swap_first = to_partner(0)
    moves_second = third_step(1, moves_second)
    moves_first = first_step(0, swap_first)
    result(1, moves_second)
    moves_first = second_step(0, moves_first)
    moves_first = third_step(0, moves_first)
    result(0, moves_first)


def f32_shape(*shape):
    return jax.ShapeDtypeStruct(shape, jnp.float32)


def places(text):
    return [pl.BlockSpec(memory_space=pltpu.VMEM if letter == "v" else pl.ANY) for letter in text]


def talking_call(kernel, ident, mebibytes, in_places, out_places, outs, scratch, *operands):
    return pl.pallas_call(
        kernel,
        out_shape=tuple(outs),
        in_specs=places(in_places),
        out_specs=tuple(places(out_places)),
        scratch_shapes=scratch,
        compiler_params=pltpu.CompilerParams(
            collective_id=ident, has_side_effects=True, vmem_limit_bytes=mebibytes * 2**20
        ),
    )(*operands)


def inside(start, count, limit):
    positions = start + jnp.arange(count)
    return (positions >= 0) & (positions < limit)


def local(dec_input, target, conv_first, conv_second, rgb_weight, vgg_first, vgg_second, vgg_third):
    g, r, c = position()
    channels = dec_input.shape[-1]
    frame0, row0, col0 = 6 * g, 8 * r, 16 * c
    half, f32, dma, vmem = jnp.bfloat16, jnp.float32, pltpu.SemaphoreType.DMA, pltpu.VMEM
    cells, hidden, slope1, slope2, colour_near, guide_near = talking_call(
        forward_kernel,
        3,
        28,
        "hvhhv",
        "hhhhvv",
        (
            b16(8, 10, 32, 128), b16(8, 10, 32, 128), f32_shape(6, 128, 128), f32_shape(8, 10, 32, 128),
            b16(3, 8, 16, 128), b16(3, 32, 128),
        ),
        [
            vmem((24, 8, 16, 128), half), vmem((3456, 128), half), vmem((3456, 128), half), vmem((16, 128), f32),
            vmem((12, 14, 32, 128), half), vmem((10, 12, 32, 128), half),
            vmem((10, 128, 128), f32), vmem((8, 10, 32, 128), f32), dma((3,)), dma((4,)),
            vmem((12, 8, 16, 128), half), vmem((8, 48, 128), half), vmem((8, 48, 128), half),
            vmem((2, 12, 3, 16, 128), half), vmem((2, 3, 48, 128), half), vmem((2, 3, 48, 128), half),
            vmem((2, 32, 128), half),
            vmem((12, 3, 16, 128), half), vmem((12, 3, 16, 128), half),
            vmem((8, 48, 128), half), vmem((8, 48, 128), half), vmem((4, 3, 48, 128), half),
            dma((10,)), dma((10,)),
            vmem((1152, 384), half), vmem((1152, 384), half), vmem((6, 16, 128), half),
            dma((3, 6)), dma((3, 8)), dma(()),
        ],
        dec_input.reshape(24, 8, 16, channels), target, conv_first, conv_second, rgb_weight,
    )
    images = jnp.transpose(colour_near[:, :, :3].reshape(3, 8, 3, 8, 16), (0, 3, 2, 1, 4))
    guides = jnp.transpose(guide_near[:, :24].reshape(3, 3, 8, 128), (0, 2, 1, 3))
    planes = jnp.concatenate([images.reshape(24, 3, 128), guides.reshape(24, 3, 128)], axis=1)
    planes = jnp.where(inside(row0 - 8, 24, 64)[:, None, None], planes, jnp.zeros_like(planes))
    planes = jnp.pad(planes.astype(jnp.float32), ((0, 0), (0, 2), (0, 0)))
    returned = perceptual_strip(planes, first_weights(vgg_first), (vgg_second, vgg_third))
    pixels = returned[:, :, :8, :96].reshape(8, 3, 8, 3, 32)
    pixels = jnp.transpose(pixels, (0, 3, 1, 2, 4)).reshape(8, 3, 24, 32)[:, :, 7:17]
    keep_frames = inside(frame0 - 1, 8, 24)[:, None, None, None]
    keep_rows = inside(row0 - 1, 10, 64)[None, None, :, None]
    keep_cols = inside(col0 - 8, 32, 128)[None, None, None, :]
    pixels = jnp.where(keep_frames & keep_rows & keep_cols, pixels, jnp.zeros_like(pixels))
    pixels = jnp.pad(pixels.reshape(8, 3, 320), ((0, 0), (0, 13), (0, 0)))
    sums = talking_call(
        backward_kernel,
        1,
        34,
        "vhhhhhv",
        "v",
        (f32_shape(2, 16, 128),),
        [
            vmem((8, 10, 32, 128), half), vmem((8, 10, 32, 128), half), vmem((6, 128, 128), f32),
            vmem((8, 10, 32, 128), f32), vmem((3456, 128), half), vmem((16, 128), f32), dma((5,)),
            pltpu.VMEM((1152, 384), half),
            pltpu.VMEM((8, 10, 16, 384), half),
            pltpu.VMEM((8, 10, 32, 128), half),
            pltpu.VMEM((768, 128), half),
            pltpu.VMEM((3464, 128), jnp.float32),
            pltpu.VMEM((2, 2, 8, 4, 4, 16, 128), half),
            pltpu.VMEM((2, 8, 4, 4, 16, 128), half),
            pltpu.VMEM((2, 8, 4, 4, 16, 128), half),
            pltpu.VMEM((2, 3, 4, 4, 16, 128), half),
            pltpu.VMEM((2, 3, 4, 4, 16, 128), half),
            pltpu.VMEM((2, 4, 4, 16, 128), half),
            pltpu.VMEM((2, 4, 4, 16, 128), half),
            pltpu.VMEM((2, 3, 4, 16, 128), half),
            pltpu.VMEM((2, 3, 4, 16, 128), half),
            pltpu.VMEM((2, 8, 16, 128), half),
            pltpu.VMEM((2, 7, 16, 128), half),
            dma((2, 20)),
            dma((2, 20)),
        ],
        pixels, cells, hidden, slope1, slope2, conv_second, rgb_weight,
    )[0]
    flat = sums[:, :14].reshape(2, 14 * 128)
    own_sums = lax.dynamic_slice_in_dim(flat, lax.rem(c, 2) * 64, 1728, axis=1)
    return own_sums[0], own_sums[1]


def solution(mesh):
    in_specs = (
        P(None, None, "row", "col", None),
        P(None, None, "col", "row", None),
        P(),
        P(),
        P(),
        P(),
        P(),
        P(),
    )
    out_specs = (P(("grp", "row", "col")), P(("grp", "row", "col")))
    return jax.shard_map(local, mesh=mesh, in_specs=in_specs, out_specs=out_specs, check_vma=False)
```

```python
import functools

import jax
import jax.numpy as jnp
from jax import lax
from jax.experimental import pallas as pl
from jax.experimental.pallas import tpu as pltpu
from jax.sharding import PartitionSpec as P

MESH = pl.DeviceIdType.MESH

gelu_scale = 0.7978845608028654
gelu_cubic = 0.044715


def position():
    return lax.axis_index("grp"), lax.axis_index("row"), lax.axis_index("col")


def same_place(one, other):
    return (one[0] == other[0]) & (one[1] == other[1]) & (one[2] == other[2])


def row_count(r):
    return 1 + jnp.where(r > 0, 1, 0) + jnp.where(r < 7, 1, 0)


def in_vmem(count):
    return [pl.BlockSpec(memory_space=pltpu.VMEM)] * count


def b16(*shape):
    return jax.ShapeDtypeStruct(shape, jnp.bfloat16)


def transposed_dot(one, other):
    return lax.dot_general(one, other, (((0,), (0,)), ((), ())), preferred_element_type=jnp.float32)


def side_by_side(value):
    cols = value.shape[0]
    at = lax.broadcasted_iota(jnp.int32, value.shape, 0)
    before = jnp.where(at == 0, 0.0, pltpu.roll(value, 1, 0))
    after = jnp.where(at == cols - 1, 0.0, pltpu.roll(value, cols - 1, 0))
    return jnp.concatenate([before, value, after], axis=1).astype(jnp.bfloat16)


def three_rows(ref, row, count):
    parts = [ref[pl.ds(row + step, count)].reshape(-1, ref.shape[-1]) for step in range(3)]
    return jnp.concatenate(parts, axis=1)


def dot32(one, other):
    return jnp.dot(one, other, preferred_element_type=jnp.float32)


def gelu_both(preact, slope_too):
    square = preact * preact
    inner_tanh = jnp.tanh(gelu_scale * preact * (1.0 + gelu_cubic * square))
    half = 0.5 * (1.0 + inner_tanh)
    value = preact * half
    if not slope_too:
        return value, None
    bend = (0.5 * gelu_scale) * (1.0 + 3.0 * gelu_cubic * square)
    return value, half + preact * (1.0 - inner_tanh * inner_tanh) * bend


def perceptual_kernel(
    near_ref, guide_ref, w1_ref, vgg_second_ref, vgg_third_ref, w1_back_ref, out_ref,
    planes_ref, guides,
    taps, act1, slope1, pooled, delta3, diff2, slope2, delta2, delta1, tmp, pixels, strip,
    w2_ref, w3_ref, w3_back_ref, w2_back_ref, send_sem, recv_sem, own_sem,
):
    g, r, c = position()
    me = (g, r, c)
    barrier = pltpu.get_barrier_semaphore()
    perceives = g < 3
    own_frame = 8 * g + c
    home = own_frame // 6
    place = lax.rem(own_frame, 6)
    ahead = perceives & (place == 0) & (home > 0)
    behind = perceives & (place == 5) & (home < 3)

    def sources(do):
        for slot in range(8):
            source_frame = 6 * g - 1 + slot

            def each(step, slot=slot, source_frame=source_frame):
                source = (source_frame // 8, r + step, lax.rem(source_frame, 8))
                pl.when(jnp.logical_not(same_place(source, me)))(
                    functools.partial(do, step, slot, source)
                )

            pl.when((source_frame >= 0) & (source_frame < 24))(functools.partial(on_rows, r, each))

    def greet(step, slot, source):
        pl.semaphore_signal(barrier, inc=1, device_id=source, device_id_type=MESH)

    sources(greet)
    lay_out_perceptual(vgg_second_ref, vgg_third_ref, w2_ref, w3_ref, w3_back_ref, w2_back_ref)
    row0 = 8 * r - 8
    kind = lax.broadcasted_iota(jnp.int32, (8, 128), 0)
    block = lax.broadcasted_iota(jnp.int32, (8, 128), 1) // 16
    for part in range(3):
        guides[...] = guide_ref[part].astype(jnp.float32)
        tiles = [near_ref[part, column].astype(jnp.float32)[0:8] for column in range(8)]
        here = (kind < 3) & (row0 + 8 * part >= 0) & (row0 + 8 * part < 64)
        seen = (row0 + 8 * part >= 0) & (row0 + 8 * part < 64)
        for i in range(8):
            image = jnp.zeros((8, 128), jnp.float32)
            for column in range(8):
                turned = pltpu.roll(tiles[column], (16 * column - 16 * i) % 128, 1)
                image = jnp.where(block == column, turned, image)
            planes_ref[8 * part + i] = jnp.where(here, image, 0.0)
            planes_ref[8 * part + i, 3:6] = jnp.where(seen, guides[pl.ds(i, 3, 8)], 0.0)
    lane = lax.broadcasted_iota(jnp.int32, (192, 128), 1)
    planes = planes_ref[...].reshape(192, 128)
    before = jnp.where(lane == 0, 0.0, pltpu.roll(planes, 1, 1))
    after = jnp.where(lane == 127, 0.0, pltpu.roll(planes, 127, 1))
    taps[:, 0:8] = before.reshape(24, 8, 128)
    taps[:, 8:16] = planes.reshape(24, 8, 128)
    taps[:, 16:24] = after.reshape(24, 8, 128)

    def shown(row):
        return (row0 + row >= 0) & (row0 + row < 64)

    def kept(row, value):
        return jnp.where(shown(row), value, 0.0)

    def first_rows(low, high, slope_too):
        @pl.loop(low, high)
        def _(i):
            cells = taps[pl.ds(i, 3)].reshape(72, 128).astype(jnp.bfloat16)
            value, slope = gelu_both(transposed_dot(cells, w1_ref[...]), slope_too)
            act1[i] = side_by_side(kept(i + 1, value))
            if slope_too:
                slope1[i - 6] = slope

    first_rows(0, 6, False)
    first_rows(6, 16, True)
    first_rows(16, 22, False)

    def second_rows(low, high, slope_too):
        @pl.loop(low, high)
        def _(p):
            plane = dot32(three_rows(act1, 2 * p, 2), w2_ref[...])
            value, slope = gelu_both(plane, slope_too)
            value = kept(2 * p + 2, value)
            if slope_too:
                difference = 0.25 * (value - pltpu.roll(value, 64, 1))
                diff2[pl.ds(2 * p - 4, 2)] = difference.reshape(2, 128, 128)
                slope2[pl.ds(2 * p - 4, 2)] = slope.reshape(2, 128, 128)
            tmp[...] = value[:128] + value[128:]
            mean = 0.25 * (tmp[pl.ds(0, 64, 2)] + tmp[pl.ds(1, 64, 2)])
            pooled[p] = side_by_side(mean)

    second_rows(0, 2, False)
    second_rows(2, 8, True)
    second_rows(8, 10, False)

    @pl.loop(0, 4)
    def _(half):
        j = 2 * half
        plane = dot32(three_rows(pooled, j, 2), w3_ref[...])
        value, slope = gelu_both(plane[:, :128], True)
        guide, _ = gelu_both(plane[:, 128:], False)
        delta = 0.5 * (value - guide) * slope
        delta3[j] = side_by_side(kept(2 * j + 4, delta[:64]))
        delta3[j + 1] = side_by_side(kept(2 * j + 6, delta[64:]))

    @pl.loop(0, 6)
    def _(m):
        grad = 0.25 * dot32(three_rows(delta3, m, 1), w3_back_ref[...])
        tmp[pl.ds(0, 64, 2)] = grad
        tmp[pl.ds(1, 64, 2)] = grad
        spread = tmp[...]
        for k in range(2):
            delta = (spread + diff2[2 * m + k]) * slope2[2 * m + k]
            delta2[2 * m + k] = side_by_side(kept(2 * m + 6, delta))

    @pl.loop(0, 5)
    def _(half):
        n = 2 * half
        grad = dot32(three_rows(delta2, n, 2), w2_back_ref[...])
        for k in range(2):
            delta = grad[128 * k : 128 * (k + 1)] * slope1[n + k]
            delta1[n + k] = side_by_side(kept(n + k + 7, delta))

    @pl.loop(0, 8)
    def _(q):
        grad = lax.dot_general(
            w1_back_ref[...],
            three_rows(delta1, q, 1),
            (((1,), (1,)), ((), ())),
            preferred_element_type=jnp.float32,
        )
        own = planes_ref[q + 8]
        direct = (1.0 / 6.0) * (own - pltpu.roll(own, 5, 0))
        pixels[pl.ds(pl.multiple_of(q * 8, 8), 8)] = grad + direct

    colour_rows = [pixels[pl.ds(k, 8, 8)] for k in range(3)]
    third = lax.broadcasted_iota(jnp.int32, (8, 128), 1) // 32
    for column in range(8):
        turned = [pltpu.roll(v, (32 * k + 8 - 16 * column) % 128, 1) for k, v in enumerate(colour_rows)]
        part = jnp.where(third == 0, turned[0], jnp.where(third == 1, turned[1], turned[2]))
        strip[column] = jnp.concatenate([part, jnp.zeros((8, 128), jnp.float32)], axis=0).astype(jnp.bfloat16)

    groups = jnp.where(perceives, 1, 0) + jnp.where(ahead, 1, 0) + jnp.where(behind, 1, 0)
    to_itself = perceives & (home == g) | ahead & (home == g + 1) | behind & (home == g - 1)
    awaited = 8 * row_count(r) * groups - jnp.where(to_itself, 1, 0)
    pl.when(perceives)(lambda: pl.semaphore_wait(barrier, awaited))

    def targets(do):
        for kind, (group, needed) in enumerate(((home, perceives), (home - 1, ahead), (home + 1, behind))):

            def each(step, kind=kind, group=group):
                for column in range(8):
                    peer = (group, r + step, column)
                    do(kind, step, column, peer, jnp.logical_not(same_place(peer, me)))

            pl.when(needed)(functools.partial(on_rows, r, each))

    def outgoing(kind, step, column, peer):
        place_there = own_frame - 6 * peer[0] + 1
        return pltpu.make_async_remote_copy(
            src_ref=strip.at[column],
            dst_ref=out_ref.at[place_there, 1 - step],
            send_sem=send_sem.at[kind, step + 1, column],
            recv_sem=recv_sem.at[place_there, 1 - step],
            device_id=peer,
            device_id_type=MESH,
        )

    def kept():
        return pltpu.make_async_copy(strip.at[c], out_ref.at[own_frame - 6 * g + 1, 1], own_sem)

    def start(kind, step, column, peer, away):
        pl.when(away)(lambda: outgoing(kind, step, column, peer).start())
        if step == 0:
            pl.when(jnp.logical_not(away))(lambda: kept().start())

    def finish(kind, step, column, peer, away):
        pl.when(away)(lambda: outgoing(kind, step, column, peer).wait_send())
        if step == 0:
            pl.when(jnp.logical_not(away))(lambda: kept().wait())

    def arrive(step, slot, source):
        pltpu.make_async_remote_copy(
            src_ref=strip.at[0],
            dst_ref=out_ref.at[slot, step + 1],
            send_sem=send_sem.at[0, 0, 0],
            recv_sem=recv_sem.at[slot, step + 1],
            device_id=source,
            device_id_type=MESH,
        ).wait_recv()

    targets(start)
    sources(arrive)
    targets(finish)


def two_blocks(weight):
    _, i, o = weight.shape
    return jnp.pad(weight, ((0, 0), (0, i), (0, o))) + jnp.pad(weight, ((0, 0), (i, 0), (o, 0)))


def first_weights(vgg_first):
    first = vgg_first.reshape(9, 3, 64)
    w1 = jnp.pad(two_blocks(first), ((0, 0), (0, 2), (0, 0))).reshape(72, 128)
    w1_back = jnp.pad(jnp.transpose(first[::-1], (1, 0, 2)), ((0, 5), (0, 0), (0, 64))).reshape(8, 1152)
    return w1, w1_back


def perceptual_strip(near, guides, first, others):
    f32, half = jnp.float32, jnp.bfloat16
    return pl.pallas_call(
        perceptual_kernel,
        out_shape=b16(8, 3, 16, 128),
        in_specs=in_vmem(6),
        out_specs=in_vmem(1)[0],
        scratch_shapes=[
            pltpu.VMEM((24, 8, 128), f32),
            pltpu.VMEM((32, 128), f32),
            pltpu.VMEM((24, 24, 128), f32),
            pltpu.VMEM((22, 128, 384), half),
            pltpu.VMEM((10, 128, 128), f32),
            pltpu.VMEM((10, 64, 384), half),
            pltpu.VMEM((8, 64, 384), half),
            pltpu.VMEM((12, 128, 128), f32),
            pltpu.VMEM((12, 128, 128), f32),
            pltpu.VMEM((12, 128, 384), half),
            pltpu.VMEM((10, 128, 384), half),
            pltpu.VMEM((128, 128), f32),
            pltpu.VMEM((64, 128), f32),
            pltpu.VMEM((8, 16, 128), half),
            pltpu.VMEM((1152, 128), half),
            pltpu.VMEM((1152, 256), half),
            pltpu.VMEM((1152, 128), half),
            pltpu.VMEM((1152, 128), half),
            pltpu.SemaphoreType.DMA((3, 3, 8)),
            pltpu.SemaphoreType.DMA((8, 3)),
            pltpu.SemaphoreType.DMA(()),
        ],
        compiler_params=pltpu.CompilerParams(
            collective_id=4, has_side_effects=True, vmem_limit_bytes=24 * 2**20
        ),
    )(near, guides, first[0], *others, first[1])


def taps_in_lanes(weight_ref, out_ref):
    for q in range(9):
        for k in range(3):
            tap = 3 * q + k
            out_ref[128 * q : 128 * (q + 1), 128 * k : 128 * (k + 1)] = weight_ref[
                128 * tap : 128 * (tap + 1), :
            ]


def turned_taps(weight_ref, out_ref):
    for q in range(9):
        for k in range(3):
            tap = 26 - 3 * q - k
            block = weight_ref[128 * tap : 128 * (tap + 1), :].astype(jnp.float32)
            out_ref[128 * q : 128 * (q + 1), 128 * k : 128 * (k + 1)] = block.T.astype(jnp.bfloat16)


def conv_rows(source, frame, starts, count, taps_ref):
    size = len(starts) * count * 32

    def near(dt, dr):
        rows = [source[frame + dt, pl.ds(start + dr, count)].reshape(count * 32, 128) for start in starts]
        return rows[0] if len(rows) == 1 else jnp.concatenate(rows, axis=0)

    parts = [near(dt, dr) for dt in range(3) for dr in range(3)]
    sums = dot32(jnp.concatenate(parts, axis=1), taps_ref[...])
    total = pltpu.roll(sums[:, :128], 1, 0) + sums[:, 128:256]
    total += pltpu.roll(sums[:, 256:], size - 1, 0)
    return total.reshape(len(starts) * count, 32, 128)


def silu_parts(preact):
    gate = 1.0 / (1.0 + jnp.exp(-preact))
    return preact * gate, gate * (1.0 + preact * (1.0 - gate))


def on_rows(r, do):
    for step in (-1, 0, 1):
        pl.when((r + step >= 0) & (r + step < 8))(functools.partial(do, step))


def lay_out_perceptual(second_ref, third_ref, w2_out, w3_out, w3_back_out, w2_back_out):
    f32, half = jnp.float32, jnp.bfloat16
    for t in range(9):
        turned_block = second_ref[:, 64 * t : 64 * (t + 1)].astype(f32)
        block = turned_block.T
        wide = third_ref[64 * t : 64 * (t + 1), :].astype(f32)
        none, low, high = jnp.zeros((64, 64), f32), 128 * t, 128 * (8 - t)
        w2_out[low : low + 64] = jnp.concatenate([block, none], axis=1).astype(half)
        w2_out[low + 64 : low + 128] = jnp.concatenate([none, block], axis=1).astype(half)
        w3_out[low : low + 64, :128] = wide.astype(half)
        w3_out[low : low + 64, 128:] = jnp.zeros((64, 128), half)
        w3_out[low + 64 : low + 128, :128] = jnp.zeros((64, 128), half)
        w3_out[low + 64 : low + 128, 128:] = wide.astype(half)
        w2_back_out[high : high + 64] = jnp.concatenate([turned_block, none], axis=1).astype(half)
        w2_back_out[high + 64 : high + 128] = jnp.zeros((64, 128), half)
        turned = jnp.concatenate([wide.T, jnp.zeros((128, 64), f32)], axis=1)
        w3_back_out[high : high + 128] = turned.astype(half)


def forward_kernel(
    video_hbm, target_ref, first_hbm, second_hbm, rgb_ref,
    cells_hbm, hidden_hbm, slope1_hbm, slope2_hbm, near_out, guide_out,
    video, first_ref, second_ref, rgb16, cells, hidden_out, slope1_out, slope2_out, load_sem, store_sem,
    tile, left_send, right_send, edge_tile, edge_left, edge_right, guide_send,
    top_in, bottom_in, left_in, right_in, corner_in, halo_send, halo_recv,
    taps1, taps2, colours, send_sem, recv_sem, own_sem,
):
    loads = [
        pltpu.make_async_copy(video_hbm, video, load_sem.at[0]),
        pltpu.make_async_copy(first_hbm, first_ref, load_sem.at[1]),
        pltpu.make_async_copy(second_hbm, second_ref, load_sem.at[2]),
    ]
    for load in loads:
        load.start()
    g, r, c = position()
    me = (g, r, c)
    f32, half = jnp.float32, jnp.bfloat16
    barrier = pltpu.get_barrier_semaphore()
    perceives = g < 3
    source_group = (8 * g + c) // 6
    west, east = lax.rem(c + 7, 8), lax.rem(c + 1, 8)
    has_up, has_down = r > 0, r < 7
    group_up, group_down = jnp.where(r == 4, 3 - g, g), jnp.where(r == 3, 3 - g, g)

    def sources(do):
        def each(step):
            for column in range(8):
                source = (source_group, r + step, column)
                pl.when(jnp.logical_not(same_place(source, me)))(
                    functools.partial(do, step, column, source)
                )

        pl.when(perceives)(lambda: on_rows(r, each))

    def signal(peer):
        pl.semaphore_signal(barrier, inc=1, device_id=peer, device_id_type=MESH)

    signal((g, r, west))
    signal((g, r, east))

    @pl.when(has_up)
    def _():
        for column in (west, c, east):
            signal((group_up, r - 1, column))

    @pl.when(has_down)
    def _():
        for column in (west, c, east):
            signal((group_down, r + 1, column))

    sources(lambda step, column, source: signal(source))

    def guide_of(group):
        block = jnp.minimum(group, 2)
        rows = [target_ref[k, block, 0].astype(f32) for k in range(3)] + [jnp.zeros((8, 128), f32)]
        return jnp.concatenate(rows, axis=0).astype(half)

    guide_out[1] = guide_of(g)
    guide_send[0] = guide_of(group_up)
    guide_send[1] = guide_of(group_down)
    rgb16[...] = jnp.zeros((16, 128), f32)
    rgb16[0:3] = rgb_ref[...].astype(f32)
    loads[0].wait()

    def frames_of(group, rows):
        values = []
        for f in range(12):
            frame = 6 * group - 3 + f
            value = video[jnp.minimum(jnp.maximum(frame, 0), 23), rows]
            values.append(jnp.where((frame >= 0) & (frame < 24), value, jnp.zeros_like(value)))
        return values

    def sides(values, row):
        near = [value[row].astype(f32) for value in values]
        west_side = jnp.concatenate([v[0:4] for v in near], axis=0).astype(half)
        return west_side, jnp.concatenate([v[12:16] for v in near], axis=0).astype(half)

    for edge, (group, rows) in enumerate(((group_up, slice(0, 3)), (group_down, slice(5, 8)))):
        values = frames_of(group, rows)
        for f in range(12):
            edge_tile[edge, f] = values[f]
        for row in range(3):
            edge_left[edge, row], edge_right[edge, row] = sides(values, row)
    values = frames_of(g, slice(0, 8))
    for f in range(12):
        tile[f] = values[f]
    for row in range(8):
        left_send[row], right_send[row] = sides(values, row)

    to_itself = jnp.where(perceives & (2 * g + c < 6), 1, 0)
    pl.semaphore_wait(barrier, 9 * row_count(r) - 1 - to_itself)

    def remote(src, dst, slot, peer):
        return pltpu.make_async_remote_copy(
            src_ref=src,
            dst_ref=dst,
            send_sem=halo_send.at[slot],
            recv_sem=halo_recv.at[slot],
            device_id=peer,
            device_id_type=MESH,
        )

    sideways = [remote(left_send, right_in, 0, (g, r, west)), remote(right_send, left_in, 1, (g, r, east))]

    def to_row(edge, group, row_index, strip_in, corners, guide_slot, first_slot):
        return [
            remote(edge_tile.at[edge], strip_in, first_slot, (group, row_index, c)),
            remote(edge_left.at[edge], corner_in.at[corners + 1], first_slot + 1, (group, row_index, west)),
            remote(edge_right.at[edge], corner_in.at[corners], first_slot + 2, (group, row_index, east)),
            remote(guide_send.at[edge], guide_out.at[guide_slot], first_slot + 3, (group, row_index, c)),
        ]

    upward = to_row(0, group_up, r - 1, bottom_in, 2, 2, 2)
    downward = to_row(1, group_down, r + 1, top_in, 0, 0, 6)

    def start(copies):
        for copy in copies:
            copy.start()

    def sent(copies):
        for copy in copies:
            copy.wait_send()

    def landed(copies):
        for copy in copies:
            copy.wait_recv()

    pl.when(has_up)(lambda: start(upward))
    pl.when(has_down)(lambda: start(downward))
    start(sideways)

    loads[1].wait()
    taps_in_lanes(first_ref, taps1)
    loads[2].wait()
    taps_in_lanes(second_ref, taps2)

    def assemble(first_row, count, real, own, left, right):
        col = lax.broadcasted_iota(jnp.int32, (count, 32, 128), 1) + (16 * c - 8)
        shown = (col >= 0) & (col < 128) & real
        for quad in range(3):
            before = left[:, 16 * quad : 16 * (quad + 1)].astype(f32)
            after = right[:, 16 * quad : 16 * (quad + 1)].astype(f32)
            for k in range(4):
                f, eight = 4 * quad + k, slice(8 * (k // 2), 8 * (k // 2) + 8)
                one = before[:, eight].reshape(8 * count, 128)
                two = after[:, eight].reshape(8 * count, 128)
                if k % 2 == 0:
                    one = pltpu.roll(one, 4, 0)
                else:
                    two = pltpu.roll(two, 8 * count - 4, 0)
                sides = [one.reshape(count, 8, 128), own(f).astype(f32), two.reshape(count, 8, 128)]
                value = jnp.where(shown, jnp.concatenate(sides, axis=1), 0.0)
                cells[f, first_row : first_row + count] = value.astype(half)

    row = lax.broadcasted_iota(jnp.int32, (6, 32, 128), 0)
    col = lax.broadcasted_iota(jnp.int32, (6, 32, 128), 1) + (16 * c - 8)
    in_cols = (col >= 0) & (col < 128)

    def in_frames(f):
        frame = 6 * g - 2 + f
        return jnp.where((frame >= 0) & (frame < 24), 1.0, 0.0)

    landed(sideways)
    assemble(3, 8, True, lambda f: tile[f], left_in[...], right_in[...])

    @pl.loop(0, 10)
    def _(f):
        value, slope = silu_parts(conv_rows(cells, f, (3,), 6, taps1))
        value = jnp.where(in_cols, value, 0.0) * in_frames(f)
        hidden_out[f, 3:9] = value.astype(half)
        slope1_out[f, 16:112] = slope[:, 8:24].reshape(96, 128)

    pl.when(has_up)(lambda: landed(downward))
    pl.when(has_down)(lambda: landed(upward))
    assemble(0, 3, has_up, lambda f: top_in[f], corner_in[0], corner_in[1])
    assemble(11, 3, has_down, lambda f: bottom_in[f], corner_in[2], corner_in[3])
    image_row = jnp.where(row < 3, row, row + 6) + (8 * r - 2)
    in_image = in_cols & (image_row >= 0) & (image_row < 64)

    @pl.loop(0, 10)
    def _(f):
        value, slope = silu_parts(conv_rows(cells, f, (0, 9), 3, taps1))
        value = (jnp.where(in_image, value, 0.0) * in_frames(f)).astype(half)
        hidden_out[f, 0:3] = value[0:3]
        hidden_out[f, 9:12] = value[3:6]
        slope1_out[f, 0:16] = slope[2, 8:24]
        slope1_out[f, 112:128] = slope[3, 8:24]

    stores = [
        pltpu.make_async_copy(cells.at[pl.ds(2, 8), pl.ds(2, 10)], cells_hbm, store_sem.at[0]),
        pltpu.make_async_copy(hidden_out.at[pl.ds(1, 8), pl.ds(1, 10)], hidden_hbm, store_sem.at[1]),
        pltpu.make_async_copy(slope1_out.at[pl.ds(2, 6)], slope1_hbm, store_sem.at[2]),
        pltpu.make_async_copy(slope2_out, slope2_hbm, store_sem.at[3]),
    ]
    start(stores[:3])

    def target(step, slot):
        frame = 6 * g + slot
        return (frame // 8, r + step, lax.rem(frame, 8))

    def outgoing(step, slot):
        return pltpu.make_async_remote_copy(
            src_ref=colours.at[slot],
            dst_ref=near_out.at[1 - step, c],
            send_sem=send_sem.at[step + 1, slot],
            recv_sem=recv_sem.at[1 - step, c],
            device_id=target(step, slot),
            device_id_type=MESH,
        )

    def kept(slot):
        return pltpu.make_async_copy(colours.at[slot], near_out.at[1, c], own_sem)

    def start_colour(slot, step):
        away = jnp.logical_not(same_place(target(step, slot), me))
        pl.when(away)(lambda: outgoing(step, slot).start())
        if step == 0:
            pl.when(jnp.logical_not(away))(lambda: kept(slot).start())

    def finish(slot, step):
        away = jnp.logical_not(same_place(target(step, slot), me))
        pl.when(away)(lambda: outgoing(step, slot).wait_send())
        if step == 0:
            pl.when(jnp.logical_not(away))(lambda: kept(slot).wait())

    def arrive(step, column, source):
        pltpu.make_async_remote_copy(
            src_ref=colours.at[0],
            dst_ref=near_out.at[step + 1, column],
            send_sem=send_sem.at[0, 0],
            recv_sem=recv_sem.at[step + 1, column],
            device_id=source,
            device_id_type=MESH,
        ).wait_recv()

    @pl.loop(0, 6)
    def _(slot):
        value, slope = silu_parts(conv_rows(hidden_out, slot + 1, (0,), 10, taps2))
        slope2_out[slot + 1] = slope
        own = value[1:9, 8:24].reshape(128, 128).astype(jnp.bfloat16)
        colour = lax.dot_general(
            rgb16[...].astype(half), own, (((1,), (1,)), ((), ())), preferred_element_type=jnp.float32
        )
        colours[slot] = colour.astype(jnp.bfloat16)
        on_rows(r, functools.partial(start_colour, slot))

    @pl.loop(0, 2)
    def _(end):
        slope2_out[7 * end] = silu_parts(conv_rows(hidden_out, 7 * end, (0,), 10, taps2))[1]

    stores[3].start()
    sources(arrive)

    @pl.loop(0, 6)
    def _(slot):
        on_rows(r, functools.partial(finish, slot))

    for store in stores:
        store.wait()

    sent(sideways)
    pl.when(has_up)(lambda: sent(upward))
    pl.when(has_down)(lambda: sent(downward))


def columns_in_lanes(source, frame0, row0, out_ref):
    @pl.loop(0, 8)
    def _(f):
        value = source[f + frame0, pl.ds(row0, 10)].reshape(320, 128).astype(jnp.float32)
        parts = [pltpu.roll(value, 1, 0), value, pltpu.roll(value, 319, 0)]
        for k, part in enumerate(parts):
            own = part.reshape(10, 32, 128)[:, 8:24]
            out_ref[f, :, :, 128 * k : 128 * (k + 1)] = own.astype(jnp.bfloat16)


def weight_terms(columns, delta, terms):
    @pl.loop(0, 9)
    def _(q):
        cells = columns[pl.ds(q // 3, 6), pl.ds(lax.rem(q, 3), 8)].reshape(768, 384)
        terms[pl.ds(pl.multiple_of(384 * q, 384), 384)] = transposed_dot(cells, delta[...])


def by_chip(terms, out_ref, which):
    @pl.loop(0, 8)
    def _(z):
        for chip in range(16):
            start = 432 * z + 27 * chip
            out_ref[which, 0, z, chip // 4, chip % 4] = terms[pl.ds(start, 16)].astype(jnp.bfloat16)
            out_ref[which, 1, z, chip // 4, chip % 4] = terms[pl.ds(start + 13, 16)].astype(jnp.bfloat16)


def backward_kernel(
    pixel_ref, cells_hbm, hidden_hbm, slope1_hbm, slope2_hbm, second_hbm, rgb_ref, out_ref,
    cells_ref, hidden_ref, slope1_ref, slope2_ref, second_ref, rgb16, load_sem,
    taps, columns, field, delta, terms,
    sending, core_in, held, x_in, y_in, mid_x, mid_y, yy_in, xx_in, last, z_in, send_sem, recv_sem,
):
    g, r, c = position()
    loads = [
        pltpu.make_async_copy(src, dst, load_sem.at[k])
        for k, (src, dst) in enumerate(
            (
                (second_hbm, second_ref), (slope2_hbm, slope2_ref), (hidden_hbm, hidden_ref),
                (slope1_hbm, slope1_ref), (cells_hbm, cells_ref),
            )
        )
    ]
    for load in loads:
        load.start()
    zh, x, y, core = r // 4, lax.rem(r, 4), c // 2, lax.rem(c, 2)
    z = g * 2 + zh
    other = 1 - core

    def at_x(step):
        return (g, zh * 4 + lax.rem(x + step, 4), c)

    def at_y(step):
        return (g, r, lax.rem(y + step, 4) * 2 + core)

    def at_z(step):
        to = lax.rem(z + step, 8)
        return (to // 2, lax.rem(to, 2) * 4 + x, c)

    partner = (g, r, y * 2 + other)
    barrier = pltpu.get_barrier_semaphore()
    everyone = [partner] + [at_x(s) for s in (1, 2, 3)] + [at_y(s) for s in (1, 2, 3)]
    everyone += [at_z(s) for s in range(1, 8)]
    for peer in everyone:
        pl.semaphore_signal(barrier, inc=1, device_id=peer, device_id_type=MESH)

    def send(src, dst, which, slot, peer):
        copy = pltpu.make_async_remote_copy(
            src_ref=src,
            dst_ref=dst,
            send_sem=send_sem.at[which, slot],
            recv_sem=recv_sem.at[which, slot],
            device_id=peer,
            device_id_type=MESH,
        )
        copy.start()
        return copy

    f32, half = jnp.float32, jnp.bfloat16

    def summed(own, received):
        total = own.astype(f32)
        for k in range(3):
            total += received[k].astype(f32)
        return total.astype(half)

    def to_partner(which):
        return send(sending.at[which, other], core_in.at[which], which, 0, partner)

    def first_step(which, copy):
        copy.wait()

        @pl.loop(0, 8)
        def _(k):
            pair = sending[which, core, k].astype(f32) + core_in[which, k].astype(f32)
            held[which, k] = pair.astype(half)

        low, high = held.at[which, pl.ds(0, 4)], held.at[which, pl.ds(4, 4)]
        copies = []
        for s in (1, 2, 3):
            copies.append(send(low.at[:, lax.rem(x + s, 4)], x_in.at[which, s - 1], which, s, at_x(s)))
            copies.append(send(high.at[:, :, lax.rem(y + s, 4)], y_in.at[which, s - 1], which, 3 + s, at_y(s)))
        return copies

    def second_step(which, copies):
        for copy in copies:
            copy.wait()
        mid_x[which] = summed(held[which, 0:4, x], [x_in[which, k] for k in range(3)])
        mid_y[which] = summed(held[which, 4:8, :, y], [y_in[which, k] for k in range(3)])
        after = []
        for s in (1, 2, 3):
            after.append(send(mid_x.at[which, :, lax.rem(y + s, 4)], yy_in.at[which, s - 1], which, 6 + s, at_y(s)))
            after.append(send(mid_y.at[which, :, lax.rem(x + s, 4)], xx_in.at[which, s - 1], which, 9 + s, at_x(s)))
        return after

    def third_step(which, copies):
        for copy in copies:
            copy.wait()
        last[which, 0:4] = summed(mid_x[which, :, y], [yy_in[which, k] for k in range(3)])
        last[which, 4:8] = summed(mid_y[which, :, x], [xx_in[which, k] for k in range(3)])
        return [
            send(last.at[which, lax.rem(z + s, 8)], z_in.at[which, s - 1], which, 12 + s, at_z(s))
            for s in range(1, 8)
        ]

    def result(which, copies):
        for copy in copies:
            copy.wait()
        total = last[which, z].astype(f32)
        for k in range(7):
            total += z_in[which, k].astype(f32)
        out_ref[which] = total

    rgb16[...] = jnp.zeros((16, 128), f32)
    rgb16[0:3] = rgb_ref[...].astype(f32)
    loads[0].wait()
    turned_taps(second_ref, taps)
    loads[1].wait()

    lane = lax.broadcasted_iota(jnp.int32, (8, 128), 1)
    col = lax.rem(lane, 32) + (16 * c - 8)
    in_cols = (lane < 96) & (col >= 0) & (col < 128)

    @pl.loop(0, 8)
    def _(f):
        frame = 6 * g - 1 + f
        known = in_cols & (frame >= 0) & (frame < 24)
        parts = []
        for part in range(3):
            seen = known & (r + part - 1 >= 0) & (r + part - 1 < 8)
            parts.append(jnp.where(seen, pixel_ref[f, part].astype(f32)[0:8], 0.0))
        turned = jnp.concatenate(parts, axis=0).T
        for i in range(10):
            hidden_grad = turned[0:32, i + 7 : i + 8] * rgb16[0:1]
            for k in (1, 2):
                hidden_grad += turned[32 * k : 32 * (k + 1), i + 7 : i + 8] * rgb16[k : k + 1]
            field[f, i] = (hidden_grad * slope2_ref[f, i]).astype(half)

    @pl.loop(0, 6)
    def _(f):
        own = field[f + 1, 1:9].astype(f32)[:, 8:24].reshape(128, 128).astype(half)
        delta[pl.ds(pl.multiple_of(128 * f, 128), 128)] = own

    loads[2].wait()
    columns_in_lanes(hidden_ref, 0, 0, columns)
    terms[pl.ds(3456, 8)] = jnp.zeros((8, 128), f32)
    weight_terms(columns, delta, terms)
    by_chip(terms, sending, 1)
    pl.semaphore_wait(barrier, len(everyone))
    swap_second = to_partner(1)
    loads[3].wait()

    @pl.loop(0, 6)
    def _(f):
        back = conv_rows(field, f, (0,), 8, taps)[:, 8:24].reshape(128, 128)
        value = (back * slope1_ref[f]).astype(half)
        delta[pl.ds(pl.multiple_of(128 * f, 128), 128)] = value

    moves_second = first_step(1, swap_second)
    loads[4].wait()
    columns_in_lanes(cells_ref, 0, 0, columns)
    weight_terms(columns, delta, terms)
    moves_second = second_step(1, moves_second)
    by_chip(terms, sending, 0)
    swap_first = to_partner(0)
    moves_second = third_step(1, moves_second)
    moves_first = first_step(0, swap_first)
    result(1, moves_second)
    moves_first = second_step(0, moves_first)
    moves_first = third_step(0, moves_first)
    result(0, moves_first)


def f32_shape(*shape):
    return jax.ShapeDtypeStruct(shape, jnp.float32)


def places(text):
    return [pl.BlockSpec(memory_space=pltpu.VMEM if letter == "v" else pltpu.HBM) for letter in text]


def talking_call(kernel, ident, mebibytes, in_places, out_places, outs, scratch, *operands):
    return pl.pallas_call(
        kernel,
        out_shape=tuple(outs),
        in_specs=places(in_places),
        out_specs=tuple(places(out_places)),
        scratch_shapes=scratch,
        compiler_params=pltpu.CompilerParams(
            collective_id=ident, has_side_effects=True, vmem_limit_bytes=mebibytes * 2**20
        ),
    )(*operands)


def local(dec_input, target, conv_first, conv_second, rgb_weight, vgg_first, vgg_second, vgg_third):
    g, r, c = position()
    channels = dec_input.shape[-1]
    half, f32, dma, vmem = jnp.bfloat16, jnp.float32, pltpu.SemaphoreType.DMA, pltpu.VMEM
    cells, hidden, slope1, slope2, colour_near, guide_near = talking_call(
        forward_kernel,
        3,
        58,
        "hvhhv",
        "hhhhvv",
        (
            b16(8, 10, 32, 128), b16(8, 10, 32, 128), f32_shape(6, 128, 128), f32_shape(8, 10, 32, 128),
            b16(3, 8, 16, 128), b16(3, 32, 128),
        ),
        [
            vmem((24, 8, 16, 128), half), vmem((3456, 128), half), vmem((3456, 128), half), vmem((16, 128), f32),
            vmem((12, 14, 32, 128), half), vmem((10, 12, 32, 128), half),
            vmem((10, 128, 128), f32), vmem((8, 10, 32, 128), f32), dma((3,)), dma((4,)),
            vmem((12, 8, 16, 128), half), vmem((8, 48, 128), half), vmem((8, 48, 128), half),
            vmem((2, 12, 3, 16, 128), half), vmem((2, 3, 48, 128), half), vmem((2, 3, 48, 128), half),
            vmem((2, 32, 128), half),
            vmem((12, 3, 16, 128), half), vmem((12, 3, 16, 128), half),
            vmem((8, 48, 128), half), vmem((8, 48, 128), half), vmem((4, 3, 48, 128), half),
            dma((10,)), dma((10,)),
            vmem((1152, 384), half), vmem((1152, 384), half), vmem((6, 16, 128), half),
            dma((3, 6)), dma((3, 8)), dma(()),
        ],
        dec_input.reshape(24, 8, 16, channels), target, conv_first, conv_second, rgb_weight,
    )
    pixels = perceptual_strip(
        colour_near, guide_near, first_weights(vgg_first), (vgg_second.T, vgg_third)
    )
    sums = talking_call(
        backward_kernel,
        1,
        58,
        "vhhhhhv",
        "v",
        (f32_shape(2, 16, 128),),
        [
            vmem((8, 10, 32, 128), half), vmem((8, 10, 32, 128), half), vmem((6, 128, 128), f32),
            vmem((8, 10, 32, 128), f32), vmem((3456, 128), half), vmem((16, 128), f32), dma((5,)),
            pltpu.VMEM((1152, 384), half),
            pltpu.VMEM((8, 10, 16, 384), half),
            pltpu.VMEM((8, 10, 32, 128), half),
            pltpu.VMEM((768, 128), half),
            pltpu.VMEM((3464, 128), jnp.float32),
            pltpu.VMEM((2, 2, 8, 4, 4, 16, 128), half),
            pltpu.VMEM((2, 8, 4, 4, 16, 128), half),
            pltpu.VMEM((2, 8, 4, 4, 16, 128), half),
            pltpu.VMEM((2, 3, 4, 4, 16, 128), half),
            pltpu.VMEM((2, 3, 4, 4, 16, 128), half),
            pltpu.VMEM((2, 4, 4, 16, 128), half),
            pltpu.VMEM((2, 4, 4, 16, 128), half),
            pltpu.VMEM((2, 3, 4, 16, 128), half),
            pltpu.VMEM((2, 3, 4, 16, 128), half),
            pltpu.VMEM((2, 8, 16, 128), half),
            pltpu.VMEM((2, 7, 16, 128), half),
            dma((2, 20)),
            dma((2, 20)),
        ],
        pixels, cells, hidden, slope1, slope2, conv_second, rgb_weight,
    )[0]
    flat = sums[:, :14].reshape(2, 14 * 128)
    own_sums = lax.dynamic_slice_in_dim(flat, lax.rem(c, 2) * 64, 1728, axis=1)
    return own_sums[0], own_sums[1]


def solution(mesh):
    in_specs = (
        P(None, None, "row", "col", None),
        P(None, None, "col", "row", None),
        P(),
        P(),
        P(),
        P(),
        P(),
        P(),
    )
    out_specs = (P(("grp", "row", "col")), P(("grp", "row", "col")))
    return jax.shard_map(local, mesh=mesh, in_specs=in_specs, out_specs=out_specs, check_vma=False)
```

```python
import functools

import jax
import jax.numpy as jnp
from jax import lax
from jax.experimental import pallas as pl
from jax.experimental.pallas import tpu as pltpu
from jax.sharding import PartitionSpec as P

MESH = pl.DeviceIdType.MESH

gelu_scale = 0.7978845608028654
gelu_cubic = 0.044715


def position():
    return lax.axis_index("grp"), lax.axis_index("row"), lax.axis_index("col")


def same_place(one, other):
    return (one[0] == other[0]) & (one[1] == other[1]) & (one[2] == other[2])


def row_count(r):
    return 1 + jnp.where(r > 0, 1, 0) + jnp.where(r < 7, 1, 0)


def in_vmem(count):
    return [pl.BlockSpec(memory_space=pltpu.VMEM)] * count


def b16(*shape):
    return jax.ShapeDtypeStruct(shape, jnp.bfloat16)


def transposed_dot(one, other):
    return lax.dot_general(one, other, (((0,), (0,)), ((), ())), preferred_element_type=jnp.float32)


def side_by_side(value):
    cols = value.shape[0]
    at = lax.broadcasted_iota(jnp.int32, value.shape, 0)
    before = jnp.where(at == 0, 0.0, pltpu.roll(value, 1, 0))
    after = jnp.where(at == cols - 1, 0.0, pltpu.roll(value, cols - 1, 0))
    return jnp.concatenate([before, value, after], axis=1).astype(jnp.bfloat16)


def three_rows(ref, row, count):
    parts = [ref[pl.ds(row + step, count)].reshape(-1, ref.shape[-1]) for step in range(3)]
    return jnp.concatenate(parts, axis=1)


def dot32(one, other):
    return jnp.dot(one, other, preferred_element_type=jnp.float32)


def gelu_both(preact, slope_too):
    square = preact * preact
    inner_tanh = jnp.tanh(gelu_scale * preact * (1.0 + gelu_cubic * square))
    half = 0.5 * (1.0 + inner_tanh)
    value = preact * half
    if not slope_too:
        return value, None
    bend = (0.5 * gelu_scale) * (1.0 + 3.0 * gelu_cubic * square)
    return value, half + preact * (1.0 - inner_tanh * inner_tanh) * bend


def perceptual_kernel(
    near_ref, guide_ref, w1_ref, vgg_second_ref, vgg_third_ref, w1_back_ref, out_ref,
    planes_ref, guides,
    taps, act1, slope1, pooled, delta3, diff2, slope2, delta2, delta1, tmp, pixels, strip,
    w2_ref, w3_ref, w3_back_ref, w2_back_ref, send_sem, recv_sem, own_sem,
):
    g, r, c = position()
    me = (g, r, c)
    barrier = pltpu.get_barrier_semaphore()
    perceives = g < 3
    own_frame = 8 * g + c
    home = own_frame // 6
    place = lax.rem(own_frame, 6)
    ahead = perceives & (place == 0) & (home > 0)
    behind = perceives & (place == 5) & (home < 3)

    def sources(do):
        for slot in range(8):
            source_frame = 6 * g - 1 + slot

            def each(step, slot=slot, source_frame=source_frame):
                source = (source_frame // 8, r + step, lax.rem(source_frame, 8))
                pl.when(jnp.logical_not(same_place(source, me)))(
                    functools.partial(do, step, slot, source)
                )

            pl.when((source_frame >= 0) & (source_frame < 24))(functools.partial(on_rows, r, each))

    def greet(step, slot, source):
        pl.semaphore_signal(barrier, inc=1, device_id=source, device_id_type=MESH)

    sources(greet)
    lay_out_perceptual(vgg_second_ref, vgg_third_ref, w2_ref, w3_ref, w3_back_ref, w2_back_ref)
    row0 = 8 * r - 8
    kind = lax.broadcasted_iota(jnp.int32, (8, 128), 0)
    block = lax.broadcasted_iota(jnp.int32, (8, 128), 1) // 16
    for part in range(3):
        guides[...] = guide_ref[part].astype(jnp.float32)
        tiles = [near_ref[part, column].astype(jnp.float32)[0:8] for column in range(8)]
        here = (kind < 3) & (row0 + 8 * part >= 0) & (row0 + 8 * part < 64)
        seen = (row0 + 8 * part >= 0) & (row0 + 8 * part < 64)
        for i in range(8):
            image = jnp.zeros((8, 128), jnp.float32)
            for column in range(8):
                turned = pltpu.roll(tiles[column], (16 * column - 16 * i) % 128, 1)
                image = jnp.where(block == column, turned, image)
            planes_ref[8 * part + i] = jnp.where(here, image, 0.0)
            planes_ref[8 * part + i, 3:6] = jnp.where(seen, guides[pl.ds(i, 3, 8)], 0.0)
    lane = lax.broadcasted_iota(jnp.int32, (192, 128), 1)
    planes = planes_ref[...].reshape(192, 128)
    before = jnp.where(lane == 0, 0.0, pltpu.roll(planes, 1, 1))
    after = jnp.where(lane == 127, 0.0, pltpu.roll(planes, 127, 1))
    taps[:, 0:8] = before.reshape(24, 8, 128)
    taps[:, 8:16] = planes.reshape(24, 8, 128)
    taps[:, 16:24] = after.reshape(24, 8, 128)

    def shown(row):
        return (row0 + row >= 0) & (row0 + row < 64)

    def kept(row, value):
        return jnp.where(shown(row), value, 0.0)

    def first_rows(low, high, slope_too):
        @pl.loop(low, high)
        def _(i):
            cells = taps[pl.ds(i, 3)].reshape(72, 128).astype(jnp.bfloat16)
            value, slope = gelu_both(transposed_dot(cells, w1_ref[...]), slope_too)
            act1[i] = side_by_side(kept(i + 1, value))
            if slope_too:
                slope1[i - 6] = slope

    first_rows(0, 6, False)
    first_rows(6, 16, True)
    first_rows(16, 22, False)

    def second_rows(low, high, slope_too):
        @pl.loop(low, high)
        def _(p):
            plane = dot32(three_rows(act1, 2 * p, 2), w2_ref[...])
            value, slope = gelu_both(plane, slope_too)
            value = kept(2 * p + 2, value)
            if slope_too:
                difference = 0.25 * (value - pltpu.roll(value, 64, 1))
                diff2[pl.ds(2 * p - 4, 2)] = difference.reshape(2, 128, 128)
                slope2[pl.ds(2 * p - 4, 2)] = slope.reshape(2, 128, 128)
            tmp[...] = value[:128] + value[128:]
            mean = 0.25 * (tmp[pl.ds(0, 64, 2)] + tmp[pl.ds(1, 64, 2)])
            pooled[p] = side_by_side(mean)

    second_rows(0, 2, False)
    second_rows(2, 8, True)
    second_rows(8, 10, False)

    @pl.loop(0, 4)
    def _(half):
        j = 2 * half
        plane = dot32(three_rows(pooled, j, 2), w3_ref[...])
        value, slope = gelu_both(plane[:, :128], True)
        guide, _ = gelu_both(plane[:, 128:], False)
        delta = 0.5 * (value - guide) * slope
        delta3[j] = side_by_side(kept(2 * j + 4, delta[:64]))
        delta3[j + 1] = side_by_side(kept(2 * j + 6, delta[64:]))

    @pl.loop(0, 6)
    def _(m):
        grad = 0.25 * dot32(three_rows(delta3, m, 1), w3_back_ref[...])
        tmp[pl.ds(0, 64, 2)] = grad
        tmp[pl.ds(1, 64, 2)] = grad
        spread = tmp[...]
        for k in range(2):
            delta = (spread + diff2[2 * m + k]) * slope2[2 * m + k]
            delta2[2 * m + k] = side_by_side(kept(2 * m + 6, delta))

    @pl.loop(0, 5)
    def _(half):
        n = 2 * half
        grad = dot32(three_rows(delta2, n, 2), w2_back_ref[...])
        for k in range(2):
            delta = grad[128 * k : 128 * (k + 1)] * slope1[n + k]
            delta1[n + k] = side_by_side(kept(n + k + 7, delta))

    @pl.loop(0, 8)
    def _(q):
        grad = lax.dot_general(
            w1_back_ref[...],
            three_rows(delta1, q, 1),
            (((1,), (1,)), ((), ())),
            preferred_element_type=jnp.float32,
        )
        own = planes_ref[q + 8]
        direct = (1.0 / 6.0) * (own - pltpu.roll(own, 5, 0))
        pixels[pl.ds(pl.multiple_of(q * 8, 8), 8)] = grad + direct

    colour_rows = [pixels[pl.ds(k, 8, 8)] for k in range(3)]
    third = lax.broadcasted_iota(jnp.int32, (8, 128), 1) // 32
    for column in range(8):
        turned = [pltpu.roll(v, (32 * k + 8 - 16 * column) % 128, 1) for k, v in enumerate(colour_rows)]
        part = jnp.where(third == 0, turned[0], jnp.where(third == 1, turned[1], turned[2]))
        strip[column] = jnp.concatenate([part, jnp.zeros((8, 128), jnp.float32)], axis=0).astype(jnp.bfloat16)

    groups = jnp.where(perceives, 1, 0) + jnp.where(ahead, 1, 0) + jnp.where(behind, 1, 0)
    to_itself = perceives & (home == g) | ahead & (home == g + 1) | behind & (home == g - 1)
    awaited = 8 * row_count(r) * groups - jnp.where(to_itself, 1, 0)
    pl.when(perceives)(lambda: pl.semaphore_wait(barrier, awaited))

    def targets(do):
        for kind, (group, needed) in enumerate(((home, perceives), (home - 1, ahead), (home + 1, behind))):

            def each(step, kind=kind, group=group):
                for column in range(8):
                    peer = (group, r + step, column)
                    do(kind, step, column, peer, jnp.logical_not(same_place(peer, me)))

            pl.when(needed)(functools.partial(on_rows, r, each))

    def outgoing(kind, step, column, peer):
        place_there = own_frame - 6 * peer[0] + 1
        return pltpu.make_async_remote_copy(
            src_ref=strip.at[column],
            dst_ref=out_ref.at[place_there, 1 - step],
            send_sem=send_sem.at[kind, step + 1, column],
            recv_sem=recv_sem.at[place_there, 1 - step],
            device_id=peer,
            device_id_type=MESH,
        )

    def kept():
        return pltpu.make_async_copy(strip.at[c], out_ref.at[own_frame - 6 * g + 1, 1], own_sem)

    def start(kind, step, column, peer, away):
        pl.when(away)(lambda: outgoing(kind, step, column, peer).start())
        if step == 0:
            pl.when(jnp.logical_not(away))(lambda: kept().start())

    def finish(kind, step, column, peer, away):
        pl.when(away)(lambda: outgoing(kind, step, column, peer).wait_send())
        if step == 0:
            pl.when(jnp.logical_not(away))(lambda: kept().wait())

    def arrive(step, slot, source):
        pltpu.make_async_remote_copy(
            src_ref=strip.at[0],
            dst_ref=out_ref.at[slot, step + 1],
            send_sem=send_sem.at[0, 0, 0],
            recv_sem=recv_sem.at[slot, step + 1],
            device_id=source,
            device_id_type=MESH,
        ).wait_recv()

    targets(start)
    sources(arrive)
    targets(finish)


def two_blocks(weight):
    _, i, o = weight.shape
    return jnp.pad(weight, ((0, 0), (0, i), (0, o))) + jnp.pad(weight, ((0, 0), (i, 0), (o, 0)))


def first_weights(vgg_first):
    first = vgg_first.reshape(9, 3, 64)
    w1 = jnp.pad(two_blocks(first), ((0, 0), (0, 2), (0, 0))).reshape(72, 128)
    w1_back = jnp.pad(jnp.transpose(first[::-1], (1, 0, 2)), ((0, 5), (0, 0), (0, 64))).reshape(8, 1152)
    return w1, w1_back


def perceptual_strip(near, guides, first, others):
    f32, half = jnp.float32, jnp.bfloat16
    return pl.pallas_call(
        perceptual_kernel,
        out_shape=b16(8, 3, 16, 128),
        in_specs=in_vmem(6),
        out_specs=in_vmem(1)[0],
        scratch_shapes=[
            pltpu.VMEM((24, 8, 128), f32),
            pltpu.VMEM((32, 128), f32),
            pltpu.VMEM((24, 24, 128), f32),
            pltpu.VMEM((22, 128, 384), half),
            pltpu.VMEM((10, 128, 128), f32),
            pltpu.VMEM((10, 64, 384), half),
            pltpu.VMEM((8, 64, 384), half),
            pltpu.VMEM((12, 128, 128), f32),
            pltpu.VMEM((12, 128, 128), f32),
            pltpu.VMEM((12, 128, 384), half),
            pltpu.VMEM((10, 128, 384), half),
            pltpu.VMEM((128, 128), f32),
            pltpu.VMEM((64, 128), f32),
            pltpu.VMEM((8, 16, 128), half),
            pltpu.VMEM((1152, 128), half),
            pltpu.VMEM((1152, 256), half),
            pltpu.VMEM((1152, 128), half),
            pltpu.VMEM((1152, 128), half),
            pltpu.SemaphoreType.DMA((3, 3, 8)),
            pltpu.SemaphoreType.DMA((8, 3)),
            pltpu.SemaphoreType.DMA(()),
        ],
        compiler_params=pltpu.CompilerParams(
            collective_id=4, has_side_effects=True, vmem_limit_bytes=24 * 2**20
        ),
    )(near, guides, first[0], *others, first[1])


def taps_in_lanes(weight_ref, out_ref):
    for q in range(9):
        for k in range(3):
            tap = 3 * q + k
            out_ref[128 * q : 128 * (q + 1), 128 * k : 128 * (k + 1)] = weight_ref[
                128 * tap : 128 * (tap + 1), :
            ]


def turned_taps(weight_ref, out_ref):
    for q in range(9):
        for k in range(3):
            tap = 26 - 3 * q - k
            block = weight_ref[128 * tap : 128 * (tap + 1), :].astype(jnp.float32)
            out_ref[128 * q : 128 * (q + 1), 128 * k : 128 * (k + 1)] = block.T.astype(jnp.bfloat16)


def conv_rows(source, frame, starts, count, taps_ref):
    size = len(starts) * count * 32

    def near(dt, dr):
        rows = [source[frame + dt, pl.ds(start + dr, count)].reshape(count * 32, 128) for start in starts]
        return rows[0] if len(rows) == 1 else jnp.concatenate(rows, axis=0)

    parts = [near(dt, dr) for dt in range(3) for dr in range(3)]
    sums = dot32(jnp.concatenate(parts, axis=1), taps_ref[...])
    total = pltpu.roll(sums[:, :128], 1, 0) + sums[:, 128:256]
    total += pltpu.roll(sums[:, 256:], size - 1, 0)
    return total.reshape(len(starts) * count, 32, 128)


def silu_parts(preact):
    gate = 1.0 / (1.0 + jnp.exp(-preact))
    return preact * gate, gate * (1.0 + preact * (1.0 - gate))


def on_rows(r, do):
    for step in (-1, 0, 1):
        pl.when((r + step >= 0) & (r + step < 8))(functools.partial(do, step))


def lay_out_perceptual(second_ref, third_ref, w2_out, w3_out, w3_back_out, w2_back_out):
    f32, half = jnp.float32, jnp.bfloat16
    for t in range(9):
        turned_block = second_ref[:, 64 * t : 64 * (t + 1)].astype(f32)
        block = turned_block.T
        wide = third_ref[64 * t : 64 * (t + 1), :].astype(f32)
        none, low, high = jnp.zeros((64, 64), f32), 128 * t, 128 * (8 - t)
        w2_out[low : low + 64] = jnp.concatenate([block, none], axis=1).astype(half)
        w2_out[low + 64 : low + 128] = jnp.concatenate([none, block], axis=1).astype(half)
        w3_out[low : low + 64, :128] = wide.astype(half)
        w3_out[low : low + 64, 128:] = jnp.zeros((64, 128), half)
        w3_out[low + 64 : low + 128, :128] = jnp.zeros((64, 128), half)
        w3_out[low + 64 : low + 128, 128:] = wide.astype(half)
        w2_back_out[high : high + 64] = jnp.concatenate([turned_block, none], axis=1).astype(half)
        w2_back_out[high + 64 : high + 128] = jnp.zeros((64, 128), half)
        turned = jnp.concatenate([wide.T, jnp.zeros((128, 64), f32)], axis=1)
        w3_back_out[high : high + 128] = turned.astype(half)


def forward_kernel(
    video_hbm, target_ref, first_hbm, second_hbm, rgb_ref,
    cells_hbm, hidden_hbm, slope1_hbm, slope2_hbm, near_out, guide_out,
    video, first_ref, second_ref, rgb16, cells, hidden_out, slope1_out, slope2_out, load_sem, store_sem,
    tile, left_send, right_send, left_in, right_in, rows_in, to_west, to_east, from_east, from_west,
    halo_send, halo_recv, edge_send, edge_recv,
    taps1, taps2, colours, send_sem, recv_sem, own_sem,
):
    loads = [
        pltpu.make_async_copy(video_hbm, video, load_sem.at[0]),
        pltpu.make_async_copy(first_hbm, first_ref, load_sem.at[1]),
        pltpu.make_async_copy(second_hbm, second_ref, load_sem.at[2]),
    ]
    for load in loads:
        load.start()
    g, r, c = position()
    me = (g, r, c)
    f32, half = jnp.float32, jnp.bfloat16
    barrier = pltpu.get_barrier_semaphore()
    perceives = g < 3
    source_group = (8 * g + c) // 6
    west, east = lax.rem(c + 7, 8), lax.rem(c + 1, 8)
    has_up, has_down = r > 0, r < 7
    has_prev, has_next = g > 0, g < 3

    def sources(do):
        def each(step):
            for column in range(8):
                source = (source_group, r + step, column)
                pl.when(jnp.logical_not(same_place(source, me)))(
                    functools.partial(do, step, column, source)
                )

        pl.when(perceives)(lambda: on_rows(r, each))

    def signal(peer):
        pl.semaphore_signal(barrier, inc=1, device_id=peer, device_id_type=MESH)

    signal((g, r, west))
    signal((g, r, east))

    pl.when(has_up)(lambda: signal((g, r - 1, c)))
    pl.when(has_down)(lambda: signal((g, r + 1, c)))

    @pl.when(has_prev)
    def _():
        for column in (west, c, east):
            signal((g - 1, r, column))

    @pl.when(has_next)
    def _():
        for column in (west, c, east):
            signal((g + 1, r, column))

    sources(lambda step, column, source: signal(source))

    block = jnp.minimum(g, 2)
    guide = [target_ref[k, block, 0].astype(f32) for k in range(3)] + [jnp.zeros((8, 128), f32)]
    guide_out[1] = jnp.concatenate(guide, axis=0).astype(half)
    rgb16[...] = jnp.zeros((16, 128), f32)
    rgb16[0:3] = rgb_ref[...].astype(f32)
    loads[0].wait()

    for f in range(12):
        frame = 6 * g - 3 + f
        value = video[jnp.minimum(jnp.maximum(frame, 0), 23)]
        tile[f] = jnp.where((frame >= 0) & (frame < 24), value, jnp.zeros_like(value))

    to_itself = jnp.where(perceives & (2 * g + c < 6), 1, 0)
    groups_near = jnp.where(has_prev, 1, 0) + jnp.where(has_next, 1, 0)
    pl.semaphore_wait(barrier, 7 * row_count(r) + 1 + 3 * groups_near - to_itself)

    def remote(src, dst, slot, peer):
        return pltpu.make_async_remote_copy(
            src_ref=src,
            dst_ref=dst,
            send_sem=halo_send.at[slot],
            recv_sem=halo_recv.at[slot],
            device_id=peer,
            device_id_type=MESH,
        )

    sideways = [remote(left_send, right_in, 0, (g, r, west)), remote(right_send, left_in, 1, (g, r, east))]

    def to_row(row_index, rows, edge, guide_slot, first_slot):
        strip = tile.at[pl.ds(3, 6), pl.ds(rows, 3)]
        return [
            remote(strip, rows_in.at[edge, pl.ds(3, 6)], first_slot, (g, row_index, c)),
            remote(guide_out.at[1], guide_out.at[guide_slot], first_slot + 1, (g, row_index, c)),
        ]

    upward = to_row(r - 1, 0, 1, 2, 2)
    downward = to_row(r + 1, 5, 0, 0, 4)

    def across(edge):
        def copy(src, dst, slot, peer):
            return pltpu.make_async_remote_copy(
                src_ref=src,
                dst_ref=dst,
                send_sem=edge_send.at[edge, slot],
                recv_sem=edge_recv.at[edge, slot],
                device_id=peer,
                device_id_type=MESH,
            )

        mine, wests, easts = rows_in.at[edge], to_west.at[edge], to_east.at[edge]
        in_east, in_west, two = from_east.at[edge], from_west.at[edge], pl.ds(1, 2)
        level = [
            copy(wests, in_east.at[two], 0, (g, r, west)),
            copy(easts, in_west.at[two], 1, (g, r, east)),
        ]
        onward = [
            copy(mine.at[pl.ds(6, 3)], mine.at[pl.ds(0, 3)], 2, (g + 1, r, c)),
            copy(wests.at[1], in_east.at[0], 3, (g + 1, r, west)),
            copy(easts.at[1], in_west.at[0], 4, (g + 1, r, east)),
        ]
        back = [
            copy(mine.at[pl.ds(3, 3)], mine.at[pl.ds(9, 3)], 5, (g - 1, r, c)),
            copy(wests.at[0], in_east.at[3], 6, (g - 1, r, west)),
            copy(easts.at[0], in_west.at[3], 7, (g - 1, r, east)),
        ]
        return level, onward, back

    edges = [across(0), across(1)]

    def pass_on(edge):
        values = [rows_in[edge, 3 + f].astype(f32) for f in range(6)]
        for part in range(2):
            near = values[3 * part : 3 * part + 3]
            spare = jnp.zeros((3, 4, 128), f32)
            to_west[edge, part] = jnp.concatenate([v[:, 0:4] for v in near] + [spare], axis=1).astype(half)
            to_east[edge, part] = jnp.concatenate([v[:, 12:16] for v in near] + [spare], axis=1).astype(half)
        level, onward, back = edges[edge]
        start(level)
        pl.when(has_next)(lambda: start(onward))
        pl.when(has_prev)(lambda: start(back))

    def passed(edge, done):
        level, onward, back = edges[edge]
        done(level)
        if done is landed:
            pl.when(has_prev)(lambda: done(onward))
            pl.when(has_next)(lambda: done(back))
        else:
            pl.when(has_next)(lambda: done(onward))
            pl.when(has_prev)(lambda: done(back))

    def start(copies):
        for copy in copies:
            copy.start()

    def sent(copies):
        for copy in copies:
            copy.wait_send()

    def landed(copies):
        for copy in copies:
            copy.wait_recv()

    pl.when(has_up)(lambda: start(upward))
    pl.when(has_down)(lambda: start(downward))
    for line in range(8):
        near = [tile[f, line].astype(f32) for f in range(12)]
        left_send[line] = jnp.concatenate([v[0:4] for v in near], axis=0).astype(half)
        right_send[line] = jnp.concatenate([v[12:16] for v in near], axis=0).astype(half)
    start(sideways)

    loads[1].wait()
    taps_in_lanes(first_ref, taps1)
    loads[2].wait()
    taps_in_lanes(second_ref, taps2)

    def assemble(first_row, count, real, own, left, right, per):
        col = lax.broadcasted_iota(jnp.int32, (count, 32, 128), 1) + (16 * c - 8)
        shown = (col >= 0) & (col < 128) & real
        for part in range(12 // per):
            before, after = left(part).astype(f32), right(part).astype(f32)
            for k in range(per):
                f, eight = per * part + k, slice(8 * (k // 2), 8 * (k // 2) + 8)
                one = before[:, eight].reshape(8 * count, 128)
                two = after[:, eight].reshape(8 * count, 128)
                if k % 2 == 0:
                    one = pltpu.roll(one, 4, 0)
                else:
                    two = pltpu.roll(two, 8 * count - 4, 0)
                sides = [one.reshape(count, 8, 128), own(f).astype(f32), two.reshape(count, 8, 128)]
                frame = 6 * g - 3 + f
                here = shown & (frame >= 0) & (frame < 24)
                value = jnp.where(here, jnp.concatenate(sides, axis=1), 0.0)
                cells[f, first_row : first_row + count] = value.astype(half)

    row = lax.broadcasted_iota(jnp.int32, (6, 32, 128), 0)
    col = lax.broadcasted_iota(jnp.int32, (6, 32, 128), 1) + (16 * c - 8)
    in_cols = (col >= 0) & (col < 128)

    def in_frames(f):
        frame = 6 * g - 2 + f
        return jnp.where((frame >= 0) & (frame < 24), 1.0, 0.0)

    landed(sideways)
    assemble(
        3, 8, r >= 0, lambda f: tile[f],
        lambda part: left_in[:, 16 * part : 16 * (part + 1)],
        lambda part: right_in[:, 16 * part : 16 * (part + 1)],
        4,
    )

    def inner(f):
        value, slope = silu_parts(conv_rows(cells, f, (3,), 6, taps1))
        value = jnp.where(in_cols, value, 0.0) * in_frames(f)
        hidden_out[f, 3:9] = value.astype(half)
        slope1_out[f, 16:112] = slope[:, 8:24].reshape(96, 128)

    pl.loop(0, 3)(inner)

    @pl.when(has_up)
    def _():
        landed(downward)
        pass_on(0)

    @pl.when(has_down)
    def _():
        landed(upward)
        pass_on(1)

    pl.loop(3, 10)(inner)

    pl.when(has_up)(lambda: passed(0, landed))
    pl.when(has_down)(lambda: passed(1, landed))
    for edge, real in ((0, has_up), (1, has_down)):
        assemble(
            11 * edge, 3, real,
            lambda f, edge=edge: rows_in[edge, f],
            lambda part, edge=edge: from_west[edge, part],
            lambda part, edge=edge: from_east[edge, part],
            3,
        )
    image_row = jnp.where(row < 3, row, row + 6) + (8 * r - 2)
    in_image = in_cols & (image_row >= 0) & (image_row < 64)

    @pl.loop(0, 10)
    def _(f):
        value, slope = silu_parts(conv_rows(cells, f, (0, 9), 3, taps1))
        value = (jnp.where(in_image, value, 0.0) * in_frames(f)).astype(half)
        hidden_out[f, 0:3] = value[0:3]
        hidden_out[f, 9:12] = value[3:6]
        slope1_out[f, 0:16] = slope[2, 8:24]
        slope1_out[f, 112:128] = slope[3, 8:24]

    stores = [
        pltpu.make_async_copy(cells.at[pl.ds(2, 8), pl.ds(2, 10)], cells_hbm, store_sem.at[0]),
        pltpu.make_async_copy(hidden_out.at[pl.ds(1, 8), pl.ds(1, 10)], hidden_hbm, store_sem.at[1]),
        pltpu.make_async_copy(slope1_out.at[pl.ds(2, 6)], slope1_hbm, store_sem.at[2]),
        pltpu.make_async_copy(slope2_out, slope2_hbm, store_sem.at[3]),
    ]
    start(stores[:3])

    def target(step, slot):
        frame = 6 * g + slot
        return (frame // 8, r + step, lax.rem(frame, 8))

    def outgoing(step, slot):
        return pltpu.make_async_remote_copy(
            src_ref=colours.at[slot],
            dst_ref=near_out.at[1 - step, c],
            send_sem=send_sem.at[step + 1, slot],
            recv_sem=recv_sem.at[1 - step, c],
            device_id=target(step, slot),
            device_id_type=MESH,
        )

    def kept(slot):
        return pltpu.make_async_copy(colours.at[slot], near_out.at[1, c], own_sem)

    def start_colour(slot, step):
        away = jnp.logical_not(same_place(target(step, slot), me))
        pl.when(away)(lambda: outgoing(step, slot).start())
        if step == 0:
            pl.when(jnp.logical_not(away))(lambda: kept(slot).start())

    def finish(slot, step):
        away = jnp.logical_not(same_place(target(step, slot), me))
        pl.when(away)(lambda: outgoing(step, slot).wait_send())
        if step == 0:
            pl.when(jnp.logical_not(away))(lambda: kept(slot).wait())

    def arrive(step, column, source):
        pltpu.make_async_remote_copy(
            src_ref=colours.at[0],
            dst_ref=near_out.at[step + 1, column],
            send_sem=send_sem.at[0, 0],
            recv_sem=recv_sem.at[step + 1, column],
            device_id=source,
            device_id_type=MESH,
        ).wait_recv()

    @pl.loop(0, 6)
    def _(slot):
        value, slope = silu_parts(conv_rows(hidden_out, slot + 1, (0,), 10, taps2))
        slope2_out[slot + 1] = slope
        own = value[1:9, 8:24].reshape(128, 128).astype(jnp.bfloat16)
        colour = lax.dot_general(
            rgb16[...].astype(half), own, (((1,), (1,)), ((), ())), preferred_element_type=jnp.float32
        )
        colours[slot] = colour.astype(jnp.bfloat16)
        on_rows(r, functools.partial(start_colour, slot))

    @pl.loop(0, 2)
    def _(end):
        slope2_out[7 * end] = silu_parts(conv_rows(hidden_out, 7 * end, (0,), 10, taps2))[1]

    stores[3].start()
    sources(arrive)

    @pl.loop(0, 6)
    def _(slot):
        on_rows(r, functools.partial(finish, slot))

    for store in stores:
        store.wait()

    sent(sideways)
    pl.when(has_up)(lambda: sent(upward))
    pl.when(has_down)(lambda: sent(downward))
    pl.when(has_up)(lambda: passed(0, sent))
    pl.when(has_down)(lambda: passed(1, sent))


def columns_in_lanes(source, frame0, row0, out_ref):
    @pl.loop(0, 8)
    def _(f):
        value = source[f + frame0, pl.ds(row0, 10)].reshape(320, 128).astype(jnp.float32)
        parts = [pltpu.roll(value, 1, 0), value, pltpu.roll(value, 319, 0)]
        for k, part in enumerate(parts):
            own = part.reshape(10, 32, 128)[:, 8:24]
            out_ref[f, :, :, 128 * k : 128 * (k + 1)] = own.astype(jnp.bfloat16)


def weight_terms(columns, delta, terms):
    @pl.loop(0, 9)
    def _(q):
        cells = columns[pl.ds(q // 3, 6), pl.ds(lax.rem(q, 3), 8)].reshape(768, 384)
        terms[pl.ds(pl.multiple_of(384 * q, 384), 384)] = transposed_dot(cells, delta[...])


def by_chip(terms, out_ref, which):
    @pl.loop(0, 8)
    def _(z):
        for chip in range(16):
            start = 432 * z + 27 * chip
            out_ref[which, 0, z, chip // 4, chip % 4] = terms[pl.ds(start, 16)].astype(jnp.bfloat16)
            out_ref[which, 1, z, chip // 4, chip % 4] = terms[pl.ds(start + 13, 16)].astype(jnp.bfloat16)


def backward_kernel(
    pixel_ref, cells_hbm, hidden_hbm, slope1_hbm, slope2_hbm, second_hbm, rgb_ref, out_ref,
    cells_ref, hidden_ref, slope1_ref, slope2_ref, second_ref, rgb16, load_sem,
    taps, columns, field, delta, terms,
    sending, core_in, held, x_in, y_in, mid_x, mid_y, yy_in, xx_in, last, z_in, send_sem, recv_sem,
):
    g, r, c = position()
    loads = [
        pltpu.make_async_copy(src, dst, load_sem.at[k])
        for k, (src, dst) in enumerate(
            (
                (second_hbm, second_ref), (slope2_hbm, slope2_ref), (hidden_hbm, hidden_ref),
                (slope1_hbm, slope1_ref), (cells_hbm, cells_ref),
            )
        )
    ]
    for load in loads:
        load.start()
    zh, x, y, core = r // 4, lax.rem(r, 4), c // 2, lax.rem(c, 2)
    z = g * 2 + zh
    other = 1 - core

    def at_x(step):
        return (g, zh * 4 + lax.rem(x + step, 4), c)

    def at_y(step):
        return (g, r, lax.rem(y + step, 4) * 2 + core)

    def at_z(step):
        to = lax.rem(z + step, 8)
        return (to // 2, lax.rem(to, 2) * 4 + x, c)

    partner = (g, r, y * 2 + other)
    barrier = pltpu.get_barrier_semaphore()
    everyone = [partner] + [at_x(s) for s in (1, 2, 3)] + [at_y(s) for s in (1, 2, 3)]
    everyone += [at_z(s) for s in range(1, 8)]
    for peer in everyone:
        pl.semaphore_signal(barrier, inc=1, device_id=peer, device_id_type=MESH)

    def send(src, dst, which, slot, peer):
        copy = pltpu.make_async_remote_copy(
            src_ref=src,
            dst_ref=dst,
            send_sem=send_sem.at[which, slot],
            recv_sem=recv_sem.at[which, slot],
            device_id=peer,
            device_id_type=MESH,
        )
        copy.start()
        return copy

    f32, half = jnp.float32, jnp.bfloat16

    def summed(own, received):
        total = own.astype(f32)
        for k in range(3):
            total += received[k].astype(f32)
        return total.astype(half)

    def to_partner(which):
        return send(sending.at[which, other], core_in.at[which], which, 0, partner)

    def first_step(which, copy):
        copy.wait()

        @pl.loop(0, 8)
        def _(k):
            pair = sending[which, core, k].astype(f32) + core_in[which, k].astype(f32)
            held[which, k] = pair.astype(half)

        low, high = held.at[which, pl.ds(0, 4)], held.at[which, pl.ds(4, 4)]
        copies = []
        for s in (1, 2, 3):
            copies.append(send(low.at[:, lax.rem(x + s, 4)], x_in.at[which, s - 1], which, s, at_x(s)))
            copies.append(send(high.at[:, :, lax.rem(y + s, 4)], y_in.at[which, s - 1], which, 3 + s, at_y(s)))
        return copies

    def second_step(which, copies):
        for copy in copies:
            copy.wait()
        mid_x[which] = summed(held[which, 0:4, x], [x_in[which, k] for k in range(3)])
        mid_y[which] = summed(held[which, 4:8, :, y], [y_in[which, k] for k in range(3)])
        after = []
        for s in (1, 2, 3):
            after.append(send(mid_x.at[which, :, lax.rem(y + s, 4)], yy_in.at[which, s - 1], which, 6 + s, at_y(s)))
            after.append(send(mid_y.at[which, :, lax.rem(x + s, 4)], xx_in.at[which, s - 1], which, 9 + s, at_x(s)))
        return after

    def third_step(which, copies):
        for copy in copies:
            copy.wait()
        last[which, 0:4] = summed(mid_x[which, :, y], [yy_in[which, k] for k in range(3)])
        last[which, 4:8] = summed(mid_y[which, :, x], [xx_in[which, k] for k in range(3)])
        return [
            send(last.at[which, lax.rem(z + s, 8)], z_in.at[which, s - 1], which, 12 + s, at_z(s))
            for s in range(1, 8)
        ]

    def result(which, copies):
        for copy in copies:
            copy.wait()
        total = last[which, z].astype(f32)
        for k in range(7):
            total += z_in[which, k].astype(f32)
        out_ref[which] = total

    rgb16[...] = jnp.zeros((16, 128), f32)
    rgb16[0:3] = rgb_ref[...].astype(f32)
    loads[0].wait()
    turned_taps(second_ref, taps)
    loads[1].wait()

    lane = lax.broadcasted_iota(jnp.int32, (8, 128), 1)
    col = lax.rem(lane, 32) + (16 * c - 8)
    in_cols = (lane < 96) & (col >= 0) & (col < 128)

    @pl.loop(0, 8)
    def _(f):
        frame = 6 * g - 1 + f
        known = in_cols & (frame >= 0) & (frame < 24)
        parts = []
        for part in range(3):
            seen = known & (r + part - 1 >= 0) & (r + part - 1 < 8)
            parts.append(jnp.where(seen, pixel_ref[f, part].astype(f32)[0:8], 0.0))
        turned = jnp.concatenate(parts, axis=0).T
        for i in range(10):
            hidden_grad = turned[0:32, i + 7 : i + 8] * rgb16[0:1]
            for k in (1, 2):
                hidden_grad += turned[32 * k : 32 * (k + 1), i + 7 : i + 8] * rgb16[k : k + 1]
            field[f, i] = (hidden_grad * slope2_ref[f, i]).astype(half)

    @pl.loop(0, 6)
    def _(f):
        own = field[f + 1, 1:9].astype(f32)[:, 8:24].reshape(128, 128).astype(half)
        delta[pl.ds(pl.multiple_of(128 * f, 128), 128)] = own

    loads[2].wait()
    columns_in_lanes(hidden_ref, 0, 0, columns)
    terms[pl.ds(3456, 8)] = jnp.zeros((8, 128), f32)
    weight_terms(columns, delta, terms)
    by_chip(terms, sending, 1)
    pl.semaphore_wait(barrier, len(everyone))
    swap_second = to_partner(1)
    loads[3].wait()

    @pl.loop(0, 6)
    def _(f):
        back = conv_rows(field, f, (0,), 8, taps)[:, 8:24].reshape(128, 128)
        value = (back * slope1_ref[f]).astype(half)
        delta[pl.ds(pl.multiple_of(128 * f, 128), 128)] = value

    moves_second = first_step(1, swap_second)
    loads[4].wait()
    columns_in_lanes(cells_ref, 0, 0, columns)
    weight_terms(columns, delta, terms)
    moves_second = second_step(1, moves_second)
    by_chip(terms, sending, 0)
    swap_first = to_partner(0)
    moves_second = third_step(1, moves_second)
    moves_first = first_step(0, swap_first)
    result(1, moves_second)
    moves_first = second_step(0, moves_first)
    moves_first = third_step(0, moves_first)
    result(0, moves_first)


def f32_shape(*shape):
    return jax.ShapeDtypeStruct(shape, jnp.float32)


def places(text):
    return [pl.BlockSpec(memory_space=pltpu.VMEM if letter == "v" else pltpu.HBM) for letter in text]


def talking_call(kernel, ident, mebibytes, in_places, out_places, outs, scratch, *operands):
    return pl.pallas_call(
        kernel,
        out_shape=tuple(outs),
        in_specs=places(in_places),
        out_specs=tuple(places(out_places)),
        scratch_shapes=scratch,
        compiler_params=pltpu.CompilerParams(
            collective_id=ident, has_side_effects=True, vmem_limit_bytes=mebibytes * 2**20
        ),
    )(*operands)


def local(dec_input, target, conv_first, conv_second, rgb_weight, vgg_first, vgg_second, vgg_third):
    g, r, c = position()
    channels = dec_input.shape[-1]
    half, f32, dma, vmem = jnp.bfloat16, jnp.float32, pltpu.SemaphoreType.DMA, pltpu.VMEM
    cells, hidden, slope1, slope2, colour_near, guide_near = talking_call(
        forward_kernel,
        3,
        58,
        "hvhhv",
        "hhhhvv",
        (
            b16(8, 10, 32, 128), b16(8, 10, 32, 128), f32_shape(6, 128, 128), f32_shape(8, 10, 32, 128),
            b16(3, 8, 16, 128), b16(3, 32, 128),
        ),
        [
            vmem((24, 8, 16, 128), half), vmem((3456, 128), half), vmem((3456, 128), half), vmem((16, 128), f32),
            vmem((12, 14, 32, 128), half), vmem((10, 12, 32, 128), half),
            vmem((10, 128, 128), f32), vmem((8, 10, 32, 128), f32), dma((3,)), dma((4,)),
            vmem((12, 8, 16, 128), half), vmem((8, 48, 128), half), vmem((8, 48, 128), half),
            vmem((8, 48, 128), half), vmem((8, 48, 128), half), vmem((2, 12, 3, 16, 128), half),
            vmem((2, 2, 3, 16, 128), half), vmem((2, 2, 3, 16, 128), half),
            vmem((2, 4, 3, 16, 128), half), vmem((2, 4, 3, 16, 128), half),
            dma((6,)), dma((6,)), dma((2, 8)), dma((2, 8)),
            vmem((1152, 384), half), vmem((1152, 384), half), vmem((6, 16, 128), half),
            dma((3, 6)), dma((3, 8)), dma(()),
        ],
        dec_input.reshape(24, 8, 16, channels), target, conv_first, conv_second, rgb_weight,
    )
    pixels = perceptual_strip(
        colour_near, guide_near, first_weights(vgg_first), (vgg_second.T, vgg_third)
    )
    sums = talking_call(
        backward_kernel,
        1,
        58,
        "vhhhhhv",
        "v",
        (f32_shape(2, 16, 128),),
        [
            vmem((8, 10, 32, 128), half), vmem((8, 10, 32, 128), half), vmem((6, 128, 128), f32),
            vmem((8, 10, 32, 128), f32), vmem((3456, 128), half), vmem((16, 128), f32), dma((5,)),
            pltpu.VMEM((1152, 384), half),
            pltpu.VMEM((8, 10, 16, 384), half),
            pltpu.VMEM((8, 10, 32, 128), half),
            pltpu.VMEM((768, 128), half),
            pltpu.VMEM((3464, 128), jnp.float32),
            pltpu.VMEM((2, 2, 8, 4, 4, 16, 128), half),
            pltpu.VMEM((2, 8, 4, 4, 16, 128), half),
            pltpu.VMEM((2, 8, 4, 4, 16, 128), half),
            pltpu.VMEM((2, 3, 4, 4, 16, 128), half),
            pltpu.VMEM((2, 3, 4, 4, 16, 128), half),
            pltpu.VMEM((2, 4, 4, 16, 128), half),
            pltpu.VMEM((2, 4, 4, 16, 128), half),
            pltpu.VMEM((2, 3, 4, 16, 128), half),
            pltpu.VMEM((2, 3, 4, 16, 128), half),
            pltpu.VMEM((2, 8, 16, 128), half),
            pltpu.VMEM((2, 7, 16, 128), half),
            dma((2, 20)),
            dma((2, 20)),
        ],
        pixels, cells, hidden, slope1, slope2, conv_second, rgb_weight,
    )[0]
    flat = sums[:, :14].reshape(2, 14 * 128)
    own_sums = lax.dynamic_slice_in_dim(flat, lax.rem(c, 2) * 64, 1728, axis=1)
    return own_sums[0], own_sums[1]


def solution(mesh):
    in_specs = (
        P(None, None, "row", "col", None),
        P(None, None, "col", "row", None),
        P(),
        P(),
        P(),
        P(),
        P(),
        P(),
    )
    out_specs = (P(("grp", "row", "col")), P(("grp", "row", "col")))
    return jax.shard_map(local, mesh=mesh, in_specs=in_specs, out_specs=out_specs, check_vma=False)
```

```python
import functools

import jax
import jax.numpy as jnp
from jax import lax
from jax.experimental import pallas as pl
from jax.experimental.pallas import tpu as pltpu
from jax.sharding import PartitionSpec as P

MESH = pl.DeviceIdType.MESH

gelu_scale = 0.7978845608028654
gelu_cubic = 0.044715


def position():
    return lax.axis_index("grp"), lax.axis_index("row"), lax.axis_index("col")


def same_place(one, other):
    return (one[0] == other[0]) & (one[1] == other[1]) & (one[2] == other[2])


def row_count(r):
    return 1 + jnp.where(r > 0, 1, 0) + jnp.where(r < 7, 1, 0)


def in_vmem(count):
    return [pl.BlockSpec(memory_space=pltpu.VMEM)] * count


def b16(*shape):
    return jax.ShapeDtypeStruct(shape, jnp.bfloat16)


def transposed_dot(one, other):
    return lax.dot_general(one, other, (((0,), (0,)), ((), ())), preferred_element_type=jnp.float32)


def side_by_side(value):
    cols = value.shape[0]
    at = lax.broadcasted_iota(jnp.int32, value.shape, 0)
    before = jnp.where(at == 0, 0.0, pltpu.roll(value, 1, 0))
    after = jnp.where(at == cols - 1, 0.0, pltpu.roll(value, cols - 1, 0))
    return jnp.concatenate([before, value, after], axis=1).astype(jnp.bfloat16)


def three_rows(ref, row, count):
    parts = [ref[pl.ds(row + step, count)].reshape(-1, ref.shape[-1]) for step in range(3)]
    return jnp.concatenate(parts, axis=1)


def dot32(one, other):
    return jnp.dot(one, other, preferred_element_type=jnp.float32)


def gelu_both(preact, slope_too):
    square = preact * preact
    inner_tanh = jnp.tanh(gelu_scale * preact * (1.0 + gelu_cubic * square))
    half = 0.5 * (1.0 + inner_tanh)
    value = preact * half
    if not slope_too:
        return value, None
    bend = (0.5 * gelu_scale) * (1.0 + 3.0 * gelu_cubic * square)
    return value, half + preact * (1.0 - inner_tanh * inner_tanh) * bend


def perceptual_kernel(
    near_ref, guide_ref, w1_ref, vgg_second_ref, vgg_third_ref, w1_back_ref, out_ref,
    planes_ref, guides,
    taps, act1, slope1, pooled, delta3, diff2, slope2, delta2, delta1, tmp, pixels, strip,
    w2_ref, w3_ref, w3_back_ref, w2_back_ref, send_sem, recv_sem, own_sem,
):
    g, r, c = position()
    me = (g, r, c)
    barrier = pltpu.get_barrier_semaphore()
    perceives = g < 3
    own_frame = 8 * g + c
    home = own_frame // 6
    place = lax.rem(own_frame, 6)
    ahead = perceives & (place == 0) & (home > 0)
    behind = perceives & (place == 5) & (home < 3)

    def sources(do):
        for slot in range(8):
            source_frame = 6 * g - 1 + slot

            def each(step, slot=slot, source_frame=source_frame):
                source = (source_frame // 8, r + step, lax.rem(source_frame, 8))
                pl.when(jnp.logical_not(same_place(source, me)))(
                    functools.partial(do, step, slot, source)
                )

            pl.when((source_frame >= 0) & (source_frame < 24))(functools.partial(on_rows, r, each))

    def greet(step, slot, source):
        pl.semaphore_signal(barrier, inc=1, device_id=source, device_id_type=MESH)

    sources(greet)
    lay_out_perceptual(vgg_second_ref, vgg_third_ref, w2_ref, w3_ref, w3_back_ref, w2_back_ref)
    row0 = 8 * r - 8
    kind = lax.broadcasted_iota(jnp.int32, (8, 128), 0)
    block = lax.broadcasted_iota(jnp.int32, (8, 128), 1) // 16
    for part in range(3):
        guides[...] = guide_ref[part].astype(jnp.float32)
        tiles = [near_ref[part, column].astype(jnp.float32)[0:8] for column in range(8)]
        here = (kind < 3) & (row0 + 8 * part >= 0) & (row0 + 8 * part < 64)
        seen = (row0 + 8 * part >= 0) & (row0 + 8 * part < 64)
        for i in range(8):
            image = jnp.zeros((8, 128), jnp.float32)
            for column in range(8):
                turned = pltpu.roll(tiles[column], (16 * column - 16 * i) % 128, 1)
                image = jnp.where(block == column, turned, image)
            planes_ref[8 * part + i] = jnp.where(here, image, 0.0)
            planes_ref[8 * part + i, 3:6] = jnp.where(seen, guides[pl.ds(i, 3, 8)], 0.0)
    lane = lax.broadcasted_iota(jnp.int32, (192, 128), 1)
    planes = planes_ref[...].reshape(192, 128)
    before = jnp.where(lane == 0, 0.0, pltpu.roll(planes, 1, 1))
    after = jnp.where(lane == 127, 0.0, pltpu.roll(planes, 127, 1))
    taps[:, 0:8] = before.reshape(24, 8, 128)
    taps[:, 8:16] = planes.reshape(24, 8, 128)
    taps[:, 16:24] = after.reshape(24, 8, 128)

    def shown(row):
        return (row0 + row >= 0) & (row0 + row < 64)

    def kept(row, value):
        return jnp.where(shown(row), value, 0.0)

    def first_rows(low, high, slope_too):
        @pl.loop(low, high)
        def _(i):
            cells = taps[pl.ds(i, 3)].reshape(72, 128).astype(jnp.bfloat16)
            value, slope = gelu_both(transposed_dot(cells, w1_ref[...]), slope_too)
            act1[i] = side_by_side(kept(i + 1, value))
            if slope_too:
                slope1[i - 6] = slope

    first_rows(0, 6, False)
    first_rows(6, 16, True)
    first_rows(16, 22, False)

    def second_rows(low, high, slope_too):
        @pl.loop(low, high)
        def _(p):
            plane = dot32(three_rows(act1, 2 * p, 2), w2_ref[...])
            value, slope = gelu_both(plane, slope_too)
            value = kept(2 * p + 2, value)
            if slope_too:
                difference = 0.25 * (value - pltpu.roll(value, 64, 1))
                diff2[pl.ds(2 * p - 4, 2)] = difference.reshape(2, 128, 128)
                slope2[pl.ds(2 * p - 4, 2)] = slope.reshape(2, 128, 128)
            tmp[...] = value[:128] + value[128:]
            mean = 0.25 * (tmp[pl.ds(0, 64, 2)] + tmp[pl.ds(1, 64, 2)])
            pooled[p] = side_by_side(mean)

    second_rows(0, 2, False)
    second_rows(2, 8, True)
    second_rows(8, 10, False)

    @pl.loop(0, 4)
    def _(half):
        j = 2 * half
        plane = dot32(three_rows(pooled, j, 2), w3_ref[...])
        value, slope = gelu_both(plane[:, :128], True)
        guide, _ = gelu_both(plane[:, 128:], False)
        delta = 0.5 * (value - guide) * slope
        delta3[j] = side_by_side(kept(2 * j + 4, delta[:64]))
        delta3[j + 1] = side_by_side(kept(2 * j + 6, delta[64:]))

    @pl.loop(0, 6)
    def _(m):
        grad = 0.25 * dot32(three_rows(delta3, m, 1), w3_back_ref[...])
        tmp[pl.ds(0, 64, 2)] = grad
        tmp[pl.ds(1, 64, 2)] = grad
        spread = tmp[...]
        for k in range(2):
            delta = (spread + diff2[2 * m + k]) * slope2[2 * m + k]
            delta2[2 * m + k] = side_by_side(kept(2 * m + 6, delta))

    @pl.loop(0, 5)
    def _(half):
        n = 2 * half
        grad = dot32(three_rows(delta2, n, 2), w2_back_ref[...])
        for k in range(2):
            delta = grad[128 * k : 128 * (k + 1)] * slope1[n + k]
            delta1[n + k] = side_by_side(kept(n + k + 7, delta))

    @pl.loop(0, 8)
    def _(q):
        grad = lax.dot_general(
            w1_back_ref[...],
            three_rows(delta1, q, 1),
            (((1,), (1,)), ((), ())),
            preferred_element_type=jnp.float32,
        )
        own = planes_ref[q + 8]
        direct = (1.0 / 6.0) * (own - pltpu.roll(own, 5, 0))
        pixels[pl.ds(pl.multiple_of(q * 8, 8), 8)] = grad + direct

    colour_rows = [pixels[pl.ds(k, 8, 8)] for k in range(3)]
    third = lax.broadcasted_iota(jnp.int32, (8, 128), 1) // 32
    for column in range(8):
        turned = [pltpu.roll(v, (32 * k + 8 - 16 * column) % 128, 1) for k, v in enumerate(colour_rows)]
        part = jnp.where(third == 0, turned[0], jnp.where(third == 1, turned[1], turned[2]))
        strip[column] = jnp.concatenate([part, jnp.zeros((8, 128), jnp.float32)], axis=0).astype(jnp.bfloat16)

    groups = jnp.where(perceives, 1, 0) + jnp.where(ahead, 1, 0) + jnp.where(behind, 1, 0)
    to_itself = perceives & (home == g) | ahead & (home == g + 1) | behind & (home == g - 1)
    awaited = 8 * row_count(r) * groups - jnp.where(to_itself, 1, 0)
    pl.when(perceives)(lambda: pl.semaphore_wait(barrier, awaited))

    def targets(do):
        for kind, (group, needed) in enumerate(((home, perceives), (home - 1, ahead), (home + 1, behind))):

            def each(step, kind=kind, group=group):
                for column in range(8):
                    peer = (group, r + step, column)
                    do(kind, step, column, peer, jnp.logical_not(same_place(peer, me)))

            pl.when(needed)(functools.partial(on_rows, r, each))

    def outgoing(kind, step, column, peer):
        place_there = own_frame - 6 * peer[0] + 1
        return pltpu.make_async_remote_copy(
            src_ref=strip.at[column],
            dst_ref=out_ref.at[place_there, 1 - step],
            send_sem=send_sem.at[kind, step + 1, column],
            recv_sem=recv_sem.at[place_there, 1 - step],
            device_id=peer,
            device_id_type=MESH,
        )

    def kept():
        return pltpu.make_async_copy(strip.at[c], out_ref.at[own_frame - 6 * g + 1, 1], own_sem)

    def start(kind, step, column, peer, away):
        pl.when(away)(lambda: outgoing(kind, step, column, peer).start())
        if step == 0:
            pl.when(jnp.logical_not(away))(lambda: kept().start())

    def finish(kind, step, column, peer, away):
        pl.when(away)(lambda: outgoing(kind, step, column, peer).wait_send())
        if step == 0:
            pl.when(jnp.logical_not(away))(lambda: kept().wait())

    def arrive(step, slot, source):
        pltpu.make_async_remote_copy(
            src_ref=strip.at[0],
            dst_ref=out_ref.at[slot, step + 1],
            send_sem=send_sem.at[0, 0, 0],
            recv_sem=recv_sem.at[slot, step + 1],
            device_id=source,
            device_id_type=MESH,
        ).wait_recv()

    targets(start)
    sources(arrive)
    targets(finish)


def two_blocks(weight):
    _, i, o = weight.shape
    return jnp.pad(weight, ((0, 0), (0, i), (0, o))) + jnp.pad(weight, ((0, 0), (i, 0), (o, 0)))


def first_weights(vgg_first):
    first = vgg_first.reshape(9, 3, 64)
    w1 = jnp.pad(two_blocks(first), ((0, 0), (0, 2), (0, 0))).reshape(72, 128)
    w1_back = jnp.pad(jnp.transpose(first[::-1], (1, 0, 2)), ((0, 5), (0, 0), (0, 64))).reshape(8, 1152)
    return w1, w1_back


def perceptual_strip(near, guides, first, others):
    f32, half = jnp.float32, jnp.bfloat16
    return pl.pallas_call(
        perceptual_kernel,
        out_shape=b16(8, 3, 16, 128),
        in_specs=in_vmem(6),
        out_specs=in_vmem(1)[0],
        scratch_shapes=[
            pltpu.VMEM((24, 8, 128), f32),
            pltpu.VMEM((32, 128), f32),
            pltpu.VMEM((24, 24, 128), f32),
            pltpu.VMEM((22, 128, 384), half),
            pltpu.VMEM((10, 128, 128), f32),
            pltpu.VMEM((10, 64, 384), half),
            pltpu.VMEM((8, 64, 384), half),
            pltpu.VMEM((12, 128, 128), f32),
            pltpu.VMEM((12, 128, 128), f32),
            pltpu.VMEM((12, 128, 384), half),
            pltpu.VMEM((10, 128, 384), half),
            pltpu.VMEM((128, 128), f32),
            pltpu.VMEM((64, 128), f32),
            pltpu.VMEM((8, 16, 128), half),
            pltpu.VMEM((1152, 128), half),
            pltpu.VMEM((1152, 256), half),
            pltpu.VMEM((1152, 128), half),
            pltpu.VMEM((1152, 128), half),
            pltpu.SemaphoreType.DMA((3, 3, 8)),
            pltpu.SemaphoreType.DMA((8, 3)),
            pltpu.SemaphoreType.DMA(()),
        ],
        compiler_params=pltpu.CompilerParams(
            collective_id=4, has_side_effects=True, vmem_limit_bytes=24 * 2**20
        ),
    )(near, guides, first[0], *others, first[1])


def taps_in_lanes(weight_ref, out_ref):
    for q in range(9):
        for k in range(3):
            tap = 3 * q + k
            out_ref[128 * q : 128 * (q + 1), 128 * k : 128 * (k + 1)] = weight_ref[
                128 * tap : 128 * (tap + 1), :
            ]


def turned_taps(weight_ref, out_ref):
    for q in range(9):
        for k in range(3):
            tap = 26 - 3 * q - k
            block = weight_ref[128 * tap : 128 * (tap + 1), :].astype(jnp.float32)
            out_ref[128 * q : 128 * (q + 1), 128 * k : 128 * (k + 1)] = block.T.astype(jnp.bfloat16)


def conv_rows(source, frame, starts, count, taps_ref):
    size = len(starts) * count * 32

    def near(dt, dr):
        rows = [source[frame + dt, pl.ds(start + dr, count)].reshape(count * 32, 128) for start in starts]
        return rows[0] if len(rows) == 1 else jnp.concatenate(rows, axis=0)

    parts = [near(dt, dr) for dt in range(3) for dr in range(3)]
    sums = dot32(jnp.concatenate(parts, axis=1), taps_ref[...])
    total = pltpu.roll(sums[:, :128], 1, 0) + sums[:, 128:256]
    total += pltpu.roll(sums[:, 256:], size - 1, 0)
    return total.reshape(len(starts) * count, 32, 128)


def silu_parts(preact):
    gate = 1.0 / (1.0 + jnp.exp(-preact))
    return preact * gate, gate * (1.0 + preact * (1.0 - gate))


def on_rows(r, do):
    for step in (-1, 0, 1):
        pl.when((r + step >= 0) & (r + step < 8))(functools.partial(do, step))


def lay_out_perceptual(second_ref, third_ref, w2_out, w3_out, w3_back_out, w2_back_out):
    f32, half = jnp.float32, jnp.bfloat16
    for t in range(9):
        turned_block = second_ref[:, 64 * t : 64 * (t + 1)].astype(f32)
        block = turned_block.T
        wide = third_ref[64 * t : 64 * (t + 1), :].astype(f32)
        none, low, high = jnp.zeros((64, 64), f32), 128 * t, 128 * (8 - t)
        w2_out[low : low + 64] = jnp.concatenate([block, none], axis=1).astype(half)
        w2_out[low + 64 : low + 128] = jnp.concatenate([none, block], axis=1).astype(half)
        w3_out[low : low + 64, :128] = wide.astype(half)
        w3_out[low : low + 64, 128:] = jnp.zeros((64, 128), half)
        w3_out[low + 64 : low + 128, :128] = jnp.zeros((64, 128), half)
        w3_out[low + 64 : low + 128, 128:] = wide.astype(half)
        w2_back_out[high : high + 64] = jnp.concatenate([turned_block, none], axis=1).astype(half)
        w2_back_out[high + 64 : high + 128] = jnp.zeros((64, 128), half)
        turned = jnp.concatenate([wide.T, jnp.zeros((128, 64), f32)], axis=1)
        w3_back_out[high : high + 128] = turned.astype(half)


def forward_kernel(
    video_hbm, target_ref, first_hbm, second_hbm, rgb_ref,
    cells_hbm, hidden_hbm, slope1_hbm, slope2_hbm, turned_hbm, near_out, guide_out,
    video, first_ref, second_ref, rgb16, cells, hidden_out, slope1_out, slope2_out, load_sem, store_sem,
    tile, left_send, right_send, left_in, right_in, rows_in, to_west, to_east, from_east, from_west,
    halo_send, halo_recv, edge_send, edge_recv,
    taps1, taps2, turned, cell_columns, hidden_columns, colours, send_sem, recv_sem, own_sem,
):
    loads = [
        pltpu.make_async_copy(video_hbm, video, load_sem.at[0]),
        pltpu.make_async_copy(first_hbm, first_ref, load_sem.at[1]),
        pltpu.make_async_copy(second_hbm, second_ref, load_sem.at[2]),
    ]
    for load in loads:
        load.start()
    g, r, c = position()
    me = (g, r, c)
    f32, half = jnp.float32, jnp.bfloat16
    barrier = pltpu.get_barrier_semaphore()
    perceives = g < 3
    source_group = (8 * g + c) // 6
    west, east = lax.rem(c + 7, 8), lax.rem(c + 1, 8)
    has_up, has_down = r > 0, r < 7
    has_prev, has_next = g > 0, g < 3

    def sources(do):
        def each(step):
            for column in range(8):
                source = (source_group, r + step, column)
                pl.when(jnp.logical_not(same_place(source, me)))(
                    functools.partial(do, step, column, source)
                )

        pl.when(perceives)(lambda: on_rows(r, each))

    def signal(peer):
        pl.semaphore_signal(barrier, inc=1, device_id=peer, device_id_type=MESH)

    signal((g, r, west))
    signal((g, r, east))

    pl.when(has_up)(lambda: signal((g, r - 1, c)))
    pl.when(has_down)(lambda: signal((g, r + 1, c)))

    @pl.when(has_prev)
    def _():
        for column in (west, c, east):
            signal((g - 1, r, column))

    @pl.when(has_next)
    def _():
        for column in (west, c, east):
            signal((g + 1, r, column))

    sources(lambda step, column, source: signal(source))

    block = jnp.minimum(g, 2)
    guide = [target_ref[k, block, 0].astype(f32) for k in range(3)] + [jnp.zeros((8, 128), f32)]
    guide_out[1] = jnp.concatenate(guide, axis=0).astype(half)
    rgb16[...] = jnp.zeros((16, 128), f32)
    rgb16[0:3] = rgb_ref[...].astype(f32)
    loads[0].wait()

    for f in range(12):
        frame = 6 * g - 3 + f
        value = video[jnp.minimum(jnp.maximum(frame, 0), 23)]
        tile[f] = jnp.where((frame >= 0) & (frame < 24), value, jnp.zeros_like(value))

    to_itself = jnp.where(perceives & (2 * g + c < 6), 1, 0)
    groups_near = jnp.where(has_prev, 1, 0) + jnp.where(has_next, 1, 0)
    pl.semaphore_wait(barrier, 7 * row_count(r) + 1 + 3 * groups_near - to_itself)

    def remote(src, dst, slot, peer):
        return pltpu.make_async_remote_copy(
            src_ref=src,
            dst_ref=dst,
            send_sem=halo_send.at[slot],
            recv_sem=halo_recv.at[slot],
            device_id=peer,
            device_id_type=MESH,
        )

    sideways = [remote(left_send, right_in, 0, (g, r, west)), remote(right_send, left_in, 1, (g, r, east))]

    def to_row(row_index, rows, edge, guide_slot, first_slot):
        strip = tile.at[pl.ds(3, 6), pl.ds(rows, 3)]
        return [
            remote(strip, rows_in.at[edge, pl.ds(3, 6)], first_slot, (g, row_index, c)),
            remote(guide_out.at[1], guide_out.at[guide_slot], first_slot + 1, (g, row_index, c)),
        ]

    upward = to_row(r - 1, 0, 1, 2, 2)
    downward = to_row(r + 1, 5, 0, 0, 4)

    def across(edge):
        def copy(src, dst, slot, peer):
            return pltpu.make_async_remote_copy(
                src_ref=src,
                dst_ref=dst,
                send_sem=edge_send.at[edge, slot],
                recv_sem=edge_recv.at[edge, slot],
                device_id=peer,
                device_id_type=MESH,
            )

        mine, wests, easts = rows_in.at[edge], to_west.at[edge], to_east.at[edge]
        in_east, in_west, two = from_east.at[edge], from_west.at[edge], pl.ds(1, 2)
        level = [
            copy(wests, in_east.at[two], 0, (g, r, west)),
            copy(easts, in_west.at[two], 1, (g, r, east)),
        ]
        onward = [
            copy(mine.at[pl.ds(6, 3)], mine.at[pl.ds(0, 3)], 2, (g + 1, r, c)),
            copy(wests.at[1], in_east.at[0], 3, (g + 1, r, west)),
            copy(easts.at[1], in_west.at[0], 4, (g + 1, r, east)),
        ]
        back = [
            copy(mine.at[pl.ds(3, 3)], mine.at[pl.ds(9, 3)], 5, (g - 1, r, c)),
            copy(wests.at[0], in_east.at[3], 6, (g - 1, r, west)),
            copy(easts.at[0], in_west.at[3], 7, (g - 1, r, east)),
        ]
        return level, onward, back

    edges = [across(0), across(1)]

    def pass_on(edge):
        values = [rows_in[edge, 3 + f].astype(f32) for f in range(6)]
        for part in range(2):
            near = values[3 * part : 3 * part + 3]
            spare = jnp.zeros((3, 4, 128), f32)
            to_west[edge, part] = jnp.concatenate([v[:, 0:4] for v in near] + [spare], axis=1).astype(half)
            to_east[edge, part] = jnp.concatenate([v[:, 12:16] for v in near] + [spare], axis=1).astype(half)
        level, onward, back = edges[edge]
        start(level)
        pl.when(has_next)(lambda: start(onward))
        pl.when(has_prev)(lambda: start(back))

    def passed(edge, done):
        level, onward, back = edges[edge]
        done(level)
        if done is landed:
            pl.when(has_prev)(lambda: done(onward))
            pl.when(has_next)(lambda: done(back))
        else:
            pl.when(has_next)(lambda: done(onward))
            pl.when(has_prev)(lambda: done(back))

    def start(copies):
        for copy in copies:
            copy.start()

    def sent(copies):
        for copy in copies:
            copy.wait_send()

    def landed(copies):
        for copy in copies:
            copy.wait_recv()

    pl.when(has_up)(lambda: start(upward))
    pl.when(has_down)(lambda: start(downward))
    for line in range(8):
        near = [tile[f, line].astype(f32) for f in range(12)]
        left_send[line] = jnp.concatenate([v[0:4] for v in near], axis=0).astype(half)
        right_send[line] = jnp.concatenate([v[12:16] for v in near], axis=0).astype(half)
    start(sideways)

    loads[1].wait()
    taps_in_lanes(first_ref, taps1)
    loads[2].wait()
    taps_in_lanes(second_ref, taps2)

    def assemble(first_row, count, real, own, left, right, per):
        col = lax.broadcasted_iota(jnp.int32, (count, 32, 128), 1) + (16 * c - 8)
        shown = (col >= 0) & (col < 128) & real
        for part in range(12 // per):
            before, after = left(part).astype(f32), right(part).astype(f32)
            for k in range(per):
                f, eight = per * part + k, slice(8 * (k // 2), 8 * (k // 2) + 8)
                one = before[:, eight].reshape(8 * count, 128)
                two = after[:, eight].reshape(8 * count, 128)
                if k % 2 == 0:
                    one = pltpu.roll(one, 4, 0)
                else:
                    two = pltpu.roll(two, 8 * count - 4, 0)
                sides = [one.reshape(count, 8, 128), own(f).astype(f32), two.reshape(count, 8, 128)]
                frame = 6 * g - 3 + f
                here = shown & (frame >= 0) & (frame < 24)
                value = jnp.where(here, jnp.concatenate(sides, axis=1), 0.0)
                cells[f, first_row : first_row + count] = value.astype(half)

    row = lax.broadcasted_iota(jnp.int32, (6, 32, 128), 0)
    col = lax.broadcasted_iota(jnp.int32, (6, 32, 128), 1) + (16 * c - 8)
    in_cols = (col >= 0) & (col < 128)

    def in_frames(f):
        frame = 6 * g - 2 + f
        return jnp.where((frame >= 0) & (frame < 24), 1.0, 0.0)

    landed(sideways)
    assemble(
        3, 8, r >= 0, lambda f: tile[f],
        lambda part: left_in[:, 16 * part : 16 * (part + 1)],
        lambda part: right_in[:, 16 * part : 16 * (part + 1)],
        4,
    )

    def inner(f):
        value, slope = silu_parts(conv_rows(cells, f, (3,), 6, taps1))
        value = jnp.where(in_cols, value, 0.0) * in_frames(f)
        hidden_out[f, 3:9] = value.astype(half)
        slope1_out[f, 16:112] = slope[:, 8:24].reshape(96, 128)

    pl.loop(0, 3)(inner)

    @pl.when(has_up)
    def _():
        landed(downward)
        pass_on(0)

    @pl.when(has_down)
    def _():
        landed(upward)
        pass_on(1)

    pl.loop(3, 10)(inner)

    pl.when(has_up)(lambda: passed(0, landed))
    pl.when(has_down)(lambda: passed(1, landed))
    for edge, real in ((0, has_up), (1, has_down)):
        assemble(
            11 * edge, 3, real,
            lambda f, edge=edge: rows_in[edge, f],
            lambda part, edge=edge: from_west[edge, part],
            lambda part, edge=edge: from_east[edge, part],
            3,
        )
    image_row = jnp.where(row < 3, row, row + 6) + (8 * r - 2)
    in_image = in_cols & (image_row >= 0) & (image_row < 64)

    @pl.loop(0, 10)
    def _(f):
        value, slope = silu_parts(conv_rows(cells, f, (0, 9), 3, taps1))
        value = (jnp.where(in_image, value, 0.0) * in_frames(f)).astype(half)
        hidden_out[f, 0:3] = value[0:3]
        hidden_out[f, 9:12] = value[3:6]
        slope1_out[f, 0:16] = slope[2, 8:24]
        slope1_out[f, 112:128] = slope[3, 8:24]

    stores = [
        pltpu.make_async_copy(slope1_out.at[pl.ds(2, 6)], slope1_hbm, store_sem.at[0]),
        pltpu.make_async_copy(slope2_out, slope2_hbm, store_sem.at[1]),
        pltpu.make_async_copy(hidden_columns, hidden_hbm, store_sem.at[2]),
        pltpu.make_async_copy(cell_columns, cells_hbm, store_sem.at[3]),
        pltpu.make_async_copy(turned, turned_hbm, store_sem.at[4]),
    ]
    stores[0].start()

    def target(step, slot):
        frame = 6 * g + slot
        return (frame // 8, r + step, lax.rem(frame, 8))

    def outgoing(step, slot):
        return pltpu.make_async_remote_copy(
            src_ref=colours.at[slot],
            dst_ref=near_out.at[1 - step, c],
            send_sem=send_sem.at[step + 1, slot],
            recv_sem=recv_sem.at[1 - step, c],
            device_id=target(step, slot),
            device_id_type=MESH,
        )

    def kept(slot):
        return pltpu.make_async_copy(colours.at[slot], near_out.at[1, c], own_sem)

    def start_colour(slot, step):
        away = jnp.logical_not(same_place(target(step, slot), me))
        pl.when(away)(lambda: outgoing(step, slot).start())
        if step == 0:
            pl.when(jnp.logical_not(away))(lambda: kept(slot).start())

    def finish(slot, step):
        away = jnp.logical_not(same_place(target(step, slot), me))
        pl.when(away)(lambda: outgoing(step, slot).wait_send())
        if step == 0:
            pl.when(jnp.logical_not(away))(lambda: kept(slot).wait())

    def arrive(step, column, source):
        pltpu.make_async_remote_copy(
            src_ref=colours.at[0],
            dst_ref=near_out.at[step + 1, column],
            send_sem=send_sem.at[0, 0],
            recv_sem=recv_sem.at[step + 1, column],
            device_id=source,
            device_id_type=MESH,
        ).wait_recv()

    @pl.loop(0, 6)
    def _(slot):
        value, slope = silu_parts(conv_rows(hidden_out, slot + 1, (0,), 10, taps2))
        slope2_out[slot + 1] = slope
        own = value[1:9, 8:24].reshape(128, 128).astype(jnp.bfloat16)
        colour = lax.dot_general(
            rgb16[...].astype(half), own, (((1,), (1,)), ((), ())), preferred_element_type=jnp.float32
        )
        colours[slot] = colour.astype(jnp.bfloat16)
        on_rows(r, functools.partial(start_colour, slot))

    @pl.loop(0, 2)
    def _(end):
        slope2_out[7 * end] = silu_parts(conv_rows(hidden_out, 7 * end, (0,), 10, taps2))[1]

    stores[1].start()
    columns_in_lanes(hidden_out, 1, 1, hidden_columns)
    stores[2].start()
    columns_in_lanes(cells, 2, 2, cell_columns)
    stores[3].start()
    turned_taps(second_ref, turned)
    stores[4].start()
    sources(arrive)

    @pl.loop(0, 6)
    def _(slot):
        on_rows(r, functools.partial(finish, slot))

    for store in stores:
        store.wait()

    sent(sideways)
    pl.when(has_up)(lambda: sent(upward))
    pl.when(has_down)(lambda: sent(downward))
    pl.when(has_up)(lambda: passed(0, sent))
    pl.when(has_down)(lambda: passed(1, sent))


def columns_in_lanes(source, frame0, row0, out_ref):
    @pl.loop(0, 8)
    def _(f):
        value = source[f + frame0, pl.ds(row0, 10)].reshape(320, 128).astype(jnp.float32)
        parts = [pltpu.roll(value, 1, 0), value, pltpu.roll(value, 319, 0)]
        for k, part in enumerate(parts):
            own = part.reshape(10, 32, 128)[:, 8:24]
            out_ref[f, :, :, 128 * k : 128 * (k + 1)] = own.astype(jnp.bfloat16)


def weight_terms(columns, delta, terms, low, high):
    @pl.loop(low, high)
    def _(q):
        cells = columns[pl.ds(q // 3, 6), pl.ds(lax.rem(q, 3), 8)].reshape(768, 384)
        terms[pl.ds(pl.multiple_of(384 * q, 384), 384)] = transposed_dot(cells, delta[...])


def by_chip(terms, out_ref, which, low, high):
    @pl.loop(low, high)
    def _(z):
        for chip in range(16):
            start = 432 * z + 27 * chip
            out_ref[which, 0, z, chip // 4, chip % 4] = terms[pl.ds(start, 16)].astype(jnp.bfloat16)
            out_ref[which, 1, z, chip // 4, chip % 4] = terms[pl.ds(start + 13, 16)].astype(jnp.bfloat16)


def backward_kernel(
    pixel_ref, cells_hbm, hidden_hbm, slope1_hbm, slope2_hbm, turned_hbm, rgb_ref, first_out, second_out,
    cells_ref, hidden_ref, slope1_ref, slope2_ref, taps, rgb16, load_sem,
    field, delta, terms,
    sending, core_in, held, x_in, y_in, mid_x, mid_y, yy_in, xx_in, last, z_in, send_sem, recv_sem,
):
    g, r, c = position()
    loads = [
        pltpu.make_async_copy(src, dst, load_sem.at[k])
        for k, (src, dst) in enumerate(
            (
                (slope2_hbm, slope2_ref), (hidden_hbm, hidden_ref), (turned_hbm, taps),
                (slope1_hbm, slope1_ref), (cells_hbm, cells_ref),
            )
        )
    ]
    for load in loads:
        load.start()
    zh, x, y, core = r // 4, lax.rem(r, 4), c // 2, lax.rem(c, 2)
    z = g * 2 + zh
    other = 1 - core

    def at_x(step):
        return (g, zh * 4 + lax.rem(x + step, 4), c)

    def at_y(step):
        return (g, r, lax.rem(y + step, 4) * 2 + core)

    def at_z(step):
        to = lax.rem(z + step, 8)
        return (to // 2, lax.rem(to, 2) * 4 + x, c)

    partner = (g, r, y * 2 + other)
    barrier = pltpu.get_barrier_semaphore()
    everyone = [partner] + [at_x(s) for s in (1, 2, 3)] + [at_y(s) for s in (1, 2, 3)]
    everyone += [at_z(s) for s in range(1, 8)]
    for peer in everyone:
        pl.semaphore_signal(barrier, inc=1, device_id=peer, device_id_type=MESH)

    def send(src, dst, which, slot, peer):
        copy = pltpu.make_async_remote_copy(
            src_ref=src,
            dst_ref=dst,
            send_sem=send_sem.at[which, slot],
            recv_sem=recv_sem.at[which, slot],
            device_id=peer,
            device_id_type=MESH,
        )
        copy.start()
        return copy

    f32, half = jnp.float32, jnp.bfloat16

    def summed(own, received):
        total = own.astype(f32)
        for k in range(3):
            total += received[k].astype(f32)
        return total.astype(half)

    def to_partner(which, part):
        some = pl.ds(4 * part, 4)
        return send(sending.at[which, other, some], core_in.at[which, some], which, 20 * part, partner)

    def first_step(which, part, copy):
        copy.wait()

        @pl.loop(4 * part, 4 * part + 4)
        def _(k):
            pair = sending[which, core, k].astype(f32) + core_in[which, k].astype(f32)
            held[which, k] = pair.astype(half)

        some = held.at[which, pl.ds(4 * part, 4)]
        if part == 0:
            return [
                send(some.at[:, lax.rem(x + s, 4)], x_in.at[which, s - 1], which, s, at_x(s)) for s in (1, 2, 3)
            ]
        return [
            send(some.at[:, :, lax.rem(y + s, 4)], y_in.at[which, s - 1], which, 3 + s, at_y(s)) for s in (1, 2, 3)
        ]

    def second_step(which, part, copies):
        for copy in copies:
            copy.wait()
        if part == 0:
            mid_x[which] = summed(held[which, 0:4, x], [x_in[which, k] for k in range(3)])
            return [
                send(mid_x.at[which, :, lax.rem(y + s, 4)], yy_in.at[which, s - 1], which, 6 + s, at_y(s))
                for s in (1, 2, 3)
            ]
        mid_y[which] = summed(held[which, 4:8, :, y], [y_in[which, k] for k in range(3)])
        return [
            send(mid_y.at[which, :, lax.rem(x + s, 4)], xx_in.at[which, s - 1], which, 9 + s, at_x(s))
            for s in (1, 2, 3)
        ]

    def third_step(which, copies):
        for copy in copies:
            copy.wait()
        last[which, 0:4] = summed(mid_x[which, :, y], [yy_in[which, k] for k in range(3)])
        last[which, 4:8] = summed(mid_y[which, :, x], [xx_in[which, k] for k in range(3)])
        return [
            send(last.at[which, lax.rem(z + s, 8)], z_in.at[which, s - 1], which, 12 + s, at_z(s))
            for s in range(1, 8)
        ]

    def result(which, copies, out_ref):
        for copy in copies:
            copy.wait()
        total = last[which, z].astype(f32)
        for k in range(7):
            total += z_in[which, k].astype(f32)
        turned = pltpu.roll(total, 64, 1)
        low_half = lax.broadcasted_iota(jnp.int32, (16, 128), 1) < 64
        shifted = jnp.where(low_half, turned, pltpu.roll(turned, 15, 0))
        out_ref[...] = jnp.where(core == 1, shifted, total)

    rgb16[...] = jnp.zeros((16, 128), f32)
    rgb16[0:3] = rgb_ref[...].astype(f32)
    loads[0].wait()

    lane = lax.broadcasted_iota(jnp.int32, (8, 128), 1)
    col = lax.rem(lane, 32) + (16 * c - 8)
    in_cols = (lane < 96) & (col >= 0) & (col < 128)

    @pl.loop(0, 8)
    def _(f):
        frame = 6 * g - 1 + f
        known = in_cols & (frame >= 0) & (frame < 24)
        parts = []
        for part in range(3):
            seen = known & (r + part - 1 >= 0) & (r + part - 1 < 8)
            parts.append(jnp.where(seen, pixel_ref[f, part].astype(f32)[0:8], 0.0))
        turned = jnp.concatenate(parts, axis=0).T
        for i in range(10):
            hidden_grad = turned[0:32, i + 7 : i + 8] * rgb16[0:1]
            for k in (1, 2):
                hidden_grad += turned[32 * k : 32 * (k + 1), i + 7 : i + 8] * rgb16[k : k + 1]
            field[f, i] = (hidden_grad * slope2_ref[f, i]).astype(half)

    @pl.loop(0, 6)
    def _(f):
        own = field[f + 1, 1:9].astype(f32)[:, 8:24].reshape(128, 128).astype(half)
        delta[pl.ds(pl.multiple_of(128 * f, 128), 128)] = own

    loads[1].wait()
    terms[pl.ds(3456, 8)] = jnp.zeros((8, 128), f32)
    weight_terms(hidden_ref, delta, terms, 0, 5)
    by_chip(terms, sending, 1, 0, 4)
    pl.semaphore_wait(barrier, len(everyone))
    swap_low = to_partner(1, 0)
    weight_terms(hidden_ref, delta, terms, 5, 9)
    by_chip(terms, sending, 1, 4, 8)
    swap_high = to_partner(1, 1)
    second_low = first_step(1, 0, swap_low)
    loads[2].wait()
    loads[3].wait()

    def back_frame(f):
        back = conv_rows(field, f, (0,), 8, taps)[:, 8:24].reshape(128, 128)
        value = (back * slope1_ref[f]).astype(half)
        delta[pl.ds(pl.multiple_of(128 * f, 128), 128)] = value

    pl.loop(0, 2)(back_frame)
    second_high = first_step(1, 1, swap_high)
    pl.loop(2, 6)(back_frame)
    loads[4].wait()
    second_low = second_step(1, 0, second_low)
    weight_terms(cells_ref, delta, terms, 0, 5)
    by_chip(terms, sending, 0, 0, 4)
    swap_low = to_partner(0, 0)
    second_high = second_step(1, 1, second_high)
    weight_terms(cells_ref, delta, terms, 5, 9)
    by_chip(terms, sending, 0, 4, 8)
    swap_high = to_partner(0, 1)
    first_low = first_step(0, 0, swap_low)
    moves_second = third_step(1, second_low + second_high)
    first_high = first_step(0, 1, swap_high)
    result(1, moves_second, second_out)
    first_low = second_step(0, 0, first_low)
    first_high = second_step(0, 1, first_high)
    result(0, third_step(0, first_low + first_high), first_out)


def f32_shape(*shape):
    return jax.ShapeDtypeStruct(shape, jnp.float32)


def places(text):
    return [pl.BlockSpec(memory_space=pltpu.VMEM if letter == "v" else pltpu.HBM) for letter in text]


def talking_call(kernel, ident, mebibytes, in_places, out_places, outs, scratch, *operands):
    return pl.pallas_call(
        kernel,
        out_shape=tuple(outs),
        in_specs=places(in_places),
        out_specs=tuple(places(out_places)),
        scratch_shapes=scratch,
        compiler_params=pltpu.CompilerParams(
            collective_id=ident, has_side_effects=True, vmem_limit_bytes=mebibytes * 2**20
        ),
    )(*operands)


def local(dec_input, target, conv_first, conv_second, rgb_weight, vgg_first, vgg_second, vgg_third):
    g, r, c = position()
    channels = dec_input.shape[-1]
    half, f32, dma, vmem = jnp.bfloat16, jnp.float32, pltpu.SemaphoreType.DMA, pltpu.VMEM
    cells, hidden, slope1, slope2, turned, colour_near, guide_near = talking_call(
        forward_kernel,
        3,
        58,
        "hvhhv",
        "hhhhhvv",
        (
            b16(8, 10, 16, 384), b16(8, 10, 16, 384), f32_shape(6, 128, 128), f32_shape(8, 10, 32, 128),
            b16(1152, 384),
            b16(3, 8, 16, 128), b16(3, 32, 128),
        ),
        [
            vmem((24, 8, 16, 128), half), vmem((3456, 128), half), vmem((3456, 128), half), vmem((16, 128), f32),
            vmem((12, 14, 32, 128), half), vmem((10, 12, 32, 128), half),
            vmem((10, 128, 128), f32), vmem((8, 10, 32, 128), f32), dma((3,)), dma((5,)),
            vmem((12, 8, 16, 128), half), vmem((8, 48, 128), half), vmem((8, 48, 128), half),
            vmem((8, 48, 128), half), vmem((8, 48, 128), half), vmem((2, 12, 3, 16, 128), half),
            vmem((2, 2, 3, 16, 128), half), vmem((2, 2, 3, 16, 128), half),
            vmem((2, 4, 3, 16, 128), half), vmem((2, 4, 3, 16, 128), half),
            dma((6,)), dma((6,)), dma((2, 8)), dma((2, 8)),
            vmem((1152, 384), half), vmem((1152, 384), half), vmem((1152, 384), half),
            vmem((8, 10, 16, 384), half), vmem((8, 10, 16, 384), half), vmem((6, 16, 128), half),
            dma((3, 6)), dma((3, 8)), dma(()),
        ],
        dec_input.reshape(24, 8, 16, channels), target, conv_first, conv_second, rgb_weight,
    )
    pixels = perceptual_strip(
        colour_near, guide_near, first_weights(vgg_first), (vgg_second.T, vgg_third)
    )
    sums = talking_call(
        backward_kernel,
        1,
        58,
        "vhhhhhv",
        "vv",
        (f32_shape(16, 128), f32_shape(16, 128)),
        [
            vmem((8, 10, 16, 384), half), vmem((8, 10, 16, 384), half), vmem((6, 128, 128), f32),
            vmem((8, 10, 32, 128), f32), vmem((1152, 384), half), vmem((16, 128), f32), dma((5,)),
            pltpu.VMEM((8, 10, 32, 128), half),
            pltpu.VMEM((768, 128), half),
            pltpu.VMEM((3464, 128), jnp.float32),
            pltpu.VMEM((2, 2, 8, 4, 4, 16, 128), half),
            pltpu.VMEM((2, 8, 4, 4, 16, 128), half),
            pltpu.VMEM((2, 8, 4, 4, 16, 128), half),
            pltpu.VMEM((2, 3, 4, 4, 16, 128), half),
            pltpu.VMEM((2, 3, 4, 4, 16, 128), half),
            pltpu.VMEM((2, 4, 4, 16, 128), half),
            pltpu.VMEM((2, 4, 4, 16, 128), half),
            pltpu.VMEM((2, 3, 4, 16, 128), half),
            pltpu.VMEM((2, 3, 4, 16, 128), half),
            pltpu.VMEM((2, 8, 16, 128), half),
            pltpu.VMEM((2, 7, 16, 128), half),
            dma((2, 21)),
            dma((2, 21)),
        ],
        pixels, cells, hidden, slope1, slope2, turned, rgb_weight,
    )
    return sums[0].reshape(2048)[:1728], sums[1].reshape(2048)[:1728]


def solution(mesh):
    in_specs = (
        P(None, None, "row", "col", None),
        P(None, None, "col", "row", None),
        P(),
        P(),
        P(),
        P(),
        P(),
        P(),
    )
    out_specs = (P(("grp", "row", "col")), P(("grp", "row", "col")))
    return jax.shard_map(local, mesh=mesh, in_specs=in_specs, out_specs=out_specs, check_vma=False)
```

```python
import functools

import jax
import jax.numpy as jnp
from jax import lax
from jax.experimental import pallas as pl
from jax.experimental.pallas import tpu as pltpu
from jax.sharding import PartitionSpec as P

MESH = pl.DeviceIdType.MESH

gelu_scale = 0.7978845608028654
gelu_cubic = 0.044715


def position():
    return lax.axis_index("grp"), lax.axis_index("row"), lax.axis_index("col")


def same_place(one, other):
    return (one[0] == other[0]) & (one[1] == other[1]) & (one[2] == other[2])


def row_count(r):
    return 1 + jnp.where(r > 0, 1, 0) + jnp.where(r < 7, 1, 0)


def in_vmem(count):
    return [pl.BlockSpec(memory_space=pltpu.VMEM)] * count


def b16(*shape):
    return jax.ShapeDtypeStruct(shape, jnp.bfloat16)


def transposed_dot(one, other):
    return lax.dot_general(one, other, (((0,), (0,)), ((), ())), preferred_element_type=jnp.float32)


def side_by_side(value):
    cols = value.shape[0]
    at = lax.broadcasted_iota(jnp.int32, value.shape, 0)
    before = jnp.where(at == 0, 0.0, pltpu.roll(value, 1, 0))
    after = jnp.where(at == cols - 1, 0.0, pltpu.roll(value, cols - 1, 0))
    return jnp.concatenate([before, value, after], axis=1).astype(jnp.bfloat16)


def three_rows(ref, row, count):
    parts = [ref[pl.ds(row + step, count)].reshape(-1, ref.shape[-1]) for step in range(3)]
    return jnp.concatenate(parts, axis=1)


def dot32(one, other):
    return jnp.dot(one, other, preferred_element_type=jnp.float32)


def gelu_both(preact, slope_too):
    square = preact * preact
    inner_tanh = jnp.tanh(gelu_scale * preact * (1.0 + gelu_cubic * square))
    half = 0.5 * (1.0 + inner_tanh)
    value = preact * half
    if not slope_too:
        return value, None
    bend = (0.5 * gelu_scale) * (1.0 + 3.0 * gelu_cubic * square)
    return value, half + preact * (1.0 - inner_tanh * inner_tanh) * bend


def perceptual_kernel(
    near_hbm, guide_hbm, vgg_first_ref, vgg_second_ref, vgg_third_ref, out_ref,
    near_ref, guide_ref, load_sem, first32, w1_ref, w1_back32, w1_back_ref, planes_ref, guides,
    taps, act1, slope1, pooled, delta3, diff2, slope2, delta2, delta1, tmp, pixels, strip,
    w2_ref, w3_ref, w3_back_ref, w2_back_ref, send_sem, recv_sem, own_sem,
):
    g, r, c = position()
    me = (g, r, c)
    barrier = pltpu.get_barrier_semaphore()
    perceives = g < 3
    own_frame = 8 * g + c
    home = own_frame // 6
    place = lax.rem(own_frame, 6)
    ahead = perceives & (place == 0) & (home > 0)
    behind = perceives & (place == 5) & (home < 3)

    def sources(do):
        for slot in range(8):
            source_frame = 6 * g - 1 + slot

            def each(step, slot=slot, source_frame=source_frame):
                source = (source_frame // 8, r + step, lax.rem(source_frame, 8))
                pl.when(jnp.logical_not(same_place(source, me)))(
                    functools.partial(do, step, slot, source)
                )

            pl.when((source_frame >= 0) & (source_frame < 24))(functools.partial(on_rows, r, each))

    def greet(step, slot, source):
        pl.semaphore_signal(barrier, inc=1, device_id=source, device_id_type=MESH)

    loads = [
        pltpu.make_async_copy(near_hbm, near_ref, load_sem.at[0]),
        pltpu.make_async_copy(guide_hbm, guide_ref, load_sem.at[1]),
    ]
    for load in loads:
        load.start()
    sources(greet)
    weight = vgg_first_ref[...].astype(jnp.float32)
    first32[...] = jnp.zeros((72, 128), jnp.float32)
    w1_back32[...] = jnp.zeros((8, 1152), jnp.float32)
    for t in range(9):
        block = weight[3 * t : 3 * t + 3]
        first32[8 * t : 8 * t + 3, 0:64] = block
        first32[8 * t + 3 : 8 * t + 6, 64:128] = block
        w1_back32[0:3, 128 * (8 - t) : 128 * (8 - t) + 64] = block
    w1_ref[...] = first32[...].astype(jnp.bfloat16)
    w1_back_ref[...] = w1_back32[...].astype(jnp.bfloat16)
    lay_out_perceptual(vgg_second_ref, vgg_third_ref, w2_ref, w3_ref, w3_back_ref, w2_back_ref)
    row0 = 8 * r - 8
    for load in loads:
        load.wait()
    kind = lax.broadcasted_iota(jnp.int32, (8, 128), 0)
    block = lax.broadcasted_iota(jnp.int32, (8, 128), 1) // 16
    for part in range(3):
        guides[...] = guide_ref[part].astype(jnp.float32)
        tiles = [near_ref[part, column].astype(jnp.float32)[0:8] for column in range(8)]
        here = (kind < 3) & (row0 + 8 * part >= 0) & (row0 + 8 * part < 64)
        seen = (row0 + 8 * part >= 0) & (row0 + 8 * part < 64)
        for i in range(8):
            image = jnp.zeros((8, 128), jnp.float32)
            for column in range(8):
                turned = pltpu.roll(tiles[column], (16 * column - 16 * i) % 128, 1)
                image = jnp.where(block == column, turned, image)
            planes_ref[8 * part + i] = jnp.where(here, image, 0.0)
            planes_ref[8 * part + i, 3:6] = jnp.where(seen, guides[pl.ds(i, 3, 8)], 0.0)
    lane = lax.broadcasted_iota(jnp.int32, (192, 128), 1)
    planes = planes_ref[...].reshape(192, 128)
    before = jnp.where(lane == 0, 0.0, pltpu.roll(planes, 1, 1))
    after = jnp.where(lane == 127, 0.0, pltpu.roll(planes, 127, 1))
    taps[:, 0:8] = before.reshape(24, 8, 128)
    taps[:, 8:16] = planes.reshape(24, 8, 128)
    taps[:, 16:24] = after.reshape(24, 8, 128)

    def shown(row):
        return (row0 + row >= 0) & (row0 + row < 64)

    def kept(row, value):
        return jnp.where(shown(row), value, 0.0)

    def first_rows(low, high, slope_too):
        @pl.loop(low, high, unroll=2)
        def _(i):
            cells = taps[pl.ds(i, 3)].reshape(72, 128).astype(jnp.bfloat16)
            value, slope = gelu_both(transposed_dot(cells, w1_ref[...]), slope_too)
            act1[i] = side_by_side(kept(i + 1, value))
            if slope_too:
                slope1[i - 6] = slope

    first_rows(0, 6, False)
    first_rows(6, 16, True)
    first_rows(16, 22, False)

    def second_rows(low, high, slope_too):
        @pl.loop(low, high, unroll=2)
        def _(p):
            plane = dot32(three_rows(act1, 2 * p, 2), w2_ref[...])
            value, slope = gelu_both(plane, slope_too)
            value = kept(2 * p + 2, value)
            if slope_too:
                difference = 0.25 * (value - pltpu.roll(value, 64, 1))
                diff2[pl.ds(2 * p - 4, 2)] = difference.reshape(2, 128, 128)
                slope2[pl.ds(2 * p - 4, 2)] = slope.reshape(2, 128, 128)
            tmp[...] = value[:128] + value[128:]
            mean = 0.25 * (tmp[pl.ds(0, 64, 2)] + tmp[pl.ds(1, 64, 2)])
            pooled[p] = side_by_side(mean)

    second_rows(0, 2, False)
    second_rows(2, 8, True)
    second_rows(8, 10, False)

    @pl.loop(0, 4, unroll=2)
    def _(half):
        j = 2 * half
        plane = dot32(three_rows(pooled, j, 2), w3_ref[...])
        value, slope = gelu_both(plane[:, :128], True)
        guide, _ = gelu_both(plane[:, 128:], False)
        delta = 0.5 * (value - guide) * slope
        delta3[j] = side_by_side(kept(2 * j + 4, delta[:64]))
        delta3[j + 1] = side_by_side(kept(2 * j + 6, delta[64:]))

    @pl.loop(0, 6, unroll=3)
    def _(m):
        grad = 0.25 * dot32(three_rows(delta3, m, 1), w3_back_ref[...])
        tmp[pl.ds(0, 64, 2)] = grad
        tmp[pl.ds(1, 64, 2)] = grad
        spread = tmp[...]
        for k in range(2):
            delta = (spread + diff2[2 * m + k]) * slope2[2 * m + k]
            delta2[2 * m + k] = side_by_side(kept(2 * m + 6, delta))

    @pl.loop(0, 5, unroll=5)
    def _(half):
        n = 2 * half
        grad = dot32(three_rows(delta2, n, 2), w2_back_ref[...])
        for k in range(2):
            delta = grad[128 * k : 128 * (k + 1)] * slope1[n + k]
            delta1[n + k] = side_by_side(kept(n + k + 7, delta))

    @pl.loop(0, 8, unroll=4)
    def _(q):
        grad = lax.dot_general(
            w1_back_ref[...],
            three_rows(delta1, q, 1),
            (((1,), (1,)), ((), ())),
            preferred_element_type=jnp.float32,
        )
        own = planes_ref[q + 8]
        direct = (1.0 / 6.0) * (own - pltpu.roll(own, 5, 0))
        pixels[pl.ds(pl.multiple_of(q * 8, 8), 8)] = grad + direct

    colour_rows = [pixels[pl.ds(k, 8, 8)] for k in range(3)]
    third = lax.broadcasted_iota(jnp.int32, (8, 128), 1) // 32
    for column in range(8):
        turned = [pltpu.roll(v, (32 * k + 8 - 16 * column) % 128, 1) for k, v in enumerate(colour_rows)]
        part = jnp.where(third == 0, turned[0], jnp.where(third == 1, turned[1], turned[2]))
        strip[column] = jnp.concatenate([part, jnp.zeros((8, 128), jnp.float32)], axis=0).astype(jnp.bfloat16)

    groups = jnp.where(perceives, 1, 0) + jnp.where(ahead, 1, 0) + jnp.where(behind, 1, 0)
    to_itself = perceives & (home == g) | ahead & (home == g + 1) | behind & (home == g - 1)
    awaited = 8 * row_count(r) * groups - jnp.where(to_itself, 1, 0)
    pl.when(perceives)(lambda: pl.semaphore_wait(barrier, awaited))

    def targets(do):
        for kind, (group, needed) in enumerate(((home, perceives), (home - 1, ahead), (home + 1, behind))):

            def each(step, kind=kind, group=group):
                for column in range(8):
                    peer = (group, r + step, column)
                    do(kind, step, column, peer, jnp.logical_not(same_place(peer, me)))

            pl.when(needed)(functools.partial(on_rows, r, each))

    def outgoing(kind, step, column, peer):
        place_there = own_frame - 6 * peer[0] + 1
        return pltpu.make_async_remote_copy(
            src_ref=strip.at[column],
            dst_ref=out_ref.at[place_there, 1 - step],
            send_sem=send_sem.at[kind, step + 1, column],
            recv_sem=recv_sem.at[place_there, 1 - step],
            device_id=peer,
            device_id_type=MESH,
        )

    def kept():
        return pltpu.make_async_copy(strip.at[c], out_ref.at[own_frame - 6 * g + 1, 1], own_sem)

    def start(kind, step, column, peer, away):
        pl.when(away)(lambda: outgoing(kind, step, column, peer).start())
        if step == 0:
            pl.when(jnp.logical_not(away))(lambda: kept().start())

    def finish(kind, step, column, peer, away):
        pl.when(away)(lambda: outgoing(kind, step, column, peer).wait_send())
        if step == 0:
            pl.when(jnp.logical_not(away))(lambda: kept().wait())

    def arrive(step, slot, source):
        pltpu.make_async_remote_copy(
            src_ref=strip.at[0],
            dst_ref=out_ref.at[slot, step + 1],
            send_sem=send_sem.at[0, 0, 0],
            recv_sem=recv_sem.at[slot, step + 1],
            device_id=source,
            device_id_type=MESH,
        ).wait_recv()

    targets(start)
    sources(arrive)
    targets(finish)


def perceptual_strip(near, guides, *weights):
    f32, half = jnp.float32, jnp.bfloat16
    return pl.pallas_call(
        perceptual_kernel,
        out_shape=b16(8, 3, 16, 128),
        in_specs=places("hhvvv"),
        out_specs=in_vmem(1)[0],
        scratch_shapes=[
            pltpu.VMEM((3, 8, 16, 128), half),
            pltpu.VMEM((3, 32, 128), half),
            pltpu.SemaphoreType.DMA((2,)),
            pltpu.VMEM((72, 128), f32),
            pltpu.VMEM((72, 128), half),
            pltpu.VMEM((8, 1152), f32),
            pltpu.VMEM((8, 1152), half),
            pltpu.VMEM((24, 8, 128), f32),
            pltpu.VMEM((32, 128), f32),
            pltpu.VMEM((24, 24, 128), f32),
            pltpu.VMEM((22, 128, 384), half),
            pltpu.VMEM((10, 128, 128), f32),
            pltpu.VMEM((10, 64, 384), half),
            pltpu.VMEM((8, 64, 384), half),
            pltpu.VMEM((12, 128, 128), f32),
            pltpu.VMEM((12, 128, 128), f32),
            pltpu.VMEM((12, 128, 384), half),
            pltpu.VMEM((10, 128, 384), half),
            pltpu.VMEM((128, 128), f32),
            pltpu.VMEM((64, 128), f32),
            pltpu.VMEM((8, 16, 128), half),
            pltpu.VMEM((1152, 128), half),
            pltpu.VMEM((1152, 256), half),
            pltpu.VMEM((1152, 128), half),
            pltpu.VMEM((1152, 128), half),
            pltpu.SemaphoreType.DMA((3, 3, 8)),
            pltpu.SemaphoreType.DMA((8, 3)),
            pltpu.SemaphoreType.DMA(()),
        ],
        compiler_params=pltpu.CompilerParams(
            collective_id=4, has_side_effects=True, vmem_limit_bytes=58 * 2**20
        ),
    )(near, guides, *weights)


def taps_in_lanes(weight_ref, out_ref):
    for q in range(9):
        for k in range(3):
            tap = 3 * q + k
            out_ref[128 * q : 128 * (q + 1), 128 * k : 128 * (k + 1)] = weight_ref[
                128 * tap : 128 * (tap + 1), :
            ]


def turned_taps(weight_ref, out_ref):
    for q in range(9):
        for k in range(3):
            tap = 26 - 3 * q - k
            block = weight_ref[128 * tap : 128 * (tap + 1), :].astype(jnp.float32)
            out_ref[128 * q : 128 * (q + 1), 128 * k : 128 * (k + 1)] = block.T.astype(jnp.bfloat16)


def conv_rows(source, frame, starts, count, taps_ref):
    size = len(starts) * count * 32

    def near(dt, dr):
        rows = [source[frame + dt, pl.ds(start + dr, count)].reshape(count * 32, 128) for start in starts]
        return rows[0] if len(rows) == 1 else jnp.concatenate(rows, axis=0)

    parts = [near(dt, dr) for dt in range(3) for dr in range(3)]
    sums = dot32(jnp.concatenate(parts, axis=1), taps_ref[...])
    total = pltpu.roll(sums[:, :128], 1, 0) + sums[:, 128:256]
    total += pltpu.roll(sums[:, 256:], size - 1, 0)
    return total.reshape(len(starts) * count, 32, 128)


def silu_parts(preact):
    gate = 0.5 * (1.0 + jnp.tanh(0.5 * preact))
    return preact * gate, gate * (1.0 + preact * (1.0 - gate))


def on_rows(r, do):
    for step in (-1, 1, 0):
        pl.when((r + step >= 0) & (r + step < 8))(functools.partial(do, step))


def lay_out_perceptual(second_ref, third_ref, w2_out, w3_out, w3_back_out, w2_back_out):
    f32, half = jnp.float32, jnp.bfloat16
    for t in range(9):
        turned_block = second_ref[:, 64 * t : 64 * (t + 1)].astype(f32)
        block = turned_block.T
        wide = third_ref[64 * t : 64 * (t + 1), :].astype(f32)
        none, low, high = jnp.zeros((64, 64), f32), 128 * t, 128 * (8 - t)
        w2_out[low : low + 64] = jnp.concatenate([block, none], axis=1).astype(half)
        w2_out[low + 64 : low + 128] = jnp.concatenate([none, block], axis=1).astype(half)
        w3_out[low : low + 64, :128] = wide.astype(half)
        w3_out[low : low + 64, 128:] = jnp.zeros((64, 128), half)
        w3_out[low + 64 : low + 128, :128] = jnp.zeros((64, 128), half)
        w3_out[low + 64 : low + 128, 128:] = wide.astype(half)
        w2_back_out[high : high + 64] = jnp.concatenate([turned_block, none], axis=1).astype(half)
        w2_back_out[high + 64 : high + 128] = jnp.zeros((64, 128), half)
        turned = jnp.concatenate([wide.T, jnp.zeros((128, 64), f32)], axis=1)
        w3_back_out[high : high + 128] = turned.astype(half)


def forward_kernel(
    video_hbm, target_ref, first_hbm, second_hbm, rgb_ref,
    cells_hbm, hidden_hbm, slope1_hbm, slope2_hbm, turned_hbm, near_out, guide_out,
    video, first_ref, second_ref, rgb16, cells, hidden_out, slope1_out, slope2_out, load_sem, store_sem,
    tile, left_send, right_send, left_in, right_in, rows_in, to_west, to_east, from_east, from_west,
    halo_send, halo_recv, edge_send, edge_recv,
    taps1, taps2, turned, cell_columns, hidden_columns, colours, send_sem, recv_sem, own_sem,
):
    loads = [
        pltpu.make_async_copy(video_hbm, video, load_sem.at[0]),
        pltpu.make_async_copy(first_hbm, first_ref, load_sem.at[1]),
        pltpu.make_async_copy(second_hbm, second_ref, load_sem.at[2]),
    ]
    for load in loads:
        load.start()
    g, r, c = position()
    me = (g, r, c)
    f32, half = jnp.float32, jnp.bfloat16
    barrier = pltpu.get_barrier_semaphore()
    perceives = g < 3
    source_group = (8 * g + c) // 6
    west, east = lax.rem(c + 7, 8), lax.rem(c + 1, 8)
    has_up, has_down = r > 0, r < 7
    has_prev, has_next = g > 0, g < 3

    def sources(do):
        def each(step):
            for column in range(8):
                source = (source_group, r + step, column)
                pl.when(jnp.logical_not(same_place(source, me)))(
                    functools.partial(do, step, column, source)
                )

        pl.when(perceives)(lambda: on_rows(r, each))

    def signal(peer):
        pl.semaphore_signal(barrier, inc=1, device_id=peer, device_id_type=MESH)

    signal((g, r, west))
    signal((g, r, east))

    pl.when(has_up)(lambda: signal((g, r - 1, c)))
    pl.when(has_down)(lambda: signal((g, r + 1, c)))

    @pl.when(has_prev)
    def _():
        for column in (west, c, east):
            signal((g - 1, r, column))

    @pl.when(has_next)
    def _():
        for column in (west, c, east):
            signal((g + 1, r, column))

    sources(lambda step, column, source: signal(source))

    block = jnp.minimum(g, 2)
    guide = [target_ref[k, block, 0].astype(f32) for k in range(3)] + [jnp.zeros((8, 128), f32)]
    guide_out[1] = jnp.concatenate(guide, axis=0).astype(half)
    rgb16[...] = jnp.zeros((16, 128), f32)
    rgb16[0:3] = rgb_ref[...].astype(f32)
    loads[0].wait()

    for f in range(12):
        frame = 6 * g - 3 + f
        value = video[jnp.minimum(jnp.maximum(frame, 0), 23)]
        tile[f] = jnp.where((frame >= 0) & (frame < 24), value, jnp.zeros_like(value))

    to_itself = jnp.where(perceives & (2 * g + c < 6), 1, 0)
    groups_near = jnp.where(has_prev, 1, 0) + jnp.where(has_next, 1, 0)
    pl.semaphore_wait(barrier, 7 * row_count(r) + 1 + 3 * groups_near - to_itself)

    def remote(src, dst, slot, peer):
        return pltpu.make_async_remote_copy(
            src_ref=src,
            dst_ref=dst,
            send_sem=halo_send.at[slot],
            recv_sem=halo_recv.at[slot],
            device_id=peer,
            device_id_type=MESH,
        )

    sideways = [remote(left_send, right_in, 0, (g, r, west)), remote(right_send, left_in, 1, (g, r, east))]

    def to_row(row_index, rows, edge, guide_slot, first_slot):
        strip = tile.at[pl.ds(3, 6), pl.ds(rows, 3)]
        return [
            remote(strip, rows_in.at[edge, pl.ds(3, 6)], first_slot, (g, row_index, c)),
            remote(guide_out.at[1], guide_out.at[guide_slot], first_slot + 1, (g, row_index, c)),
        ]

    upward = to_row(r - 1, 0, 1, 2, 2)
    downward = to_row(r + 1, 5, 0, 0, 4)

    def across(edge):
        def copy(src, dst, slot, peer):
            return pltpu.make_async_remote_copy(
                src_ref=src,
                dst_ref=dst,
                send_sem=edge_send.at[edge, slot],
                recv_sem=edge_recv.at[edge, slot],
                device_id=peer,
                device_id_type=MESH,
            )

        mine, wests, easts = rows_in.at[edge], to_west.at[edge], to_east.at[edge]
        in_east, in_west, two = from_east.at[edge], from_west.at[edge], pl.ds(1, 2)
        level = [
            copy(wests, in_east.at[two], 0, (g, r, west)),
            copy(easts, in_west.at[two], 1, (g, r, east)),
        ]
        onward = [
            copy(mine.at[pl.ds(6, 3)], mine.at[pl.ds(0, 3)], 2, (g + 1, r, c)),
            copy(wests.at[1], in_east.at[0], 3, (g + 1, r, west)),
            copy(easts.at[1], in_west.at[0], 4, (g + 1, r, east)),
        ]
        back = [
            copy(mine.at[pl.ds(3, 3)], mine.at[pl.ds(9, 3)], 5, (g - 1, r, c)),
            copy(wests.at[0], in_east.at[3], 6, (g - 1, r, west)),
            copy(easts.at[0], in_west.at[3], 7, (g - 1, r, east)),
        ]
        return level, onward, back

    edges = [across(0), across(1)]

    def pass_on(edge):
        values = [rows_in[edge, 3 + f].astype(f32) for f in range(6)]
        for part in range(2):
            near = values[3 * part : 3 * part + 3]
            spare = jnp.zeros((3, 4, 128), f32)
            to_west[edge, part] = jnp.concatenate([v[:, 0:4] for v in near] + [spare], axis=1).astype(half)
            to_east[edge, part] = jnp.concatenate([v[:, 12:16] for v in near] + [spare], axis=1).astype(half)
        level, onward, back = edges[edge]
        start(level)
        pl.when(has_next)(lambda: start(onward))
        pl.when(has_prev)(lambda: start(back))

    def passed(edge, done):
        level, onward, back = edges[edge]
        done(level)
        if done is landed:
            pl.when(has_prev)(lambda: done(onward))
            pl.when(has_next)(lambda: done(back))
        else:
            pl.when(has_next)(lambda: done(onward))
            pl.when(has_prev)(lambda: done(back))

    def start(copies):
        for copy in copies:
            copy.start()

    def sent(copies):
        for copy in copies:
            copy.wait_send()

    def landed(copies):
        for copy in copies:
            copy.wait_recv()

    pl.when(has_up)(lambda: start(upward))
    pl.when(has_down)(lambda: start(downward))
    for line in range(8):
        near = [tile[f, line].astype(f32) for f in range(12)]
        left_send[line] = jnp.concatenate([v[0:4] for v in near], axis=0).astype(half)
        right_send[line] = jnp.concatenate([v[12:16] for v in near], axis=0).astype(half)
    start(sideways)

    loads[1].wait()
    taps_in_lanes(first_ref, taps1)
    loads[2].wait()
    taps_in_lanes(second_ref, taps2)

    def assemble(first_row, count, real, own, left, right, per):
        col = lax.broadcasted_iota(jnp.int32, (count, 32, 128), 1) + (16 * c - 8)
        shown = (col >= 0) & (col < 128) & real
        for part in range(12 // per):
            before, after = left(part).astype(f32), right(part).astype(f32)
            for k in range(per):
                f, eight = per * part + k, slice(8 * (k // 2), 8 * (k // 2) + 8)
                one = before[:, eight].reshape(8 * count, 128)
                two = after[:, eight].reshape(8 * count, 128)
                if k % 2 == 0:
                    one = pltpu.roll(one, 4, 0)
                else:
                    two = pltpu.roll(two, 8 * count - 4, 0)
                sides = [one.reshape(count, 8, 128), own(f).astype(f32), two.reshape(count, 8, 128)]
                frame = 6 * g - 3 + f
                here = shown & (frame >= 0) & (frame < 24)
                value = jnp.where(here, jnp.concatenate(sides, axis=1), 0.0)
                cells[f, first_row : first_row + count] = value.astype(half)

    row = lax.broadcasted_iota(jnp.int32, (6, 32, 128), 0)
    col = lax.broadcasted_iota(jnp.int32, (6, 32, 128), 1) + (16 * c - 8)
    in_cols = (col >= 0) & (col < 128)

    def in_frames(f):
        frame = 6 * g - 2 + f
        return jnp.where((frame >= 0) & (frame < 24), 1.0, 0.0)

    landed(sideways)
    assemble(
        3, 8, r >= 0, lambda f: tile[f],
        lambda part: left_in[:, 16 * part : 16 * (part + 1)],
        lambda part: right_in[:, 16 * part : 16 * (part + 1)],
        4,
    )

    def inner(f):
        value, slope = silu_parts(conv_rows(cells, f, (3,), 6, taps1))
        value = jnp.where(in_cols, value, 0.0) * in_frames(f)
        hidden_out[f, 3:9] = value.astype(half)
        slope1_out[f, 16:112] = slope[:, 8:24].reshape(96, 128)

    pl.loop(0, 2, unroll=2)(inner)

    @pl.when(has_up)
    def _():
        landed(downward)
        pass_on(0)

    @pl.when(has_down)
    def _():
        landed(upward)
        pass_on(1)

    pl.loop(2, 10, unroll=2)(inner)

    pl.when(has_up)(lambda: passed(0, landed))
    pl.when(has_down)(lambda: passed(1, landed))
    for edge, real in ((0, has_up), (1, has_down)):
        assemble(
            11 * edge, 3, real,
            lambda f, edge=edge: rows_in[edge, f],
            lambda part, edge=edge: from_west[edge, part],
            lambda part, edge=edge: from_east[edge, part],
            3,
        )
    image_row = jnp.where(row < 3, row, row + 6) + (8 * r - 2)
    in_image = in_cols & (image_row >= 0) & (image_row < 64)

    @pl.loop(0, 10, unroll=2)
    def _(f):
        value, slope = silu_parts(conv_rows(cells, f, (0, 9), 3, taps1))
        value = (jnp.where(in_image, value, 0.0) * in_frames(f)).astype(half)
        hidden_out[f, 0:3] = value[0:3]
        hidden_out[f, 9:12] = value[3:6]
        slope1_out[f, 0:16] = slope[2, 8:24]
        slope1_out[f, 112:128] = slope[3, 8:24]

    stores = [
        pltpu.make_async_copy(slope1_out.at[pl.ds(2, 6)], slope1_hbm, store_sem.at[0]),
        pltpu.make_async_copy(slope2_out, slope2_hbm, store_sem.at[1]),
        pltpu.make_async_copy(hidden_columns, hidden_hbm, store_sem.at[2]),
        pltpu.make_async_copy(cell_columns, cells_hbm, store_sem.at[3]),
        pltpu.make_async_copy(turned, turned_hbm, store_sem.at[4]),
    ]
    stores[0].start()

    def target(step, slot):
        frame = 6 * g + slot
        return (frame // 8, r + step, lax.rem(frame, 8))

    def outgoing(step, slot):
        return pltpu.make_async_remote_copy(
            src_ref=colours.at[slot],
            dst_ref=near_out.at[1 - step, c],
            send_sem=send_sem.at[step + 1, slot],
            recv_sem=recv_sem.at[1 - step, c],
            device_id=target(step, slot),
            device_id_type=MESH,
        )

    def kept(slot):
        return pltpu.make_async_copy(colours.at[slot], near_out.at[1, c], own_sem)

    def start_colour(slot, step):
        away = jnp.logical_not(same_place(target(step, slot), me))
        pl.when(away)(lambda: outgoing(step, slot).start())
        if step == 0:
            pl.when(jnp.logical_not(away))(lambda: kept(slot).start())

    def finish(slot, step):
        away = jnp.logical_not(same_place(target(step, slot), me))
        pl.when(away)(lambda: outgoing(step, slot).wait_send())
        if step == 0:
            pl.when(jnp.logical_not(away))(lambda: kept(slot).wait())

    def arrive(step, column, source):
        pltpu.make_async_remote_copy(
            src_ref=colours.at[0],
            dst_ref=near_out.at[step + 1, column],
            send_sem=send_sem.at[0, 0],
            recv_sem=recv_sem.at[step + 1, column],
            device_id=source,
            device_id_type=MESH,
        ).wait_recv()

    @pl.loop(0, 6)
    def _(slot):
        value, slope = silu_parts(conv_rows(hidden_out, slot + 1, (0,), 10, taps2))
        slope2_out[slot + 1] = slope
        own = value[1:9, 8:24].reshape(128, 128).astype(jnp.bfloat16)
        colour = lax.dot_general(
            rgb16[...].astype(half), own, (((1,), (1,)), ((), ())), preferred_element_type=jnp.float32
        )
        colours[slot] = colour.astype(jnp.bfloat16)
        on_rows(r, functools.partial(start_colour, slot))

    @pl.loop(0, 2)
    def _(end):
        slope2_out[7 * end] = silu_parts(conv_rows(hidden_out, 7 * end, (0,), 10, taps2))[1]

    stores[1].start()
    columns_in_lanes(hidden_out, 1, 1, hidden_columns)
    stores[2].start()
    columns_in_lanes(cells, 2, 2, cell_columns)
    stores[3].start()
    turned_taps(second_ref, turned)
    stores[4].start()
    sources(arrive)

    @pl.loop(0, 6)
    def _(slot):
        on_rows(r, functools.partial(finish, slot))

    for store in stores:
        store.wait()

    sent(sideways)
    pl.when(has_up)(lambda: sent(upward))
    pl.when(has_down)(lambda: sent(downward))
    pl.when(has_up)(lambda: passed(0, sent))
    pl.when(has_down)(lambda: passed(1, sent))


def columns_in_lanes(source, frame0, row0, out_ref):
    @pl.loop(0, 8)
    def _(f):
        value = source[f + frame0, pl.ds(row0, 10)].reshape(320, 128).astype(jnp.float32)
        parts = [pltpu.roll(value, 1, 0), value, pltpu.roll(value, 319, 0)]
        for k, part in enumerate(parts):
            own = part.reshape(10, 32, 128)[:, 8:24]
            out_ref[f, :, :, 128 * k : 128 * (k + 1)] = own.astype(jnp.bfloat16)


def weight_terms(columns, delta, terms, low, high):
    @pl.loop(low, high)
    def _(q):
        cells = columns[pl.ds(q // 3, 6), pl.ds(lax.rem(q, 3), 8)].reshape(768, 384)
        terms[pl.ds(pl.multiple_of(384 * q, 384), 384)] = transposed_dot(cells, delta[...])


def by_chip(terms, out_ref, which, low, high):
    @pl.loop(low, high)
    def _(z):
        for chip in range(16):
            start = 432 * z + 27 * chip
            out_ref[which, 0, z, chip // 4, chip % 4] = terms[pl.ds(start, 16)].astype(jnp.bfloat16)
            out_ref[which, 1, z, chip // 4, chip % 4] = terms[pl.ds(start + 13, 16)].astype(jnp.bfloat16)


def backward_kernel(
    pixel_hbm, cells_hbm, hidden_hbm, slope1_hbm, slope2_hbm, turned_hbm, rgb_ref, out_ref,
    pixel_ref, cells_ref, hidden_ref, slope1_ref, slope2_ref, taps, rgb16, load_sem,
    field, delta, terms,
    sending, core_in, held, x_in, y_in, mid_x, mid_y, yy_in, xx_in, last, z_in, send_sem, recv_sem,
):
    g, r, c = position()
    loads = [
        pltpu.make_async_copy(src, dst, load_sem.at[k])
        for k, (src, dst) in enumerate(
            (
                (slope2_hbm, slope2_ref), (hidden_hbm, hidden_ref), (turned_hbm, taps),
                (slope1_hbm, slope1_ref), (cells_hbm, cells_ref), (pixel_hbm, pixel_ref),
            )
        )
    ]
    for load in loads:
        load.start()
    zh, x, y, core = r // 4, lax.rem(r, 4), c // 2, lax.rem(c, 2)
    z = g * 2 + zh
    other = 1 - core

    def at_x(step):
        return (g, zh * 4 + lax.rem(x + step, 4), c)

    def at_y(step):
        return (g, r, lax.rem(y + step, 4) * 2 + core)

    def at_z(step):
        to = lax.rem(z + step, 8)
        return (to // 2, lax.rem(to, 2) * 4 + x, c)

    partner = (g, r, y * 2 + other)
    barrier = pltpu.get_barrier_semaphore()
    everyone = [partner] + [at_x(s) for s in (1, 2, 3)] + [at_y(s) for s in (1, 2, 3)]
    everyone += [at_z(s) for s in range(1, 8)]
    for peer in everyone:
        pl.semaphore_signal(barrier, inc=1, device_id=peer, device_id_type=MESH)

    def send(src, dst, which, slot, peer):
        copy = pltpu.make_async_remote_copy(
            src_ref=src,
            dst_ref=dst,
            send_sem=send_sem.at[which, slot],
            recv_sem=recv_sem.at[which, slot],
            device_id=peer,
            device_id_type=MESH,
        )
        copy.start()
        return copy

    f32, half = jnp.float32, jnp.bfloat16

    def summed(own, received):
        total = own.astype(f32)
        for k in range(3):
            total += received[k].astype(f32)
        return total.astype(half)

    def to_partner(which, part):
        some = pl.ds(4 * part, 4)
        return send(sending.at[which, other, some], core_in.at[which, some], which, 20 * part, partner)

    def first_step(which, part, copy):
        copy.wait()

        @pl.loop(4 * part, 4 * part + 4)
        def _(k):
            pair = sending[which, core, k].astype(f32) + core_in[which, k].astype(f32)
            held[which, k] = pair.astype(half)

        some = held.at[which, pl.ds(4 * part, 4)]
        if part == 0:
            return [
                send(some.at[:, lax.rem(x + s, 4)], x_in.at[which, s - 1], which, s, at_x(s)) for s in (1, 2, 3)
            ]
        return [
            send(some.at[:, :, lax.rem(y + s, 4)], y_in.at[which, s - 1], which, 3 + s, at_y(s)) for s in (1, 2, 3)
        ]

    def second_step(which, part, copies):
        for copy in copies:
            copy.wait()
        if part == 0:
            mid_x[which] = summed(held[which, 0:4, x], [x_in[which, k] for k in range(3)])
            return [
                send(mid_x.at[which, :, lax.rem(y + s, 4)], yy_in.at[which, s - 1], which, 6 + s, at_y(s))
                for s in (1, 2, 3)
            ]
        mid_y[which] = summed(held[which, 4:8, :, y], [y_in[which, k] for k in range(3)])
        return [
            send(mid_y.at[which, :, lax.rem(x + s, 4)], xx_in.at[which, s - 1], which, 9 + s, at_x(s))
            for s in (1, 2, 3)
        ]

    def third_step(which, copies):
        for copy in copies:
            copy.wait()
        last[which, 0:4] = summed(mid_x[which, :, y], [yy_in[which, k] for k in range(3)])
        last[which, 4:8] = summed(mid_y[which, :, x], [xx_in[which, k] for k in range(3)])
        return [
            send(last.at[which, lax.rem(z + s, 8)], z_in.at[which, s - 1], which, 12 + s, at_z(s))
            for s in range(1, 8)
        ]

    def result(which, copies):
        for copy in copies:
            copy.wait()
        total = last[which, z].astype(f32)
        for k in range(7):
            total += z_in[which, k].astype(f32)
        turned = pltpu.roll(total, 64, 1)
        low_half = lax.broadcasted_iota(jnp.int32, (16, 128), 1) < 64
        shifted = jnp.where(low_half, turned, pltpu.roll(turned, 15, 0))
        out_ref[which] = jnp.where(core == 1, shifted, total)

    rgb16[...] = jnp.zeros((16, 128), f32)
    rgb16[0:3] = rgb_ref[...].astype(f32)
    loads[0].wait()
    loads[5].wait()

    lane = lax.broadcasted_iota(jnp.int32, (8, 128), 1)
    col = lax.rem(lane, 32) + (16 * c - 8)
    in_cols = (lane < 96) & (col >= 0) & (col < 128)

    @pl.loop(0, 8, unroll=2)
    def _(f):
        frame = 6 * g - 1 + f
        known = in_cols & (frame >= 0) & (frame < 24)
        parts = []
        for part in range(3):
            seen = known & (r + part - 1 >= 0) & (r + part - 1 < 8)
            parts.append(jnp.where(seen, pixel_ref[f, part].astype(f32)[0:8], 0.0))
        turned = jnp.concatenate(parts, axis=0).T
        for i in range(10):
            hidden_grad = turned[0:32, i + 7 : i + 8] * rgb16[0:1]
            for k in (1, 2):
                hidden_grad += turned[32 * k : 32 * (k + 1), i + 7 : i + 8] * rgb16[k : k + 1]
            field[f, i] = (hidden_grad * slope2_ref[f, i]).astype(half)

    @pl.loop(0, 6)
    def _(f):
        own = field[f + 1, 1:9].astype(f32)[:, 8:24].reshape(128, 128).astype(half)
        delta[pl.ds(pl.multiple_of(128 * f, 128), 128)] = own

    loads[1].wait()
    terms[pl.ds(3456, 8)] = jnp.zeros((8, 128), f32)
    weight_terms(hidden_ref, delta, terms, 0, 5)
    by_chip(terms, sending, 1, 0, 4)
    pl.semaphore_wait(barrier, len(everyone))
    swap_low = to_partner(1, 0)
    weight_terms(hidden_ref, delta, terms, 5, 9)
    by_chip(terms, sending, 1, 4, 8)
    swap_high = to_partner(1, 1)
    second_low = first_step(1, 0, swap_low)
    loads[2].wait()
    loads[3].wait()

    def back_frame(f):
        back = conv_rows(field, f, (0,), 8, taps)[:, 8:24].reshape(128, 128)
        value = (back * slope1_ref[f]).astype(half)
        delta[pl.ds(pl.multiple_of(128 * f, 128), 128)] = value

    pl.loop(0, 2, unroll=2)(back_frame)
    second_high = first_step(1, 1, swap_high)
    pl.loop(2, 6, unroll=2)(back_frame)
    loads[4].wait()
    second_low = second_step(1, 0, second_low)
    weight_terms(cells_ref, delta, terms, 0, 5)
    by_chip(terms, sending, 0, 0, 4)
    swap_low = to_partner(0, 0)
    second_high = second_step(1, 1, second_high)
    weight_terms(cells_ref, delta, terms, 5, 9)
    by_chip(terms, sending, 0, 4, 8)
    swap_high = to_partner(0, 1)
    first_low = first_step(0, 0, swap_low)
    moves_second = third_step(1, second_low + second_high)
    first_high = first_step(0, 1, swap_high)
    result(1, moves_second)
    first_low = second_step(0, 0, first_low)
    first_high = second_step(0, 1, first_high)
    result(0, third_step(0, first_low + first_high))


def f32_shape(*shape):
    return jax.ShapeDtypeStruct(shape, jnp.float32)


def places(text):
    return [pl.BlockSpec(memory_space=pltpu.VMEM if letter == "v" else pltpu.HBM) for letter in text]


def talking_call(kernel, ident, mebibytes, in_places, out_places, outs, scratch, *operands):
    return pl.pallas_call(
        kernel,
        out_shape=tuple(outs),
        in_specs=places(in_places),
        out_specs=tuple(places(out_places)),
        scratch_shapes=scratch,
        compiler_params=pltpu.CompilerParams(
            collective_id=ident, has_side_effects=True, vmem_limit_bytes=mebibytes * 2**20
        ),
    )(*operands)


def local(dec_input, target, conv_first, conv_second, rgb_weight, vgg_first, vgg_second, vgg_third):
    g, r, c = position()
    channels = dec_input.shape[-1]
    half, f32, dma, vmem = jnp.bfloat16, jnp.float32, pltpu.SemaphoreType.DMA, pltpu.VMEM
    cells, hidden, slope1, slope2, turned, colour_near, guide_near = talking_call(
        forward_kernel,
        3,
        58,
        "hvhhv",
        "hhhhhvv",
        (
            b16(8, 10, 16, 384), b16(8, 10, 16, 384), f32_shape(6, 128, 128), f32_shape(8, 10, 32, 128),
            b16(1152, 384),
            b16(3, 8, 16, 128), b16(3, 32, 128),
        ),
        [
            vmem((24, 8, 16, 128), half), vmem((3456, 128), half), vmem((3456, 128), half), vmem((16, 128), f32),
            vmem((12, 14, 32, 128), half), vmem((10, 12, 32, 128), half),
            vmem((10, 128, 128), f32), vmem((8, 10, 32, 128), f32), dma((3,)), dma((5,)),
            vmem((12, 8, 16, 128), half), vmem((8, 48, 128), half), vmem((8, 48, 128), half),
            vmem((8, 48, 128), half), vmem((8, 48, 128), half), vmem((2, 12, 3, 16, 128), half),
            vmem((2, 2, 3, 16, 128), half), vmem((2, 2, 3, 16, 128), half),
            vmem((2, 4, 3, 16, 128), half), vmem((2, 4, 3, 16, 128), half),
            dma((6,)), dma((6,)), dma((2, 8)), dma((2, 8)),
            vmem((1152, 384), half), vmem((1152, 384), half), vmem((1152, 384), half),
            vmem((8, 10, 16, 384), half), vmem((8, 10, 16, 384), half), vmem((6, 16, 128), half),
            dma((3, 6)), dma((3, 8)), dma(()),
        ],
        dec_input.reshape(24, 8, 16, channels), target, conv_first, conv_second, rgb_weight,
    )
    pixels = perceptual_strip(colour_near, guide_near, vgg_first, vgg_second.T, vgg_third)
    sums = talking_call(
        backward_kernel,
        1,
        58,
        "hhhhhhv",
        "v",
        (f32_shape(2, 16, 128),),
        [
            vmem((8, 3, 16, 128), half),
            vmem((8, 10, 16, 384), half), vmem((8, 10, 16, 384), half), vmem((6, 128, 128), f32),
            vmem((8, 10, 32, 128), f32), vmem((1152, 384), half), vmem((16, 128), f32), dma((6,)),
            pltpu.VMEM((8, 10, 32, 128), half),
            pltpu.VMEM((768, 128), half),
            pltpu.VMEM((3464, 128), jnp.float32),
            pltpu.VMEM((2, 2, 8, 4, 4, 16, 128), half),
            pltpu.VMEM((2, 8, 4, 4, 16, 128), half),
            pltpu.VMEM((2, 8, 4, 4, 16, 128), half),
            pltpu.VMEM((2, 3, 4, 4, 16, 128), half),
            pltpu.VMEM((2, 3, 4, 4, 16, 128), half),
            pltpu.VMEM((2, 4, 4, 16, 128), half),
            pltpu.VMEM((2, 4, 4, 16, 128), half),
            pltpu.VMEM((2, 3, 4, 16, 128), half),
            pltpu.VMEM((2, 3, 4, 16, 128), half),
            pltpu.VMEM((2, 8, 16, 128), half),
            pltpu.VMEM((2, 7, 16, 128), half),
            dma((2, 21)),
            dma((2, 21)),
        ],
        pixels, cells, hidden, slope1, slope2, turned, rgb_weight,
    )
    flat = sums[0].reshape(2, 2048)[:, :1728]
    return flat[0], flat[1]


def solution(mesh):
    in_specs = (
        P(None, None, "row", "col", None),
        P(None, None, "col", "row", None),
        P(),
        P(),
        P(),
        P(),
        P(),
        P(),
    )
    out_specs = (P(("grp", "row", "col")), P(("grp", "row", "col")))
    return jax.shard_map(local, mesh=mesh, in_specs=in_specs, out_specs=out_specs, check_vma=False)
```

```python
import functools

import jax
import jax.numpy as jnp
from jax import lax
from jax.experimental import pallas as pl
from jax.experimental.pallas import tpu as pltpu
from jax.sharding import PartitionSpec as P

MESH = pl.DeviceIdType.MESH

gelu_scale = 0.7978845608028654
gelu_cubic = 0.044715


def position():
    return lax.axis_index("grp"), lax.axis_index("row"), lax.axis_index("col")


def same_place(one, other):
    return (one[0] == other[0]) & (one[1] == other[1]) & (one[2] == other[2])


def row_count(r):
    return 1 + jnp.where(r > 0, 1, 0) + jnp.where(r < 7, 1, 0)


def in_vmem(count):
    return [pl.BlockSpec(memory_space=pltpu.VMEM)] * count


def b16(*shape):
    return jax.ShapeDtypeStruct(shape, jnp.bfloat16)


def transposed_dot(one, other):
    return lax.dot_general(one, other, (((0,), (0,)), ((), ())), preferred_element_type=jnp.float32)


def side_by_side(value):
    cols = value.shape[0]
    at = lax.broadcasted_iota(jnp.int32, value.shape, 0)
    before = jnp.where(at == 0, 0.0, pltpu.roll(value, 1, 0))
    after = jnp.where(at == cols - 1, 0.0, pltpu.roll(value, cols - 1, 0))
    return jnp.concatenate([before, value, after], axis=1).astype(jnp.bfloat16)


def three_rows(ref, row, count):
    parts = [ref[pl.ds(row + step, count)].reshape(-1, ref.shape[-1]) for step in range(3)]
    return jnp.concatenate(parts, axis=1)


def dot32(one, other):
    return jnp.dot(one, other, preferred_element_type=jnp.float32)


def gelu_both(preact, slope_too):
    square = preact * preact
    inner_tanh = jnp.tanh(gelu_scale * preact * (1.0 + gelu_cubic * square))
    half = 0.5 * (1.0 + inner_tanh)
    value = preact * half
    if not slope_too:
        return value, None
    bend = (0.5 * gelu_scale) * (1.0 + 3.0 * gelu_cubic * square)
    return value, half + preact * (1.0 - inner_tanh * inner_tanh) * bend


def turned_columns(columns, out_ref):
    @pl.loop(0, 8)
    def _(f):
        value = columns[f]
        for dr in range(3):
            for k in range(3):
                block = value[dr : dr + 8, :, 128 * k : 128 * (k + 1)].reshape(128, 128)
                place = pl.ds(pl.multiple_of(128 * f, 128), 128)
                out_ref[dr, 128 * k : 128 * (k + 1), place] = block.T


def perceptual_kernel(
    near_hbm, guide_hbm, vgg_first_ref, vgg_second_ref, vgg_third_ref, hidden_hbm, cells_hbm,
    out_ref, hidden_turned_hbm, cells_turned_hbm,
    hidden_ref, cells_ref, hidden_turned, cells_turned, store_sem, near_ref, guide_ref, load_sem, first32, w1_ref, w1_back32, w1_back_ref, planes_ref, guides,
    taps, act1, slope1, pooled, delta3, diff2, slope2, delta2, delta1, tmp, pixels, strip,
    w2_ref, w3_ref, w3_back_ref, w2_back_ref, send_sem, recv_sem, own_sem,
):
    g, r, c = position()
    me = (g, r, c)
    barrier = pltpu.get_barrier_semaphore()
    perceives = g < 3
    own_frame = 8 * g + c
    home = own_frame // 6
    place = lax.rem(own_frame, 6)
    ahead = perceives & (place == 0) & (home > 0)
    behind = perceives & (place == 5) & (home < 3)

    def sources(do):
        for slot in range(8):
            source_frame = 6 * g - 1 + slot

            def each(step, slot=slot, source_frame=source_frame):
                source = (source_frame // 8, r + step, lax.rem(source_frame, 8))
                pl.when(jnp.logical_not(same_place(source, me)))(
                    functools.partial(do, step, slot, source)
                )

            pl.when((source_frame >= 0) & (source_frame < 24))(functools.partial(on_rows, r, each))

    def greet(step, slot, source):
        pl.semaphore_signal(barrier, inc=1, device_id=source, device_id_type=MESH)

    loads = [
        pltpu.make_async_copy(near_hbm, near_ref, load_sem.at[0]),
        pltpu.make_async_copy(guide_hbm, guide_ref, load_sem.at[1]),
        pltpu.make_async_copy(hidden_hbm, hidden_ref, load_sem.at[2]),
        pltpu.make_async_copy(cells_hbm, cells_ref, load_sem.at[3]),
    ]
    stores = [
        pltpu.make_async_copy(hidden_turned, hidden_turned_hbm, store_sem.at[0]),
        pltpu.make_async_copy(cells_turned, cells_turned_hbm, store_sem.at[1]),
    ]
    for load in loads:
        load.start()
    sources(greet)
    weight = vgg_first_ref[...].astype(jnp.float32)
    first32[...] = jnp.zeros((72, 128), jnp.float32)
    w1_back32[...] = jnp.zeros((8, 1152), jnp.float32)
    for t in range(9):
        block = weight[3 * t : 3 * t + 3]
        first32[8 * t : 8 * t + 3, 0:64] = block
        first32[8 * t + 3 : 8 * t + 6, 64:128] = block
        w1_back32[0:3, 128 * (8 - t) : 128 * (8 - t) + 64] = block
    w1_ref[...] = first32[...].astype(jnp.bfloat16)
    w1_back_ref[...] = w1_back32[...].astype(jnp.bfloat16)
    lay_out_perceptual(vgg_second_ref, vgg_third_ref, w2_ref, w3_ref, w3_back_ref, w2_back_ref)
    row0 = 8 * r - 8
    for load in loads[:2]:
        load.wait()
    kind = lax.broadcasted_iota(jnp.int32, (8, 128), 0)
    block = lax.broadcasted_iota(jnp.int32, (8, 128), 1) // 16
    for part in range(3):
        guides[...] = guide_ref[part].astype(jnp.float32)
        tiles = [near_ref[part, column].astype(jnp.float32)[0:8] for column in range(8)]
        here = (kind < 3) & (row0 + 8 * part >= 0) & (row0 + 8 * part < 64)
        seen = (row0 + 8 * part >= 0) & (row0 + 8 * part < 64)
        for i in range(8):
            image = jnp.zeros((8, 128), jnp.float32)
            for column in range(8):
                turned = pltpu.roll(tiles[column], (16 * column - 16 * i) % 128, 1)
                image = jnp.where(block == column, turned, image)
            planes_ref[8 * part + i] = jnp.where(here, image, 0.0)
            planes_ref[8 * part + i, 3:6] = jnp.where(seen, guides[pl.ds(i, 3, 8)], 0.0)
    lane = lax.broadcasted_iota(jnp.int32, (192, 128), 1)
    planes = planes_ref[...].reshape(192, 128)
    before = jnp.where(lane == 0, 0.0, pltpu.roll(planes, 1, 1))
    after = jnp.where(lane == 127, 0.0, pltpu.roll(planes, 127, 1))
    taps[:, 0:8] = before.reshape(24, 8, 128)
    taps[:, 8:16] = planes.reshape(24, 8, 128)
    taps[:, 16:24] = after.reshape(24, 8, 128)

    def shown(row):
        return (row0 + row >= 0) & (row0 + row < 64)

    def kept(row, value):
        return jnp.where(shown(row), value, 0.0)

    def first_rows(low, high, slope_too):
        @pl.loop(low, high, unroll=2)
        def _(i):
            cells = taps[pl.ds(i, 3)].reshape(72, 128).astype(jnp.bfloat16)
            value, slope = gelu_both(transposed_dot(cells, w1_ref[...]), slope_too)
            act1[i] = side_by_side(kept(i + 1, value))
            if slope_too:
                slope1[i - 6] = slope

    first_rows(0, 6, False)
    first_rows(6, 16, True)
    first_rows(16, 22, False)

    def second_rows(low, high, slope_too):
        @pl.loop(low, high, unroll=2)
        def _(p):
            plane = dot32(three_rows(act1, 2 * p, 2), w2_ref[...])
            value, slope = gelu_both(plane, slope_too)
            value = kept(2 * p + 2, value)
            if slope_too:
                difference = 0.25 * (value - pltpu.roll(value, 64, 1))
                diff2[pl.ds(2 * p - 4, 2)] = difference.reshape(2, 128, 128)
                slope2[pl.ds(2 * p - 4, 2)] = slope.reshape(2, 128, 128)
            tmp[...] = value[:128] + value[128:]
            mean = 0.25 * (tmp[pl.ds(0, 64, 2)] + tmp[pl.ds(1, 64, 2)])
            pooled[p] = side_by_side(mean)

    second_rows(0, 2, False)
    second_rows(2, 8, True)
    second_rows(8, 10, False)

    @pl.loop(0, 4, unroll=2)
    def _(half):
        j = 2 * half
        plane = dot32(three_rows(pooled, j, 2), w3_ref[...])
        value, slope = gelu_both(plane[:, :128], True)
        guide, _ = gelu_both(plane[:, 128:], False)
        delta = 0.5 * (value - guide) * slope
        delta3[j] = side_by_side(kept(2 * j + 4, delta[:64]))
        delta3[j + 1] = side_by_side(kept(2 * j + 6, delta[64:]))

    @pl.loop(0, 6, unroll=3)
    def _(m):
        grad = 0.25 * dot32(three_rows(delta3, m, 1), w3_back_ref[...])
        tmp[pl.ds(0, 64, 2)] = grad
        tmp[pl.ds(1, 64, 2)] = grad
        spread = tmp[...]
        for k in range(2):
            delta = (spread + diff2[2 * m + k]) * slope2[2 * m + k]
            delta2[2 * m + k] = side_by_side(kept(2 * m + 6, delta))

    @pl.loop(0, 5, unroll=5)
    def _(half):
        n = 2 * half
        grad = dot32(three_rows(delta2, n, 2), w2_back_ref[...])
        for k in range(2):
            delta = grad[128 * k : 128 * (k + 1)] * slope1[n + k]
            delta1[n + k] = side_by_side(kept(n + k + 7, delta))

    @pl.loop(0, 8, unroll=4)
    def _(q):
        grad = lax.dot_general(
            w1_back_ref[...],
            three_rows(delta1, q, 1),
            (((1,), (1,)), ((), ())),
            preferred_element_type=jnp.float32,
        )
        own = planes_ref[q + 8]
        direct = (1.0 / 6.0) * (own - pltpu.roll(own, 5, 0))
        pixels[pl.ds(pl.multiple_of(q * 8, 8), 8)] = grad + direct

    colour_rows = [pixels[pl.ds(k, 8, 8)] for k in range(3)]
    third = lax.broadcasted_iota(jnp.int32, (8, 128), 1) // 32
    for column in range(8):
        turned = [pltpu.roll(v, (32 * k + 8 - 16 * column) % 128, 1) for k, v in enumerate(colour_rows)]
        part = jnp.where(third == 0, turned[0], jnp.where(third == 1, turned[1], turned[2]))
        strip[column] = jnp.concatenate([part, jnp.zeros((8, 128), jnp.float32)], axis=0).astype(jnp.bfloat16)

    groups = jnp.where(perceives, 1, 0) + jnp.where(ahead, 1, 0) + jnp.where(behind, 1, 0)
    to_itself = perceives & (home == g) | ahead & (home == g + 1) | behind & (home == g - 1)
    awaited = 8 * row_count(r) * groups - jnp.where(to_itself, 1, 0)
    pl.when(perceives)(lambda: pl.semaphore_wait(barrier, awaited))

    def targets(do):
        for kind, (group, needed) in enumerate(((home, perceives), (home - 1, ahead), (home + 1, behind))):

            def each(step, kind=kind, group=group):
                for column in range(8):
                    peer = (group, r + step, column)
                    do(kind, step, column, peer, jnp.logical_not(same_place(peer, me)))

            pl.when(needed)(functools.partial(on_rows, r, each))

    def outgoing(kind, step, column, peer):
        place_there = own_frame - 6 * peer[0] + 1
        return pltpu.make_async_remote_copy(
            src_ref=strip.at[column],
            dst_ref=out_ref.at[place_there, 1 - step],
            send_sem=send_sem.at[kind, step + 1, column],
            recv_sem=recv_sem.at[place_there, 1 - step],
            device_id=peer,
            device_id_type=MESH,
        )

    def kept():
        return pltpu.make_async_copy(strip.at[c], out_ref.at[own_frame - 6 * g + 1, 1], own_sem)

    def start(kind, step, column, peer, away):
        pl.when(away)(lambda: outgoing(kind, step, column, peer).start())
        if step == 0:
            pl.when(jnp.logical_not(away))(lambda: kept().start())

    def finish(kind, step, column, peer, away):
        pl.when(away)(lambda: outgoing(kind, step, column, peer).wait_send())
        if step == 0:
            pl.when(jnp.logical_not(away))(lambda: kept().wait())

    def arrive(step, slot, source):
        pltpu.make_async_remote_copy(
            src_ref=strip.at[0],
            dst_ref=out_ref.at[slot, step + 1],
            send_sem=send_sem.at[0, 0, 0],
            recv_sem=recv_sem.at[slot, step + 1],
            device_id=source,
            device_id_type=MESH,
        ).wait_recv()

    targets(start)
    loads[2].wait()
    turned_columns(hidden_ref, hidden_turned)
    stores[0].start()
    loads[3].wait()
    turned_columns(cells_ref, cells_turned)
    stores[1].start()
    sources(arrive)
    targets(finish)
    for store in stores:
        store.wait()


def perceptual_strip(*operands):
    f32, half = jnp.float32, jnp.bfloat16
    return pl.pallas_call(
        perceptual_kernel,
        out_shape=(b16(8, 3, 16, 128), b16(3, 384, 1024), b16(3, 384, 1024)),
        in_specs=places("hhvvvhh"),
        out_specs=tuple(places("vhh")),
        scratch_shapes=[
            pltpu.VMEM((8, 10, 16, 384), half),
            pltpu.VMEM((8, 10, 16, 384), half),
            pltpu.VMEM((3, 384, 1024), half),
            pltpu.VMEM((3, 384, 1024), half),
            pltpu.SemaphoreType.DMA((2,)),
            pltpu.VMEM((3, 8, 16, 128), half),
            pltpu.VMEM((3, 32, 128), half),
            pltpu.SemaphoreType.DMA((4,)),
            pltpu.VMEM((72, 128), f32),
            pltpu.VMEM((72, 128), half),
            pltpu.VMEM((8, 1152), f32),
            pltpu.VMEM((8, 1152), half),
            pltpu.VMEM((24, 8, 128), f32),
            pltpu.VMEM((32, 128), f32),
            pltpu.VMEM((24, 24, 128), f32),
            pltpu.VMEM((22, 128, 384), half),
            pltpu.VMEM((10, 128, 128), f32),
            pltpu.VMEM((10, 64, 384), half),
            pltpu.VMEM((8, 64, 384), half),
            pltpu.VMEM((12, 128, 128), f32),
            pltpu.VMEM((12, 128, 128), f32),
            pltpu.VMEM((12, 128, 384), half),
            pltpu.VMEM((10, 128, 384), half),
            pltpu.VMEM((128, 128), f32),
            pltpu.VMEM((64, 128), f32),
            pltpu.VMEM((8, 16, 128), half),
            pltpu.VMEM((1152, 128), half),
            pltpu.VMEM((1152, 256), half),
            pltpu.VMEM((1152, 128), half),
            pltpu.VMEM((1152, 128), half),
            pltpu.SemaphoreType.DMA((3, 3, 8)),
            pltpu.SemaphoreType.DMA((8, 3)),
            pltpu.SemaphoreType.DMA(()),
        ],
        compiler_params=pltpu.CompilerParams(
            collective_id=4, has_side_effects=True, vmem_limit_bytes=58 * 2**20
        ),
    )(*operands)


def taps_in_lanes(weight_ref, out_ref):
    for q in range(9):
        for k in range(3):
            tap = 3 * q + k
            out_ref[128 * q : 128 * (q + 1), 128 * k : 128 * (k + 1)] = weight_ref[
                128 * tap : 128 * (tap + 1), :
            ]


def turned_taps(weight_ref, out_ref):
    for q in range(9):
        for k in range(3):
            tap = 26 - 3 * q - k
            block = weight_ref[128 * tap : 128 * (tap + 1), :].astype(jnp.float32)
            out_ref[128 * q : 128 * (q + 1), 128 * k : 128 * (k + 1)] = block.T.astype(jnp.bfloat16)


def conv_rows(source, frame, starts, count, taps_ref):
    size = len(starts) * count * 32

    def near(dt, dr):
        rows = [source[frame + dt, pl.ds(start + dr, count)].reshape(count * 32, 128) for start in starts]
        return rows[0] if len(rows) == 1 else jnp.concatenate(rows, axis=0)

    parts = [near(dt, dr) for dt in range(3) for dr in range(3)]
    sums = dot32(jnp.concatenate(parts, axis=1), taps_ref[...])
    total = pltpu.roll(sums[:, :128], 1, 0) + sums[:, 128:256]
    total += pltpu.roll(sums[:, 256:], size - 1, 0)
    return total.reshape(len(starts) * count, 32, 128)


def silu_parts(preact):
    gate = 0.5 * (1.0 + jnp.tanh(0.5 * preact))
    return preact * gate, gate * (1.0 + preact * (1.0 - gate))


def on_rows(r, do):
    for step in (-1, 1, 0):
        pl.when((r + step >= 0) & (r + step < 8))(functools.partial(do, step))


def lay_out_perceptual(second_ref, third_ref, w2_out, w3_out, w3_back_out, w2_back_out):
    f32, half = jnp.float32, jnp.bfloat16
    for t in range(9):
        turned_block = second_ref[:, 64 * t : 64 * (t + 1)].astype(f32)
        block = turned_block.T
        wide = third_ref[64 * t : 64 * (t + 1), :].astype(f32)
        none, low, high = jnp.zeros((64, 64), f32), 128 * t, 128 * (8 - t)
        w2_out[low : low + 64] = jnp.concatenate([block, none], axis=1).astype(half)
        w2_out[low + 64 : low + 128] = jnp.concatenate([none, block], axis=1).astype(half)
        w3_out[low : low + 64, :128] = wide.astype(half)
        w3_out[low : low + 64, 128:] = jnp.zeros((64, 128), half)
        w3_out[low + 64 : low + 128, :128] = jnp.zeros((64, 128), half)
        w3_out[low + 64 : low + 128, 128:] = wide.astype(half)
        w2_back_out[high : high + 64] = jnp.concatenate([turned_block, none], axis=1).astype(half)
        w2_back_out[high + 64 : high + 128] = jnp.zeros((64, 128), half)
        turned = jnp.concatenate([wide.T, jnp.zeros((128, 64), f32)], axis=1)
        w3_back_out[high : high + 128] = turned.astype(half)


def forward_kernel(
    video_hbm, target_ref, first_hbm, second_hbm, rgb_ref,
    cells_hbm, hidden_hbm, slope1_hbm, slope2_hbm, turned_hbm, near_out, guide_out,
    video, first_ref, second_ref, rgb16, cells, hidden_out, slope1_out, slope2_out, load_sem, store_sem,
    tile, left_send, right_send, left_in, right_in, rows_in, to_west, to_east, from_east, from_west,
    halo_send, halo_recv, edge_send, edge_recv,
    taps1, taps2, turned, cell_columns, hidden_columns, colours, send_sem, recv_sem, own_sem,
):
    loads = [
        pltpu.make_async_copy(video_hbm, video, load_sem.at[0]),
        pltpu.make_async_copy(first_hbm, first_ref, load_sem.at[1]),
        pltpu.make_async_copy(second_hbm, second_ref, load_sem.at[2]),
    ]
    for load in loads:
        load.start()
    g, r, c = position()
    me = (g, r, c)
    f32, half = jnp.float32, jnp.bfloat16
    barrier = pltpu.get_barrier_semaphore()
    perceives = g < 3
    source_group = (8 * g + c) // 6
    west, east = lax.rem(c + 7, 8), lax.rem(c + 1, 8)
    has_up, has_down = r > 0, r < 7
    has_prev, has_next = g > 0, g < 3

    def sources(do):
        def each(step):
            for column in range(8):
                source = (source_group, r + step, column)
                pl.when(jnp.logical_not(same_place(source, me)))(
                    functools.partial(do, step, column, source)
                )

        pl.when(perceives)(lambda: on_rows(r, each))

    def signal(peer):
        pl.semaphore_signal(barrier, inc=1, device_id=peer, device_id_type=MESH)

    signal((g, r, west))
    signal((g, r, east))

    pl.when(has_up)(lambda: signal((g, r - 1, c)))
    pl.when(has_down)(lambda: signal((g, r + 1, c)))

    @pl.when(has_prev)
    def _():
        for column in (west, c, east):
            signal((g - 1, r, column))

    @pl.when(has_next)
    def _():
        for column in (west, c, east):
            signal((g + 1, r, column))

    sources(lambda step, column, source: signal(source))

    block = jnp.minimum(g, 2)
    guide = [target_ref[k, block, 0].astype(f32) for k in range(3)] + [jnp.zeros((8, 128), f32)]
    guide_out[1] = jnp.concatenate(guide, axis=0).astype(half)
    rgb16[...] = jnp.zeros((16, 128), f32)
    rgb16[0:3] = rgb_ref[...].astype(f32)
    loads[0].wait()

    for f in range(12):
        frame = 6 * g - 3 + f
        value = video[jnp.minimum(jnp.maximum(frame, 0), 23)]
        tile[f] = jnp.where((frame >= 0) & (frame < 24), value, jnp.zeros_like(value))

    to_itself = jnp.where(perceives & (2 * g + c < 6), 1, 0)
    groups_near = jnp.where(has_prev, 1, 0) + jnp.where(has_next, 1, 0)
    pl.semaphore_wait(barrier, 7 * row_count(r) + 1 + 3 * groups_near - to_itself)

    def remote(src, dst, slot, peer):
        return pltpu.make_async_remote_copy(
            src_ref=src,
            dst_ref=dst,
            send_sem=halo_send.at[slot],
            recv_sem=halo_recv.at[slot],
            device_id=peer,
            device_id_type=MESH,
        )

    sideways = [remote(left_send, right_in, 0, (g, r, west)), remote(right_send, left_in, 1, (g, r, east))]

    def to_row(row_index, rows, edge, guide_slot, first_slot):
        strip = tile.at[pl.ds(3, 6), pl.ds(rows, 3)]
        return [
            remote(strip, rows_in.at[edge, pl.ds(3, 6)], first_slot, (g, row_index, c)),
            remote(guide_out.at[1], guide_out.at[guide_slot], first_slot + 1, (g, row_index, c)),
        ]

    upward = to_row(r - 1, 0, 1, 2, 2)
    downward = to_row(r + 1, 5, 0, 0, 4)

    def across(edge):
        def copy(src, dst, slot, peer):
            return pltpu.make_async_remote_copy(
                src_ref=src,
                dst_ref=dst,
                send_sem=edge_send.at[edge, slot],
                recv_sem=edge_recv.at[edge, slot],
                device_id=peer,
                device_id_type=MESH,
            )

        mine, wests, easts = rows_in.at[edge], to_west.at[edge], to_east.at[edge]
        in_east, in_west, two = from_east.at[edge], from_west.at[edge], pl.ds(1, 2)
        level = [
            copy(wests, in_east.at[two], 0, (g, r, west)),
            copy(easts, in_west.at[two], 1, (g, r, east)),
        ]
        onward = [
            copy(mine.at[pl.ds(6, 3)], mine.at[pl.ds(0, 3)], 2, (g + 1, r, c)),
            copy(wests.at[1], in_east.at[0], 3, (g + 1, r, west)),
            copy(easts.at[1], in_west.at[0], 4, (g + 1, r, east)),
        ]
        back = [
            copy(mine.at[pl.ds(3, 3)], mine.at[pl.ds(9, 3)], 5, (g - 1, r, c)),
            copy(wests.at[0], in_east.at[3], 6, (g - 1, r, west)),
            copy(easts.at[0], in_west.at[3], 7, (g - 1, r, east)),
        ]
        return level, onward, back

    edges = [across(0), across(1)]

    def pass_on(edge):
        values = [rows_in[edge, 3 + f].astype(f32) for f in range(6)]
        for part in range(2):
            near = values[3 * part : 3 * part + 3]
            spare = jnp.zeros((3, 4, 128), f32)
            to_west[edge, part] = jnp.concatenate([v[:, 0:4] for v in near] + [spare], axis=1).astype(half)
            to_east[edge, part] = jnp.concatenate([v[:, 12:16] for v in near] + [spare], axis=1).astype(half)
        level, onward, back = edges[edge]
        start(level)
        pl.when(has_next)(lambda: start(onward))
        pl.when(has_prev)(lambda: start(back))

    def passed(edge, done):
        level, onward, back = edges[edge]
        done(level)
        if done is landed:
            pl.when(has_prev)(lambda: done(onward))
            pl.when(has_next)(lambda: done(back))
        else:
            pl.when(has_next)(lambda: done(onward))
            pl.when(has_prev)(lambda: done(back))

    def start(copies):
        for copy in copies:
            copy.start()

    def sent(copies):
        for copy in copies:
            copy.wait_send()

    def landed(copies):
        for copy in copies:
            copy.wait_recv()

    pl.when(has_up)(lambda: start(upward))
    pl.when(has_down)(lambda: start(downward))
    for line in range(8):
        near = [tile[f, line].astype(f32) for f in range(12)]
        left_send[line] = jnp.concatenate([v[0:4] for v in near], axis=0).astype(half)
        right_send[line] = jnp.concatenate([v[12:16] for v in near], axis=0).astype(half)
    start(sideways)

    loads[1].wait()
    taps_in_lanes(first_ref, taps1)
    loads[2].wait()
    taps_in_lanes(second_ref, taps2)

    def assemble(first_row, count, real, own, left, right, per):
        col = lax.broadcasted_iota(jnp.int32, (count, 32, 128), 1) + (16 * c - 8)
        shown = (col >= 0) & (col < 128) & real
        for part in range(12 // per):
            before, after = left(part).astype(f32), right(part).astype(f32)
            for k in range(per):
                f, eight = per * part + k, slice(8 * (k // 2), 8 * (k // 2) + 8)
                one = before[:, eight].reshape(8 * count, 128)
                two = after[:, eight].reshape(8 * count, 128)
                if k % 2 == 0:
                    one = pltpu.roll(one, 4, 0)
                else:
                    two = pltpu.roll(two, 8 * count - 4, 0)
                sides = [one.reshape(count, 8, 128), own(f).astype(f32), two.reshape(count, 8, 128)]
                frame = 6 * g - 3 + f
                here = shown & (frame >= 0) & (frame < 24)
                value = jnp.where(here, jnp.concatenate(sides, axis=1), 0.0)
                cells[f, first_row : first_row + count] = value.astype(half)

    row = lax.broadcasted_iota(jnp.int32, (6, 32, 128), 0)
    col = lax.broadcasted_iota(jnp.int32, (6, 32, 128), 1) + (16 * c - 8)
    in_cols = (col >= 0) & (col < 128)

    def in_frames(f):
        frame = 6 * g - 2 + f
        return jnp.where((frame >= 0) & (frame < 24), 1.0, 0.0)

    landed(sideways)
    assemble(
        3, 8, r >= 0, lambda f: tile[f],
        lambda part: left_in[:, 16 * part : 16 * (part + 1)],
        lambda part: right_in[:, 16 * part : 16 * (part + 1)],
        4,
    )

    def inner(f):
        value, slope = silu_parts(conv_rows(cells, f, (3,), 6, taps1))
        value = jnp.where(in_cols, value, 0.0) * in_frames(f)
        hidden_out[f, 3:9] = value.astype(half)
        slope1_out[f, 16:112] = slope[:, 8:24].reshape(96, 128)

    pl.loop(0, 2, unroll=2)(inner)

    @pl.when(has_up)
    def _():
        landed(downward)
        pass_on(0)

    @pl.when(has_down)
    def _():
        landed(upward)
        pass_on(1)

    pl.loop(2, 10, unroll=2)(inner)

    pl.when(has_up)(lambda: passed(0, landed))
    pl.when(has_down)(lambda: passed(1, landed))
    for edge, real in ((0, has_up), (1, has_down)):
        assemble(
            11 * edge, 3, real,
            lambda f, edge=edge: rows_in[edge, f],
            lambda part, edge=edge: from_west[edge, part],
            lambda part, edge=edge: from_east[edge, part],
            3,
        )
    image_row = jnp.where(row < 3, row, row + 6) + (8 * r - 2)
    in_image = in_cols & (image_row >= 0) & (image_row < 64)

    @pl.loop(0, 10, unroll=2)
    def _(f):
        value, slope = silu_parts(conv_rows(cells, f, (0, 9), 3, taps1))
        value = (jnp.where(in_image, value, 0.0) * in_frames(f)).astype(half)
        hidden_out[f, 0:3] = value[0:3]
        hidden_out[f, 9:12] = value[3:6]
        slope1_out[f, 0:16] = slope[2, 8:24]
        slope1_out[f, 112:128] = slope[3, 8:24]

    stores = [
        pltpu.make_async_copy(slope1_out.at[pl.ds(2, 6)], slope1_hbm, store_sem.at[0]),
        pltpu.make_async_copy(slope2_out, slope2_hbm, store_sem.at[1]),
        pltpu.make_async_copy(hidden_columns, hidden_hbm, store_sem.at[2]),
        pltpu.make_async_copy(cell_columns, cells_hbm, store_sem.at[3]),
        pltpu.make_async_copy(turned, turned_hbm, store_sem.at[4]),
    ]
    stores[0].start()

    def target(step, slot):
        frame = 6 * g + slot
        return (frame // 8, r + step, lax.rem(frame, 8))

    def outgoing(step, slot):
        return pltpu.make_async_remote_copy(
            src_ref=colours.at[slot],
            dst_ref=near_out.at[1 - step, c],
            send_sem=send_sem.at[step + 1, slot],
            recv_sem=recv_sem.at[1 - step, c],
            device_id=target(step, slot),
            device_id_type=MESH,
        )

    def kept(slot):
        return pltpu.make_async_copy(colours.at[slot], near_out.at[1, c], own_sem)

    def start_colour(slot, step):
        away = jnp.logical_not(same_place(target(step, slot), me))
        pl.when(away)(lambda: outgoing(step, slot).start())
        if step == 0:
            pl.when(jnp.logical_not(away))(lambda: kept(slot).start())

    def finish(slot, step):
        away = jnp.logical_not(same_place(target(step, slot), me))
        pl.when(away)(lambda: outgoing(step, slot).wait_send())
        if step == 0:
            pl.when(jnp.logical_not(away))(lambda: kept(slot).wait())

    def arrive(step, column, source):
        pltpu.make_async_remote_copy(
            src_ref=colours.at[0],
            dst_ref=near_out.at[step + 1, column],
            send_sem=send_sem.at[0, 0],
            recv_sem=recv_sem.at[step + 1, column],
            device_id=source,
            device_id_type=MESH,
        ).wait_recv()

    @pl.loop(0, 6)
    def _(slot):
        value, slope = silu_parts(conv_rows(hidden_out, slot + 1, (0,), 10, taps2))
        slope2_out[slot + 1] = slope
        own = value[1:9, 8:24].reshape(128, 128).astype(jnp.bfloat16)
        colour = lax.dot_general(
            rgb16[...].astype(half), own, (((1,), (1,)), ((), ())), preferred_element_type=jnp.float32
        )
        colours[slot] = colour.astype(jnp.bfloat16)
        on_rows(r, functools.partial(start_colour, slot))

    @pl.loop(0, 2)
    def _(end):
        slope2_out[7 * end] = silu_parts(conv_rows(hidden_out, 7 * end, (0,), 10, taps2))[1]

    stores[1].start()
    columns_in_lanes(hidden_out, 1, 1, hidden_columns)
    stores[2].start()
    columns_in_lanes(cells, 2, 2, cell_columns)
    stores[3].start()
    turned_taps(second_ref, turned)
    stores[4].start()
    sources(arrive)

    @pl.loop(0, 6)
    def _(slot):
        on_rows(r, functools.partial(finish, slot))

    for store in stores:
        store.wait()

    sent(sideways)
    pl.when(has_up)(lambda: sent(upward))
    pl.when(has_down)(lambda: sent(downward))
    pl.when(has_up)(lambda: passed(0, sent))
    pl.when(has_down)(lambda: passed(1, sent))


def columns_in_lanes(source, frame0, row0, out_ref):
    @pl.loop(0, 8)
    def _(f):
        value = source[f + frame0, pl.ds(row0, 10)].reshape(320, 128).astype(jnp.float32)
        parts = [pltpu.roll(value, 1, 0), value, pltpu.roll(value, 319, 0)]
        for k, part in enumerate(parts):
            own = part.reshape(10, 32, 128)[:, 8:24]
            out_ref[f, :, :, 128 * k : 128 * (k + 1)] = own.astype(jnp.bfloat16)


def weight_terms(columns, delta, terms, low, high):
    for q in range(low, high):
        cells = columns[q % 3, :, 128 * (q // 3) : 128 * (q // 3) + 768]
        terms[384 * q : 384 * (q + 1)] = dot32(cells, delta[...])


def by_chip(terms, out_ref, which, low, high):
    @pl.loop(low, high)
    def _(z):
        for chip in range(16):
            start = 432 * z + 27 * chip
            out_ref[which, 0, z, chip // 4, chip % 4] = terms[pl.ds(start, 16)].astype(jnp.bfloat16)
            out_ref[which, 1, z, chip // 4, chip % 4] = terms[pl.ds(start + 13, 16)].astype(jnp.bfloat16)


def backward_kernel(
    pixel_hbm, cells_hbm, hidden_hbm, slope1_hbm, slope2_hbm, turned_hbm, rgb_ref, out_ref,
    pixel_ref, cells_ref, hidden_ref, slope1_ref, slope2_ref, taps, rgb16, load_sem,
    field, delta, terms,
    sending, core_in, held, x_in, y_in, mid_x, mid_y, yy_in, xx_in, last, z_in, send_sem, recv_sem,
):
    g, r, c = position()
    loads = [
        pltpu.make_async_copy(src, dst, load_sem.at[k])
        for k, (src, dst) in enumerate(
            (
                (slope2_hbm, slope2_ref), (hidden_hbm, hidden_ref), (turned_hbm, taps),
                (slope1_hbm, slope1_ref), (cells_hbm, cells_ref), (pixel_hbm, pixel_ref),
            )
        )
    ]
    for load in loads[5:] + loads[:5]:
        load.start()
    zh, x, y, core = r // 4, lax.rem(r, 4), c // 2, lax.rem(c, 2)
    z = g * 2 + zh
    other = 1 - core

    def at_x(step):
        return (g, zh * 4 + lax.rem(x + step, 4), c)

    def at_y(step):
        return (g, r, lax.rem(y + step, 4) * 2 + core)

    def at_z(step):
        to = lax.rem(z + step, 8)
        return (to // 2, lax.rem(to, 2) * 4 + x, c)

    partner = (g, r, y * 2 + other)
    barrier = pltpu.get_barrier_semaphore()
    everyone = [partner] + [at_x(s) for s in (1, 2, 3)] + [at_y(s) for s in (1, 2, 3)]
    everyone += [at_z(s) for s in range(1, 8)]
    for peer in everyone:
        pl.semaphore_signal(barrier, inc=1, device_id=peer, device_id_type=MESH)

    def send(src, dst, which, slot, peer):
        copy = pltpu.make_async_remote_copy(
            src_ref=src,
            dst_ref=dst,
            send_sem=send_sem.at[which, slot],
            recv_sem=recv_sem.at[which, slot],
            device_id=peer,
            device_id_type=MESH,
        )
        copy.start()
        return copy

    f32, half = jnp.float32, jnp.bfloat16

    def summed(own, received):
        total = own.astype(f32)
        for k in range(3):
            total += received[k].astype(f32)
        return total.astype(half)

    def to_partner(which, part):
        some = pl.ds(4 * part, 4)
        return send(sending.at[which, other, some], core_in.at[which, some], which, 20 * part, partner)

    def first_step(which, part, copy):
        copy.wait()

        @pl.loop(4 * part, 4 * part + 4)
        def _(k):
            pair = sending[which, core, k].astype(f32) + core_in[which, k].astype(f32)
            held[which, k] = pair.astype(half)

        some = held.at[which, pl.ds(4 * part, 4)]
        if part == 0:
            return [
                send(some.at[:, lax.rem(x + s, 4)], x_in.at[which, s - 1], which, s, at_x(s)) for s in (1, 2, 3)
            ]
        return [
            send(some.at[:, :, lax.rem(y + s, 4)], y_in.at[which, s - 1], which, 3 + s, at_y(s)) for s in (1, 2, 3)
        ]

    def second_step(which, part, copies):
        for copy in copies:
            copy.wait()
        if part == 0:
            mid_x[which] = summed(held[which, 0:4, x], [x_in[which, k] for k in range(3)])
            return [
                send(mid_x.at[which, :, lax.rem(y + s, 4)], yy_in.at[which, s - 1], which, 6 + s, at_y(s))
                for s in (1, 2, 3)
            ]
        mid_y[which] = summed(held[which, 4:8, :, y], [y_in[which, k] for k in range(3)])
        return [
            send(mid_y.at[which, :, lax.rem(x + s, 4)], xx_in.at[which, s - 1], which, 9 + s, at_x(s))
            for s in (1, 2, 3)
        ]

    def third_step(which, copies):
        for copy in copies:
            copy.wait()
        last[which, 0:4] = summed(mid_x[which, :, y], [yy_in[which, k] for k in range(3)])
        last[which, 4:8] = summed(mid_y[which, :, x], [xx_in[which, k] for k in range(3)])
        return [
            send(last.at[which, lax.rem(z + s, 8)], z_in.at[which, s - 1], which, 12 + s, at_z(s))
            for s in range(1, 8)
        ]

    def result(which, copies):
        for copy in copies:
            copy.wait()
        total = last[which, z].astype(f32)
        for k in range(7):
            total += z_in[which, k].astype(f32)
        turned = pltpu.roll(total, 64, 1)
        low_half = lax.broadcasted_iota(jnp.int32, (16, 128), 1) < 64
        shifted = jnp.where(low_half, turned, pltpu.roll(turned, 15, 0))
        out_ref[which] = jnp.where(core == 1, shifted, total)

    rgb16[...] = jnp.zeros((16, 128), f32)
    rgb16[0:3] = rgb_ref[...].astype(f32)
    loads[0].wait()
    loads[5].wait()

    lane = lax.broadcasted_iota(jnp.int32, (8, 128), 1)
    col = lax.rem(lane, 32) + (16 * c - 8)
    in_cols = (lane < 96) & (col >= 0) & (col < 128)

    @pl.loop(0, 8, unroll=2)
    def _(f):
        frame = 6 * g - 1 + f
        known = in_cols & (frame >= 0) & (frame < 24)
        parts = []
        for part in range(3):
            seen = known & (r + part - 1 >= 0) & (r + part - 1 < 8)
            parts.append(jnp.where(seen, pixel_ref[f, part].astype(f32)[0:8], 0.0))
        turned = jnp.concatenate(parts, axis=0).T
        for i in range(10):
            hidden_grad = turned[0:32, i + 7 : i + 8] * rgb16[0:1]
            for k in (1, 2):
                hidden_grad += turned[32 * k : 32 * (k + 1), i + 7 : i + 8] * rgb16[k : k + 1]
            field[f, i] = (hidden_grad * slope2_ref[f, i]).astype(half)

    @pl.loop(0, 6)
    def _(f):
        own = field[f + 1, 1:9].astype(f32)[:, 8:24].reshape(128, 128).astype(half)
        delta[pl.ds(pl.multiple_of(128 * f, 128), 128)] = own

    loads[1].wait()
    terms[pl.ds(3456, 8)] = jnp.zeros((8, 128), f32)
    weight_terms(hidden_ref, delta, terms, 0, 5)
    by_chip(terms, sending, 1, 0, 4)
    pl.semaphore_wait(barrier, len(everyone))
    swap_low = to_partner(1, 0)
    weight_terms(hidden_ref, delta, terms, 5, 9)
    by_chip(terms, sending, 1, 4, 8)
    swap_high = to_partner(1, 1)
    second_low = first_step(1, 0, swap_low)
    loads[2].wait()
    loads[3].wait()

    def back_frame(f):
        back = conv_rows(field, f, (0,), 8, taps)[:, 8:24].reshape(128, 128)
        value = (back * slope1_ref[f]).astype(half)
        delta[pl.ds(pl.multiple_of(128 * f, 128), 128)] = value

    pl.loop(0, 2, unroll=2)(back_frame)
    second_high = first_step(1, 1, swap_high)
    pl.loop(2, 6, unroll=2)(back_frame)
    loads[4].wait()
    second_low = second_step(1, 0, second_low)
    weight_terms(cells_ref, delta, terms, 0, 5)
    by_chip(terms, sending, 0, 0, 4)
    swap_low = to_partner(0, 0)
    second_high = second_step(1, 1, second_high)
    weight_terms(cells_ref, delta, terms, 5, 9)
    by_chip(terms, sending, 0, 4, 8)
    swap_high = to_partner(0, 1)
    first_low = first_step(0, 0, swap_low)
    moves_second = third_step(1, second_low + second_high)
    first_high = first_step(0, 1, swap_high)
    result(1, moves_second)
    first_low = second_step(0, 0, first_low)
    first_high = second_step(0, 1, first_high)
    result(0, third_step(0, first_low + first_high))


def f32_shape(*shape):
    return jax.ShapeDtypeStruct(shape, jnp.float32)


def places(text):
    return [pl.BlockSpec(memory_space=pltpu.VMEM if letter == "v" else pltpu.HBM) for letter in text]


def talking_call(kernel, ident, mebibytes, in_places, out_places, outs, scratch, *operands):
    return pl.pallas_call(
        kernel,
        out_shape=tuple(outs),
        in_specs=places(in_places),
        out_specs=tuple(places(out_places)),
        scratch_shapes=scratch,
        compiler_params=pltpu.CompilerParams(
            collective_id=ident, has_side_effects=True, vmem_limit_bytes=mebibytes * 2**20
        ),
    )(*operands)


def local(dec_input, target, conv_first, conv_second, rgb_weight, vgg_first, vgg_second, vgg_third):
    g, r, c = position()
    channels = dec_input.shape[-1]
    half, f32, dma, vmem = jnp.bfloat16, jnp.float32, pltpu.SemaphoreType.DMA, pltpu.VMEM
    cells, hidden, slope1, slope2, turned, colour_near, guide_near = talking_call(
        forward_kernel,
        3,
        58,
        "hvhhv",
        "hhhhhvv",
        (
            b16(8, 10, 16, 384), b16(8, 10, 16, 384), f32_shape(6, 128, 128), f32_shape(8, 10, 32, 128),
            b16(1152, 384),
            b16(3, 8, 16, 128), b16(3, 32, 128),
        ),
        [
            vmem((24, 8, 16, 128), half), vmem((3456, 128), half), vmem((3456, 128), half), vmem((16, 128), f32),
            vmem((12, 14, 32, 128), half), vmem((10, 12, 32, 128), half),
            vmem((10, 128, 128), f32), vmem((8, 10, 32, 128), f32), dma((3,)), dma((5,)),
            vmem((12, 8, 16, 128), half), vmem((8, 48, 128), half), vmem((8, 48, 128), half),
            vmem((8, 48, 128), half), vmem((8, 48, 128), half), vmem((2, 12, 3, 16, 128), half),
            vmem((2, 2, 3, 16, 128), half), vmem((2, 2, 3, 16, 128), half),
            vmem((2, 4, 3, 16, 128), half), vmem((2, 4, 3, 16, 128), half),
            dma((6,)), dma((6,)), dma((2, 8)), dma((2, 8)),
            vmem((1152, 384), half), vmem((1152, 384), half), vmem((1152, 384), half),
            vmem((8, 10, 16, 384), half), vmem((8, 10, 16, 384), half), vmem((6, 16, 128), half),
            dma((3, 6)), dma((3, 8)), dma(()),
        ],
        dec_input.reshape(24, 8, 16, channels), target, conv_first, conv_second, rgb_weight,
    )
    pixels, hidden_turned, cells_turned = perceptual_strip(
        colour_near, guide_near, vgg_first, vgg_second.T, vgg_third, hidden, cells
    )
    sums = talking_call(
        backward_kernel,
        1,
        58,
        "hhhhhhv",
        "v",
        (f32_shape(2, 16, 128),),
        [
            vmem((8, 3, 16, 128), half),
            vmem((3, 384, 1024), half), vmem((3, 384, 1024), half), vmem((6, 128, 128), f32),
            vmem((8, 10, 32, 128), f32), vmem((1152, 384), half), vmem((16, 128), f32), dma((6,)),
            pltpu.VMEM((8, 10, 32, 128), half),
            pltpu.VMEM((768, 128), half),
            pltpu.VMEM((3464, 128), jnp.float32),
            pltpu.VMEM((2, 2, 8, 4, 4, 16, 128), half),
            pltpu.VMEM((2, 8, 4, 4, 16, 128), half),
            pltpu.VMEM((2, 8, 4, 4, 16, 128), half),
            pltpu.VMEM((2, 3, 4, 4, 16, 128), half),
            pltpu.VMEM((2, 3, 4, 4, 16, 128), half),
            pltpu.VMEM((2, 4, 4, 16, 128), half),
            pltpu.VMEM((2, 4, 4, 16, 128), half),
            pltpu.VMEM((2, 3, 4, 16, 128), half),
            pltpu.VMEM((2, 3, 4, 16, 128), half),
            pltpu.VMEM((2, 8, 16, 128), half),
            pltpu.VMEM((2, 7, 16, 128), half),
            dma((2, 21)),
            dma((2, 21)),
        ],
        pixels, cells_turned, hidden_turned, slope1, slope2, turned, rgb_weight,
    )
    flat = sums[0].reshape(2, 2048)[:, :1728]
    return flat[0], flat[1]


def solution(mesh):
    in_specs = (
        P(None, None, "row", "col", None),
        P(None, None, "col", "row", None),
        P(),
        P(),
        P(),
        P(),
        P(),
        P(),
    )
    out_specs = (P(("grp", "row", "col")), P(("grp", "row", "col")))
    return jax.shard_map(local, mesh=mesh, in_specs=in_specs, out_specs=out_specs, check_vma=False)
```

```python
import functools

import jax
import jax.numpy as jnp
from jax import lax
from jax.experimental import pallas as pl
from jax.experimental.pallas import tpu as pltpu
from jax.sharding import PartitionSpec as P

MESH = pl.DeviceIdType.MESH

gelu_scale = 0.7978845608028654
gelu_cubic = 0.044715


def position():
    return lax.axis_index("grp"), lax.axis_index("row"), lax.axis_index("col")


def same_place(one, other):
    return (one[0] == other[0]) & (one[1] == other[1]) & (one[2] == other[2])


def row_count(r):
    return 1 + jnp.where(r > 0, 1, 0) + jnp.where(r < 7, 1, 0)


def in_vmem(count):
    return [pl.BlockSpec(memory_space=pltpu.VMEM)] * count


def b16(*shape):
    return jax.ShapeDtypeStruct(shape, jnp.bfloat16)


def transposed_dot(one, other):
    return lax.dot_general(one, other, (((0,), (0,)), ((), ())), preferred_element_type=jnp.float32)


def side_by_side(value):
    cols = value.shape[0]
    at = lax.broadcasted_iota(jnp.int32, value.shape, 0)
    before = jnp.where(at == 0, 0.0, pltpu.roll(value, 1, 0))
    after = jnp.where(at == cols - 1, 0.0, pltpu.roll(value, cols - 1, 0))
    return jnp.concatenate([before, value, after], axis=1).astype(jnp.bfloat16)


def three_rows(ref, row, count):
    parts = [ref[pl.ds(row + step, count)].reshape(-1, ref.shape[-1]) for step in range(3)]
    return jnp.concatenate(parts, axis=1)


def dot32(one, other):
    return jnp.dot(one, other, preferred_element_type=jnp.float32)


def gelu_both(preact, slope_too):
    square = preact * preact
    inner_tanh = jnp.tanh(gelu_scale * preact * (1.0 + gelu_cubic * square))
    half = 0.5 * (1.0 + inner_tanh)
    value = preact * half
    if not slope_too:
        return value, None
    bend = (0.5 * gelu_scale) * (1.0 + 3.0 * gelu_cubic * square)
    return value, half + preact * (1.0 - inner_tanh * inner_tanh) * bend


def turned_columns(columns, out_ref):
    @pl.loop(0, 8)
    def _(f):
        value = columns[f]
        for dr in range(3):
            for k in range(3):
                block = value[dr : dr + 8, :, 128 * k : 128 * (k + 1)].reshape(128, 128)
                place = pl.ds(pl.multiple_of(128 * f, 128), 128)
                out_ref[dr, 128 * k : 128 * (k + 1), place] = block.T


def perceptual_kernel(
    near_hbm, guide_hbm, vgg_first_ref, vgg_second_ref, vgg_third_ref, hidden_hbm, cells_hbm,
    out_ref, hidden_turned_hbm, cells_turned_hbm,
    hidden_ref, cells_ref, hidden_turned, cells_turned, store_sem, near_ref, guide_ref, load_sem, first32, w1_ref, w1_back32, w1_back_ref, planes_ref, guides,
    taps, act1, slope1, pooled, delta3, diff2, slope2, delta2, delta1, tmp, pixels, strip,
    w2_ref, w3_ref, w3_back_ref, w2_back_ref, send_sem, recv_sem, own_sem,
):
    g, r, c = position()
    me = (g, r, c)
    barrier = pltpu.get_barrier_semaphore()
    perceives = g < 3
    own_frame = 8 * g + c
    home = own_frame // 6
    place = lax.rem(own_frame, 6)
    ahead = perceives & (place == 0) & (home > 0)
    behind = perceives & (place == 5) & (home < 3)

    def sources(do):
        for slot in range(8):
            source_frame = 6 * g - 1 + slot

            def each(step, slot=slot, source_frame=source_frame):
                source = (source_frame // 8, r + step, lax.rem(source_frame, 8))
                pl.when(jnp.logical_not(same_place(source, me)))(
                    functools.partial(do, step, slot, source)
                )

            pl.when((source_frame >= 0) & (source_frame < 24))(functools.partial(on_rows, r, each))

    def greet(step, slot, source):
        pl.semaphore_signal(barrier, inc=1, device_id=source, device_id_type=MESH)

    loads = [
        pltpu.make_async_copy(near_hbm, near_ref, load_sem.at[0]),
        pltpu.make_async_copy(guide_hbm, guide_ref, load_sem.at[1]),
        pltpu.make_async_copy(hidden_hbm, hidden_ref, load_sem.at[2]),
        pltpu.make_async_copy(cells_hbm, cells_ref, load_sem.at[3]),
    ]
    stores = [
        pltpu.make_async_copy(hidden_turned, hidden_turned_hbm, store_sem.at[0]),
        pltpu.make_async_copy(cells_turned, cells_turned_hbm, store_sem.at[1]),
    ]
    for load in loads:
        load.start()
    sources(greet)
    weight = vgg_first_ref[...].astype(jnp.float32)
    first32[...] = jnp.zeros((72, 128), jnp.float32)
    w1_back32[...] = jnp.zeros((8, 1152), jnp.float32)
    for t in range(9):
        block = weight[3 * t : 3 * t + 3]
        first32[8 * t : 8 * t + 3, 0:64] = block
        first32[8 * t + 3 : 8 * t + 6, 64:128] = block
        w1_back32[0:3, 128 * (8 - t) : 128 * (8 - t) + 64] = block
    w1_ref[...] = first32[...].astype(jnp.bfloat16)
    w1_back_ref[...] = w1_back32[...].astype(jnp.bfloat16)
    lay_out_perceptual(vgg_second_ref, vgg_third_ref, w2_ref, w3_ref, w3_back_ref, w2_back_ref)
    row0 = 8 * r - 8
    for load in loads[:2]:
        load.wait()
    kind = lax.broadcasted_iota(jnp.int32, (8, 128), 0)
    block = lax.broadcasted_iota(jnp.int32, (8, 128), 1) // 16
    for part in range(3):
        guides[...] = guide_ref[part].astype(jnp.float32)
        tiles = [near_ref[part, column].astype(jnp.float32)[0:8] for column in range(8)]
        here = (kind < 3) & (row0 + 8 * part >= 0) & (row0 + 8 * part < 64)
        seen = (row0 + 8 * part >= 0) & (row0 + 8 * part < 64)
        for i in range(8):
            image = jnp.zeros((8, 128), jnp.float32)
            for column in range(8):
                turned = pltpu.roll(tiles[column], (16 * column - 16 * i) % 128, 1)
                image = jnp.where(block == column, turned, image)
            planes_ref[8 * part + i] = jnp.where(here, image, 0.0)
            planes_ref[8 * part + i, 3:6] = jnp.where(seen, guides[pl.ds(i, 3, 8)], 0.0)
    lane = lax.broadcasted_iota(jnp.int32, (192, 128), 1)
    planes = planes_ref[...].reshape(192, 128)
    before = jnp.where(lane == 0, 0.0, pltpu.roll(planes, 1, 1))
    after = jnp.where(lane == 127, 0.0, pltpu.roll(planes, 127, 1))
    taps[:, 0:8] = before.reshape(24, 8, 128)
    taps[:, 8:16] = planes.reshape(24, 8, 128)
    taps[:, 16:24] = after.reshape(24, 8, 128)

    def shown(row):
        return (row0 + row >= 0) & (row0 + row < 64)

    def kept(row, value):
        return jnp.where(shown(row), value, 0.0)

    def first_rows(low, high, slope_too):
        @pl.loop(low, high, unroll=2)
        def _(i):
            cells = taps[pl.ds(i, 3)].reshape(72, 128).astype(jnp.bfloat16)
            value, slope = gelu_both(transposed_dot(cells, w1_ref[...]), slope_too)
            act1[i] = side_by_side(kept(i + 1, value))
            if slope_too:
                slope1[i - 6] = slope

    first_rows(0, 6, False)
    first_rows(6, 16, True)
    first_rows(16, 22, False)

    def second_rows(low, high, slope_too):
        @pl.loop(low, high, unroll=2)
        def _(p):
            plane = dot32(three_rows(act1, 2 * p, 2), w2_ref[...])
            value, slope = gelu_both(plane, slope_too)
            value = kept(2 * p + 2, value)
            if slope_too:
                difference = 0.25 * (value - pltpu.roll(value, 64, 1))
                diff2[pl.ds(2 * p - 4, 2)] = difference.reshape(2, 128, 128)
                slope2[pl.ds(2 * p - 4, 2)] = slope.reshape(2, 128, 128)
            tmp[...] = value[:128] + value[128:]
            mean = 0.25 * (tmp[pl.ds(0, 64, 2)] + tmp[pl.ds(1, 64, 2)])
            pooled[p] = side_by_side(mean)

    second_rows(0, 2, False)
    second_rows(2, 8, True)
    second_rows(8, 10, False)

    @pl.loop(0, 4, unroll=2)
    def _(half):
        j = 2 * half
        plane = dot32(three_rows(pooled, j, 2), w3_ref[...])
        value, slope = gelu_both(plane[:, :128], True)
        guide, _ = gelu_both(plane[:, 128:], False)
        delta = 0.5 * (value - guide) * slope
        delta3[j] = side_by_side(kept(2 * j + 4, delta[:64]))
        delta3[j + 1] = side_by_side(kept(2 * j + 6, delta[64:]))

    @pl.loop(0, 6, unroll=3)
    def _(m):
        grad = 0.25 * dot32(three_rows(delta3, m, 1), w3_back_ref[...])
        tmp[pl.ds(0, 64, 2)] = grad
        tmp[pl.ds(1, 64, 2)] = grad
        spread = tmp[...]
        for k in range(2):
            delta = (spread + diff2[2 * m + k]) * slope2[2 * m + k]
            delta2[2 * m + k] = side_by_side(kept(2 * m + 6, delta))

    @pl.loop(0, 5, unroll=5)
    def _(half):
        n = 2 * half
        grad = dot32(three_rows(delta2, n, 2), w2_back_ref[...])
        for k in range(2):
            delta = grad[128 * k : 128 * (k + 1)] * slope1[n + k]
            delta1[n + k] = side_by_side(kept(n + k + 7, delta))

    @pl.loop(0, 8, unroll=4)
    def _(q):
        grad = lax.dot_general(
            w1_back_ref[...],
            three_rows(delta1, q, 1),
            (((1,), (1,)), ((), ())),
            preferred_element_type=jnp.float32,
        )
        own = planes_ref[q + 8]
        direct = (1.0 / 6.0) * (own - pltpu.roll(own, 5, 0))
        pixels[pl.ds(pl.multiple_of(q * 8, 8), 8)] = grad + direct

    colour_rows = [pixels[pl.ds(k, 8, 8)] for k in range(3)]
    third = lax.broadcasted_iota(jnp.int32, (8, 128), 1) // 32
    for column in range(8):
        turned = [pltpu.roll(v, (32 * k + 8 - 16 * column) % 128, 1) for k, v in enumerate(colour_rows)]
        part = jnp.where(third == 0, turned[0], jnp.where(third == 1, turned[1], turned[2]))
        strip[column] = jnp.concatenate([part, jnp.zeros((8, 128), jnp.float32)], axis=0).astype(jnp.bfloat16)

    groups = jnp.where(perceives, 1, 0) + jnp.where(ahead, 1, 0) + jnp.where(behind, 1, 0)
    to_itself = perceives & (home == g) | ahead & (home == g + 1) | behind & (home == g - 1)
    awaited = 8 * row_count(r) * groups - jnp.where(to_itself, 1, 0)
    pl.when(perceives)(lambda: pl.semaphore_wait(barrier, awaited))

    def targets(do):
        for kind, (group, needed) in enumerate(((home, perceives), (home - 1, ahead), (home + 1, behind))):

            def each(step, kind=kind, group=group):
                for column in range(8):
                    peer = (group, r + step, column)
                    do(kind, step, column, peer, jnp.logical_not(same_place(peer, me)))

            pl.when(needed)(functools.partial(on_rows, r, each))

    def outgoing(kind, step, column, peer):
        place_there = own_frame - 6 * peer[0] + 1
        return pltpu.make_async_remote_copy(
            src_ref=strip.at[column],
            dst_ref=out_ref.at[place_there, 1 - step],
            send_sem=send_sem.at[kind, step + 1, column],
            recv_sem=recv_sem.at[place_there, 1 - step],
            device_id=peer,
            device_id_type=MESH,
        )

    def kept():
        return pltpu.make_async_copy(strip.at[c], out_ref.at[own_frame - 6 * g + 1, 1], own_sem)

    def start(kind, step, column, peer, away):
        pl.when(away)(lambda: outgoing(kind, step, column, peer).start())
        if step == 0:
            pl.when(jnp.logical_not(away))(lambda: kept().start())

    def finish(kind, step, column, peer, away):
        pl.when(away)(lambda: outgoing(kind, step, column, peer).wait_send())
        if step == 0:
            pl.when(jnp.logical_not(away))(lambda: kept().wait())

    def arrive(step, slot, source):
        pltpu.make_async_remote_copy(
            src_ref=strip.at[0],
            dst_ref=out_ref.at[slot, step + 1],
            send_sem=send_sem.at[0, 0, 0],
            recv_sem=recv_sem.at[slot, step + 1],
            device_id=source,
            device_id_type=MESH,
        ).wait_recv()

    targets(start)
    loads[2].wait()
    turned_columns(hidden_ref, hidden_turned)
    stores[0].start()
    loads[3].wait()
    turned_columns(cells_ref, cells_turned)
    stores[1].start()
    sources(arrive)
    targets(finish)
    for store in stores:
        store.wait()


def perceptual_strip(*operands):
    f32, half = jnp.float32, jnp.bfloat16
    return pl.pallas_call(
        perceptual_kernel,
        out_shape=(b16(8, 3, 16, 128), b16(3, 384, 1024), b16(3, 384, 1024)),
        in_specs=places("hhvvvhh"),
        out_specs=tuple(places("vhh")),
        scratch_shapes=[
            pltpu.VMEM((8, 10, 16, 384), half),
            pltpu.VMEM((8, 10, 16, 384), half),
            pltpu.VMEM((3, 384, 1024), half),
            pltpu.VMEM((3, 384, 1024), half),
            pltpu.SemaphoreType.DMA((2,)),
            pltpu.VMEM((3, 8, 16, 128), half),
            pltpu.VMEM((3, 32, 128), half),
            pltpu.SemaphoreType.DMA((4,)),
            pltpu.VMEM((72, 128), f32),
            pltpu.VMEM((72, 128), half),
            pltpu.VMEM((8, 1152), f32),
            pltpu.VMEM((8, 1152), half),
            pltpu.VMEM((24, 8, 128), f32),
            pltpu.VMEM((32, 128), f32),
            pltpu.VMEM((24, 24, 128), f32),
            pltpu.VMEM((22, 128, 384), half),
            pltpu.VMEM((10, 128, 128), f32),
            pltpu.VMEM((10, 64, 384), half),
            pltpu.VMEM((8, 64, 384), half),
            pltpu.VMEM((12, 128, 128), f32),
            pltpu.VMEM((12, 128, 128), f32),
            pltpu.VMEM((12, 128, 384), half),
            pltpu.VMEM((10, 128, 384), half),
            pltpu.VMEM((128, 128), f32),
            pltpu.VMEM((64, 128), f32),
            pltpu.VMEM((8, 16, 128), half),
            pltpu.VMEM((1152, 128), half),
            pltpu.VMEM((1152, 256), half),
            pltpu.VMEM((1152, 128), half),
            pltpu.VMEM((1152, 128), half),
            pltpu.SemaphoreType.DMA((3, 3, 8)),
            pltpu.SemaphoreType.DMA((8, 3)),
            pltpu.SemaphoreType.DMA(()),
        ],
        compiler_params=pltpu.CompilerParams(
            collective_id=4, has_side_effects=True, vmem_limit_bytes=58 * 2**20
        ),
    )(*operands)


def taps_in_lanes(weight_ref, out_ref):
    for q in range(9):
        for k in range(3):
            tap = 3 * q + k
            out_ref[128 * q : 128 * (q + 1), 128 * k : 128 * (k + 1)] = weight_ref[
                128 * tap : 128 * (tap + 1), :
            ]


def turned_taps(weight_ref, out_ref):
    for q in range(9):
        for k in range(3):
            tap = 26 - 3 * q - k
            block = weight_ref[128 * tap : 128 * (tap + 1), :].astype(jnp.float32)
            out_ref[128 * q : 128 * (q + 1), 128 * k : 128 * (k + 1)] = block.T.astype(jnp.bfloat16)


def conv_rows(source, frame, starts, count, taps_ref):
    size = len(starts) * count * 32

    def near(dt, dr):
        rows = [source[frame + dt, pl.ds(start + dr, count)].reshape(count * 32, 128) for start in starts]
        return rows[0] if len(rows) == 1 else jnp.concatenate(rows, axis=0)

    parts = [near(dt, dr) for dt in range(3) for dr in range(3)]
    sums = dot32(jnp.concatenate(parts, axis=1), taps_ref[...])
    total = pltpu.roll(sums[:, :128], 1, 0) + sums[:, 128:256]
    total += pltpu.roll(sums[:, 256:], size - 1, 0)
    return total.reshape(len(starts) * count, 32, 128)


def silu_parts(preact):
    gate = 0.5 * (1.0 + jnp.tanh(0.5 * preact))
    return preact * gate, gate * (1.0 + preact * (1.0 - gate))


def on_rows(r, do):
    for step in (-1, 1, 0):
        pl.when((r + step >= 0) & (r + step < 8))(functools.partial(do, step))


def lay_out_perceptual(second_ref, third_ref, w2_out, w3_out, w3_back_out, w2_back_out):
    f32, half = jnp.float32, jnp.bfloat16
    for t in range(9):
        turned_block = second_ref[:, 64 * t : 64 * (t + 1)].astype(f32)
        block = turned_block.T
        wide = third_ref[64 * t : 64 * (t + 1), :].astype(f32)
        none, low, high = jnp.zeros((64, 64), f32), 128 * t, 128 * (8 - t)
        w2_out[low : low + 64] = jnp.concatenate([block, none], axis=1).astype(half)
        w2_out[low + 64 : low + 128] = jnp.concatenate([none, block], axis=1).astype(half)
        w3_out[low : low + 64, :128] = wide.astype(half)
        w3_out[low : low + 64, 128:] = jnp.zeros((64, 128), half)
        w3_out[low + 64 : low + 128, :128] = jnp.zeros((64, 128), half)
        w3_out[low + 64 : low + 128, 128:] = wide.astype(half)
        w2_back_out[high : high + 64] = jnp.concatenate([turned_block, none], axis=1).astype(half)
        w2_back_out[high + 64 : high + 128] = jnp.zeros((64, 128), half)
        turned = jnp.concatenate([wide.T, jnp.zeros((128, 64), f32)], axis=1)
        w3_back_out[high : high + 128] = turned.astype(half)


def forward_kernel(
    video_hbm, target_ref, first_hbm, second_hbm, rgb_ref,
    cells_hbm, hidden_hbm, slope1_hbm, slope2_hbm, turned_hbm, near_out, guide_out,
    video, first_ref, second_ref, rgb16, cells, hidden_out, slope1_out, slope2_out, load_sem, store_sem,
    tile, left_send, right_send, left_in, right_in, rows_in, to_west, to_east, from_east, from_west,
    halo_send, halo_recv, edge_send, edge_recv,
    taps1, taps2, turned, cell_columns, hidden_columns, colours, send_sem, recv_sem, own_sem,
):
    loads = [
        pltpu.make_async_copy(video_hbm, video, load_sem.at[0]),
        pltpu.make_async_copy(first_hbm, first_ref, load_sem.at[1]),
        pltpu.make_async_copy(second_hbm, second_ref, load_sem.at[2]),
    ]
    for load in loads:
        load.start()
    g, r, c = position()
    me = (g, r, c)
    f32, half = jnp.float32, jnp.bfloat16
    barrier = pltpu.get_barrier_semaphore()
    perceives = g < 3
    source_group = (8 * g + c) // 6
    west, east = lax.rem(c + 7, 8), lax.rem(c + 1, 8)
    has_up, has_down = r > 0, r < 7
    has_prev, has_next = g > 0, g < 3

    def sources(do):
        def each(step):
            for column in range(8):
                source = (source_group, r + step, column)
                pl.when(jnp.logical_not(same_place(source, me)))(
                    functools.partial(do, step, column, source)
                )

        pl.when(perceives)(lambda: on_rows(r, each))

    def signal(peer):
        pl.semaphore_signal(barrier, inc=1, device_id=peer, device_id_type=MESH)

    signal((g, r, west))
    signal((g, r, east))

    pl.when(has_up)(lambda: signal((g, r - 1, c)))
    pl.when(has_down)(lambda: signal((g, r + 1, c)))

    @pl.when(has_prev)
    def _():
        for column in (west, c, east):
            signal((g - 1, r, column))

    @pl.when(has_next)
    def _():
        for column in (west, c, east):
            signal((g + 1, r, column))

    sources(lambda step, column, source: signal(source))

    block = jnp.minimum(g, 2)
    guide = [target_ref[k, block, 0].astype(f32) for k in range(3)] + [jnp.zeros((8, 128), f32)]
    guide_out[1] = jnp.concatenate(guide, axis=0).astype(half)
    rgb16[...] = jnp.zeros((16, 128), f32)
    rgb16[0:3] = rgb_ref[...].astype(f32)
    loads[0].wait()

    for f in range(12):
        frame = 6 * g - 3 + f
        value = video[jnp.minimum(jnp.maximum(frame, 0), 23)]
        tile[f] = jnp.where((frame >= 0) & (frame < 24), value, jnp.zeros_like(value))

    to_itself = jnp.where(perceives & (2 * g + c < 6), 1, 0)
    groups_near = jnp.where(has_prev, 1, 0) + jnp.where(has_next, 1, 0)
    pl.semaphore_wait(barrier, 7 * row_count(r) + 1 + 3 * groups_near - to_itself)

    def remote(src, dst, slot, peer):
        return pltpu.make_async_remote_copy(
            src_ref=src,
            dst_ref=dst,
            send_sem=halo_send.at[slot],
            recv_sem=halo_recv.at[slot],
            device_id=peer,
            device_id_type=MESH,
        )

    sideways = [remote(left_send, right_in, 0, (g, r, west)), remote(right_send, left_in, 1, (g, r, east))]

    def to_row(row_index, rows, edge, guide_slot, first_slot):
        strip = tile.at[pl.ds(3, 6), pl.ds(rows, 3)]
        return [
            remote(strip, rows_in.at[edge, pl.ds(3, 6)], first_slot, (g, row_index, c)),
            remote(guide_out.at[1], guide_out.at[guide_slot], first_slot + 1, (g, row_index, c)),
        ]

    upward = to_row(r - 1, 0, 1, 2, 2)
    downward = to_row(r + 1, 5, 0, 0, 4)

    def across(edge):
        def copy(src, dst, slot, peer):
            return pltpu.make_async_remote_copy(
                src_ref=src,
                dst_ref=dst,
                send_sem=edge_send.at[edge, slot],
                recv_sem=edge_recv.at[edge, slot],
                device_id=peer,
                device_id_type=MESH,
            )

        mine, wests, easts = rows_in.at[edge], to_west.at[edge], to_east.at[edge]
        in_east, in_west, two = from_east.at[edge], from_west.at[edge], pl.ds(1, 2)
        level = [
            copy(wests, in_east.at[two], 0, (g, r, west)),
            copy(easts, in_west.at[two], 1, (g, r, east)),
        ]
        onward = [
            copy(mine.at[pl.ds(6, 3)], mine.at[pl.ds(0, 3)], 2, (g + 1, r, c)),
            copy(wests.at[1], in_east.at[0], 3, (g + 1, r, west)),
            copy(easts.at[1], in_west.at[0], 4, (g + 1, r, east)),
        ]
        back = [
            copy(mine.at[pl.ds(3, 3)], mine.at[pl.ds(9, 3)], 5, (g - 1, r, c)),
            copy(wests.at[0], in_east.at[3], 6, (g - 1, r, west)),
            copy(easts.at[0], in_west.at[3], 7, (g - 1, r, east)),
        ]
        return level, onward, back

    edges = [across(0), across(1)]

    def pass_on(edge):
        values = [rows_in[edge, 3 + f].astype(f32) for f in range(6)]
        for part in range(2):
            near = values[3 * part : 3 * part + 3]
            spare = jnp.zeros((3, 4, 128), f32)
            to_west[edge, part] = jnp.concatenate([v[:, 0:4] for v in near] + [spare], axis=1).astype(half)
            to_east[edge, part] = jnp.concatenate([v[:, 12:16] for v in near] + [spare], axis=1).astype(half)
        level, onward, back = edges[edge]
        start(level)
        pl.when(has_next)(lambda: start(onward))
        pl.when(has_prev)(lambda: start(back))

    def passed(edge, done):
        level, onward, back = edges[edge]
        done(level)
        if done is landed:
            pl.when(has_prev)(lambda: done(onward))
            pl.when(has_next)(lambda: done(back))
        else:
            pl.when(has_next)(lambda: done(onward))
            pl.when(has_prev)(lambda: done(back))

    def start(copies):
        for copy in copies:
            copy.start()

    def sent(copies):
        for copy in copies:
            copy.wait_send()

    def landed(copies):
        for copy in copies:
            copy.wait_recv()

    pl.when(has_up)(lambda: start(upward))
    pl.when(has_down)(lambda: start(downward))
    for line in range(8):
        near = [tile[f, line].astype(f32) for f in range(12)]
        left_send[line] = jnp.concatenate([v[0:4] for v in near], axis=0).astype(half)
        right_send[line] = jnp.concatenate([v[12:16] for v in near], axis=0).astype(half)
    start(sideways)

    loads[1].wait()
    taps_in_lanes(first_ref, taps1)
    loads[2].wait()
    taps_in_lanes(second_ref, taps2)

    def assemble(first_row, count, real, own, left, right, per):
        col = lax.broadcasted_iota(jnp.int32, (count, 32, 128), 1) + (16 * c - 8)
        shown = (col >= 0) & (col < 128) & real
        for part in range(12 // per):
            before, after = left(part).astype(f32), right(part).astype(f32)
            for k in range(per):
                f, eight = per * part + k, slice(8 * (k // 2), 8 * (k // 2) + 8)
                one = before[:, eight].reshape(8 * count, 128)
                two = after[:, eight].reshape(8 * count, 128)
                if k % 2 == 0:
                    one = pltpu.roll(one, 4, 0)
                else:
                    two = pltpu.roll(two, 8 * count - 4, 0)
                sides = [one.reshape(count, 8, 128), own(f).astype(f32), two.reshape(count, 8, 128)]
                frame = 6 * g - 3 + f
                here = shown & (frame >= 0) & (frame < 24)
                value = jnp.where(here, jnp.concatenate(sides, axis=1), 0.0)
                cells[f, first_row : first_row + count] = value.astype(half)

    row = lax.broadcasted_iota(jnp.int32, (6, 32, 128), 0)
    col = lax.broadcasted_iota(jnp.int32, (6, 32, 128), 1) + (16 * c - 8)
    in_cols = (col >= 0) & (col < 128)

    def in_frames(f):
        frame = 6 * g - 2 + f
        return jnp.where((frame >= 0) & (frame < 24), 1.0, 0.0)

    landed(sideways)
    assemble(
        3, 8, r >= 0, lambda f: tile[f],
        lambda part: left_in[:, 16 * part : 16 * (part + 1)],
        lambda part: right_in[:, 16 * part : 16 * (part + 1)],
        4,
    )

    def inner(f):
        value, slope = silu_parts(conv_rows(cells, f, (3,), 6, taps1))
        value = jnp.where(in_cols, value, 0.0) * in_frames(f)
        hidden_out[f, 3:9] = value.astype(half)
        slope1_out[f, 16:112] = slope[:, 8:24].reshape(96, 128)

    pl.loop(0, 2, unroll=2)(inner)

    @pl.when(has_up)
    def _():
        landed(downward)
        pass_on(0)

    @pl.when(has_down)
    def _():
        landed(upward)
        pass_on(1)

    pl.loop(2, 10, unroll=2)(inner)

    pl.when(has_up)(lambda: passed(0, landed))
    pl.when(has_down)(lambda: passed(1, landed))
    for edge, real in ((0, has_up), (1, has_down)):
        assemble(
            11 * edge, 3, real,
            lambda f, edge=edge: rows_in[edge, f],
            lambda part, edge=edge: from_west[edge, part],
            lambda part, edge=edge: from_east[edge, part],
            3,
        )
    image_row = jnp.where(row < 3, row, row + 6) + (8 * r - 2)
    in_image = in_cols & (image_row >= 0) & (image_row < 64)

    @pl.loop(0, 10, unroll=2)
    def _(f):
        value, slope = silu_parts(conv_rows(cells, f, (0, 9), 3, taps1))
        value = (jnp.where(in_image, value, 0.0) * in_frames(f)).astype(half)
        hidden_out[f, 0:3] = value[0:3]
        hidden_out[f, 9:12] = value[3:6]
        slope1_out[f, 0:16] = slope[2, 8:24]
        slope1_out[f, 112:128] = slope[3, 8:24]

    stores = [
        pltpu.make_async_copy(slope1_out.at[pl.ds(2, 6)], slope1_hbm, store_sem.at[0]),
        pltpu.make_async_copy(slope2_out, slope2_hbm, store_sem.at[1]),
        pltpu.make_async_copy(hidden_columns, hidden_hbm, store_sem.at[2]),
        pltpu.make_async_copy(cell_columns, cells_hbm, store_sem.at[3]),
        pltpu.make_async_copy(turned, turned_hbm, store_sem.at[4]),
    ]
    stores[0].start()

    def target(step, slot):
        frame = 6 * g + slot
        return (frame // 8, r + step, lax.rem(frame, 8))

    def outgoing(step, slot):
        return pltpu.make_async_remote_copy(
            src_ref=colours.at[slot],
            dst_ref=near_out.at[1 - step, c],
            send_sem=send_sem.at[step + 1, slot],
            recv_sem=recv_sem.at[1 - step, c],
            device_id=target(step, slot),
            device_id_type=MESH,
        )

    def kept(slot):
        return pltpu.make_async_copy(colours.at[slot], near_out.at[1, c], own_sem)

    def start_colour(slot, step):
        away = jnp.logical_not(same_place(target(step, slot), me))
        pl.when(away)(lambda: outgoing(step, slot).start())
        if step == 0:
            pl.when(jnp.logical_not(away))(lambda: kept(slot).start())

    def finish(slot, step):
        away = jnp.logical_not(same_place(target(step, slot), me))
        pl.when(away)(lambda: outgoing(step, slot).wait_send())
        if step == 0:
            pl.when(jnp.logical_not(away))(lambda: kept(slot).wait())

    def arrive(step, column, source):
        pltpu.make_async_remote_copy(
            src_ref=colours.at[0],
            dst_ref=near_out.at[step + 1, column],
            send_sem=send_sem.at[0, 0],
            recv_sem=recv_sem.at[step + 1, column],
            device_id=source,
            device_id_type=MESH,
        ).wait_recv()

    @pl.loop(0, 6)
    def _(slot):
        value, slope = silu_parts(conv_rows(hidden_out, slot + 1, (0,), 10, taps2))
        slope2_out[slot + 1] = slope
        own = value[1:9, 8:24].reshape(128, 128).astype(jnp.bfloat16)
        colour = lax.dot_general(
            rgb16[...].astype(half), own, (((1,), (1,)), ((), ())), preferred_element_type=jnp.float32
        )
        colours[slot] = colour.astype(jnp.bfloat16)
        on_rows(r, functools.partial(start_colour, slot))

    @pl.loop(0, 2)
    def _(end):
        slope2_out[7 * end] = silu_parts(conv_rows(hidden_out, 7 * end, (0,), 10, taps2))[1]

    stores[1].start()
    columns_in_lanes(hidden_out, 1, 1, hidden_columns)
    stores[2].start()
    columns_in_lanes(cells, 2, 2, cell_columns)
    stores[3].start()
    turned_taps(second_ref, turned)
    stores[4].start()
    sources(arrive)

    @pl.loop(0, 6)
    def _(slot):
        on_rows(r, functools.partial(finish, slot))

    for store in stores:
        store.wait()

    sent(sideways)
    pl.when(has_up)(lambda: sent(upward))
    pl.when(has_down)(lambda: sent(downward))
    pl.when(has_up)(lambda: passed(0, sent))
    pl.when(has_down)(lambda: passed(1, sent))


def columns_in_lanes(source, frame0, row0, out_ref):
    @pl.loop(0, 8)
    def _(f):
        value = source[f + frame0, pl.ds(row0, 10)].reshape(320, 128).astype(jnp.float32)
        parts = [pltpu.roll(value, 1, 0), value, pltpu.roll(value, 319, 0)]
        for k, part in enumerate(parts):
            own = part.reshape(10, 32, 128)[:, 8:24]
            out_ref[f, :, :, 128 * k : 128 * (k + 1)] = own.astype(jnp.bfloat16)


def weight_terms(columns, delta, terms, low, high):
    for q in range(low, high):
        cells = columns[q % 3, :, 128 * (q // 3) : 128 * (q // 3) + 768]
        terms[384 * q : 384 * (q + 1)] = dot32(cells, delta[...])


def by_chip(terms, out_ref, which, low, high):
    @pl.loop(low, high)
    def _(z):
        for chip in range(16):
            start = 432 * z + 27 * chip
            out_ref[which, 0, z, chip // 4, chip % 4] = terms[pl.ds(start, 16)].astype(jnp.bfloat16)
            out_ref[which, 1, z, chip // 4, chip % 4] = terms[pl.ds(start + 13, 16)].astype(jnp.bfloat16)


def backward_kernel(
    pixel_hbm, cells_hbm, hidden_hbm, slope1_hbm, slope2_hbm, turned_hbm, rgb_ref, out_ref,
    pixel_ref, cells_ref, hidden_ref, slope1_ref, slope2_ref, taps, rgb16, load_sem,
    field, delta, terms,
    sending, core_in, held, x_in, y_in, mid_x, mid_y, yy_in, xx_in, last, z_in, send_sem, recv_sem,
):
    g, r, c = position()
    loads = [
        pltpu.make_async_copy(src, dst, load_sem.at[k])
        for k, (src, dst) in enumerate(
            (
                (slope2_hbm, slope2_ref), (hidden_hbm, hidden_ref), (turned_hbm, taps),
                (slope1_hbm, slope1_ref), (cells_hbm, cells_ref), (pixel_hbm, pixel_ref),
            )
        )
    ]
    for load in loads[5:] + loads[:5]:
        load.start()
    zh, x, y, core = r // 4, lax.rem(r, 4), c // 2, lax.rem(c, 2)
    z = g * 2 + zh
    other = 1 - core

    def at_x(step):
        return (g, zh * 4 + lax.rem(x + step, 4), c)

    def at_y(step):
        return (g, r, lax.rem(y + step, 4) * 2 + core)

    def at_z(step):
        to = lax.rem(z + step, 8)
        return (to // 2, lax.rem(to, 2) * 4 + x, c)

    partner = (g, r, y * 2 + other)
    barrier = pltpu.get_barrier_semaphore()
    everyone = [partner] + [at_x(s) for s in (1, 2, 3)] + [at_y(s) for s in (1, 2, 3)]
    everyone += [at_z(s) for s in range(1, 8)]
    for peer in everyone:
        pl.semaphore_signal(barrier, inc=1, device_id=peer, device_id_type=MESH)

    def send(src, dst, which, slot, peer):
        copy = pltpu.make_async_remote_copy(
            src_ref=src,
            dst_ref=dst,
            send_sem=send_sem.at[which, slot],
            recv_sem=recv_sem.at[which, slot],
            device_id=peer,
            device_id_type=MESH,
        )
        copy.start()
        return copy

    f32, half = jnp.float32, jnp.bfloat16

    def summed(own, received):
        total = own.astype(f32)
        for k in range(3):
            total += received[k].astype(f32)
        return total.astype(half)

    def to_partner(which, part):
        some = pl.ds(4 * part, 4)
        return send(sending.at[which, other, some], core_in.at[which, some], which, 20 * part, partner)

    def first_step(which, part, copy):
        copy.wait()

        @pl.loop(4 * part, 4 * part + 4)
        def _(k):
            pair = sending[which, core, k].astype(f32) + core_in[which, k].astype(f32)
            held[which, k] = pair.astype(half)

        some = held.at[which, pl.ds(4 * part, 4)]
        if part == 0:
            return [
                send(some.at[:, lax.rem(x + s, 4)], x_in.at[which, s - 1], which, s, at_x(s)) for s in (1, 2, 3)
            ]
        return [
            send(some.at[:, :, lax.rem(y + s, 4)], y_in.at[which, s - 1], which, 3 + s, at_y(s)) for s in (1, 2, 3)
        ]

    def second_step(which, part, copies):
        for copy in copies:
            copy.wait()
        if part == 0:
            mid_x[which] = summed(held[which, 0:4, x], [x_in[which, k] for k in range(3)])
            return [
                send(mid_x.at[which, :, lax.rem(y + s, 4)], yy_in.at[which, s - 1], which, 6 + s, at_y(s))
                for s in (1, 2, 3)
            ]
        mid_y[which] = summed(held[which, 4:8, :, y], [y_in[which, k] for k in range(3)])
        return [
            send(mid_y.at[which, :, lax.rem(x + s, 4)], xx_in.at[which, s - 1], which, 9 + s, at_x(s))
            for s in (1, 2, 3)
        ]

    def third_step(which, copies):
        for copy in copies:
            copy.wait()
        last[which, 0:4] = summed(mid_x[which, :, y], [yy_in[which, k] for k in range(3)])
        last[which, 4:8] = summed(mid_y[which, :, x], [xx_in[which, k] for k in range(3)])
        return [
            send(last.at[which, lax.rem(z + s, 8)], z_in.at[which, s - 1], which, 12 + s, at_z(s))
            for s in range(1, 8)
        ]

    def result(which, copies):
        for copy in copies:
            copy.wait()
        total = last[which, z].astype(f32)
        for k in range(7):
            total += z_in[which, k].astype(f32)
        turned = pltpu.roll(total, 64, 1)
        low_half = lax.broadcasted_iota(jnp.int32, (16, 128), 1) < 64
        shifted = jnp.where(low_half, turned, pltpu.roll(turned, 15, 0))
        out_ref[which] = jnp.where(core == 1, shifted, total)

    rgb16[...] = jnp.zeros((16, 128), f32)
    rgb16[0:3] = rgb_ref[...].astype(f32)
    loads[0].wait()
    loads[5].wait()

    lane = lax.broadcasted_iota(jnp.int32, (8, 128), 1)
    col = lax.rem(lane, 32) + (16 * c - 8)
    in_cols = (lane < 96) & (col >= 0) & (col < 128)

    @pl.loop(0, 8, unroll=2)
    def _(f):
        frame = 6 * g - 1 + f
        known = in_cols & (frame >= 0) & (frame < 24)
        parts = []
        for part in range(3):
            seen = known & (r + part - 1 >= 0) & (r + part - 1 < 8)
            parts.append(jnp.where(seen, pixel_ref[f, part].astype(f32)[0:8], 0.0))
        turned = jnp.concatenate(parts, axis=0).T
        for i in range(10):
            hidden_grad = turned[0:32, i + 7 : i + 8] * rgb16[0:1]
            for k in (1, 2):
                hidden_grad += turned[32 * k : 32 * (k + 1), i + 7 : i + 8] * rgb16[k : k + 1]
            field[f, i] = (hidden_grad * slope2_ref[f, i]).astype(half)

    @pl.loop(0, 6)
    def _(f):
        own = field[f + 1, 1:9].astype(f32)[:, 8:24].reshape(128, 128).astype(half)
        delta[pl.ds(pl.multiple_of(128 * f, 128), 128)] = own

    loads[1].wait()
    terms[pl.ds(3456, 8)] = jnp.zeros((8, 128), f32)
    weight_terms(hidden_ref, delta, terms, 0, 5)
    by_chip(terms, sending, 1, 0, 4)
    pl.semaphore_wait(barrier, len(everyone))
    swap_low = to_partner(1, 0)
    weight_terms(hidden_ref, delta, terms, 5, 9)
    by_chip(terms, sending, 1, 4, 8)
    swap_high = to_partner(1, 1)
    second_low = first_step(1, 0, swap_low)
    loads[2].wait()
    loads[3].wait()

    def back_frame(f):
        back = conv_rows(field, f, (0,), 8, taps)[:, 8:24].reshape(128, 128)
        value = (back * slope1_ref[f]).astype(half)
        delta[pl.ds(pl.multiple_of(128 * f, 128), 128)] = value

    pl.loop(0, 2, unroll=2)(back_frame)
    second_high = first_step(1, 1, swap_high)
    pl.loop(2, 6, unroll=2)(back_frame)
    loads[4].wait()
    weight_terms(cells_ref, delta, terms, 0, 5)
    by_chip(terms, sending, 0, 0, 4)
    swap_low = to_partner(0, 0)
    weight_terms(cells_ref, delta, terms, 5, 9)
    by_chip(terms, sending, 0, 4, 8)
    swap_high = to_partner(0, 1)
    first_low = first_step(0, 0, swap_low)
    first_high = first_step(0, 1, swap_high)
    second_low = second_step(1, 0, second_low)
    second_high = second_step(1, 1, second_high)
    moves_second = third_step(1, second_low + second_high)
    first_low = second_step(0, 0, first_low)
    first_high = second_step(0, 1, first_high)
    moves_first = third_step(0, first_low + first_high)
    result(1, moves_second)
    result(0, moves_first)


def f32_shape(*shape):
    return jax.ShapeDtypeStruct(shape, jnp.float32)


def places(text):
    return [pl.BlockSpec(memory_space=pltpu.VMEM if letter == "v" else pltpu.HBM) for letter in text]


def talking_call(kernel, ident, mebibytes, in_places, out_places, outs, scratch, *operands):
    return pl.pallas_call(
        kernel,
        out_shape=tuple(outs),
        in_specs=places(in_places),
        out_specs=tuple(places(out_places)),
        scratch_shapes=scratch,
        compiler_params=pltpu.CompilerParams(
            collective_id=ident, has_side_effects=True, vmem_limit_bytes=mebibytes * 2**20
        ),
    )(*operands)


def local(dec_input, target, conv_first, conv_second, rgb_weight, vgg_first, vgg_second, vgg_third):
    g, r, c = position()
    channels = dec_input.shape[-1]
    half, f32, dma, vmem = jnp.bfloat16, jnp.float32, pltpu.SemaphoreType.DMA, pltpu.VMEM
    cells, hidden, slope1, slope2, turned, colour_near, guide_near = talking_call(
        forward_kernel,
        3,
        58,
        "hvhhv",
        "hhhhhvv",
        (
            b16(8, 10, 16, 384), b16(8, 10, 16, 384), f32_shape(6, 128, 128), f32_shape(8, 10, 32, 128),
            b16(1152, 384),
            b16(3, 8, 16, 128), b16(3, 32, 128),
        ),
        [
            vmem((24, 8, 16, 128), half), vmem((3456, 128), half), vmem((3456, 128), half), vmem((16, 128), f32),
            vmem((12, 14, 32, 128), half), vmem((10, 12, 32, 128), half),
            vmem((10, 128, 128), f32), vmem((8, 10, 32, 128), f32), dma((3,)), dma((5,)),
            vmem((12, 8, 16, 128), half), vmem((8, 48, 128), half), vmem((8, 48, 128), half),
            vmem((8, 48, 128), half), vmem((8, 48, 128), half), vmem((2, 12, 3, 16, 128), half),
            vmem((2, 2, 3, 16, 128), half), vmem((2, 2, 3, 16, 128), half),
            vmem((2, 4, 3, 16, 128), half), vmem((2, 4, 3, 16, 128), half),
            dma((6,)), dma((6,)), dma((2, 8)), dma((2, 8)),
            vmem((1152, 384), half), vmem((1152, 384), half), vmem((1152, 384), half),
            vmem((8, 10, 16, 384), half), vmem((8, 10, 16, 384), half), vmem((6, 16, 128), half),
            dma((3, 6)), dma((3, 8)), dma(()),
        ],
        dec_input.reshape(24, 8, 16, channels), target, conv_first, conv_second, rgb_weight,
    )
    pixels, hidden_turned, cells_turned = perceptual_strip(
        colour_near, guide_near, vgg_first, vgg_second.T, vgg_third, hidden, cells
    )
    sums = talking_call(
        backward_kernel,
        1,
        58,
        "hhhhhhv",
        "v",
        (f32_shape(2, 16, 128),),
        [
            vmem((8, 3, 16, 128), half),
            vmem((3, 384, 1024), half), vmem((3, 384, 1024), half), vmem((6, 128, 128), f32),
            vmem((8, 10, 32, 128), f32), vmem((1152, 384), half), vmem((16, 128), f32), dma((6,)),
            pltpu.VMEM((8, 10, 32, 128), half),
            pltpu.VMEM((768, 128), half),
            pltpu.VMEM((3464, 128), jnp.float32),
            pltpu.VMEM((2, 2, 8, 4, 4, 16, 128), half),
            pltpu.VMEM((2, 8, 4, 4, 16, 128), half),
            pltpu.VMEM((2, 8, 4, 4, 16, 128), half),
            pltpu.VMEM((2, 3, 4, 4, 16, 128), half),
            pltpu.VMEM((2, 3, 4, 4, 16, 128), half),
            pltpu.VMEM((2, 4, 4, 16, 128), half),
            pltpu.VMEM((2, 4, 4, 16, 128), half),
            pltpu.VMEM((2, 3, 4, 16, 128), half),
            pltpu.VMEM((2, 3, 4, 16, 128), half),
            pltpu.VMEM((2, 8, 16, 128), half),
            pltpu.VMEM((2, 7, 16, 128), half),
            dma((2, 21)),
            dma((2, 21)),
        ],
        pixels, cells_turned, hidden_turned, slope1, slope2, turned, rgb_weight,
    )
    flat = sums[0].reshape(2, 2048)[:, :1728]
    return flat[0], flat[1]


def solution(mesh):
    in_specs = (
        P(None, None, "row", "col", None),
        P(None, None, "col", "row", None),
        P(),
        P(),
        P(),
        P(),
        P(),
        P(),
    )
    out_specs = (P(("grp", "row", "col")), P(("grp", "row", "col")))
    return jax.shard_map(local, mesh=mesh, in_specs=in_specs, out_specs=out_specs, check_vma=False)
```

```python
import functools

import jax
import jax.numpy as jnp
from jax import lax
from jax.experimental import pallas as pl
from jax.experimental.pallas import tpu as pltpu
from jax.sharding import PartitionSpec as P

MESH = pl.DeviceIdType.MESH

gelu_scale = 0.7978845608028654
gelu_cubic = 0.044715


def position():
    return lax.axis_index("grp"), lax.axis_index("row"), lax.axis_index("col")


def same_place(one, other):
    return (one[0] == other[0]) & (one[1] == other[1]) & (one[2] == other[2])


def row_count(r):
    return 1 + jnp.where(r > 0, 1, 0) + jnp.where(r < 7, 1, 0)


def in_vmem(count):
    return [pl.BlockSpec(memory_space=pltpu.VMEM)] * count


def b16(*shape):
    return jax.ShapeDtypeStruct(shape, jnp.bfloat16)


def transposed_dot(one, other):
    return lax.dot_general(one, other, (((0,), (0,)), ((), ())), preferred_element_type=jnp.float32)


def side_by_side(value):
    cols = value.shape[0]
    at = lax.broadcasted_iota(jnp.int32, value.shape, 0)
    before = jnp.where(at == 0, 0.0, pltpu.roll(value, 1, 0))
    after = jnp.where(at == cols - 1, 0.0, pltpu.roll(value, cols - 1, 0))
    return jnp.concatenate([before, value, after], axis=1).astype(jnp.bfloat16)


def three_rows(ref, row, count):
    parts = [ref[pl.ds(row + step, count)].reshape(-1, ref.shape[-1]) for step in range(3)]
    return jnp.concatenate(parts, axis=1)


def dot32(one, other):
    return jnp.dot(one, other, preferred_element_type=jnp.float32)


def gelu_both(preact, slope_too):
    square = preact * preact
    inner_tanh = jnp.tanh(gelu_scale * preact * (1.0 + gelu_cubic * square))
    half = 0.5 * (1.0 + inner_tanh)
    value = preact * half
    if not slope_too:
        return value, None
    bend = (0.5 * gelu_scale) * (1.0 + 3.0 * gelu_cubic * square)
    return value, half + preact * (1.0 - inner_tanh * inner_tanh) * bend


def turned_columns(columns, out_ref):
    @pl.loop(0, 8)
    def _(f):
        value = columns[f]
        for dr in range(3):
            for k in range(3):
                block = value[dr : dr + 8, :, 128 * k : 128 * (k + 1)].reshape(128, 128)
                place = pl.ds(pl.multiple_of(128 * f, 128), 128)
                out_ref[dr, 128 * k : 128 * (k + 1), place] = block.T


def perceptual_kernel(
    near_hbm, guide_hbm, vgg_first_ref, vgg_second_ref, vgg_third_ref, hidden_hbm, cells_hbm,
    out_ref, hidden_turned_hbm, cells_turned_hbm,
    hidden_ref, cells_ref, hidden_turned, cells_turned, store_sem, near_ref, guide_ref, load_sem, first32, w1_ref, w1_back32, w1_back_ref, planes_ref, guides,
    taps, act1, slope1, pooled, delta3, diff2, slope2, delta2, delta1, tmp, pixels, strip,
    w2_ref, w3_ref, w3_back_ref, w2_back_ref, send_sem, recv_sem, own_sem,
):
    g, r, c = position()
    me = (g, r, c)
    barrier = pltpu.get_barrier_semaphore()
    perceives = g < 3
    own_frame = 8 * g + c
    home = own_frame // 6
    place = lax.rem(own_frame, 6)
    ahead = perceives & (place == 0) & (home > 0)
    behind = perceives & (place == 5) & (home < 3)

    def sources(do):
        for slot in range(8):
            source_frame = 6 * g - 1 + slot

            def each(step, slot=slot, source_frame=source_frame):
                source = (source_frame // 8, r + step, lax.rem(source_frame, 8))
                pl.when(jnp.logical_not(same_place(source, me)))(
                    functools.partial(do, step, slot, source)
                )

            pl.when((source_frame >= 0) & (source_frame < 24))(functools.partial(on_rows, r, each))

    def greet(step, slot, source):
        pl.semaphore_signal(barrier, inc=1, device_id=source, device_id_type=MESH)

    loads = [
        pltpu.make_async_copy(near_hbm, near_ref, load_sem.at[0]),
        pltpu.make_async_copy(guide_hbm, guide_ref, load_sem.at[1]),
        pltpu.make_async_copy(hidden_hbm, hidden_ref, load_sem.at[2]),
        pltpu.make_async_copy(cells_hbm, cells_ref, load_sem.at[3]),
    ]
    stores = [
        pltpu.make_async_copy(hidden_turned, hidden_turned_hbm, store_sem.at[0]),
        pltpu.make_async_copy(cells_turned, cells_turned_hbm, store_sem.at[1]),
    ]
    for load in loads:
        load.start()
    sources(greet)
    weight = vgg_first_ref[...].astype(jnp.float32)
    first32[...] = jnp.zeros((72, 128), jnp.float32)
    w1_back32[...] = jnp.zeros((8, 1152), jnp.float32)
    for t in range(9):
        block = weight[3 * t : 3 * t + 3]
        first32[8 * t : 8 * t + 3, 0:64] = block
        first32[8 * t + 3 : 8 * t + 6, 64:128] = block
        w1_back32[0:3, 128 * (8 - t) : 128 * (8 - t) + 64] = block
    w1_ref[...] = first32[...].astype(jnp.bfloat16)
    w1_back_ref[...] = w1_back32[...].astype(jnp.bfloat16)
    lay_out_perceptual(vgg_second_ref, vgg_third_ref, w2_ref, w3_ref, w3_back_ref, w2_back_ref)
    row0 = 8 * r - 8
    for load in loads[:2]:
        load.wait()
    kind = lax.broadcasted_iota(jnp.int32, (8, 128), 0)
    block = lax.broadcasted_iota(jnp.int32, (8, 128), 1) // 16
    for part in range(3):
        guides[...] = guide_ref[part].astype(jnp.float32)
        tiles = [near_ref[part, column].astype(jnp.float32)[0:8] for column in range(8)]
        here = (kind < 3) & (row0 + 8 * part >= 0) & (row0 + 8 * part < 64)
        seen = (row0 + 8 * part >= 0) & (row0 + 8 * part < 64)
        for i in range(8):
            image = jnp.zeros((8, 128), jnp.float32)
            for column in range(8):
                turned = pltpu.roll(tiles[column], (16 * column - 16 * i) % 128, 1)
                image = jnp.where(block == column, turned, image)
            planes_ref[8 * part + i] = jnp.where(here, image, 0.0)
            planes_ref[8 * part + i, 3:6] = jnp.where(seen, guides[pl.ds(i, 3, 8)], 0.0)
    lane = lax.broadcasted_iota(jnp.int32, (192, 128), 1)
    planes = planes_ref[...].reshape(192, 128)
    before = jnp.where(lane == 0, 0.0, pltpu.roll(planes, 1, 1))
    after = jnp.where(lane == 127, 0.0, pltpu.roll(planes, 127, 1))
    taps[:, 0:8] = before.reshape(24, 8, 128)
    taps[:, 8:16] = planes.reshape(24, 8, 128)
    taps[:, 16:24] = after.reshape(24, 8, 128)

    def shown(row):
        return (row0 + row >= 0) & (row0 + row < 64)

    def kept(row, value):
        return jnp.where(shown(row), value, 0.0)

    def first_rows(low, high, slope_too):
        @pl.loop(low, high, unroll=2)
        def _(i):
            cells = taps[pl.ds(i, 3)].reshape(72, 128).astype(jnp.bfloat16)
            value, slope = gelu_both(transposed_dot(cells, w1_ref[...]), slope_too)
            act1[i] = side_by_side(kept(i + 1, value))
            if slope_too:
                slope1[i - 6] = slope

    first_rows(0, 6, False)
    first_rows(6, 16, True)
    first_rows(16, 22, False)

    def second_rows(low, high, slope_too):
        @pl.loop(low, high, unroll=2)
        def _(p):
            plane = dot32(three_rows(act1, 2 * p, 2), w2_ref[...])
            value, slope = gelu_both(plane, slope_too)
            value = kept(2 * p + 2, value)
            if slope_too:
                difference = 0.25 * (value - pltpu.roll(value, 64, 1))
                diff2[pl.ds(2 * p - 4, 2)] = difference.reshape(2, 128, 128)
                slope2[pl.ds(2 * p - 4, 2)] = slope.reshape(2, 128, 128)
            tmp[...] = value[:128] + value[128:]
            mean = 0.25 * (tmp[pl.ds(0, 64, 2)] + tmp[pl.ds(1, 64, 2)])
            pooled[p] = side_by_side(mean)

    second_rows(0, 2, False)
    second_rows(2, 8, True)
    second_rows(8, 10, False)

    @pl.loop(0, 4, unroll=2)
    def _(half):
        j = 2 * half
        plane = dot32(three_rows(pooled, j, 2), w3_ref[...])
        value, slope = gelu_both(plane[:, :128], True)
        guide, _ = gelu_both(plane[:, 128:], False)
        delta = 0.5 * (value - guide) * slope
        delta3[j] = side_by_side(kept(2 * j + 4, delta[:64]))
        delta3[j + 1] = side_by_side(kept(2 * j + 6, delta[64:]))

    @pl.loop(0, 6, unroll=3)
    def _(m):
        grad = 0.25 * dot32(three_rows(delta3, m, 1), w3_back_ref[...])
        tmp[pl.ds(0, 64, 2)] = grad
        tmp[pl.ds(1, 64, 2)] = grad
        spread = tmp[...]
        for k in range(2):
            delta = (spread + diff2[2 * m + k]) * slope2[2 * m + k]
            delta2[2 * m + k] = side_by_side(kept(2 * m + 6, delta))

    @pl.loop(0, 5, unroll=5)
    def _(half):
        n = 2 * half
        grad = dot32(three_rows(delta2, n, 2), w2_back_ref[...])
        for k in range(2):
            delta = grad[128 * k : 128 * (k + 1)] * slope1[n + k]
            delta1[n + k] = side_by_side(kept(n + k + 7, delta))

    @pl.loop(0, 8, unroll=4)
    def _(q):
        grad = lax.dot_general(
            w1_back_ref[...],
            three_rows(delta1, q, 1),
            (((1,), (1,)), ((), ())),
            preferred_element_type=jnp.float32,
        )
        own = planes_ref[q + 8]
        direct = (1.0 / 6.0) * (own - pltpu.roll(own, 5, 0))
        pixels[pl.ds(pl.multiple_of(q * 8, 8), 8)] = grad + direct

    colour_rows = [pixels[pl.ds(k, 8, 8)] for k in range(3)]
    third = lax.broadcasted_iota(jnp.int32, (8, 128), 1) // 32
    for column in range(8):
        turned = [pltpu.roll(v, (32 * k + 8 - 16 * column) % 128, 1) for k, v in enumerate(colour_rows)]
        part = jnp.where(third == 0, turned[0], jnp.where(third == 1, turned[1], turned[2]))
        strip[column] = jnp.concatenate([part, jnp.zeros((8, 128), jnp.float32)], axis=0).astype(jnp.bfloat16)

    groups = jnp.where(perceives, 1, 0) + jnp.where(ahead, 1, 0) + jnp.where(behind, 1, 0)
    to_itself = perceives & (home == g) | ahead & (home == g + 1) | behind & (home == g - 1)
    awaited = 8 * row_count(r) * groups - jnp.where(to_itself, 1, 0)
    pl.when(perceives)(lambda: pl.semaphore_wait(barrier, awaited))

    def targets(do):
        for kind, (group, needed) in enumerate(((home, perceives), (home - 1, ahead), (home + 1, behind))):

            def each(step, kind=kind, group=group):
                for column in range(8):
                    peer = (group, r + step, column)
                    do(kind, step, column, peer, jnp.logical_not(same_place(peer, me)))

            pl.when(needed)(functools.partial(on_rows, r, each))

    def outgoing(kind, step, column, peer):
        place_there = own_frame - 6 * peer[0] + 1
        return pltpu.make_async_remote_copy(
            src_ref=strip.at[column],
            dst_ref=out_ref.at[place_there, 1 - step],
            send_sem=send_sem.at[kind, step + 1, column],
            recv_sem=recv_sem.at[place_there, 1 - step],
            device_id=peer,
            device_id_type=MESH,
        )

    def kept():
        return pltpu.make_async_copy(strip.at[c], out_ref.at[own_frame - 6 * g + 1, 1], own_sem)

    def start(kind, step, column, peer, away):
        pl.when(away)(lambda: outgoing(kind, step, column, peer).start())
        if step == 0:
            pl.when(jnp.logical_not(away))(lambda: kept().start())

    def finish(kind, step, column, peer, away):
        pl.when(away)(lambda: outgoing(kind, step, column, peer).wait_send())
        if step == 0:
            pl.when(jnp.logical_not(away))(lambda: kept().wait())

    def arrive(step, slot, source):
        pltpu.make_async_remote_copy(
            src_ref=strip.at[0],
            dst_ref=out_ref.at[slot, step + 1],
            send_sem=send_sem.at[0, 0, 0],
            recv_sem=recv_sem.at[slot, step + 1],
            device_id=source,
            device_id_type=MESH,
        ).wait_recv()

    targets(start)
    loads[2].wait()
    turned_columns(hidden_ref, hidden_turned)
    stores[0].start()
    loads[3].wait()
    turned_columns(cells_ref, cells_turned)
    stores[1].start()
    sources(arrive)
    targets(finish)
    for store in stores:
        store.wait()


def perceptual_strip(*operands):
    f32, half = jnp.float32, jnp.bfloat16
    return pl.pallas_call(
        perceptual_kernel,
        out_shape=(b16(8, 3, 16, 128), b16(3, 384, 1024), b16(3, 384, 1024)),
        in_specs=places("hhvvvhh"),
        out_specs=tuple(places("vhh")),
        scratch_shapes=[
            pltpu.VMEM((8, 10, 16, 384), half),
            pltpu.VMEM((8, 10, 16, 384), half),
            pltpu.VMEM((3, 384, 1024), half),
            pltpu.VMEM((3, 384, 1024), half),
            pltpu.SemaphoreType.DMA((2,)),
            pltpu.VMEM((3, 8, 16, 128), half),
            pltpu.VMEM((3, 32, 128), half),
            pltpu.SemaphoreType.DMA((4,)),
            pltpu.VMEM((72, 128), f32),
            pltpu.VMEM((72, 128), half),
            pltpu.VMEM((8, 1152), f32),
            pltpu.VMEM((8, 1152), half),
            pltpu.VMEM((24, 8, 128), f32),
            pltpu.VMEM((32, 128), f32),
            pltpu.VMEM((24, 24, 128), f32),
            pltpu.VMEM((22, 128, 384), half),
            pltpu.VMEM((10, 128, 128), f32),
            pltpu.VMEM((10, 64, 384), half),
            pltpu.VMEM((8, 64, 384), half),
            pltpu.VMEM((12, 128, 128), f32),
            pltpu.VMEM((12, 128, 128), f32),
            pltpu.VMEM((12, 128, 384), half),
            pltpu.VMEM((10, 128, 384), half),
            pltpu.VMEM((128, 128), f32),
            pltpu.VMEM((64, 128), f32),
            pltpu.VMEM((8, 16, 128), half),
            pltpu.VMEM((1152, 128), half),
            pltpu.VMEM((1152, 256), half),
            pltpu.VMEM((1152, 128), half),
            pltpu.VMEM((1152, 128), half),
            pltpu.SemaphoreType.DMA((3, 3, 8)),
            pltpu.SemaphoreType.DMA((8, 3)),
            pltpu.SemaphoreType.DMA(()),
        ],
        compiler_params=pltpu.CompilerParams(
            collective_id=4, has_side_effects=True, vmem_limit_bytes=58 * 2**20
        ),
    )(*operands)


def taps_in_lanes(weight_ref, out_ref):
    for q in range(9):
        for k in range(3):
            tap = 3 * q + k
            out_ref[128 * q : 128 * (q + 1), 128 * k : 128 * (k + 1)] = weight_ref[
                128 * tap : 128 * (tap + 1), :
            ]


def turned_taps(weight_ref, out_ref):
    for q in range(9):
        for k in range(3):
            tap = 26 - 3 * q - k
            block = weight_ref[128 * tap : 128 * (tap + 1), :].astype(jnp.float32)
            out_ref[128 * q : 128 * (q + 1), 128 * k : 128 * (k + 1)] = block.T.astype(jnp.bfloat16)


def conv_rows(source, frame, starts, count, taps_ref):
    size = len(starts) * count * 32

    def near(dt, dr):
        rows = [source[frame + dt, pl.ds(start + dr, count)].reshape(count * 32, 128) for start in starts]
        return rows[0] if len(rows) == 1 else jnp.concatenate(rows, axis=0)

    parts = [near(dt, dr) for dt in range(3) for dr in range(3)]
    sums = dot32(jnp.concatenate(parts, axis=1), taps_ref[...])
    total = pltpu.roll(sums[:, :128], 1, 0) + sums[:, 128:256]
    total += pltpu.roll(sums[:, 256:], size - 1, 0)
    return total.reshape(len(starts) * count, 32, 128)


def silu_parts(preact):
    gate = 0.5 * (1.0 + jnp.tanh(0.5 * preact))
    return preact * gate, gate * (1.0 + preact * (1.0 - gate))


def on_rows(r, do):
    for step in (-1, 1, 0):
        pl.when((r + step >= 0) & (r + step < 8))(functools.partial(do, step))


def lay_out_perceptual(second_ref, third_ref, w2_out, w3_out, w3_back_out, w2_back_out):
    f32, half = jnp.float32, jnp.bfloat16
    for t in range(9):
        turned_block = second_ref[:, 64 * t : 64 * (t + 1)].astype(f32)
        block = turned_block.T
        wide = third_ref[64 * t : 64 * (t + 1), :].astype(f32)
        none, low, high = jnp.zeros((64, 64), f32), 128 * t, 128 * (8 - t)
        w2_out[low : low + 64] = jnp.concatenate([block, none], axis=1).astype(half)
        w2_out[low + 64 : low + 128] = jnp.concatenate([none, block], axis=1).astype(half)
        w3_out[low : low + 64, :128] = wide.astype(half)
        w3_out[low : low + 64, 128:] = jnp.zeros((64, 128), half)
        w3_out[low + 64 : low + 128, :128] = jnp.zeros((64, 128), half)
        w3_out[low + 64 : low + 128, 128:] = wide.astype(half)
        w2_back_out[high : high + 64] = jnp.concatenate([turned_block, none], axis=1).astype(half)
        w2_back_out[high + 64 : high + 128] = jnp.zeros((64, 128), half)
        turned = jnp.concatenate([wide.T, jnp.zeros((128, 64), f32)], axis=1)
        w3_back_out[high : high + 128] = turned.astype(half)


def forward_kernel(
    video_hbm, target_ref, first_hbm, second_hbm, rgb_ref,
    cells_hbm, hidden_hbm, slope1_hbm, slope2_hbm, turned_hbm, near_out, guide_out,
    video, first_ref, second_ref, rgb16, cells, hidden_out, slope1_out, slope2_out, load_sem, store_sem,
    tile, left_send, right_send, left_in, right_in, rows_in, to_west, to_east, from_east, from_west,
    halo_send, halo_recv, edge_send, edge_recv,
    taps1, taps2, turned, cell_columns, hidden_columns, colours, send_sem, recv_sem, own_sem,
):
    loads = [
        pltpu.make_async_copy(video_hbm, video, load_sem.at[0]),
        pltpu.make_async_copy(first_hbm, first_ref, load_sem.at[1]),
        pltpu.make_async_copy(second_hbm, second_ref, load_sem.at[2]),
    ]
    for load in loads:
        load.start()
    g, r, c = position()
    me = (g, r, c)
    f32, half = jnp.float32, jnp.bfloat16
    barrier = pltpu.get_barrier_semaphore()
    perceives = g < 3
    source_group = (8 * g + c) // 6
    west, east = lax.rem(c + 7, 8), lax.rem(c + 1, 8)
    has_up, has_down = r > 0, r < 7
    has_prev, has_next = g > 0, g < 3

    def sources(do):
        def each(step):
            for column in range(8):
                source = (source_group, r + step, column)
                pl.when(jnp.logical_not(same_place(source, me)))(
                    functools.partial(do, step, column, source)
                )

        pl.when(perceives)(lambda: on_rows(r, each))

    def signal(peer):
        pl.semaphore_signal(barrier, inc=1, device_id=peer, device_id_type=MESH)

    signal((g, r, west))
    signal((g, r, east))

    pl.when(has_up)(lambda: signal((g, r - 1, c)))
    pl.when(has_down)(lambda: signal((g, r + 1, c)))

    @pl.when(has_prev)
    def _():
        for column in (west, c, east):
            signal((g - 1, r, column))

    @pl.when(has_next)
    def _():
        for column in (west, c, east):
            signal((g + 1, r, column))

    sources(lambda step, column, source: signal(source))

    block = jnp.minimum(g, 2)
    guide = [target_ref[k, block, 0].astype(f32) for k in range(3)] + [jnp.zeros((8, 128), f32)]
    guide_out[1] = jnp.concatenate(guide, axis=0).astype(half)
    rgb16[...] = jnp.zeros((16, 128), f32)
    rgb16[0:3] = rgb_ref[...].astype(f32)
    loads[0].wait()

    for f in range(12):
        frame = 6 * g - 3 + f
        value = video[jnp.minimum(jnp.maximum(frame, 0), 23)]
        tile[f] = jnp.where((frame >= 0) & (frame < 24), value, jnp.zeros_like(value))

    to_itself = jnp.where(perceives & (2 * g + c < 6), 1, 0)
    groups_near = jnp.where(has_prev, 1, 0) + jnp.where(has_next, 1, 0)
    pl.semaphore_wait(barrier, 7 * row_count(r) + 1 + 3 * groups_near - to_itself)

    def remote(src, dst, slot, peer):
        return pltpu.make_async_remote_copy(
            src_ref=src,
            dst_ref=dst,
            send_sem=halo_send.at[slot],
            recv_sem=halo_recv.at[slot],
            device_id=peer,
            device_id_type=MESH,
        )

    sideways = [remote(left_send, right_in, 0, (g, r, west)), remote(right_send, left_in, 1, (g, r, east))]

    def to_row(row_index, rows, edge, guide_slot, first_slot):
        strip = tile.at[pl.ds(3, 6), pl.ds(rows, 3)]
        return [
            remote(strip, rows_in.at[edge, pl.ds(3, 6)], first_slot, (g, row_index, c)),
            remote(guide_out.at[1], guide_out.at[guide_slot], first_slot + 1, (g, row_index, c)),
        ]

    upward = to_row(r - 1, 0, 1, 2, 2)
    downward = to_row(r + 1, 5, 0, 0, 4)

    def across(edge):
        def copy(src, dst, slot, peer):
            return pltpu.make_async_remote_copy(
                src_ref=src,
                dst_ref=dst,
                send_sem=edge_send.at[edge, slot],
                recv_sem=edge_recv.at[edge, slot],
                device_id=peer,
                device_id_type=MESH,
            )

        mine, wests, easts = rows_in.at[edge], to_west.at[edge], to_east.at[edge]
        in_east, in_west, two = from_east.at[edge], from_west.at[edge], pl.ds(1, 2)
        level = [
            copy(wests, in_east.at[two], 0, (g, r, west)),
            copy(easts, in_west.at[two], 1, (g, r, east)),
        ]
        onward = [
            copy(mine.at[pl.ds(6, 3)], mine.at[pl.ds(0, 3)], 2, (g + 1, r, c)),
            copy(wests.at[1], in_east.at[0], 3, (g + 1, r, west)),
            copy(easts.at[1], in_west.at[0], 4, (g + 1, r, east)),
        ]
        back = [
            copy(mine.at[pl.ds(3, 3)], mine.at[pl.ds(9, 3)], 5, (g - 1, r, c)),
            copy(wests.at[0], in_east.at[3], 6, (g - 1, r, west)),
            copy(easts.at[0], in_west.at[3], 7, (g - 1, r, east)),
        ]
        return level, onward, back

    edges = [across(0), across(1)]

    def pass_on(edge):
        values = [rows_in[edge, 3 + f].astype(f32) for f in range(6)]
        for part in range(2):
            near = values[3 * part : 3 * part + 3]
            spare = jnp.zeros((3, 4, 128), f32)
            to_west[edge, part] = jnp.concatenate([v[:, 0:4] for v in near] + [spare], axis=1).astype(half)
            to_east[edge, part] = jnp.concatenate([v[:, 12:16] for v in near] + [spare], axis=1).astype(half)
        level, onward, back = edges[edge]
        start(level)
        pl.when(has_next)(lambda: start(onward))
        pl.when(has_prev)(lambda: start(back))

    def passed(edge, done):
        level, onward, back = edges[edge]
        done(level)
        if done is landed:
            pl.when(has_prev)(lambda: done(onward))
            pl.when(has_next)(lambda: done(back))
        else:
            pl.when(has_next)(lambda: done(onward))
            pl.when(has_prev)(lambda: done(back))

    def start(copies):
        for copy in copies:
            copy.start()

    def sent(copies):
        for copy in copies:
            copy.wait_send()

    def landed(copies):
        for copy in copies:
            copy.wait_recv()

    pl.when(has_up)(lambda: start(upward))
    pl.when(has_down)(lambda: start(downward))
    for line in range(8):
        near = [tile[f, line].astype(f32) for f in range(12)]
        left_send[line] = jnp.concatenate([v[0:4] for v in near], axis=0).astype(half)
        right_send[line] = jnp.concatenate([v[12:16] for v in near], axis=0).astype(half)
    start(sideways)

    loads[1].wait()
    taps_in_lanes(first_ref, taps1)
    loads[2].wait()
    taps_in_lanes(second_ref, taps2)

    def assemble(first_row, count, real, own, left, right, per):
        col = lax.broadcasted_iota(jnp.int32, (count, 32, 128), 1) + (16 * c - 8)
        shown = (col >= 0) & (col < 128) & real
        for part in range(12 // per):
            before, after = left(part).astype(f32), right(part).astype(f32)
            for k in range(per):
                f, eight = per * part + k, slice(8 * (k // 2), 8 * (k // 2) + 8)
                one = before[:, eight].reshape(8 * count, 128)
                two = after[:, eight].reshape(8 * count, 128)
                if k % 2 == 0:
                    one = pltpu.roll(one, 4, 0)
                else:
                    two = pltpu.roll(two, 8 * count - 4, 0)
                sides = [one.reshape(count, 8, 128), own(f).astype(f32), two.reshape(count, 8, 128)]
                frame = 6 * g - 3 + f
                here = shown & (frame >= 0) & (frame < 24)
                value = jnp.where(here, jnp.concatenate(sides, axis=1), 0.0)
                cells[f, first_row : first_row + count] = value.astype(half)

    row = lax.broadcasted_iota(jnp.int32, (6, 32, 128), 0)
    col = lax.broadcasted_iota(jnp.int32, (6, 32, 128), 1) + (16 * c - 8)
    in_cols = (col >= 0) & (col < 128)

    def in_frames(f):
        frame = 6 * g - 2 + f
        return jnp.where((frame >= 0) & (frame < 24), 1.0, 0.0)

    landed(sideways)
    assemble(
        3, 8, r >= 0, lambda f: tile[f],
        lambda part: left_in[:, 16 * part : 16 * (part + 1)],
        lambda part: right_in[:, 16 * part : 16 * (part + 1)],
        4,
    )

    def inner(f):
        value, slope = silu_parts(conv_rows(cells, f, (3,), 6, taps1))
        value = jnp.where(in_cols, value, 0.0) * in_frames(f)
        hidden_out[f, 3:9] = value.astype(half)
        slope1_out[f, 16:112] = slope[:, 8:24].reshape(96, 128)

    pl.loop(0, 2, unroll=2)(inner)

    @pl.when(has_up)
    def _():
        landed(downward)
        pass_on(0)

    @pl.when(has_down)
    def _():
        landed(upward)
        pass_on(1)

    pl.loop(2, 10, unroll=2)(inner)

    pl.when(has_up)(lambda: passed(0, landed))
    pl.when(has_down)(lambda: passed(1, landed))
    for edge, real in ((0, has_up), (1, has_down)):
        assemble(
            11 * edge, 3, real,
            lambda f, edge=edge: rows_in[edge, f],
            lambda part, edge=edge: from_west[edge, part],
            lambda part, edge=edge: from_east[edge, part],
            3,
        )
    image_row = jnp.where(row < 3, row, row + 6) + (8 * r - 2)
    in_image = in_cols & (image_row >= 0) & (image_row < 64)

    @pl.loop(0, 10, unroll=2)
    def _(f):
        value, slope = silu_parts(conv_rows(cells, f, (0, 9), 3, taps1))
        value = (jnp.where(in_image, value, 0.0) * in_frames(f)).astype(half)
        hidden_out[f, 0:3] = value[0:3]
        hidden_out[f, 9:12] = value[3:6]
        slope1_out[f, 0:16] = slope[2, 8:24]
        slope1_out[f, 112:128] = slope[3, 8:24]

    stores = [
        pltpu.make_async_copy(slope1_out.at[pl.ds(2, 6)], slope1_hbm, store_sem.at[0]),
        pltpu.make_async_copy(slope2_out, slope2_hbm, store_sem.at[1]),
        pltpu.make_async_copy(hidden_columns, hidden_hbm, store_sem.at[2]),
        pltpu.make_async_copy(cell_columns, cells_hbm, store_sem.at[3]),
        pltpu.make_async_copy(turned, turned_hbm, store_sem.at[4]),
    ]
    stores[0].start()

    def target(step, slot):
        frame = 6 * g + slot
        return (frame // 8, r + step, lax.rem(frame, 8))

    def outgoing(step, slot):
        return pltpu.make_async_remote_copy(
            src_ref=colours.at[slot],
            dst_ref=near_out.at[1 - step, c],
            send_sem=send_sem.at[step + 1, slot],
            recv_sem=recv_sem.at[1 - step, c],
            device_id=target(step, slot),
            device_id_type=MESH,
        )

    def kept(slot):
        return pltpu.make_async_copy(colours.at[slot], near_out.at[1, c], own_sem)

    def start_colour(slot, step):
        away = jnp.logical_not(same_place(target(step, slot), me))
        pl.when(away)(lambda: outgoing(step, slot).start())
        if step == 0:
            pl.when(jnp.logical_not(away))(lambda: kept(slot).start())

    def finish(slot, step):
        away = jnp.logical_not(same_place(target(step, slot), me))
        pl.when(away)(lambda: outgoing(step, slot).wait_send())
        if step == 0:
            pl.when(jnp.logical_not(away))(lambda: kept(slot).wait())

    def arrive(step, column, source):
        pltpu.make_async_remote_copy(
            src_ref=colours.at[0],
            dst_ref=near_out.at[step + 1, column],
            send_sem=send_sem.at[0, 0],
            recv_sem=recv_sem.at[step + 1, column],
            device_id=source,
            device_id_type=MESH,
        ).wait_recv()

    @pl.loop(0, 6)
    def _(slot):
        value, slope = silu_parts(conv_rows(hidden_out, slot + 1, (0,), 10, taps2))
        slope2_out[slot + 1] = slope
        own = value[1:9, 8:24].reshape(128, 128).astype(jnp.bfloat16)
        colour = lax.dot_general(
            rgb16[...].astype(half), own, (((1,), (1,)), ((), ())), preferred_element_type=jnp.float32
        )
        colours[slot] = colour.astype(jnp.bfloat16)
        on_rows(r, functools.partial(start_colour, slot))

    @pl.loop(0, 2)
    def _(end):
        slope2_out[7 * end] = silu_parts(conv_rows(hidden_out, 7 * end, (0,), 10, taps2))[1]

    stores[1].start()
    columns_in_lanes(hidden_out, 1, 1, hidden_columns)
    stores[2].start()
    columns_in_lanes(cells, 2, 2, cell_columns)
    stores[3].start()
    turned_taps(second_ref, turned)
    stores[4].start()
    sources(arrive)

    @pl.loop(0, 6)
    def _(slot):
        on_rows(r, functools.partial(finish, slot))

    for store in stores:
        store.wait()

    sent(sideways)
    pl.when(has_up)(lambda: sent(upward))
    pl.when(has_down)(lambda: sent(downward))
    pl.when(has_up)(lambda: passed(0, sent))
    pl.when(has_down)(lambda: passed(1, sent))


def columns_in_lanes(source, frame0, row0, out_ref):
    @pl.loop(0, 8)
    def _(f):
        value = source[f + frame0, pl.ds(row0, 10)].reshape(320, 128).astype(jnp.float32)
        parts = [pltpu.roll(value, 1, 0), value, pltpu.roll(value, 319, 0)]
        for k, part in enumerate(parts):
            own = part.reshape(10, 32, 128)[:, 8:24]
            out_ref[f, :, :, 128 * k : 128 * (k + 1)] = own.astype(jnp.bfloat16)


def weight_terms(columns, delta, terms, low, high):
    for q in range(low, high):
        cells = columns[q % 3, :, 128 * (q // 3) : 128 * (q // 3) + 768]
        terms[384 * q : 384 * (q + 1)] = dot32(cells, delta[...])


def by_chip(terms, out_ref, which, low, high):
    @pl.loop(low, high)
    def _(z):
        for chip in range(16):
            start = 432 * z + 27 * chip
            out_ref[which, 0, z, chip // 4, chip % 4] = terms[pl.ds(start, 16)].astype(jnp.bfloat16)
            out_ref[which, 1, z, chip // 4, chip % 4] = terms[pl.ds(start + 13, 16)].astype(jnp.bfloat16)


def backward_kernel(
    pixel_hbm, cells_hbm, hidden_hbm, slope1_hbm, slope2_hbm, turned_hbm, rgb_ref, out_ref,
    pixel_ref, cells_ref, hidden_ref, slope1_ref, slope2_ref, taps, rgb16, load_sem,
    field, delta, terms,
    sending, core_in, held, x_in, y_in, mid_x, mid_y, yy_in, xx_in, last, z_in, send_sem, recv_sem,
):
    g, r, c = position()
    loads = [
        pltpu.make_async_copy(src, dst, load_sem.at[k])
        for k, (src, dst) in enumerate(
            (
                (slope2_hbm, slope2_ref), (hidden_hbm, hidden_ref), (turned_hbm, taps),
                (slope1_hbm, slope1_ref), (cells_hbm, cells_ref), (pixel_hbm, pixel_ref),
            )
        )
    ]
    for load in loads[5:] + loads[:5]:
        load.start()
    zh, x, y, core = r // 4, lax.rem(r, 4), c // 2, lax.rem(c, 2)
    z = g * 2 + zh
    other = 1 - core

    def at_x(step):
        return (g, zh * 4 + lax.rem(x + step, 4), c)

    def at_y(step):
        return (g, r, lax.rem(y + step, 4) * 2 + core)

    def at_z(step):
        to = lax.rem(z + step, 8)
        return (to // 2, lax.rem(to, 2) * 4 + x, c)

    partner = (g, r, y * 2 + other)
    barrier = pltpu.get_barrier_semaphore()
    everyone = [partner] + [at_x(s) for s in (1, 2, 3)] + [at_y(s) for s in (1, 2, 3)]
    everyone += [at_z(s) for s in range(1, 8)]
    for peer in everyone:
        pl.semaphore_signal(barrier, inc=1, device_id=peer, device_id_type=MESH)

    def send(src, dst, which, slot, peer):
        copy = pltpu.make_async_remote_copy(
            src_ref=src,
            dst_ref=dst,
            send_sem=send_sem.at[which, slot],
            recv_sem=recv_sem.at[which, slot],
            device_id=peer,
            device_id_type=MESH,
        )
        copy.start()
        return copy

    f32, half = jnp.float32, jnp.bfloat16

    def summed(own, received):
        total = own.astype(f32)
        for k in range(3):
            total += received[k].astype(f32)
        return total.astype(half)

    def to_partner(which, part):
        some = pl.ds(4 * part, 4)
        return send(sending.at[which, other, some], core_in.at[which, some], which, 20 * part, partner)

    def first_step(which, part, copy):
        copy.wait()

        @pl.loop(4 * part, 4 * part + 4)
        def _(k):
            pair = sending[which, core, k].astype(f32) + core_in[which, k].astype(f32)
            held[which, k] = pair.astype(half)

        some = held.at[which, pl.ds(4 * part, 4)]
        if part == 0:
            return [
                send(some.at[:, lax.rem(x + s, 4)], x_in.at[which, s - 1], which, s, at_x(s)) for s in (1, 2, 3)
            ]
        return [
            send(some.at[:, :, lax.rem(y + s, 4)], y_in.at[which, s - 1], which, 3 + s, at_y(s)) for s in (1, 2, 3)
        ]

    def second_step(which, part, copies):
        for copy in copies:
            copy.wait()
        if part == 0:
            mid_x[which] = summed(held[which, 0:4, x], [x_in[which, k] for k in range(3)])
            return [
                send(mid_x.at[which, :, lax.rem(y + s, 4)], yy_in.at[which, s - 1], which, 6 + s, at_y(s))
                for s in (1, 2, 3)
            ]
        mid_y[which] = summed(held[which, 4:8, :, y], [y_in[which, k] for k in range(3)])
        return [
            send(mid_y.at[which, :, lax.rem(x + s, 4)], xx_in.at[which, s - 1], which, 9 + s, at_x(s))
            for s in (1, 2, 3)
        ]

    def third_step(which, copies):
        for copy in copies:
            copy.wait()
        last[which, 0:4] = summed(mid_x[which, :, y], [yy_in[which, k] for k in range(3)])
        last[which, 4:8] = summed(mid_y[which, :, x], [xx_in[which, k] for k in range(3)])
        return [
            send(last.at[which, lax.rem(z + s, 8)], z_in.at[which, s - 1], which, 12 + s, at_z(s))
            for s in range(1, 8)
        ]

    def result(which, copies):
        for copy in copies:
            copy.wait()
        total = last[which, z].astype(f32)
        for k in range(7):
            total += z_in[which, k].astype(f32)
        turned = pltpu.roll(total, 64, 1)
        low_half = lax.broadcasted_iota(jnp.int32, (16, 128), 1) < 64
        shifted = jnp.where(low_half, turned, pltpu.roll(turned, 15, 0))
        out_ref[which] = jnp.where(core == 1, shifted, total)

    rgb16[...] = jnp.zeros((16, 128), f32)
    rgb16[0:3] = rgb_ref[...].astype(f32)
    loads[0].wait()
    loads[5].wait()

    lane = lax.broadcasted_iota(jnp.int32, (8, 128), 1)
    col = lax.rem(lane, 32) + (16 * c - 8)
    in_cols = (lane < 96) & (col >= 0) & (col < 128)

    @pl.loop(0, 8, unroll=2)
    def _(f):
        frame = 6 * g - 1 + f
        known = in_cols & (frame >= 0) & (frame < 24)
        parts = []
        for part in range(3):
            seen = known & (r + part - 1 >= 0) & (r + part - 1 < 8)
            parts.append(jnp.where(seen, pixel_ref[f, part].astype(f32)[0:8], 0.0))
        turned = jnp.concatenate(parts, axis=0).T
        for i in range(10):
            hidden_grad = turned[0:32, i + 7 : i + 8] * rgb16[0:1]
            for k in (1, 2):
                hidden_grad += turned[32 * k : 32 * (k + 1), i + 7 : i + 8] * rgb16[k : k + 1]
            field[f, i] = (hidden_grad * slope2_ref[f, i]).astype(half)

    @pl.loop(0, 6)
    def _(f):
        own = field[f + 1, 1:9].astype(f32)[:, 8:24].reshape(128, 128).astype(half)
        delta[pl.ds(pl.multiple_of(128 * f, 128), 128)] = own

    loads[1].wait()
    terms[pl.ds(3456, 8)] = jnp.zeros((8, 128), f32)
    weight_terms(hidden_ref, delta, terms, 0, 5)
    by_chip(terms, sending, 1, 0, 4)
    pl.semaphore_wait(barrier, len(everyone))
    swap_low = to_partner(1, 0)
    weight_terms(hidden_ref, delta, terms, 5, 9)
    by_chip(terms, sending, 1, 4, 8)
    swap_high = to_partner(1, 1)
    loads[2].wait()
    loads[3].wait()

    def back_frame(f):
        back = conv_rows(field, f, (0,), 8, taps)[:, 8:24].reshape(128, 128)
        value = (back * slope1_ref[f]).astype(half)
        delta[pl.ds(pl.multiple_of(128 * f, 128), 128)] = value

    pl.loop(0, 2, unroll=2)(back_frame)
    second_low = first_step(1, 0, swap_low)
    pl.loop(2, 6, unroll=2)(back_frame)
    second_high = first_step(1, 1, swap_high)
    loads[4].wait()
    weight_terms(cells_ref, delta, terms, 0, 5)
    by_chip(terms, sending, 0, 0, 4)
    swap_low = to_partner(0, 0)
    weight_terms(cells_ref, delta, terms, 5, 9)
    by_chip(terms, sending, 0, 4, 8)
    swap_high = to_partner(0, 1)
    first_low = first_step(0, 0, swap_low)
    first_high = first_step(0, 1, swap_high)
    second_low = second_step(1, 0, second_low)
    second_high = second_step(1, 1, second_high)
    moves_second = third_step(1, second_low + second_high)
    first_low = second_step(0, 0, first_low)
    first_high = second_step(0, 1, first_high)
    moves_first = third_step(0, first_low + first_high)
    result(1, moves_second)
    result(0, moves_first)


def f32_shape(*shape):
    return jax.ShapeDtypeStruct(shape, jnp.float32)


def places(text):
    return [pl.BlockSpec(memory_space=pltpu.VMEM if letter == "v" else pltpu.HBM) for letter in text]


def talking_call(kernel, ident, mebibytes, in_places, out_places, outs, scratch, *operands):
    return pl.pallas_call(
        kernel,
        out_shape=tuple(outs),
        in_specs=places(in_places),
        out_specs=tuple(places(out_places)),
        scratch_shapes=scratch,
        compiler_params=pltpu.CompilerParams(
            collective_id=ident, has_side_effects=True, vmem_limit_bytes=mebibytes * 2**20
        ),
    )(*operands)


def local(dec_input, target, conv_first, conv_second, rgb_weight, vgg_first, vgg_second, vgg_third):
    g, r, c = position()
    channels = dec_input.shape[-1]
    half, f32, dma, vmem = jnp.bfloat16, jnp.float32, pltpu.SemaphoreType.DMA, pltpu.VMEM
    cells, hidden, slope1, slope2, turned, colour_near, guide_near = talking_call(
        forward_kernel,
        3,
        58,
        "hvhhv",
        "hhhhhvv",
        (
            b16(8, 10, 16, 384), b16(8, 10, 16, 384), f32_shape(6, 128, 128), f32_shape(8, 10, 32, 128),
            b16(1152, 384),
            b16(3, 8, 16, 128), b16(3, 32, 128),
        ),
        [
            vmem((24, 8, 16, 128), half), vmem((3456, 128), half), vmem((3456, 128), half), vmem((16, 128), f32),
            vmem((12, 14, 32, 128), half), vmem((10, 12, 32, 128), half),
            vmem((10, 128, 128), f32), vmem((8, 10, 32, 128), f32), dma((3,)), dma((5,)),
            vmem((12, 8, 16, 128), half), vmem((8, 48, 128), half), vmem((8, 48, 128), half),
            vmem((8, 48, 128), half), vmem((8, 48, 128), half), vmem((2, 12, 3, 16, 128), half),
            vmem((2, 2, 3, 16, 128), half), vmem((2, 2, 3, 16, 128), half),
            vmem((2, 4, 3, 16, 128), half), vmem((2, 4, 3, 16, 128), half),
            dma((6,)), dma((6,)), dma((2, 8)), dma((2, 8)),
            vmem((1152, 384), half), vmem((1152, 384), half), vmem((1152, 384), half),
            vmem((8, 10, 16, 384), half), vmem((8, 10, 16, 384), half), vmem((6, 16, 128), half),
            dma((3, 6)), dma((3, 8)), dma(()),
        ],
        dec_input.reshape(24, 8, 16, channels), target, conv_first, conv_second, rgb_weight,
    )
    pixels, hidden_turned, cells_turned = perceptual_strip(
        colour_near, guide_near, vgg_first, vgg_second.T, vgg_third, hidden, cells
    )
    sums = talking_call(
        backward_kernel,
        1,
        58,
        "hhhhhhv",
        "v",
        (f32_shape(2, 16, 128),),
        [
            vmem((8, 3, 16, 128), half),
            vmem((3, 384, 1024), half), vmem((3, 384, 1024), half), vmem((6, 128, 128), f32),
            vmem((8, 10, 32, 128), f32), vmem((1152, 384), half), vmem((16, 128), f32), dma((6,)),
            pltpu.VMEM((8, 10, 32, 128), half),
            pltpu.VMEM((768, 128), half),
            pltpu.VMEM((3464, 128), jnp.float32),
            pltpu.VMEM((2, 2, 8, 4, 4, 16, 128), half),
            pltpu.VMEM((2, 8, 4, 4, 16, 128), half),
            pltpu.VMEM((2, 8, 4, 4, 16, 128), half),
            pltpu.VMEM((2, 3, 4, 4, 16, 128), half),
            pltpu.VMEM((2, 3, 4, 4, 16, 128), half),
            pltpu.VMEM((2, 4, 4, 16, 128), half),
            pltpu.VMEM((2, 4, 4, 16, 128), half),
            pltpu.VMEM((2, 3, 4, 16, 128), half),
            pltpu.VMEM((2, 3, 4, 16, 128), half),
            pltpu.VMEM((2, 8, 16, 128), half),
            pltpu.VMEM((2, 7, 16, 128), half),
            dma((2, 21)),
            dma((2, 21)),
        ],
        pixels, cells_turned, hidden_turned, slope1, slope2, turned, rgb_weight,
    )
    flat = sums[0].reshape(2, 2048)[:, :1728]
    return flat[0], flat[1]


def solution(mesh):
    in_specs = (
        P(None, None, "row", "col", None),
        P(None, None, "col", "row", None),
        P(),
        P(),
        P(),
        P(),
        P(),
        P(),
    )
    out_specs = (P(("grp", "row", "col")), P(("grp", "row", "col")))
    return jax.shard_map(local, mesh=mesh, in_specs=in_specs, out_specs=out_specs, check_vma=False)
```
